32 devices in a mesh: section: 4 (over x, core), span: 8 (over z, y).
Axes of the slice: x: 2, y: 2, z: 4, core: 2. Of those that a mesh axis runs over, the one named last changes fastest.
Arguments:
- inverse_blocks: bfloat16 [16, 768, 768], P('section'), may hold values from -1.2 to 1.2
- coupling: float32 [16, 768], P('section'), may hold values from 0.05 to 0.3
- sources: bfloat16 [4, 768, 3072], P('section', None, 'span'), may hold values from -36 to 36
Outputs:
- basis: bfloat16 [4, 768, 3072], P('section', None, 'span')
- upper: float32 [4, 48, 48], P('section')
The draws below stay inside these ranges and needn't reach their ends.
All inputs are finite; a program needn't handle non-finite values.
Results may differ from the reference program's by a relative error of at most 0.03.
Values may be sent and summed in bfloat16 or wider, within the bound.
No kernel may reach another device: no remote copies, remote signals or barrier semaphores. Data moves between devices by JAX's collectives and lax.ppermute only.
A program may use at most 64 MiB of HBM per device.

```python
import math
import jax
import jax.numpy as jnp
from jax import lax

K = 48
STATIONS = 4
FN = 768
NZ = 64
STATIONS_ALL = 16
N_SECTION = 4


def draw_inverse_blocks(key, part):
    noise = jax.random.truncated_normal(key, -4.0, 4.0, (STATIONS_ALL, FN, FN), jnp.float32)
    blocks = 0.9 * jnp.eye(FN, dtype=jnp.float32)[None] + 0.45 * noise / jnp.sqrt(float(FN))
    return blocks.astype(jnp.bfloat16)


def draw_sources(key, part):
    key_rows = jax.random.fold_in(key, 11)
    key_base = jax.random.fold_in(key, 12)
    row_scale = jnp.exp(jax.random.uniform(key_rows, (FN,), jnp.float32, jnp.log(0.3), jnp.log(3.0)))
    positions = jnp.arange(NZ, dtype=jnp.float32) / float(max(NZ - 1, 1))
    span_scale = 0.3 * jnp.power(10.0, positions)
    base = jax.random.truncated_normal(key_base, -4.0, 4.0, (N_SECTION, FN, NZ, K), jnp.float32)
    values = base * row_scale[None, :, None, None] * span_scale[None, None, :, None]
    return values.reshape(N_SECTION, FN, NZ * K).astype(jnp.bfloat16)


def block_levels(key, shape, cuts, least, top_value):
    def one(axis_at, shards_of):
        draws = jax.random.uniform(jax.random.fold_in(jax.random.fold_in(key, 6), axis_at), (shards_of,), jnp.float32, least / len(cuts), top_value / len(cuts))
        return jnp.repeat(jnp.exp(draws), shape[axis_at] // shards_of).reshape((-1,) + (1,) * (len(shape) - axis_at - 1))

    factor_of = one(*cuts[0])
    for cut in cuts[1:]:
        factor_of = factor_of * one(*cut)
    return factor_of


def setup_inputs(seed: int = 0) -> dict:
    seeds = jax.random.split(jax.random.key(seed), 4)
    inverse_blocks = draw_inverse_blocks(jax.random.fold_in(seeds[3], 71), 0)
    coupling = jnp.clip(jnp.exp(math.log(0.3) - 1.7917595 * jax.random.uniform(seeds[1], (STATIONS_ALL, FN), jnp.float32) ** block_levels(seeds[1], (STATIONS_ALL, FN), ((0, 4),), -0.2, 0.2)), 0.05, 0.3)
    sources = draw_sources(jax.random.fold_in(seeds[3], 71), 0)
    return dict(inverse_blocks=inverse_blocks, coupling=coupling, sources=sources)


def station_step(state, blocks, rates):
    wide = state.astype(jnp.float32)
    spread = jnp.roll(wide, -1, 1) + jnp.roll(wide, 1, 1) - 2.0 * wide
    update = (wide + rates[:, None, None] * spread).astype(jnp.bfloat16)
    moved = jnp.dot(blocks.astype(jnp.float32), update.reshape(FN, -1).astype(jnp.float32), preferred_element_type=jnp.float32)
    return moved.astype(jnp.bfloat16).reshape(state.shape)

def orthonormalize(state):
    flat_rows = state.reshape(FN * NZ, K)
    summed = jnp.dot(flat_rows.T.astype(jnp.float32), flat_rows.astype(jnp.float32), preferred_element_type=jnp.float32)
    scaled = summed / float(FN * NZ)
    factor = jnp.linalg.cholesky(scaled)
    inverse = jax.scipy.linalg.solve_triangular(factor, jnp.eye(K, dtype=jnp.float32), lower=True)
    basis_rows = jnp.dot(flat_rows.astype(jnp.float32), inverse.T, precision=lax.Precision.HIGHEST)
    return (basis_rows.astype(jnp.bfloat16).reshape(FN, NZ * K), factor.T)

def reference(inverse_blocks, coupling, sources):
    incoming = jnp.zeros((FN, NZ, K), jnp.bfloat16)
    bases = []
    uppers = []
    for group_index in reversed(range(N_SECTION)):
        added = incoming.astype(jnp.float32) + sources[group_index].reshape(FN, NZ, K).astype(jnp.float32)
        state = added.astype(jnp.bfloat16)
        for station in reversed(range(STATIONS)):
            place = group_index * STATIONS + station
            state = station_step(state, inverse_blocks[place], coupling[place])
        incoming = state
        basis_one, upper_one = orthonormalize(state)
        bases.append(basis_one)
        uppers.append(upper_one)
    bases = bases[::-1]
    uppers = uppers[::-1]
    return (jnp.stack(bases), jnp.stack(uppers))
```

```python
import jax
import jax.numpy as jnp
from jax import lax
from jax.sharding import PartitionSpec as P

K = 48
STATIONS = 4
FN = 768
HALF = K // 2
AXES = ("section", "span")


def march(state, inverse_blocks, coupling, grow):
    for station in reversed(range(STATIONS)):
        wide = state.astype(jnp.float32)
        if grow:
            wide = jnp.pad(wide, ((2, 2), (0, 0), (0, 0)))
        rates = coupling[station][None, None, :]
        center = wide[1:-1]
        update = center + rates * (wide[2:] + wide[:-2] - 2.0 * center)
        flat = update.astype(jnp.bfloat16).reshape(-1, FN)
        moved = lax.dot_general(
            flat, inverse_blocks[station], (((1,), (1,)), ((), ())), preferred_element_type=jnp.float32
        )
        state = moved.astype(jnp.bfloat16).reshape(update.shape)
    return state


def local(inverse_blocks, coupling, sources):
    sections = lax.axis_size("section")
    spans = lax.axis_size("span")
    points = sources.shape[2] // K
    pairs = spans // 2
    group = lax.axis_index("section")
    upper_half = lax.axis_index("span") % 2 == 1
    odd = group % 2 == 1

    def move(value, groups, down, shift, cross=False):
        routes = []
        for g in groups:
            for s in range(spans):
                target = ((s // 2 + shift) % pairs) * 2 + (s % 2 ^ int(cross))
                routes.append((g * spans + s, (g - down) * spans + target))
        return lax.ppermute(value, AXES, routes)

    odds = [g for g in range(sections) if g % 2 == 1]
    evens = [g for g in range(sections) if g % 2 == 0]

    source = sources[0].reshape(FN, points, K).transpose(1, 2, 0)
    mine = jnp.where(upper_half, source[:, HALF:], source[:, :HALF])
    other = jnp.where(upper_half, source[:, :HALF], source[:, HALF:])
    got_odd = move(other, odds, 0, 0, True)
    got_even = move(other, evens, 0, 0, True)
    got = jnp.where(odd, got_odd, got_even)
    paired = jnp.where(
        upper_half, jnp.concatenate([got, mine], 0), jnp.concatenate([mine, got], 0)
    )
    low = move(paired[-STATIONS:], evens, 0, 1)
    high = move(paired[:STATIONS], evens, 0, -1)
    paired_wide = jnp.concatenate([low, paired, high], 0)

    arrived = None
    own_part = jnp.zeros((points, HALF, FN), jnp.bfloat16)
    cross_part = jnp.zeros((points, HALF, FN), jnp.bfloat16)
    for g in reversed(range(1, sections, 2)):
        start = paired
        if arrived is not None:
            start = (arrived.astype(jnp.float32) + paired.astype(jnp.float32)).astype(jnp.bfloat16)
        share = march(start, inverse_blocks, coupling, True)
        width = 2 * STATIONS
        direct = move(share, [g], 1, 0)
        from_low = move(share[-width:], [g], 1, 1)
        from_high = move(share[:width], [g], 1, -1)
        middle = direct.astype(jnp.float32)
        total = jnp.concatenate(
            [
                middle[:width] + from_low.astype(jnp.float32),
                middle[width:-width],
                middle[-width:] + from_high.astype(jnp.float32),
            ],
            0,
        )
        whole = total[STATIONS:-STATIONS].astype(jnp.bfloat16)
        keep = jnp.where(upper_half, whole[points:], whole[:points])
        give = jnp.where(upper_half, whole[:points], whole[points:])
        back_own = move(keep, [g - 1], -1, 0)
        back_cross = move(give, [g - 1], -1, 0, True)
        start = (total + paired_wide.astype(jnp.float32)).astype(jnp.bfloat16)
        state = march(start, inverse_blocks, coupling, False)
        if g > 1:
            arrived = move(state, [g - 1], 1, 0)
        keep = jnp.where(upper_half, state[points:], state[:points])
        give = jnp.where(upper_half, state[:points], state[points:])
        own_part = jnp.where(group == g, back_own, jnp.where(group == g - 1, keep, own_part))
        cross_part = jnp.where(group == g, back_cross, jnp.where(group == g - 1, give, cross_part))
    cross_part = jnp.where(odd, cross_part, move(cross_part, evens, 0, 0, True))

    inlet = jnp.where(
        upper_half,
        jnp.concatenate([cross_part, own_part], 1),
        jnp.concatenate([own_part, cross_part], 1),
    )
    rows = inlet.reshape(points * K, FN)
    full = lax.dot_general(rows, rows, (((1,), (1,)), ((), ())), preferred_element_type=jnp.float32)
    partial_gram = full[:K, :K]
    for point in range(1, points):
        at = point * K
        partial_gram = partial_gram + full[at : at + K, at : at + K]

    def all_sum(value):
        stride = 1
        while stride < spans:
            radix = min(8, spans // stride)
            terms = [value]
            for digit in range(1, radix):
                routes = [(s, s ^ (digit * stride)) for s in range(spans)]
                terms.append(lax.ppermute(value, "span", routes))
            while len(terms) > 1:
                terms = [a + b for a, b in zip(terms[::2], terms[1::2])]
            value = terms[0]
            stride *= radix
        return value

    scaled = all_sum(partial_gram) / float(FN * points * spans)
    factor = jnp.linalg.cholesky(scaled)
    inverse = jax.scipy.linalg.solve_triangular(factor, jnp.eye(K, dtype=jnp.float32), lower=True)
    spread = jnp.kron(jnp.eye(points, dtype=jnp.float32), inverse.T)
    first = lax.reduce_precision(spread, 8, 7)
    second = spread - first
    basis = sum(
        lax.dot_general(
            rows, part.astype(jnp.bfloat16), (((0,), (0,)), ((), ())), preferred_element_type=jnp.float32
        )
        for part in (first, second)
    )
    return (basis.astype(jnp.bfloat16)[None], factor.T[None])


def solution(mesh):
    placed = (P("section", None, None), P("section", None), P("section", None, "span"))
    return jax.shard_map(
        local,
        mesh=mesh,
        in_specs=placed,
        out_specs=(P("section", None, "span"), P("section", None, None)),
        check_vma=False,
    )
```

```python
import jax
import jax.numpy as jnp
from jax import lax
from jax.sharding import PartitionSpec as P

K = 48
STATIONS = 4
FN = 768
HALF = K // 2
WIDE = 2 * STATIONS
AXES = ("section", "span")


def march(state, inverse_blocks, coupling, grow):
    for station in reversed(range(STATIONS)):
        wide = state.astype(jnp.float32)
        if grow:
            wide = jnp.pad(wide, ((2, 2), (0, 0), (0, 0)))
        rates = coupling[station][None, None, :]
        center = wide[1:-1]
        update = center + rates * (wide[2:] + wide[:-2] - 2.0 * center)
        flat = update.astype(jnp.bfloat16).reshape(-1, FN)
        moved = lax.dot_general(
            flat, inverse_blocks[station], (((1,), (1,)), ((), ())), preferred_element_type=jnp.float32
        )
        state = moved.astype(jnp.bfloat16).reshape(update.shape)
    return state


def added(state, more):
    return (state.astype(jnp.float32) + more.astype(jnp.float32)).astype(jnp.bfloat16)


def padded(state, before, after):
    return jnp.pad(state, ((before, after), (0, 0), (0, 0)))


def local(inverse_blocks, coupling, sources):
    sections = lax.axis_size("section")
    spans = lax.axis_size("span")
    points = sources.shape[2] // K
    pairs = spans // 2
    assert sections % 2 == 0 and spans % 2 == 0 and points == WIDE
    group = lax.axis_index("section")
    upper_half = lax.axis_index("span") % 2 == 1

    def pick(if_upper, if_lower):
        return jnp.where(upper_half, if_upper, if_lower)

    def place(g, pair, side):
        return g * spans + (pair % pairs) * 2 + side

    def regroup(value, groups, route):
        routes = []
        for g in range(sections):
            for pair in range(pairs):
                for side in range(2):
                    here = place(g, pair, side)
                    routes.append((here, place(g, *route(pair, side)) if g in groups else here))
        return lax.ppermute(value, AXES, routes)

    def partner(pair, side):
        return pair, 1 - side

    def outward(pair, side):
        return pair + 2 * side - 1, side

    def outward_cross(pair, side):
        return pair + 2 * side - 1, 1 - side

    def inward(pair, side):
        return pair + 1 - 2 * side, side

    def hop(value, g, shift=0):
        routes = [
            (place(g, pair, side), place(g - 1, pair + shift, side)) for pair in range(pairs) for side in range(2)
        ]
        return lax.ppermute(value, AXES, routes)

    def kind(g):
        return (sections - 1 - g) % 4

    def of_kind(*kinds):
        return [g for g in range(sections) if kind(g) in kinds]

    source = sources[0].reshape(FN, points, K).transpose(1, 2, 0)

    def gathered(source, groups, width, wide_groups):
        mine = pick(source[:, HALF:], source[:, :HALF])
        other = pick(source[:, :HALF], source[:, HALF:])
        got = regroup(other, groups, partner)
        pair_rows = pick(jnp.concatenate([got, mine], 0), jnp.concatenate([mine, got], 0))
        near_mine = pick(mine[points - width :], mine[:width])
        near_other = pick(other[points - width :], other[:width])
        same = regroup(near_mine, wide_groups, outward)
        cross = regroup(near_other, wide_groups, outward_cross)
        low = pick(same, cross)
        high = pick(cross, same)
        return pair_rows, jnp.concatenate([low, pair_rows, high], 0)

    first = of_kind(0)
    _, start_wide = gathered(source, first, WIDE, first)
    rest = None

    arrived = None
    zero = jnp.zeros((points, HALF, FN), jnp.bfloat16)
    keep, give, low_share, high_share = zero, zero, zero, zero
    for g in reversed(range(sections)):
        which = kind(g)
        if which == 0:
            start = start_wide if arrived is None else added(arrived, start_wide)
        elif which == 1:
            start = added(arrived, rest[1])
        elif which == 2:
            start = added(arrived, rest[0])
        else:
            start = added(arrived, padded(rest[0], STATIONS, STATIONS))
        state = march(start, inverse_blocks, coupling, which >= 2)
        if rest is None:
            later, state = lax.optimization_barrier((source, state))
            rest = gathered(later, of_kind(1, 2, 3), STATIONS, of_kind(1))
        if g > 0:
            arrived = hop(state, g)
            if which == 3:
                from_low = hop(state[-2 * WIDE :], g, 1)
                from_high = hop(state[: 2 * WIDE], g, -1)
                arrived = added(arrived, jnp.concatenate([from_low, from_high], 0))
        extra = (state.shape[0] - 2 * points) // 2
        inner = state[extra : extra + 2 * points]
        here = group == g
        keep = jnp.where(here, pick(inner[points:], inner[:points]), keep)
        give = jnp.where(here, pick(inner[:points], inner[points:]), give)
        if which >= 2:
            low = padded(state[:extra], WIDE - extra, 0)
            high = padded(state[-extra:], 0, WIDE - extra)
            low_share = jnp.where(here, low, low_share)
            high_share = jnp.where(here, high, high_share)

    own_part, cross_part = keep, zero
    for shrinking, growing, width in ((0, 2, STATIONS), (1, 3, WIDE)):
        both = of_kind(shrinking, growing)
        shares = of_kind(growing)
        here = kind_is(group, sections, shrinking, growing)
        got = regroup(give, both, partner)
        to_same = pick(low_share[WIDE - width :], high_share[:width])
        to_cross = pick(high_share[:width], low_share[WIDE - width :])
        same = regroup(to_same, shares, inward)
        cross = regroup(to_cross, shares, lambda pair, side: (pair + 2 * side - 1, 1 - side))
        fill = points - width
        same = pick(padded(same, fill, 0), padded(same, 0, fill))
        cross = pick(padded(cross, fill, 0), padded(cross, 0, fill))
        sharing = kind_is(group, sections, growing, growing)
        own_part = jnp.where(sharing, added(own_part, same), own_part)
        cross_part = jnp.where(here, jnp.where(sharing, added(got, cross), got), cross_part)

    inlet = pick(jnp.concatenate([cross_part, own_part], 1), jnp.concatenate([own_part, cross_part], 1))
    rows = inlet.reshape(points * K, FN)
    full = lax.dot_general(rows, rows, (((1,), (1,)), ((), ())), preferred_element_type=jnp.float32)
    gram = full[:K, :K]
    for point in range(1, points):
        at = point * K
        gram = gram + full[at : at + K, at : at + K]
    stride = 1
    while stride < spans:
        gram = gram + lax.ppermute(gram, "span", [(s, s ^ stride) for s in range(spans)])
        stride *= 2

    scaled = gram / float(FN * points * spans)
    factor = jnp.linalg.cholesky(scaled)
    inverse = jax.scipy.linalg.solve_triangular(factor, jnp.eye(K, dtype=jnp.float32), lower=True)
    spread = jnp.kron(jnp.eye(points, dtype=jnp.float32), inverse.T)
    rough = lax.reduce_precision(spread, 8, 7)
    basis = sum(
        lax.dot_general(
            rows, part.astype(jnp.bfloat16), (((0,), (0,)), ((), ())), preferred_element_type=jnp.float32
        )
        for part in (rough, spread - rough)
    )
    return (basis.astype(jnp.bfloat16)[None], factor.T[None])


def kind_is(group, sections, one, other):
    which = (sections - 1 - group) % 4
    return jnp.logical_or(which == one, which == other)


def solution(mesh):
    placed = (P("section", None, None), P("section", None), P("section", None, "span"))
    return jax.shard_map(
        local,
        mesh=mesh,
        in_specs=placed,
        out_specs=(P("section", None, "span"), P("section", None, None)),
        check_vma=False,
    )
```

```python
import jax
import jax.numpy as jnp
from jax import lax
from jax.sharding import PartitionSpec as P

K = 48
STATIONS = 4
FN = 768
HALF = K // 2
WIDE = 2 * STATIONS
AXES = ("section", "span")


def march(state, inverse_blocks, coupling, grow):
    for station in reversed(range(STATIONS)):
        wide = state.astype(jnp.float32)
        if grow:
            wide = jnp.pad(wide, ((2, 2), (0, 0), (0, 0)))
        rates = coupling[station][None, None, :]
        center = wide[1:-1]
        update = center + rates * (wide[2:] + wide[:-2] - 2.0 * center)
        flat = update.astype(jnp.bfloat16).reshape(-1, FN)
        moved = lax.dot_general(
            flat, inverse_blocks[station], (((1,), (1,)), ((), ())), preferred_element_type=jnp.float32
        )
        state = moved.astype(jnp.bfloat16).reshape(update.shape)
    return state


def added(state, more):
    return (state.astype(jnp.float32) + more.astype(jnp.float32)).astype(jnp.bfloat16)


def padded(state, before, after):
    return jnp.pad(state, ((before, after), (0, 0), (0, 0)))


def local(inverse_blocks, coupling, sources):
    sections = lax.axis_size("section")
    spans = lax.axis_size("span")
    points = sources.shape[2] // K
    pairs = spans // 2
    assert sections % 4 == 0 and spans % 2 == 0 and points == WIDE
    group = lax.axis_index("section")
    upper_half = lax.axis_index("span") % 2 == 1

    def pick(if_upper, if_lower):
        return jnp.where(upper_half, if_upper, if_lower)

    def send(value, groups, down, route):
        routes = []
        for g in groups:
            for s in range(spans):
                routes.append((g * spans + s, (g - down) * spans + route(s)))
        return lax.ppermute(value, AXES, routes)

    def straight(s):
        return s

    def partner(s):
        return s ^ 1

    def neighbor(shift):
        return lambda s: (s + shift) % spans

    def pair_route(pair, side):
        return (pair % pairs) * 2 + side

    def outward(s):
        return pair_route(s // 2 + 2 * (s % 2) - 1, s % 2)

    def outward_cross(s):
        return pair_route(s // 2 + 2 * (s % 2) - 1, 1 - s % 2)

    def inward(s):
        return pair_route(s // 2 + 1 - 2 * (s % 2), s % 2)

    def of_kind(kind):
        return [g for g in range(sections) if (sections - 1 - g) % 4 == kind]

    def own_half(value):
        return pick(value[:, HALF:], value[:, :HALF])

    def other_half(value):
        return pick(value[:, :HALF], value[:, HALF:])

    def joined(own, other):
        return pick(jnp.concatenate([other, own], 1), jnp.concatenate([own, other], 1))

    source = sources[0].reshape(FN, points, K).transpose(1, 2, 0)
    below = send(source, of_kind(1), -1, straight)
    inlet = source
    incoming = None
    for g in reversed(of_kind(0)):
        start = source if incoming is None else added(incoming, source)
        share = march(start, inverse_blocks, coupling, True)
        with_below = added(share, padded(below, STATIONS, STATIONS))
        mine, other = own_half(with_below), other_half(with_below)
        crossed = send(other, [g], 1, partner)
        edge = pick(other[-WIDE:], other[:WIDE])
        edge_cross = send(edge, [g], 1, outward_cross)
        edge = pick(mine[-WIDE:], mine[:WIDE])
        edge_same = send(edge, [g], 1, outward)
        direct = send(mine, [g], 1, straight)

        if incoming is None:
            later, share = lax.optimization_barrier((source, share))
            got = send(other_half(later), of_kind(2), 0, partner)
            mine = own_half(later)
            pair_source = pick(jnp.concatenate([got, mine], 0), jnp.concatenate([mine, got], 0))
            low = send(later[-STATIONS:], of_kind(3), 0, neighbor(1))
            high = send(later[:STATIONS], of_kind(3), 0, neighbor(-1))
            wide_source = jnp.concatenate([low, source, high], 0)

        first, second = pick(crossed, direct), pick(direct, crossed)
        low, high = pick(edge_same, edge_cross), pick(edge_cross, edge_same)
        start = jnp.concatenate(
            [added(low, first[:WIDE]), added(first[WIDE:], second[:WIDE]), added(second[WIDE:], high)], 0
        )
        state = march(start, inverse_blocks, coupling, False)
        arrived = send(state, [g - 1], 1, straight)

        share, state, _ = lax.optimization_barrier((share, state, state))
        low = send(share[-STATIONS:], [g], 0, neighbor(1))
        high = send(share[:STATIONS], [g], 0, neighbor(-1))
        whole = added(share[STATIONS:-STATIONS], jnp.concatenate([low, high], 0))
        inlet = jnp.where(group == g, whole, inlet)
        got = send(pick(state[:points], state[points:]), [g - 1], 0, partner)
        whole = joined(pick(state[points:], state[:points]), got)
        inlet = jnp.where(group == g - 1, whole, inlet)

        share = march(added(arrived, pair_source), inverse_blocks, coupling, True)
        crossed = send(pick(share[:-WIDE], share[WIDE:]), [g - 2], 1, partner)
        edge_cross = send(pick(share[-WIDE:], share[:WIDE]), [g - 2], 1, outward_cross)
        edge_same = send(pick(share[:WIDE], share[-WIDE:]), [g - 2], 1, inward)
        direct = send(pick(share[WIDE:], share[:-WIDE]), [g - 2], 1, straight)

        whole = joined(direct, crossed)
        edge = joined(edge_same, edge_cross)
        whole = added(whole, pick(padded(edge, WIDE, 0), padded(edge, 0, WIDE)))
        back = send(whole[STATIONS:-STATIONS], [g - 3], -1, straight)
        inlet = jnp.where(group == g - 2, back, inlet)
        state = march(added(whole, wide_source), inverse_blocks, coupling, False)
        inlet = jnp.where(group == g - 3, state, inlet)
        if g > 3:
            incoming = send(state, [g - 3], 1, straight)

    rows = inlet.reshape(points * K, FN)
    full = lax.dot_general(rows, rows, (((1,), (1,)), ((), ())), preferred_element_type=jnp.float32)
    gram = full[:K, :K]
    for point in range(1, points):
        at = point * K
        gram = gram + full[at : at + K, at : at + K]
    stride = 1
    while stride < spans:
        gram = gram + lax.ppermute(gram, "span", [(s, s ^ stride) for s in range(spans)])
        stride *= 2

    scaled = gram / float(FN * points * spans)
    factor = jnp.linalg.cholesky(scaled)
    inverse = jax.scipy.linalg.solve_triangular(factor, jnp.eye(K, dtype=jnp.float32), lower=True)
    spread = jnp.kron(jnp.eye(points, dtype=jnp.float32), inverse.T)
    rough = lax.reduce_precision(spread, 8, 7)
    basis = sum(
        lax.dot_general(
            rows, part.astype(jnp.bfloat16), (((0,), (0,)), ((), ())), preferred_element_type=jnp.float32
        )
        for part in (rough, spread - rough)
    )
    return (basis.astype(jnp.bfloat16)[None], factor.T[None])


def solution(mesh):
    placed = (P("section", None, None), P("section", None), P("section", None, "span"))
    return jax.shard_map(
        local,
        mesh=mesh,
        in_specs=placed,
        out_specs=(P("section", None, "span"), P("section", None, None)),
        check_vma=False,
    )
```

```python
import functools

import jax
import jax.numpy as jnp
import numpy as np
from jax import lax
from jax.experimental import pallas as pl
from jax.experimental.pallas import tpu as pltpu
from jax.sharding import PartitionSpec as P

K = 48
STATIONS = 4
FN = 768
HALF = K // 2
POINTS = 8
ONE = POINTS * HALF
EDGE = STATIONS * HALF
WIDE = 2 * EDGE
AXES = ("section", "span")


def march_kernel(places, blocks, positions, grow, turn, coupling, weights, *refs):
    pieces, out, buffers, held, sems = refs[: len(places)], refs[-5], refs[-4:-2], refs[-2], refs[-1]
    order = list(reversed(range(STATIONS)))

    @pl.when(turn[0] == 1)
    def _():
        copies = [
            pltpu.make_async_copy(weights.at[station], held.at[step], sems.at[step])
            for step, station in enumerate(order)
        ]
        for copy in copies:
            copy.start()
        side = turn[1]
        margin = 2 * HALF if grow else 0
        count = positions
        first = buffers[0]
        first[:, : count * HALF + 2 * margin, :] = jnp.zeros(
            (blocks, count * HALF + 2 * margin, FN), jnp.float32
        )
        for piece, where in zip(pieces, places):
            block, start = where(side)
            start = margin + start
            if not isinstance(start, int):
                start = pl.multiple_of(start, 8)
            first[block, pl.ds(start, piece.shape[0]), :] += piece[...].astype(jnp.float32)
        for step, station in enumerate(order):
            source, target = buffers[step % 2], buffers[1 - step % 2]
            count = count + 2 if grow else count - 2
            rates = coupling[station : station + 1, :]
            copies[step].wait()
            if blocks == 1:
                cut = (count // 2 + 1) // 2 * 2
                chunks = [(0, 0, cut), (0, cut, count)]
            else:
                chunks = [(block, 0, count) for block in range(blocks)]
            for block, begin, end in chunks:
                at, rows = begin * HALF, (end - begin) * HALF
                left = source[block, at : at + rows, :]
                center = source[block, at + HALF : at + HALF + rows, :]
                right = source[block, at + 2 * HALF : at + 2 * HALF + rows, :]
                update = (center + rates * (left + right - 2.0 * center)).astype(jnp.bfloat16)
                moved = lax.dot_general(
                    update, held[step], (((1,), (1,)), ((), ())), preferred_element_type=jnp.float32
                )
                if step == STATIONS - 1:
                    out[block, at : at + rows, :] = moved.astype(jnp.bfloat16)
                else:
                    target[block, margin + at : margin + at + rows, :] = moved
            if grow and step < STATIONS - 1:
                empty = jnp.zeros((blocks, margin, FN), jnp.float32)
                target[:, :margin, :] = empty
                target[:, margin + count * HALF : 2 * margin + count * HALF, :] = empty


def march(turn, inverse_blocks, coupling, pieces, places, blocks, positions, grow):
    last = positions + (2 * STATIONS if grow else -2 * STATIONS)
    most = max(positions, last + 2) if grow else positions
    vmem = pl.BlockSpec(memory_space=pltpu.VMEM)
    rows = blocks * HALF * (abs(last - positions) // 2 * (positions + last) // 2)
    return pl.pallas_call(
        functools.partial(march_kernel, places, blocks, positions, grow),
        out_shape=jax.ShapeDtypeStruct((blocks, last * HALF, FN), jnp.bfloat16),
        in_specs=[pl.BlockSpec(memory_space=pltpu.SMEM), vmem, pl.BlockSpec(memory_space=pl.ANY)]
        + [vmem] * len(pieces),
        out_specs=vmem,
        scratch_shapes=[
            pltpu.VMEM((blocks, most * HALF, FN), jnp.float32),
            pltpu.VMEM((blocks, most * HALF, FN), jnp.float32),
            pltpu.VMEM((STATIONS, FN, FN), jnp.bfloat16),
            pltpu.SemaphoreType.DMA((STATIONS,)),
        ],
        compiler_params=pltpu.CompilerParams(vmem_limit_bytes=28 * 1024 * 1024),
        cost_estimate=pl.CostEstimate(
            flops=2 * rows * FN * FN, bytes_accessed=2 * STATIONS * FN * FN, transcendentals=0
        ),
    )(turn, coupling, inverse_blocks, *pieces)


def factor_kernel(scale, gram, other, rows, by_column, by_place, same_point, basis, upper):
    whole = (gram[...] + other[...]) * scale
    eye = (
        lax.broadcasted_iota(jnp.int32, (K, K), 0) == lax.broadcasted_iota(jnp.int32, (K, K), 1)
    ).astype(jnp.float32)
    table = jnp.concatenate([whole, eye], 1)
    row_index = lax.broadcasted_iota(jnp.int32, (K, 1), 0)
    pivots = jnp.zeros((K, 1), jnp.float32)
    for j in range(K):
        line = table[j : j + 1, :]
        pivot = line[:, j : j + 1]
        pivots = jnp.where(row_index == j, pivot, pivots)
        share = jnp.where(row_index > j, table[:, j : j + 1], 0.0)
        table = table - share * (line / pivot)
    table = table * lax.rsqrt(pivots)
    column = lax.broadcasted_iota(jnp.int32, (K, K), 1)
    row = lax.broadcasted_iota(jnp.int32, (K, K), 0)
    upper[...] = jnp.where(column >= row, table[:, :K], 0.0)
    inverse = table[:, K:]
    total = None
    for _ in range(2):
        term = inverse.astype(jnp.bfloat16)
        inverse = inverse - term.astype(jnp.float32)
        tall = lax.dot_general(
            by_column[...], term, (((1,), (1,)), ((), ())), preferred_element_type=jnp.float32
        ).astype(jnp.bfloat16)
        spread = lax.dot_general(
            tall, by_place[...], (((1,), (0,)), ((), ())), preferred_element_type=jnp.float32
        )
        spread = (spread * same_point[...]).astype(jnp.bfloat16)
        part = lax.dot_general(
            rows[...], spread, (((0,), (0,)), ((), ())), preferred_element_type=jnp.float32
        )
        total = part if total is None else total + part
    basis[...] = total.astype(jnp.bfloat16)


def local(inverse_blocks, coupling, sources):
    sections = lax.axis_size("section")
    spans = lax.axis_size("span")
    pairs = spans // 2
    assert sections % 4 == 0 and spans % 2 == 0 and sources.shape[2] == POINTS * K
    group = lax.axis_index("section")
    side = (lax.axis_index("span") % 2).astype(jnp.int32)
    upper_half = side == 1

    def pick(if_upper, if_lower):
        return jnp.where(upper_half, if_upper, if_lower)

    def added(state, more):
        return (state.astype(jnp.float32) + more.astype(jnp.float32)).astype(jnp.bfloat16)

    def send(value, groups, down, route):
        routes = []
        for g in groups:
            for s in range(spans):
                routes.append((g * spans + s, (g - down) * spans + route(s)))
        return lax.ppermute(value, AXES, routes)

    def straight(s):
        return s

    def partner(s):
        return s ^ 1

    def neighbor(shift):
        return lambda s: (s + shift) % spans

    def pair_route(pair, side):
        return (pair % pairs) * 2 + side

    def outward(s):
        return pair_route(s // 2 + 2 * (s % 2) - 1, s % 2)

    def outward_cross(s):
        return pair_route(s // 2 + 2 * (s % 2) - 1, 1 - s % 2)

    def inward(s):
        return pair_route(s // 2 + 1 - 2 * (s % 2), s % 2)

    def of_kind(kind):
        return [g for g in range(sections) if (sections - 1 - g) % 4 == kind]

    def turn(g):
        return jnp.stack([(group == g).astype(jnp.int32), side])

    def own_half(value):
        return pick(value[1], value[0])

    def other_half(value):
        return pick(value[0], value[1])

    def joined(own, other):
        return pick(jnp.stack([other, own]), jnp.stack([own, other]))

    half, point, column = np.meshgrid(np.arange(2), np.arange(POINTS), np.arange(HALF), indexing="ij")
    row_column = (half * HALF + column).reshape(-1)
    row_point = point.reshape(-1)
    place = np.arange(POINTS * K)
    order = jnp.asarray(place[None, :] == (row_point * K + row_column)[:, None], jnp.bfloat16)
    by_column = jnp.asarray(np.arange(K)[None, :] == row_column[:, None], jnp.bfloat16)
    by_place = jnp.asarray(np.arange(K)[:, None] == place[None, :] % K, jnp.bfloat16)
    same_point = jnp.asarray(place[None, :] // K == row_point[:, None], jnp.float32)

    source = lax.dot_general(
        order, sources[0], (((1,), (1,)), ((), ())), preferred_element_type=jnp.float32
    ).astype(jnp.bfloat16).reshape(2, ONE, FN)
    below = send(source, of_kind(1), -1, straight)
    inlet = source
    incoming = None
    pair_source = wide_source = None
    for g in reversed(of_kind(0)):
        pieces = [source[0], source[1]]
        places = [lambda side: (0, 0), lambda side: (1, 0)]
        if incoming is not None:
            pieces += [incoming[0], incoming[1]]
            places += places
        share = march(turn(g), inverse_blocks, coupling, pieces, places, 2, POINTS, True)
        with_below = added(share, jnp.pad(below, ((0, 0), (EDGE, EDGE), (0, 0))))
        mine, other = own_half(with_below), other_half(with_below)
        crossed = send(other, [g], 1, partner)
        edge_cross = send(pick(other[-WIDE:], other[:WIDE]), [g], 1, outward_cross)
        edge_same = send(pick(mine[-WIDE:], mine[:WIDE]), [g], 1, outward)
        direct = send(mine, [g], 1, straight)

        if pair_source is None:
            later, share = lax.optimization_barrier((source, share))
            got = send(other_half(later), of_kind(2), 0, partner)
            pair_source = [own_half(later), got]
            low = send(later[:, -EDGE:], of_kind(3), 0, neighbor(1))
            high = send(later[:, :EDGE], of_kind(3), 0, neighbor(-1))
            wide_source = [low, later, high]

        state = march(
            turn(g - 1),
            inverse_blocks,
            coupling,
            [crossed, edge_cross, edge_same, direct],
            [
                lambda side: (0, (1 - side) * ONE),
                lambda side: (0, side * 2 * ONE),
                lambda side: (0, (1 - side) * 2 * ONE),
                lambda side: (0, side * ONE),
            ],
            1,
            3 * POINTS,
            False,
        )[0]
        arrived = send(state, [g - 1], 1, straight)

        share, state, _ = lax.optimization_barrier((share, state, state))
        low = send(share[:, -EDGE:], [g], 0, neighbor(1))
        high = send(share[:, :EDGE], [g], 0, neighbor(-1))
        got = send(pick(state[:ONE], state[ONE:]), [g - 1], 0, partner)
        arrived, low, high, got, pair_source, wide_source = lax.optimization_barrier(
            (arrived, low, high, got, pair_source, wide_source)
        )
        whole = added(share[:, EDGE:-EDGE], jnp.concatenate([low, high], 1))
        inlet = jnp.where(group == g, whole, inlet)
        inlet = jnp.where(group == g - 1, joined(pick(state[ONE:], state[:ONE]), got), inlet)

        share = march(
            turn(g - 2),
            inverse_blocks,
            coupling,
            [arrived] + pair_source,
            [lambda side: (0, 0), lambda side: (0, side * ONE), lambda side: (0, (1 - side) * ONE)],
            1,
            2 * POINTS,
            True,
        )[0]
        crossed = send(pick(share[:-WIDE], share[WIDE:]), [g - 2], 1, partner)
        edge_cross = send(pick(share[-WIDE:], share[:WIDE]), [g - 2], 1, outward_cross)
        edge_same = send(pick(share[:WIDE], share[-WIDE:]), [g - 2], 1, inward)
        direct = send(pick(share[WIDE:], share[:-WIDE]), [g - 2], 1, straight)

        def center(state, edge):
            shift = jnp.zeros((EDGE, FN), jnp.bfloat16)
            return added(
                state[EDGE:-EDGE],
                pick(jnp.concatenate([shift, edge[:EDGE]], 0), jnp.concatenate([edge[EDGE:], shift], 0)),
            )

        back = send(joined(center(direct, edge_same), center(crossed, edge_cross)), [g - 3], -1, straight)
        low, later, high = wide_source
        state = march(
            turn(g - 3),
            inverse_blocks,
            coupling,
            [crossed, edge_cross, edge_same, direct, low[0], low[1], later[0], later[1], high[0], high[1]],
            [
                lambda side: (1 - side, 0),
                lambda side: (1 - side, side * ONE),
                lambda side: (side, side * ONE),
                lambda side: (side, 0),
                lambda side: (0, 0),
                lambda side: (1, 0),
                lambda side: (0, EDGE),
                lambda side: (1, EDGE),
                lambda side: (0, EDGE + ONE),
                lambda side: (1, EDGE + ONE),
            ],
            2,
            2 * POINTS,
            False,
        )
        inlet = jnp.where(group == g - 2, back, jnp.where(group == g - 3, state, inlet))
        if g > 3:
            incoming = send(state, [g - 3], 1, straight)

    rows = inlet.reshape(POINTS * K, FN)
    full = lax.dot_general(rows, rows, (((1,), (1,)), ((), ())), preferred_element_type=jnp.float32)
    quarters = full.reshape(2, POINTS, HALF, 2, POINTS, HALF)
    gram = sum(quarters[:, p, :, :, p, :] for p in range(POINTS)).reshape(K, K)
    strides = []
    while (1 << len(strides)) < spans:
        strides.append(1 << len(strides))
    for at, stride in enumerate(strides):
        other = lax.ppermute(gram, "span", [(s, s ^ stride) for s in range(spans)])
        if at < len(strides) - 1:
            gram = gram + other

    vmem = pl.BlockSpec(memory_space=pltpu.VMEM)
    basis, upper = pl.pallas_call(
        functools.partial(factor_kernel, 1.0 / float(FN * POINTS * spans)),
        out_shape=(
            jax.ShapeDtypeStruct((FN, POINTS * K), jnp.bfloat16),
            jax.ShapeDtypeStruct((K, K), jnp.float32),
        ),
        in_specs=[vmem] * 6,
        out_specs=(vmem, vmem),
        compiler_params=pltpu.CompilerParams(vmem_limit_bytes=16 * 1024 * 1024),
    )(gram, other, rows, by_column, by_place, same_point)
    return (basis[None], upper[None])


def solution(mesh):
    placed = (P("section", None, None), P("section", None), P("section", None, "span"))
    return jax.shard_map(
        local,
        mesh=mesh,
        in_specs=placed,
        out_specs=(P("section", None, "span"), P("section", None, None)),
        check_vma=False,
    )
```

```python
import functools

import jax
import jax.numpy as jnp
import numpy as np
from jax import lax
from jax.experimental import pallas as pl
from jax.experimental.pallas import tpu as pltpu
from jax.sharding import PartitionSpec as P

K = 48
STATIONS = 4
FN = 768
HALF = K // 2
POINTS = 8
ONE = POINTS * HALF
EDGE = STATIONS * HALF
WIDE = 2 * EDGE
TILE = 256
STEP = 4
AXES = ("section", "span")


def assembled(target, pieces, places, side, margin):
    for piece, where in zip(pieces, places):
        block, start = where(side)
        start = margin + start
        if not isinstance(start, int):
            start = pl.multiple_of(start, 8)
        target[block, pl.ds(start, piece.shape[0]), :] += piece[...].astype(jnp.float32)


def by_half(raw):
    turned = raw[...].astype(jnp.float32).T
    for point in range(POINTS):
        for half in range(2):
            at = point * K + half * HALF
            yield half, point * HALF, turned[at : at + HALF, :]


def march_kernel(places, parts, blocks, positions, grow, raws, turn, coupling, weights, *refs):
    raw_refs, refs = refs[:raws], refs[raws:]
    pieces, outs = refs[: len(places)], refs[len(places) : -7]
    states, updates, result, held, sems = refs[-7:-5], refs[-5:-3], refs[-3], refs[-2], refs[-1]
    order = list(reversed(range(STATIONS)))
    tiles = [slice(at, at + TILE) for at in range(0, FN, TILE)]

    @pl.when(turn[0] == 1)
    def _():
        copies = [
            pltpu.make_async_copy(weights.at[station], held.at[step], sems.at[step])
            for step, station in enumerate(order)
        ]
        for copy in copies:
            copy.start()
        side = turn[1]
        margin = 2 * HALF if grow else 0
        counts = [positions + (2 * step if grow else -2 * step) for step in range(STATIONS + 1)]

        def stencil(step, tile):
            rows = counts[step + 1] * HALF
            rates = coupling[order[step] : order[step] + 1, tile]
            rest = 1.0 - 2.0 * rates
            state = states[step % 2]
            for block in range(blocks):
                both = state[block, :rows, tile] + state[block, 2 * HALF : 2 * HALF + rows, tile]
                update = rest * state[block, HALF : HALF + rows, tile] + rates * both
                updates[step % 2][block * rows : (block + 1) * rows, tile] = update.astype(jnp.bfloat16)

        total = counts[0] * HALF + 2 * margin
        states[0][:, :total, :] = jnp.zeros((blocks, total, FN), jnp.float32)
        if raws:
            for half, at, value in by_half(raw_refs[0]):
                states[0][half, margin + at : margin + at + HALF, :] = value
        assembled(states[0], pieces, places, side, margin)
        for tile in tiles:
            stencil(0, tile)
        for step in range(STATIONS):
            rows = counts[step + 1] * HALF
            copies[step].wait()
            for tile in tiles:
                moved = lax.dot_general(
                    updates[step % 2][: blocks * rows, :],
                    held[step, tile, :],
                    (((1,), (1,)), ((), ())),
                    preferred_element_type=jnp.float32,
                )
                for block in range(blocks):
                    value = moved[block * rows : (block + 1) * rows]
                    if step == STATIONS - 1:
                        result[block, :, tile] = value.astype(jnp.bfloat16)
                        continue
                    state = states[(step + 1) % 2]
                    state[block, margin : margin + rows, tile] = value
                    if grow:
                        empty = jnp.zeros((margin, TILE), jnp.float32)
                        state[block, :margin, tile] = empty
                        state[block, margin + rows : 2 * margin + rows, tile] = empty
                if step < STATIONS - 1:
                    stencil(step + 1, tile)
        if not parts:
            outs[0][...] = result[...]
            return
        if raws > 1:
            outs[-1][...] = result[...]
            for half, at, value in by_half(raw_refs[1]):
                here = slice(EDGE + at, EDGE + at + HALF)
                states[0][half, here, :] = result[half, here, :].astype(jnp.float32) + value
            result[:, EDGE : EDGE + ONE, :] = states[0][:, EDGE : EDGE + ONE, :].astype(jnp.bfloat16)
        for (_, where), out in zip(parts, outs):
            block, start = where(side)
            if not isinstance(start, int):
                start = pl.multiple_of(start, EDGE)
            out[...] = result[block, pl.ds(start, out.shape[0]), :]


def march(turn, inverse_blocks, coupling, raws, pieces, places, parts, blocks, positions, grow):
    last = positions + (2 * STATIONS if grow else -2 * STATIONS)
    most = last + 2 if grow else positions
    vmem = pl.BlockSpec(memory_space=pltpu.VMEM)
    rows = blocks * HALF * STATIONS * (positions + last + (2 if grow else -2)) // 2
    whole = jax.ShapeDtypeStruct((blocks, last * HALF, FN), jnp.bfloat16)
    shapes = [jax.ShapeDtypeStruct((size, FN), jnp.bfloat16) for size, _ in parts]
    if not parts or len(raws) > 1:
        shapes.append(whole)
    return pl.pallas_call(
        functools.partial(march_kernel, places, parts, blocks, positions, grow, len(raws)),
        out_shape=shapes,
        in_specs=[pl.BlockSpec(memory_space=pltpu.SMEM), vmem, pl.BlockSpec(memory_space=pltpu.HBM)]
        + [vmem] * (len(raws) + len(pieces)),
        out_specs=[vmem] * len(shapes),
        scratch_shapes=[pltpu.VMEM((blocks, most * HALF, FN), jnp.float32)] * 2
        + [pltpu.VMEM((blocks * max(positions, last) * HALF, FN), jnp.bfloat16)] * 2
        + [
            pltpu.VMEM(whole.shape, jnp.bfloat16),
            pltpu.VMEM((STATIONS, FN, FN), jnp.bfloat16),
            pltpu.SemaphoreType.DMA((STATIONS,)),
        ],
        compiler_params=pltpu.CompilerParams(vmem_limit_bytes=32 * 1024 * 1024),
        cost_estimate=pl.CostEstimate(
            flops=2 * rows * FN * FN, bytes_accessed=2 * STATIONS * FN * FN, transcendentals=0
        ),
    )(turn, coupling, inverse_blocks, *raws, *pieces)


def center_kernel(turn, direct, crossed, edge_same, edge_cross, out):
    @pl.when(turn[0] == 1)
    def _():
        side = turn[1]
        start = pl.multiple_of(side * EDGE, EDGE)
        from_edge = pl.multiple_of((1 - side) * EDGE, EDGE)
        for block, share, edge in ((side, direct, edge_same), (1 - side, crossed, edge_cross)):
            out[block, :, :] = share[EDGE : EDGE + ONE, :]
            here = out[block, pl.ds(start, EDGE), :].astype(jnp.float32)
            more = edge[pl.ds(from_edge, EDGE), :].astype(jnp.float32)
            out[block, pl.ds(start, EDGE), :] = (here + more).astype(jnp.bfloat16)


def gram_kernel(count, kind, *refs):
    candidates, (rows, gram, sem) = refs[:count], refs[count:]
    for number, candidate in enumerate(candidates):

        @pl.when(kind[0] == number)
        def _():
            copy = pltpu.make_async_copy(candidate, rows, sem)
            copy.start()
            copy.wait()

    flat = rows[...].reshape(2 * ONE, FN)
    full = lax.dot_general(flat, flat, (((1,), (1,)), ((), ())), preferred_element_type=jnp.float32)
    lines = []
    for first in range(2):
        line = []
        for second in range(2):
            block = None
            for point in range(POINTS):
                down, along = first * ONE + point * HALF, second * ONE + point * HALF
                term = full[down : down + HALF, along : along + HALF]
                block = term if block is None else block + term
            line.append(block)
        lines.append(jnp.concatenate(line, 1))
    gram[...] = jnp.concatenate(lines, 0)


def factor_kernel(scale, grams, rows, by_column, by_place, same_point, basis, upper):
    terms = [grams[at] for at in range(grams.shape[0])]
    while len(terms) > 1:
        terms = [terms[at] + terms[at + 1] for at in range(0, len(terms), 2)]
    eye = (
        lax.broadcasted_iota(jnp.int32, (K, K), 0) == lax.broadcasted_iota(jnp.int32, (K, K), 1)
    ).astype(jnp.float32)
    table = jnp.concatenate([terms[0] * scale, eye], 1)
    row_index = lax.broadcasted_iota(jnp.int32, (K, 2 * K), 0)
    roots = jnp.zeros((K, 2 * K), jnp.float32)
    for j in range(0, K, STEP):
        lines = [table[j + m : j + m + 1, :] for m in range(STEP)]
        columns = [jnp.broadcast_to(table[:, j + m : j + m + 1], table.shape) for m in range(STEP)]
        entries = [
            [jnp.broadcast_to(lines[m][:, j + k : j + k + 1], lines[m].shape) for k in range(STEP)]
            for m in range(STEP)
        ]
        below = table
        for m in range(STEP):
            inverse = 1.0 / entries[m][m]
            for k in range(m + 1, STEP):
                ratio = entries[m][k] * inverse
                for n in range(k, STEP):
                    entries[k][n] = entries[k][n] - ratio * entries[m][n]
                lines[k] = lines[k] - ratio * lines[m]
                columns[k] = columns[k] - ratio * columns[m]
            below = below - columns[m] * (inverse * lines[m])
            roots = jnp.where(row_index == j + m, lax.rsqrt(entries[m][m]), roots)
        table = jnp.where(row_index >= j + STEP, below, table)
        for m in range(STEP):
            table = jnp.where(row_index == j + m, lines[m], table)
    table = table * roots
    column = lax.broadcasted_iota(jnp.int32, (K, K), 1)
    row = lax.broadcasted_iota(jnp.int32, (K, K), 0)
    upper[...] = jnp.where(column >= row, table[:, :K], 0.0)
    inverse = table[:, K:]
    total = None
    for _ in range(2):
        term = inverse.astype(jnp.bfloat16)
        inverse = inverse - term.astype(jnp.float32)
        tall = lax.dot_general(
            by_column[...], term, (((1,), (1,)), ((), ())), preferred_element_type=jnp.float32
        ).astype(jnp.bfloat16)
        spread = lax.dot_general(
            tall, by_place[...], (((1,), (0,)), ((), ())), preferred_element_type=jnp.float32
        )
        spread = (spread * same_point[...]).astype(jnp.bfloat16)
        part = lax.dot_general(
            rows[...], spread, (((0,), (0,)), ((), ())), preferred_element_type=jnp.float32
        )
        total = part if total is None else total + part
    basis[...] = total.astype(jnp.bfloat16)


def local(inverse_blocks, coupling, sources):
    sections = lax.axis_size("section")
    spans = lax.axis_size("span")
    pairs = spans // 2
    assert sections % 4 == 0 and spans % 2 == 0 and sources.shape[2] == POINTS * K
    group = lax.axis_index("section")
    side = (lax.axis_index("span") % 2).astype(jnp.int32)
    upper_half = side == 1

    def pick(if_upper, if_lower):
        return jnp.where(upper_half, if_upper, if_lower)

    def added(state, more):
        return (state.astype(jnp.float32) + more.astype(jnp.float32)).astype(jnp.bfloat16)

    def send(value, groups, down, route):
        routes = []
        for g in groups:
            for s in range(spans):
                routes.append((g * spans + s, (g - down) * spans + route(s)))
        return lax.ppermute(value, AXES, routes)

    def straight(s):
        return s

    def partner(s):
        return s ^ 1

    def neighbor(shift):
        return lambda s: (s + shift) % spans

    def pair_route(pair, side):
        return (pair % pairs) * 2 + side

    def outward(s):
        return pair_route(s // 2 + 2 * (s % 2) - 1, s % 2)

    def outward_cross(s):
        return pair_route(s // 2 + 2 * (s % 2) - 1, 1 - s % 2)

    def inward(s):
        return pair_route(s // 2 + 1 - 2 * (s % 2), s % 2)

    def of_kind(kind):
        return [g for g in range(sections) if (sections - 1 - g) % 4 == kind]

    def turn(g):
        return jnp.stack([(group == g).astype(jnp.int32), side])

    def own_half(value):
        return pick(value[1], value[0])

    def other_half(value):
        return pick(value[0], value[1])

    def joined(own, other):
        return pick(jnp.stack([other, own]), jnp.stack([own, other]))

    half, point, column = np.meshgrid(np.arange(2), np.arange(POINTS), np.arange(HALF), indexing="ij")
    row_column = (half * HALF + column).reshape(-1)
    row_point = point.reshape(-1)
    place = np.arange(POINTS * K)
    by_column = jnp.asarray(np.arange(K)[None, :] == row_column[:, None], jnp.bfloat16)
    by_place = jnp.asarray(np.arange(K)[:, None] == place[None, :] % K, jnp.bfloat16)
    same_point = jnp.asarray(place[None, :] // K == row_point[:, None], jnp.float32)

    raw = sources[0]
    below = send(raw, of_kind(1), -1, straight)
    incoming = None
    pair_source = wide_source = None
    candidates = []
    for g in reversed(of_kind(0)):
        pieces = [] if incoming is None else [incoming[0], incoming[1]]
        places = [lambda side: (0, 0), lambda side: (1, 0)][: len(pieces)]
        crossed, edge_cross, edge_same, direct, share = march(
            turn(g),
            inverse_blocks,
            coupling,
            [raw, below],
            pieces,
            places,
            [
                (2 * ONE, lambda side: (1 - side, 0)),
                (WIDE, lambda side: (1 - side, side * ONE)),
                (WIDE, lambda side: (side, side * ONE)),
                (2 * ONE, lambda side: (side, 0)),
            ],
            2,
            POINTS,
            True,
        )
        crossed = send(crossed, [g], 1, partner)
        edge_cross = send(edge_cross, [g], 1, outward_cross)
        edge_same = send(edge_same, [g], 1, outward)
        direct = send(direct, [g], 1, straight)

        if pair_source is None:
            later, share = lax.optimization_barrier((raw, share))
            later = later.reshape(FN, POINTS, 2, HALF).transpose(2, 1, 3, 0).reshape(2, ONE, FN)
            got = send(other_half(later), of_kind(2), 0, partner)
            pair_source = [own_half(later), got]
            low = send(later[:, -EDGE:], of_kind(3), 0, neighbor(1))
            high = send(later[:, :EDGE], of_kind(3), 0, neighbor(-1))
            wide_source = [low, later, high]

        (state,) = march(
            turn(g - 1),
            inverse_blocks,
            coupling,
            [],
            [crossed, edge_cross, edge_same, direct],
            [
                lambda side: (0, (1 - side) * ONE),
                lambda side: (0, side * 2 * ONE),
                lambda side: (0, (1 - side) * 2 * ONE),
                lambda side: (0, side * ONE),
            ],
            [(2 * ONE, lambda side: (0, 0))],
            1,
            3 * POINTS,
            False,
        )
        arrived = send(state, [g - 1], 1, straight)

        share, state, _ = lax.optimization_barrier((share, state, state))
        low = send(share[:, -EDGE:], [g], 0, neighbor(1))
        high = send(share[:, :EDGE], [g], 0, neighbor(-1))
        got = send(pick(state[:ONE], state[ONE:]), [g - 1], 0, partner)
        arrived, low, high, got, pair_source, wide_source = lax.optimization_barrier(
            (arrived, low, high, got, pair_source, wide_source)
        )
        whole = added(share[:, EDGE:-EDGE], jnp.concatenate([low, high], 1))
        candidates += [whole, joined(pick(state[ONE:], state[:ONE]), got)]

        crossed, edge_cross, edge_same, direct = march(
            turn(g - 2),
            inverse_blocks,
            coupling,
            [],
            [arrived] + pair_source,
            [lambda side: (0, 0), lambda side: (0, side * ONE), lambda side: (0, (1 - side) * ONE)],
            [
                (2 * ONE, lambda side: (0, (1 - side) * ONE)),
                (WIDE, lambda side: (0, side * 2 * ONE)),
                (WIDE, lambda side: (0, (1 - side) * 2 * ONE)),
                (2 * ONE, lambda side: (0, side * ONE)),
            ],
            1,
            2 * POINTS,
            True,
        )
        crossed = send(crossed, [g - 2], 1, partner)
        edge_cross = send(edge_cross, [g - 2], 1, outward_cross)
        edge_same = send(edge_same, [g - 2], 1, inward)
        direct = send(direct, [g - 2], 1, straight)

        vmem = pl.BlockSpec(memory_space=pltpu.VMEM)
        middle = pl.pallas_call(
            center_kernel,
            out_shape=jax.ShapeDtypeStruct((2, ONE, FN), jnp.bfloat16),
            in_specs=[pl.BlockSpec(memory_space=pltpu.SMEM)] + [vmem] * 4,
            out_specs=vmem,
        )(turn(g - 3), direct, crossed, edge_same, edge_cross)
        back = send(middle, [g - 3], -1, straight)
        low, later, high = wide_source
        (state,) = march(
            turn(g - 3),
            inverse_blocks,
            coupling,
            [],
            [crossed, edge_cross, edge_same, direct, low[0], low[1], later[0], later[1], high[0], high[1]],
            [
                lambda side: (1 - side, 0),
                lambda side: (1 - side, side * ONE),
                lambda side: (side, side * ONE),
                lambda side: (side, 0),
                lambda side: (0, 0),
                lambda side: (1, 0),
                lambda side: (0, EDGE),
                lambda side: (1, EDGE),
                lambda side: (0, EDGE + ONE),
                lambda side: (1, EDGE + ONE),
            ],
            [],
            2,
            2 * POINTS,
            False,
        )
        candidates += [back, state]
        if g > 3:
            incoming = send(state, [g - 3], 1, straight)

    smem = pl.BlockSpec(memory_space=pltpu.SMEM)
    rows, gram = pl.pallas_call(
        functools.partial(gram_kernel, len(candidates)),
        out_shape=(
            jax.ShapeDtypeStruct((2, ONE, FN), jnp.bfloat16),
            jax.ShapeDtypeStruct((K, K), jnp.float32),
        ),
        in_specs=[smem] + [pl.BlockSpec(memory_space=pl.ANY)] * len(candidates),
        out_specs=(vmem, vmem),
        scratch_shapes=[pltpu.SemaphoreType.DMA],
        compiler_params=pltpu.CompilerParams(vmem_limit_bytes=16 * 1024 * 1024),
    )((sections - 1 - group).astype(jnp.int32)[None], *candidates)
    grams = lax.all_gather(gram, "span")
    vmem = pl.BlockSpec(memory_space=pltpu.VMEM)
    basis, upper = pl.pallas_call(
        functools.partial(factor_kernel, 1.0 / float(FN * POINTS * spans)),
        out_shape=(
            jax.ShapeDtypeStruct((FN, POINTS * K), jnp.bfloat16),
            jax.ShapeDtypeStruct((K, K), jnp.float32),
        ),
        in_specs=[vmem] * 5,
        out_specs=(vmem, vmem),
        compiler_params=pltpu.CompilerParams(vmem_limit_bytes=16 * 1024 * 1024),
    )(grams, rows.reshape(POINTS * K, FN), by_column, by_place, same_point)
    return (basis[None], upper[None])


def solution(mesh):
    placed = (P("section", None, None), P("section", None), P("section", None, "span"))
    return jax.shard_map(
        local,
        mesh=mesh,
        in_specs=placed,
        out_specs=(P("section", None, "span"), P("section", None, None)),
        check_vma=False,
    )
```

```python
import functools

import jax
import jax.numpy as jnp
import numpy as np
from jax import lax
from jax.experimental import pallas as pl
from jax.experimental.pallas import tpu as pltpu
from jax.sharding import PartitionSpec as P

K = 48
STATIONS = 4
FN = 768
HALF = K // 2
POINTS = 8
ONE = POINTS * HALF
EDGE = STATIONS * HALF
WIDE = 2 * EDGE
STEP = 4
GRANT = 60 * 1024 * 1024
AXES = ("section", "span")


def by_half(raw):
    turned = raw[...].astype(jnp.float32).T
    for point in range(POINTS):
        for half in range(2):
            at = point * K + half * HALF
            yield half, point * HALF, turned[at : at + HALF, :]


def march_kernel(places, parts, blocks, positions, grow, raws, turn, coupling, weights, *refs):
    inputs = raws + len(places)
    sources, refs = refs[:inputs], refs[inputs:]
    local, refs = refs[-inputs:], refs[:-inputs]
    outs, (first, second, result, held, weight_sems, sems) = refs[:-6], refs[-6:]
    states = [first, second]
    order = list(reversed(range(STATIONS)))

    @pl.when(turn[0] == 1)
    def _():
        fetches = [
            pltpu.make_async_copy(source, here, sems.at[at])
            for at, (source, here) in enumerate(zip(sources, local))
        ]
        copies = [
            pltpu.make_async_copy(weights.at[station], held.at[step], weight_sems.at[step])
            for step, station in enumerate(order)
        ]
        for copy in fetches + copies:
            copy.start()
        side = turn[1]
        margin = 2 * HALF if grow else 0
        count = positions
        total = count * HALF + 2 * margin
        first[:, :total, :] = jnp.zeros((blocks, total, FN), jnp.float32)
        for fetch in fetches:
            fetch.wait()
        if raws:
            for half, at, value in by_half(local[0]):
                first[half, margin + at : margin + at + HALF, :] = value
        for piece, where in zip(local[raws:], places):
            block, start = where(side)
            start = margin + start
            if not isinstance(start, int):
                start = pl.multiple_of(start, 8)
            first[block, pl.ds(start, piece.shape[0]), :] += piece[...].astype(jnp.float32)
        for step, station in enumerate(order):
            source, target = states[step % 2], states[1 - step % 2]
            count = count + 2 if grow else count - 2
            rates = coupling[station : station + 1, :]
            rest = 1.0 - 2.0 * rates
            copies[step].wait()
            if blocks == 1:
                cut = (count // 2 + 1) // 2 * 2
                chunks = [(0, 0, cut), (0, cut, count)]
            else:
                chunks = [(block, 0, count) for block in range(blocks)]
            for block, begin, end in chunks:
                at, rows = begin * HALF, (end - begin) * HALF
                both = source[block, at : at + rows, :] + source[block, at + 2 * HALF : at + 2 * HALF + rows, :]
                update = rest * source[block, at + HALF : at + HALF + rows, :] + rates * both
                moved = lax.dot_general(
                    update.astype(jnp.bfloat16),
                    held[step],
                    (((1,), (1,)), ((), ())),
                    preferred_element_type=jnp.float32,
                )
                if step == STATIONS - 1:
                    result[block, at : at + rows, :] = moved.astype(jnp.bfloat16)
                else:
                    target[block, margin + at : margin + at + rows, :] = moved
            if grow and step < STATIONS - 1:
                empty = jnp.zeros((blocks, margin, FN), jnp.float32)
                target[:, :margin, :] = empty
                target[:, margin + count * HALF : 2 * margin + count * HALF, :] = empty
        if not parts:
            outs[0][...] = result[...]
            return
        if raws > 1:
            outs[-1][...] = result[...]
            for half, at, value in by_half(local[1]):
                here = slice(EDGE + at, EDGE + at + HALF)
                first[half, here, :] = result[half, here, :].astype(jnp.float32) + value
            result[:, EDGE : EDGE + ONE, :] = first[:, EDGE : EDGE + ONE, :].astype(jnp.bfloat16)
        for (_, where), out in zip(parts, outs):
            block, start = where(side)
            if not isinstance(start, int):
                start = pl.multiple_of(start, EDGE)
            out[...] = result[block, pl.ds(start, out.shape[0]), :]


def march(turn, inverse_blocks, coupling, raws, pieces, places, parts, blocks, positions, grow):
    last = positions + (2 * STATIONS if grow else -2 * STATIONS)
    most = last + 2 if grow else positions
    vmem = pl.BlockSpec(memory_space=pltpu.VMEM)
    away = pl.BlockSpec(memory_space=pl.ANY)
    rows = blocks * HALF * STATIONS * (positions + last + (2 if grow else -2)) // 2
    whole = jax.ShapeDtypeStruct((blocks, last * HALF, FN), jnp.bfloat16)
    shapes = [jax.ShapeDtypeStruct((size, FN), jnp.bfloat16) for size, _ in parts]
    if not parts or len(raws) > 1:
        shapes.append(whole)
    inputs = list(raws) + list(pieces)
    return pl.pallas_call(
        functools.partial(march_kernel, places, parts, blocks, positions, grow, len(raws)),
        out_shape=shapes,
        in_specs=[pl.BlockSpec(memory_space=pltpu.SMEM), vmem, away] + [away] * len(inputs),
        out_specs=[vmem] * len(shapes),
        scratch_shapes=[pltpu.VMEM((blocks, most * HALF, FN), jnp.float32)] * 2
        + [
            pltpu.VMEM(whole.shape, jnp.bfloat16),
            pltpu.VMEM((STATIONS, FN, FN), jnp.bfloat16),
            pltpu.SemaphoreType.DMA((STATIONS,)),
            pltpu.SemaphoreType.DMA((len(inputs),)),
        ]
        + [pltpu.VMEM(value.shape, jnp.bfloat16) for value in inputs],
        compiler_params=pltpu.CompilerParams(vmem_limit_bytes=GRANT),
        cost_estimate=pl.CostEstimate(
            flops=2 * rows * FN * FN, bytes_accessed=2 * STATIONS * FN * FN, transcendentals=0
        ),
    )(turn, coupling, inverse_blocks, *inputs)


def center_kernel(turn, direct, crossed, edge_same, edge_cross, out, local_same, local_cross, sems):
    @pl.when(turn[0] == 1)
    def _():
        side = turn[1]
        start = pl.multiple_of(side * EDGE, EDGE)
        from_edge = pl.multiple_of((1 - side) * EDGE, EDGE)
        copies = [
            pltpu.make_async_copy(direct.at[EDGE : EDGE + ONE], out.at[side], sems.at[0]),
            pltpu.make_async_copy(crossed.at[EDGE : EDGE + ONE], out.at[1 - side], sems.at[1]),
            pltpu.make_async_copy(edge_same, local_same, sems.at[2]),
            pltpu.make_async_copy(edge_cross, local_cross, sems.at[3]),
        ]
        for copy in copies:
            copy.start()
        for copy in copies:
            copy.wait()
        for block, edge in ((side, local_same), (1 - side, local_cross)):
            here = out[block, pl.ds(start, EDGE), :].astype(jnp.float32)
            more = edge[pl.ds(from_edge, EDGE), :].astype(jnp.float32)
            out[block, pl.ds(start, EDGE), :] = (here + more).astype(jnp.bfloat16)


def gram_kernel(count, kind, *refs):
    candidates, (rows, gram, sem) = refs[:count], refs[count:]
    for number, candidate in enumerate(candidates):

        @pl.when(kind[0] == number)
        def _():
            copy = pltpu.make_async_copy(candidate, rows, sem)
            copy.start()
            copy.wait()

    flat = rows[...].reshape(2 * ONE, FN)
    full = lax.dot_general(flat, flat, (((1,), (1,)), ((), ())), preferred_element_type=jnp.float32)
    lines = []
    for first in range(2):
        line = []
        for second in range(2):
            block = None
            for point in range(POINTS):
                down, along = first * ONE + point * HALF, second * ONE + point * HALF
                term = full[down : down + HALF, along : along + HALF]
                block = term if block is None else block + term
            line.append(block)
        lines.append(jnp.concatenate(line, 1))
    gram[...] = jnp.concatenate(lines, 0)


def factor_kernel(scale, gram, other, rows, by_column, by_place, same_point, basis, upper):
    eye = (
        lax.broadcasted_iota(jnp.int32, (K, K), 0) == lax.broadcasted_iota(jnp.int32, (K, K), 1)
    ).astype(jnp.float32)
    table = jnp.concatenate([(gram[...] + other[...]) * scale, eye], 1)
    row_index = lax.broadcasted_iota(jnp.int32, (K, 2 * K), 0)
    roots = jnp.zeros((K, 2 * K), jnp.float32)
    for j in range(0, K, STEP):
        lines = [table[j + m : j + m + 1, :] for m in range(STEP)]
        columns = [jnp.broadcast_to(table[:, j + m : j + m + 1], table.shape) for m in range(STEP)]
        entries = [
            [jnp.broadcast_to(lines[m][:, j + k : j + k + 1], lines[m].shape) for k in range(STEP)]
            for m in range(STEP)
        ]
        below = table
        for m in range(STEP):
            inverse = 1.0 / entries[m][m]
            for k in range(m + 1, STEP):
                ratio = entries[m][k] * inverse
                for n in range(k, STEP):
                    entries[k][n] = entries[k][n] - ratio * entries[m][n]
                lines[k] = lines[k] - ratio * lines[m]
                columns[k] = columns[k] - ratio * columns[m]
            below = below - columns[m] * (inverse * lines[m])
            roots = jnp.where(row_index == j + m, lax.rsqrt(entries[m][m]), roots)
        table = jnp.where(row_index >= j + STEP, below, table)
        for m in range(STEP):
            table = jnp.where(row_index == j + m, lines[m], table)
    table = table * roots
    column = lax.broadcasted_iota(jnp.int32, (K, K), 1)
    row = lax.broadcasted_iota(jnp.int32, (K, K), 0)
    upper[...] = jnp.where(column >= row, table[:, :K], 0.0)
    inverse = table[:, K:]
    total = None
    for _ in range(2):
        term = inverse.astype(jnp.bfloat16)
        inverse = inverse - term.astype(jnp.float32)
        tall = lax.dot_general(
            by_column[...], term, (((1,), (1,)), ((), ())), preferred_element_type=jnp.float32
        ).astype(jnp.bfloat16)
        spread = lax.dot_general(
            tall, by_place[...], (((1,), (0,)), ((), ())), preferred_element_type=jnp.float32
        )
        spread = (spread * same_point[...]).astype(jnp.bfloat16)
        part = lax.dot_general(
            rows[...], spread, (((0,), (0,)), ((), ())), preferred_element_type=jnp.float32
        )
        total = part if total is None else total + part
    basis[...] = total.astype(jnp.bfloat16)


def local(inverse_blocks, coupling, sources):
    sections = lax.axis_size("section")
    spans = lax.axis_size("span")
    pairs = spans // 2
    assert sections % 4 == 0 and spans % 2 == 0 and sources.shape[2] == POINTS * K
    group = lax.axis_index("section")
    side = (lax.axis_index("span") % 2).astype(jnp.int32)
    upper_half = side == 1

    def pick(if_upper, if_lower):
        return jnp.where(upper_half, if_upper, if_lower)

    def added(state, more):
        return (state.astype(jnp.float32) + more.astype(jnp.float32)).astype(jnp.bfloat16)

    def send(value, groups, down, route):
        routes = []
        for g in groups:
            for s in range(spans):
                routes.append((g * spans + s, (g - down) * spans + route(s)))
        return lax.ppermute(value, AXES, routes)

    def straight(s):
        return s

    def partner(s):
        return s ^ 1

    def neighbor(shift):
        return lambda s: (s + shift) % spans

    def pair_route(pair, side):
        return (pair % pairs) * 2 + side

    def outward(s):
        return pair_route(s // 2 + 2 * (s % 2) - 1, s % 2)

    def outward_cross(s):
        return pair_route(s // 2 + 2 * (s % 2) - 1, 1 - s % 2)

    def inward(s):
        return pair_route(s // 2 + 1 - 2 * (s % 2), s % 2)

    def of_kind(kind):
        return [g for g in range(sections) if (sections - 1 - g) % 4 == kind]

    def turn(g):
        return jnp.stack([(group == g).astype(jnp.int32), side])

    def own_half(value):
        return pick(value[1], value[0])

    def other_half(value):
        return pick(value[0], value[1])

    def joined(own, other):
        return pick(jnp.stack([other, own]), jnp.stack([own, other]))

    half, point, column = np.meshgrid(np.arange(2), np.arange(POINTS), np.arange(HALF), indexing="ij")
    row_column = (half * HALF + column).reshape(-1)
    row_point = point.reshape(-1)
    place = np.arange(POINTS * K)
    by_column = jnp.asarray(np.arange(K)[None, :] == row_column[:, None], jnp.bfloat16)
    by_place = jnp.asarray(np.arange(K)[:, None] == place[None, :] % K, jnp.bfloat16)
    same_point = jnp.asarray(place[None, :] // K == row_point[:, None], jnp.float32)

    raw = sources[0]
    below = send(raw, of_kind(1), -1, straight)
    incoming = None
    pair_source = wide_source = None
    candidates = []
    for g in reversed(of_kind(0)):
        pieces = [] if incoming is None else [incoming[0], incoming[1]]
        places = [lambda side: (0, 0), lambda side: (1, 0)][: len(pieces)]
        crossed, edge_cross, edge_same, direct, share = march(
            turn(g),
            inverse_blocks,
            coupling,
            [raw, below],
            pieces,
            places,
            [
                (2 * ONE, lambda side: (1 - side, 0)),
                (WIDE, lambda side: (1 - side, side * ONE)),
                (WIDE, lambda side: (side, side * ONE)),
                (2 * ONE, lambda side: (side, 0)),
            ],
            2,
            POINTS,
            True,
        )
        crossed = send(crossed, [g], 1, partner)
        edge_cross = send(edge_cross, [g], 1, outward_cross)
        edge_same = send(edge_same, [g], 1, outward)
        direct = send(direct, [g], 1, straight)

        if pair_source is None:
            later, share = lax.optimization_barrier((raw, share))
            later = later.reshape(FN, POINTS, 2, HALF).transpose(2, 1, 3, 0).reshape(2, ONE, FN)
            got = send(other_half(later), of_kind(2), 0, partner)
            pair_source = [own_half(later), got]
            low = send(later[:, -EDGE:], of_kind(3), 0, neighbor(1))
            high = send(later[:, :EDGE], of_kind(3), 0, neighbor(-1))
            wide_source = [low, later, high]

        (state,) = march(
            turn(g - 1),
            inverse_blocks,
            coupling,
            [],
            [crossed, edge_cross, edge_same, direct],
            [
                lambda side: (0, (1 - side) * ONE),
                lambda side: (0, side * 2 * ONE),
                lambda side: (0, (1 - side) * 2 * ONE),
                lambda side: (0, side * ONE),
            ],
            [(2 * ONE, lambda side: (0, 0))],
            1,
            3 * POINTS,
            False,
        )
        arrived = send(state, [g - 1], 1, straight)

        share, state, _ = lax.optimization_barrier((share, state, state))
        low = send(share[:, -EDGE:], [g], 0, neighbor(1))
        high = send(share[:, :EDGE], [g], 0, neighbor(-1))
        got = send(pick(state[:ONE], state[ONE:]), [g - 1], 0, partner)
        arrived, low, high, got, pair_source, wide_source = lax.optimization_barrier(
            (arrived, low, high, got, pair_source, wide_source)
        )
        whole = added(share[:, EDGE:-EDGE], jnp.concatenate([low, high], 1))
        candidates += [whole, joined(pick(state[ONE:], state[:ONE]), got)]

        crossed, edge_cross, edge_same, direct = march(
            turn(g - 2),
            inverse_blocks,
            coupling,
            [],
            [arrived] + pair_source,
            [lambda side: (0, 0), lambda side: (0, side * ONE), lambda side: (0, (1 - side) * ONE)],
            [
                (2 * ONE, lambda side: (0, (1 - side) * ONE)),
                (WIDE, lambda side: (0, side * 2 * ONE)),
                (WIDE, lambda side: (0, (1 - side) * 2 * ONE)),
                (2 * ONE, lambda side: (0, side * ONE)),
            ],
            1,
            2 * POINTS,
            True,
        )
        crossed = send(crossed, [g - 2], 1, partner)
        edge_cross = send(edge_cross, [g - 2], 1, outward_cross)
        edge_same = send(edge_same, [g - 2], 1, inward)
        direct = send(direct, [g - 2], 1, straight)

        vmem = pl.BlockSpec(memory_space=pltpu.VMEM)
        middle = pl.pallas_call(
            center_kernel,
            out_shape=jax.ShapeDtypeStruct((2, ONE, FN), jnp.bfloat16),
            in_specs=[pl.BlockSpec(memory_space=pltpu.SMEM)] + [pl.BlockSpec(memory_space=pl.ANY)] * 4,
            out_specs=vmem,
            scratch_shapes=[pltpu.VMEM((WIDE, FN), jnp.bfloat16)] * 2 + [pltpu.SemaphoreType.DMA((4,))],
        )(turn(g - 3), direct, crossed, edge_same, edge_cross)
        back = send(middle, [g - 3], -1, straight)
        low, later, high = wide_source
        (state,) = march(
            turn(g - 3),
            inverse_blocks,
            coupling,
            [],
            [crossed, edge_cross, edge_same, direct, low[0], low[1], later[0], later[1], high[0], high[1]],
            [
                lambda side: (1 - side, 0),
                lambda side: (1 - side, side * ONE),
                lambda side: (side, side * ONE),
                lambda side: (side, 0),
                lambda side: (0, 0),
                lambda side: (1, 0),
                lambda side: (0, EDGE),
                lambda side: (1, EDGE),
                lambda side: (0, EDGE + ONE),
                lambda side: (1, EDGE + ONE),
            ],
            [],
            2,
            2 * POINTS,
            False,
        )
        candidates += [back, state]
        if g > 3:
            incoming = send(state, [g - 3], 1, straight)

    smem = pl.BlockSpec(memory_space=pltpu.SMEM)
    rows, gram = pl.pallas_call(
        functools.partial(gram_kernel, len(candidates)),
        out_shape=(
            jax.ShapeDtypeStruct((2, ONE, FN), jnp.bfloat16),
            jax.ShapeDtypeStruct((K, K), jnp.float32),
        ),
        in_specs=[smem] + [pl.BlockSpec(memory_space=pl.ANY)] * len(candidates),
        out_specs=(vmem, vmem),
        scratch_shapes=[pltpu.SemaphoreType.DMA],
        compiler_params=pltpu.CompilerParams(vmem_limit_bytes=16 * 1024 * 1024),
    )((sections - 1 - group).astype(jnp.int32)[None], *candidates)
    strides = [1 << at for at in range(spans.bit_length() - 1)]
    for stride in strides[:-1]:
        gram = gram + lax.ppermute(gram, "span", [(s, s ^ stride) for s in range(spans)])
    other = lax.ppermute(gram, "span", [(s, s ^ strides[-1]) for s in range(spans)])
    vmem = pl.BlockSpec(memory_space=pltpu.VMEM)
    basis, upper = pl.pallas_call(
        functools.partial(factor_kernel, 1.0 / float(FN * POINTS * spans)),
        out_shape=(
            jax.ShapeDtypeStruct((FN, POINTS * K), jnp.bfloat16),
            jax.ShapeDtypeStruct((K, K), jnp.float32),
        ),
        in_specs=[vmem] * 6,
        out_specs=(vmem, vmem),
        compiler_params=pltpu.CompilerParams(vmem_limit_bytes=16 * 1024 * 1024),
    )(gram, other, rows.reshape(POINTS * K, FN), by_column, by_place, same_point)
    return (basis[None], upper[None])


def solution(mesh):
    placed = (P("section", None, None), P("section", None), P("section", None, "span"))
    return jax.shard_map(
        local,
        mesh=mesh,
        in_specs=placed,
        out_specs=(P("section", None, "span"), P("section", None, None)),
        check_vma=False,
    )
```

```python
import functools

import jax
import jax.numpy as jnp
import numpy as np
from jax import lax
from jax.experimental import pallas as pl
from jax.experimental.pallas import tpu as pltpu
from jax.sharding import PartitionSpec as P

K = 48
STATIONS = 4
FN = 768
HALF = K // 2
POINTS = 8
ONE = POINTS * HALF
EDGE = STATIONS * HALF
WIDE = 2 * EDGE
STEP = 4
GRANT = 48 * 1024 * 1024
AXES = ("section", "span")


def unrolled(raw, turned, half):
    turned[...] = raw[...].astype(jnp.float32).T
    for point in range(POINTS):
        start = pl.multiple_of(point * K + half * HALF, 8)
        yield point * HALF, turned[pl.ds(start, HALF), :]


def march_kernel(number, places, parts, blocks, positions, grow, half_of, turn, coupling, weights, *refs):
    pieces, refs = refs[: len(places)], refs[len(places) :]
    raws = []
    if half_of is not None:
        raws, turned, refs = refs[:2], refs[-1], refs[2:-1]
    outs, (first, second, result, held, sems) = refs[:-5], refs[-5:]
    states = [first, second]
    order = list(reversed(range(STATIONS)))

    @pl.when(turn[0] == number)
    def _():
        copies = [
            pltpu.make_async_copy(weights.at[station], held.at[step], sems.at[step])
            for step, station in enumerate(order)
        ]
        for copy in copies:
            copy.start()
        side = turn[1]
        margin = 2 * HALF if grow else 0
        count = positions
        total = count * HALF + 2 * margin
        first[:, :total, :] = jnp.zeros((blocks, total, FN), jnp.float32)
        if raws:
            for at, value in unrolled(raws[0], turned, half_of(side)):
                first[0, margin + at : margin + at + HALF, :] = value
        for piece, where in zip(pieces, places):
            block, start = where(side)
            start = margin + start
            if not isinstance(start, int):
                start = pl.multiple_of(start, 8)
            if len(piece.shape) == 3:
                first[:, pl.ds(start, piece.shape[1]), :] += piece[...].astype(jnp.float32)
            else:
                first[block, pl.ds(start, piece.shape[0]), :] += piece[...].astype(jnp.float32)
        for step, station in enumerate(order):
            source, target = states[step % 2], states[1 - step % 2]
            count = count + 2 if grow else count - 2
            rates = coupling[station : station + 1, :]
            rest = 1.0 - 2.0 * rates
            copies[step].wait()
            if blocks == 1:
                cut = (count // 2 + 1) // 2 * 2
                chunks = [(0, 0, cut), (0, cut, count)]
            else:
                chunks = [(block, 0, count) for block in range(blocks)]
            for block, begin, end in chunks:
                at, rows = begin * HALF, (end - begin) * HALF
                both = source[block, at : at + rows, :] + source[block, at + 2 * HALF : at + 2 * HALF + rows, :]
                update = rest * source[block, at + HALF : at + HALF + rows, :] + rates * both
                moved = lax.dot_general(
                    update.astype(jnp.bfloat16),
                    held[step],
                    (((1,), (1,)), ((), ())),
                    preferred_element_type=jnp.float32,
                )
                if step == STATIONS - 1:
                    result[block, at : at + rows, :] = moved.astype(jnp.bfloat16)
                else:
                    target[block, margin + at : margin + at + rows, :] = moved
            if grow and step < STATIONS - 1:
                empty = jnp.zeros((blocks, margin, FN), jnp.float32)
                target[:, :margin, :] = empty
                target[:, margin + count * HALF : 2 * margin + count * HALF, :] = empty
        if not parts:
            outs[0][...] = result[...]
            return
        if raws:
            outs[-1][...] = result[0]
            for at, value in unrolled(raws[1], turned, half_of(side)):
                here = slice(EDGE + at, EDGE + at + HALF)
                first[0, here, :] = result[0, here, :].astype(jnp.float32) + value
            result[0, EDGE : EDGE + ONE, :] = first[0, EDGE : EDGE + ONE, :].astype(jnp.bfloat16)
        for (_, where), out in zip(parts, outs):
            block, start = where(side)
            if not isinstance(start, int):
                start = pl.multiple_of(start, EDGE)
            out[...] = result[block, pl.ds(start, out.shape[0]), :]


def march(turn, number, inverse_blocks, coupling, pieces, places, parts, blocks, positions, grow, raws=(), half_of=None):
    last = positions + (2 * STATIONS if grow else -2 * STATIONS)
    most = last + 2 if grow else positions
    vmem = pl.BlockSpec(memory_space=pltpu.VMEM)
    rows = blocks * HALF * STATIONS * (positions + last + (2 if grow else -2)) // 2
    whole = jax.ShapeDtypeStruct((blocks, last * HALF, FN), jnp.bfloat16)
    shapes = [jax.ShapeDtypeStruct((size, FN), jnp.bfloat16) for size, _ in parts]
    if not parts:
        shapes.append(whole)
    if raws:
        shapes.append(jax.ShapeDtypeStruct((last * HALF, FN), jnp.bfloat16))
    return pl.pallas_call(
        functools.partial(march_kernel, number, places, parts, blocks, positions, grow, half_of),
        out_shape=shapes,
        in_specs=[pl.BlockSpec(memory_space=pltpu.SMEM), vmem, pl.BlockSpec(memory_space=pl.ANY)]
        + [vmem] * (len(pieces) + len(raws)),
        out_specs=[vmem] * len(shapes),
        scratch_shapes=[pltpu.VMEM((blocks, most * HALF, FN), jnp.float32)] * 2
        + [
            pltpu.VMEM(whole.shape, jnp.bfloat16),
            pltpu.VMEM((STATIONS, FN, FN), jnp.bfloat16),
            pltpu.SemaphoreType.DMA((STATIONS,)),
        ]
        + ([pltpu.VMEM((POINTS * K, FN), jnp.float32)] if raws else []),
        compiler_params=pltpu.CompilerParams(vmem_limit_bytes=GRANT),
        cost_estimate=pl.CostEstimate(
            flops=2 * rows * FN * FN, bytes_accessed=2 * STATIONS * FN * FN, transcendentals=0
        ),
    )(turn, coupling, inverse_blocks, *pieces, *raws)


def center_kernel(number, turn, direct, crossed, edge_same, edge_cross, out):
    @pl.when(turn[0] == number)
    def _():
        side = turn[1]
        start = pl.multiple_of(side * EDGE, EDGE)
        from_edge = pl.multiple_of((1 - side) * EDGE, EDGE)
        for block, share, edge in ((side, direct, edge_same), (1 - side, crossed, edge_cross)):
            out[block, :, :] = share[EDGE : EDGE + ONE, :]
            here = out[block, pl.ds(start, EDGE), :].astype(jnp.float32)
            more = edge[pl.ds(from_edge, EDGE), :].astype(jnp.float32)
            out[block, pl.ds(start, EDGE), :] = (here + more).astype(jnp.bfloat16)


def gram_kernel(count, kind, *refs):
    candidates, (rows, gram, sem) = refs[:count], refs[count:]
    for number, candidate in enumerate(candidates):

        @pl.when(kind[0] == number)
        def _():
            copy = pltpu.make_async_copy(candidate, rows, sem)
            copy.start()
            copy.wait()

    flat = rows[...].reshape(2 * ONE, FN)
    full = lax.dot_general(flat, flat, (((1,), (1,)), ((), ())), preferred_element_type=jnp.float32)
    lines = []
    for first in range(2):
        line = []
        for second in range(2):
            block = None
            for point in range(POINTS):
                down, along = first * ONE + point * HALF, second * ONE + point * HALF
                term = full[down : down + HALF, along : along + HALF]
                block = term if block is None else block + term
            line.append(block)
        lines.append(jnp.concatenate(line, 1))
    gram[...] = jnp.concatenate(lines, 0)


def factor_kernel(scale, gram, other, rows, by_column, by_place, same_point, basis, upper):
    eye = (
        lax.broadcasted_iota(jnp.int32, (K, K), 0) == lax.broadcasted_iota(jnp.int32, (K, K), 1)
    ).astype(jnp.float32)
    table = jnp.concatenate([(gram[...] + other[...]) * scale, eye], 1)
    row_index = lax.broadcasted_iota(jnp.int32, (K, 2 * K), 0)
    roots = jnp.zeros((K, 2 * K), jnp.float32)
    for j in range(0, K, STEP):
        lines = [table[j + m : j + m + 1, :] for m in range(STEP)]
        columns = [jnp.broadcast_to(table[:, j + m : j + m + 1], table.shape) for m in range(STEP)]
        entries = [
            [jnp.broadcast_to(lines[m][:, j + k : j + k + 1], lines[m].shape) for k in range(STEP)]
            for m in range(STEP)
        ]
        below = table
        for m in range(STEP):
            inverse = 1.0 / entries[m][m]
            for k in range(m + 1, STEP):
                ratio = entries[m][k] * inverse
                for n in range(k, STEP):
                    entries[k][n] = entries[k][n] - ratio * entries[m][n]
                lines[k] = lines[k] - ratio * lines[m]
                columns[k] = columns[k] - ratio * columns[m]
            below = below - columns[m] * (inverse * lines[m])
            roots = jnp.where(row_index == j + m, lax.rsqrt(entries[m][m]), roots)
        table = jnp.where(row_index >= j + STEP, below, table)
        for m in range(STEP):
            table = jnp.where(row_index == j + m, lines[m], table)
    table = table * roots
    column = lax.broadcasted_iota(jnp.int32, (K, K), 1)
    row = lax.broadcasted_iota(jnp.int32, (K, K), 0)
    upper[...] = jnp.where(column >= row, table[:, :K], 0.0)
    inverse = table[:, K:]
    total = None
    for _ in range(2):
        term = inverse.astype(jnp.bfloat16)
        inverse = inverse - term.astype(jnp.float32)
        tall = lax.dot_general(
            by_column[...], term, (((1,), (1,)), ((), ())), preferred_element_type=jnp.float32
        ).astype(jnp.bfloat16)
        spread = lax.dot_general(
            tall, by_place[...], (((1,), (0,)), ((), ())), preferred_element_type=jnp.float32
        )
        spread = (spread * same_point[...]).astype(jnp.bfloat16)
        part = lax.dot_general(
            rows[...], spread, (((0,), (0,)), ((), ())), preferred_element_type=jnp.float32
        )
        total = part if total is None else total + part
    basis[...] = total.astype(jnp.bfloat16)


def local(inverse_blocks, coupling, sources):
    sections = lax.axis_size("section")
    spans = lax.axis_size("span")
    pairs = spans // 2
    assert sections % 4 == 0 and spans % 2 == 0 and sources.shape[2] == POINTS * K
    group = lax.axis_index("section")
    side = (lax.axis_index("span") % 2).astype(jnp.int32)
    upper_half = side == 1

    def pick(if_upper, if_lower):
        return jnp.where(upper_half, if_upper, if_lower)

    def added(state, more):
        return (state.astype(jnp.float32) + more.astype(jnp.float32)).astype(jnp.bfloat16)

    def send(value, groups, down, route):
        routes = []
        for g in groups:
            for s in range(spans):
                routes.append((g * spans + s, (g - down) * spans + route(s)))
        return lax.ppermute(value, AXES, routes)

    def straight(s):
        return s

    def partner(s):
        return s ^ 1

    def neighbor(shift):
        return lambda s: (s + shift) % spans

    def pair_route(pair, side):
        return (pair % pairs) * 2 + side

    def outward(s):
        return pair_route(s // 2 + 2 * (s % 2) - 1, s % 2)

    def outward_cross(s):
        return pair_route(s // 2 + 2 * (s % 2) - 1, 1 - s % 2)

    def inward(s):
        return pair_route(s // 2 + 1 - 2 * (s % 2), s % 2)

    def of_kind(kind):
        return [g for g in range(sections) if (sections - 1 - g) % 4 == kind]

    turn = jnp.stack([group.astype(jnp.int32), side])

    def own_half(value):
        return pick(value[1], value[0])

    def other_half(value):
        return pick(value[0], value[1])

    def joined(own, other):
        return pick(jnp.stack([other, own]), jnp.stack([own, other]))

    half, point, column = np.meshgrid(np.arange(2), np.arange(POINTS), np.arange(HALF), indexing="ij")
    row_column = (half * HALF + column).reshape(-1)
    row_point = point.reshape(-1)
    place = np.arange(POINTS * K)
    by_column = jnp.asarray(np.arange(K)[None, :] == row_column[:, None], jnp.bfloat16)
    by_place = jnp.asarray(np.arange(K)[:, None] == place[None, :] % K, jnp.bfloat16)
    same_point = jnp.asarray(place[None, :] // K == row_point[:, None], jnp.float32)

    raw = sources[0]
    below = send(raw, of_kind(1), -1, straight)
    incoming = None
    pair_source = wide_source = None
    candidates = []
    for g in reversed(of_kind(0)):
        shares = []
        for half_of in (lambda side: 1 - side, lambda side: side):
            pieces = [] if incoming is None else [half_of(upper_half.astype(jnp.int32))]
            if incoming is not None:
                pieces = [lax.dynamic_index_in_dim(incoming, pieces[0], 0, keepdims=False)]
            shares.append(
                march(
                    turn,
                    g,
                    inverse_blocks,
                    coupling,
                    pieces,
                    [lambda side: (0, 0)][: len(pieces)],
                    [(2 * ONE, lambda side: (0, 0)), (WIDE, lambda side: (0, side * ONE))],
                    1,
                    POINTS,
                    True,
                    [raw, below],
                    half_of,
                )
            )
        (crossed, edge_cross, other_share), (direct, edge_same, own_share) = shares
        crossed = send(crossed, [g], 1, partner)
        edge_cross = send(edge_cross, [g], 1, outward_cross)
        edge_same = send(edge_same, [g], 1, outward)
        direct = send(direct, [g], 1, straight)

        if pair_source is None:
            later, own_share = lax.optimization_barrier((raw, own_share))
            later = later.reshape(FN, POINTS, 2, HALF).transpose(2, 1, 3, 0).reshape(2, ONE, FN)
            got = send(other_half(later), of_kind(2), 0, partner)
            pair_source = [own_half(later), got]
            low = send(later[:, -EDGE:], of_kind(3), 0, neighbor(1))
            high = send(later[:, :EDGE], of_kind(3), 0, neighbor(-1))
            wide_source = [low, later, high]

        (state,) = march(
            turn,
            g - 1,
            inverse_blocks,
            coupling,
            [crossed, edge_cross, edge_same, direct],
            [
                lambda side: (0, (1 - side) * ONE),
                lambda side: (0, side * 2 * ONE),
                lambda side: (0, (1 - side) * 2 * ONE),
                lambda side: (0, side * ONE),
            ],
            [(2 * ONE, lambda side: (0, 0))],
            1,
            3 * POINTS,
            False,
        )
        arrived = send(state, [g - 1], 1, straight)

        share, state, _ = lax.optimization_barrier((joined(own_share, other_share), state, state))
        low = send(share[:, -EDGE:], [g], 0, neighbor(1))
        high = send(share[:, :EDGE], [g], 0, neighbor(-1))
        got = send(pick(state[:ONE], state[ONE:]), [g - 1], 0, partner)
        whole = added(share[:, EDGE:-EDGE], jnp.concatenate([low, high], 1))
        paired = joined(pick(state[ONE:], state[:ONE]), got)
        arrived, whole, paired, pair_source, wide_source = lax.optimization_barrier(
            (arrived, whole, paired, pair_source, wide_source)
        )
        candidates += [whole, paired]

        crossed, edge_cross, edge_same, direct = march(
            turn,
            g - 2,
            inverse_blocks,
            coupling,
            [arrived] + pair_source,
            [lambda side: (0, 0), lambda side: (0, side * ONE), lambda side: (0, (1 - side) * ONE)],
            [
                (2 * ONE, lambda side: (0, (1 - side) * ONE)),
                (WIDE, lambda side: (0, side * 2 * ONE)),
                (WIDE, lambda side: (0, (1 - side) * 2 * ONE)),
                (2 * ONE, lambda side: (0, side * ONE)),
            ],
            1,
            2 * POINTS,
            True,
        )
        crossed = send(crossed, [g - 2], 1, partner)
        edge_cross = send(edge_cross, [g - 2], 1, outward_cross)
        edge_same = send(edge_same, [g - 2], 1, inward)
        direct = send(direct, [g - 2], 1, straight)

        vmem = pl.BlockSpec(memory_space=pltpu.VMEM)
        middle = pl.pallas_call(
            functools.partial(center_kernel, g - 3),
            out_shape=jax.ShapeDtypeStruct((2, ONE, FN), jnp.bfloat16),
            in_specs=[pl.BlockSpec(memory_space=pltpu.SMEM)] + [vmem] * 4,
            out_specs=vmem,
        )(turn, direct, crossed, edge_same, edge_cross)
        back = send(middle, [g - 3], -1, straight)
        (state,) = march(
            turn,
            g - 3,
            inverse_blocks,
            coupling,
            [crossed, edge_cross, edge_same, direct] + wide_source,
            [
                lambda side: (1 - side, 0),
                lambda side: (1 - side, side * ONE),
                lambda side: (side, side * ONE),
                lambda side: (side, 0),
                lambda side: (0, 0),
                lambda side: (0, EDGE),
                lambda side: (0, EDGE + ONE),
            ],
            [],
            2,
            2 * POINTS,
            False,
        )
        candidates += [back, state]
        if g > 3:
            incoming = send(state, [g - 3], 1, straight)

    smem = pl.BlockSpec(memory_space=pltpu.SMEM)
    rows, gram = pl.pallas_call(
        functools.partial(gram_kernel, len(candidates)),
        out_shape=(
            jax.ShapeDtypeStruct((2, ONE, FN), jnp.bfloat16),
            jax.ShapeDtypeStruct((K, K), jnp.float32),
        ),
        in_specs=[smem] + [pl.BlockSpec(memory_space=pl.ANY)] * len(candidates),
        out_specs=(vmem, vmem),
        scratch_shapes=[pltpu.SemaphoreType.DMA],
        compiler_params=pltpu.CompilerParams(vmem_limit_bytes=16 * 1024 * 1024),
    )((sections - 1 - group).astype(jnp.int32)[None], *candidates)
    strides = [1 << at for at in range(spans.bit_length() - 1)]
    for stride in strides[:-1]:
        gram = gram + lax.ppermute(gram, "span", [(s, s ^ stride) for s in range(spans)])
    other = lax.ppermute(gram, "span", [(s, s ^ strides[-1]) for s in range(spans)])
    vmem = pl.BlockSpec(memory_space=pltpu.VMEM)
    basis, upper = pl.pallas_call(
        functools.partial(factor_kernel, 1.0 / float(FN * POINTS * spans)),
        out_shape=(
            jax.ShapeDtypeStruct((FN, POINTS * K), jnp.bfloat16),
            jax.ShapeDtypeStruct((K, K), jnp.float32),
        ),
        in_specs=[vmem] * 6,
        out_specs=(vmem, vmem),
        compiler_params=pltpu.CompilerParams(vmem_limit_bytes=16 * 1024 * 1024),
    )(gram, other, rows.reshape(POINTS * K, FN), by_column, by_place, same_point)
    return (basis[None], upper[None])


def solution(mesh):
    placed = (P("section", None, None), P("section", None), P("section", None, "span"))
    return jax.shard_map(
        local,
        mesh=mesh,
        in_specs=placed,
        out_specs=(P("section", None, "span"), P("section", None, None)),
        check_vma=False,
    )
```

```python
import functools

import jax
import jax.numpy as jnp
import numpy as np
from jax import lax
from jax.experimental import pallas as pl
from jax.experimental.pallas import tpu as pltpu
from jax.sharding import PartitionSpec as P

K = 48
STATIONS = 4
FN = 768
HALF = K // 2
POINTS = 8
ONE = POINTS * HALF
EDGE = STATIONS * HALF
WIDE = 2 * EDGE
STEP = 4
GRANT = 48 * 1024 * 1024
SMALL = 16 * 1024 * 1024
AXES = ("section", "span")


def march_kernel(number, places, others, chunks_of, blocks, positions, grow, raw, turn, coupling, weights, *refs):
    refs = list(refs)
    pieces = [refs.pop(0) for _ in places]
    givers = [refs.pop(0) for _ in others[0]]
    raws = [refs.pop(0) for _ in range(2 * raw)]
    outs = refs[: -5 - 3 * raw]
    first, second, result, held, sems, *locals_ = refs[-5 - 3 * raw :]
    states = [first, second]
    order = list(reversed(range(STATIONS)))
    side = turn[1]

    @pl.when(turn[0] == number)
    def _():
        copies = [
            pltpu.make_async_copy(weights.at[station], held.at[step], sems.at[step])
            for step, station in enumerate(order)
        ]
        if raw:
            fetches = [
                pltpu.make_async_copy(away, here, locals_[2].at[at])
                for at, (away, here) in enumerate(zip(raws, locals_))
            ]
            for fetch in fetches:
                fetch.start()
        for copy in copies:
            copy.start()
        margin = 2 * HALF if grow else 0
        count = positions
        total = count * HALF + 2 * margin
        first[:, :total, :] = jnp.zeros((blocks, total, FN), jnp.float32)
        if raw:
            for fetch in fetches:
                fetch.wait()
            rows = lax.dot_general(
                locals_[1][...], locals_[0][...], (((1,), (1,)), ((), ())), preferred_element_type=jnp.float32
            )
            for half in range(2):
                first[half, margin : margin + ONE, :] = rows[half * ONE : (half + 1) * ONE]
        for piece, (where, rows) in zip(pieces, places):
            block, start = where(side)
            start = margin + start
            if not isinstance(start, int):
                start = pl.multiple_of(start, 8)
            if len(piece.shape) == 3:
                first[:, pl.ds(start, rows), :] += piece[...].astype(jnp.float32)
            else:
                first[block, pl.ds(start, rows), :] += piece[:rows, :].astype(jnp.float32)
        for step, station in enumerate(order):
            source, target = states[step % 2], states[1 - step % 2]
            count = count + 2 if grow else count - 2
            rates = coupling[station : station + 1, :]
            rest = 1.0 - 2.0 * rates
            copies[step].wait()
            for group in chunks_of(count):
                updates = []
                for block, begin, end in group:
                    at, rows = begin * HALF, (end - begin) * HALF
                    both = source[block, at : at + rows, :] + source[block, at + 2 * HALF : at + 2 * HALF + rows, :]
                    update = rest * source[block, at + HALF : at + HALF + rows, :] + rates * both
                    updates.append(update.astype(jnp.bfloat16))
                moved = lax.dot_general(
                    jnp.concatenate(updates, 0) if len(updates) > 1 else updates[0],
                    held[step],
                    (((1,), (1,)), ((), ())),
                    preferred_element_type=jnp.float32,
                )
                taken = 0
                for block, begin, end in group:
                    at, rows = begin * HALF, (end - begin) * HALF
                    value = moved[taken : taken + rows]
                    taken += rows
                    if step == STATIONS - 1:
                        result[block, at : at + rows, :] = value.astype(jnp.bfloat16)
                    else:
                        target[block, margin + at : margin + at + rows, :] = value
            if grow and step < STATIONS - 1:
                empty = jnp.zeros((blocks, margin, FN), jnp.float32)
                target[:, :margin, :] = empty
                target[:, margin + count * HALF : 2 * margin + count * HALF, :] = empty
        if len(outs) == 1:
            outs[0][...] = result[...]
        else:
            for out, where in zip(outs, others[2]):
                start = pl.multiple_of(where(side), EDGE)
                out[...] = result[0, pl.ds(start, out.shape[0]), :]

    for owner, moves in others[1]:

        @pl.when(turn[0] == owner)
        def _():
            copies = []
            for at, (giver, block, start, rows, out, to) in enumerate(moves):
                start = start(side)
                if not isinstance(start, int):
                    start = pl.multiple_of(start, EDGE)
                source = givers[giver]
                source = source.at[pl.ds(start, rows)] if block is None else source.at[block, pl.ds(start, rows)]
                copies.append(pltpu.make_async_copy(source, outs[out].at[pl.ds(to, rows)], sems.at[at]))
            for copy in copies:
                copy.start()
            for copy in copies:
                copy.wait()


def march(
    turn, number, inverse_blocks, coupling, pieces, chunks_of, blocks, positions, grow, raw=(), others=((), (), ())
):
    last = positions + (2 * STATIONS if grow else -2 * STATIONS)
    most = last + 2 if grow else positions
    vmem = pl.BlockSpec(memory_space=pltpu.VMEM)
    away = pl.BlockSpec(memory_space=pl.ANY)
    rows = blocks * HALF * STATIONS * (positions + last + (2 if grow else -2)) // 2
    whole = jax.ShapeDtypeStruct((blocks, last * HALF, FN), jnp.bfloat16)
    shapes = [whole]
    if others[2]:
        shapes = [jax.ShapeDtypeStruct((size, FN), jnp.bfloat16) for size in (2 * ONE, WIDE, WIDE, 2 * ONE)]
    values = [value for value, _, _ in pieces]
    scratch = [pltpu.VMEM((blocks, most * HALF, FN), jnp.float32)] * 2 + [
        pltpu.VMEM(whole.shape, jnp.bfloat16),
        pltpu.VMEM((STATIONS, FN, FN), jnp.bfloat16),
        pltpu.SemaphoreType.DMA((STATIONS,)),
    ]
    if raw:
        scratch += [pltpu.VMEM(value.shape, jnp.bfloat16) for value in raw] + [pltpu.SemaphoreType.DMA((2,))]
    return pl.pallas_call(
        functools.partial(
            march_kernel,
            number,
            [(where, size) for _, where, size in pieces],
            others,
            chunks_of,
            blocks,
            positions,
            grow,
            1 if raw else 0,
        ),
        out_shape=shapes,
        in_specs=[pl.BlockSpec(memory_space=pltpu.SMEM), vmem, away]
        + [vmem] * len(values)
        + [away] * (len(others[0]) + len(raw)),
        out_specs=[vmem] * len(shapes),
        scratch_shapes=scratch,
        compiler_params=pltpu.CompilerParams(vmem_limit_bytes=GRANT),
        cost_estimate=pl.CostEstimate(
            flops=2 * rows * FN * FN, bytes_accessed=2 * STATIONS * FN * FN, transcendentals=0
        ),
    )(turn, coupling, inverse_blocks, *values, *others[0], *raw)


def ship_kernel(number, turn, share, below, raw, order, crossed, edge_cross, edge_same, direct, *scratch):
    held, held_order, turned, whole, sems = scratch
    side, kind = turn[1], turn[2]
    mine = turn[0] == number
    orders = pltpu.make_async_copy(order, held_order, sems.at[0])

    def ordered(source):
        copy = pltpu.make_async_copy(source, held, sems.at[1])
        orders.start()
        copy.start()
        orders.wait()
        copy.wait()
        rows = lax.dot_general(
            held_order[...], held[...], (((1,), (1,)), ((), ())), preferred_element_type=jnp.float32
        )
        for half in range(2):
            turned[half, :, :] = rows[half * ONE : (half + 1) * ONE]

    @pl.when(mine)
    def _():
        ordered(below)
        whole[...] = share[...]
        middle = share[:, EDGE : EDGE + ONE, :].astype(jnp.float32) + turned[...]
        whole[:, EDGE : EDGE + ONE, :] = middle.astype(jnp.bfloat16)
        start = pl.multiple_of(side * ONE, ONE)
        edge_cross[...] = whole[1 - side, pl.ds(start, WIDE), :]
        edge_same[...] = whole[side, pl.ds(start, WIDE), :]
        crossed[...] = whole[1 - side]
        direct[...] = whole[side]

    @pl.when(kind >= 2)
    def _():
        ordered(raw)

    @pl.when(kind == 2)
    def _():
        crossed[:ONE, :] = turned[1 - side].astype(jnp.bfloat16)
        direct[:ONE, :] = turned[side].astype(jnp.bfloat16)

    @pl.when(kind == 3)
    def _():
        for half in range(2):
            value = turned[half].astype(jnp.bfloat16)
            edge_cross[half * EDGE : (half + 1) * EDGE, :] = value[-EDGE:]
            edge_same[half * EDGE : (half + 1) * EDGE, :] = value[:EDGE]
            direct[half * ONE : (half + 1) * ONE, :] = value


def center_kernel(number, turn, direct, crossed, edge_same, edge_cross, out):
    @pl.when(turn[0] == number)
    def _():
        side = turn[1]
        start = pl.multiple_of(side * EDGE, EDGE)
        from_edge = pl.multiple_of((1 - side) * EDGE, EDGE)
        for block, share, edge in ((side, direct, edge_same), (1 - side, crossed, edge_cross)):
            out[block, :, :] = share[EDGE : EDGE + ONE, :]
            here = out[block, pl.ds(start, EDGE), :].astype(jnp.float32)
            more = edge[pl.ds(from_edge, EDGE), :].astype(jnp.float32)
            out[block, pl.ds(start, EDGE), :] = (here + more).astype(jnp.bfloat16)


def gram_kernel(numbers, turn, *refs):
    inputs, (rows, gram, edges, sems) = refs[: 7 * len(numbers)], refs[7 * len(numbers) :]
    side = turn[1]

    def fetch(*pairs):
        copies = [pltpu.make_async_copy(source, target, sems.at[at]) for at, (source, target) in enumerate(pairs)]
        for copy in copies:
            copy.start()
        for copy in copies:
            copy.wait()

    for at, number in enumerate(numbers):
        share, low, high, state, crossed, back, last = inputs[7 * at : 7 * at + 7]

        @pl.when(turn[0] == number)
        def _():
            halves = [slice(0, EDGE), slice(EDGE, 2 * EDGE)]
            fetch(
                *[(share.at[half, EDGE : EDGE + ONE], rows.at[half]) for half in range(2)],
                *[(low.at[halves[half]], edges.at[half, :EDGE]) for half in range(2)],
                *[(high.at[halves[half]], edges.at[half, EDGE:]) for half in range(2)],
            )
            rows[...] = (rows[...].astype(jnp.float32) + edges[...].astype(jnp.float32)).astype(jnp.bfloat16)

        @pl.when(turn[0] == number - 1)
        def _():
            start = pl.multiple_of(side * ONE, ONE)
            fetch((state.at[pl.ds(start, ONE)], rows.at[side]), (crossed.at[:ONE], rows.at[1 - side]))

        @pl.when(turn[0] == number - 2)
        def _():
            fetch((back, rows))

        @pl.when(turn[0] == number - 3)
        def _():
            fetch((last, rows))

    flat = rows[...].reshape(2 * ONE, FN)
    full = lax.dot_general(flat, flat, (((1,), (1,)), ((), ())), preferred_element_type=jnp.float32)
    lines = []
    for first in range(2):
        line = []
        for second in range(2):
            block = None
            for point in range(POINTS):
                down, along = first * ONE + point * HALF, second * ONE + point * HALF
                term = full[down : down + HALF, along : along + HALF]
                block = term if block is None else block + term
            line.append(block)
        lines.append(jnp.concatenate(line, 1))
    gram[...] = jnp.concatenate(lines, 0)


def factor_kernel(scale, gram, other, rows, by_column, by_place, same_point, basis, upper):
    eye = (
        lax.broadcasted_iota(jnp.int32, (K, K), 0) == lax.broadcasted_iota(jnp.int32, (K, K), 1)
    ).astype(jnp.float32)
    table = jnp.concatenate([(gram[...] + other[...]) * scale, eye], 1)
    row_index = lax.broadcasted_iota(jnp.int32, (K, 2 * K), 0)
    roots = jnp.zeros((K, 2 * K), jnp.float32)
    for j in range(0, K, STEP):
        lines = [table[j + m : j + m + 1, :] for m in range(STEP)]
        columns = [jnp.broadcast_to(table[:, j + m : j + m + 1], table.shape) for m in range(STEP)]
        entries = [
            [jnp.broadcast_to(lines[m][:, j + k : j + k + 1], lines[m].shape) for k in range(STEP)]
            for m in range(STEP)
        ]
        below = table
        for m in range(STEP):
            inverse = 1.0 / entries[m][m]
            for k in range(m + 1, STEP):
                ratio = entries[m][k] * inverse
                for n in range(k, STEP):
                    entries[k][n] = entries[k][n] - ratio * entries[m][n]
                lines[k] = lines[k] - ratio * lines[m]
                columns[k] = columns[k] - ratio * columns[m]
            below = below - columns[m] * (inverse * lines[m])
            roots = jnp.where(row_index == j + m, lax.rsqrt(entries[m][m]), roots)
        table = jnp.where(row_index >= j + STEP, below, table)
        for m in range(STEP):
            table = jnp.where(row_index == j + m, lines[m], table)
    table = table * roots
    column = lax.broadcasted_iota(jnp.int32, (K, K), 1)
    row = lax.broadcasted_iota(jnp.int32, (K, K), 0)
    upper[...] = jnp.where(column >= row, table[:, :K], 0.0)
    inverse = table[:, K:]
    total = None
    for _ in range(2):
        term = inverse.astype(jnp.bfloat16)
        inverse = inverse - term.astype(jnp.float32)
        tall = lax.dot_general(
            by_column[...], term, (((1,), (1,)), ((), ())), preferred_element_type=jnp.float32
        ).astype(jnp.bfloat16)
        spread = lax.dot_general(
            tall, by_place[...], (((1,), (0,)), ((), ())), preferred_element_type=jnp.float32
        )
        spread = (spread * same_point[...]).astype(jnp.bfloat16)
        part = lax.dot_general(
            rows[...], spread, (((0,), (0,)), ((), ())), preferred_element_type=jnp.float32
        )
        total = part if total is None else total + part
    basis[...] = total.astype(jnp.bfloat16)


def local(inverse_blocks, coupling, sources):
    sections = lax.axis_size("section")
    spans = lax.axis_size("span")
    pairs = spans // 2
    assert sections % 4 == 0 and spans % 2 == 0 and sources.shape[2] == POINTS * K
    group = lax.axis_index("section")
    side = (lax.axis_index("span") % 2).astype(jnp.int32)

    def send(value, *legs):
        routes = []
        for groups, down, route in legs:
            for g in groups:
                for s in range(spans):
                    routes.append((g * spans + s, (g - down) * spans + route(s)))
        return lax.ppermute(value, AXES, routes)

    def straight(s):
        return s

    def partner(s):
        return s ^ 1

    def neighbor(shift):
        return lambda s: (s + shift) % spans

    def pair_route(pair, side):
        return (pair % pairs) * 2 + side

    def outward(s):
        return pair_route(s // 2 + 2 * (s % 2) - 1, s % 2)

    def outward_cross(s):
        return pair_route(s // 2 + 2 * (s % 2) - 1, 1 - s % 2)

    def inward(s):
        return pair_route(s // 2 + 1 - 2 * (s % 2), s % 2)

    def of_kind(kind):
        return [g for g in range(sections) if (sections - 1 - g) % 4 == kind]

    turn = jnp.stack([group.astype(jnp.int32), side, ((sections - 1 - group) % 4).astype(jnp.int32)])

    half, point, column = np.meshgrid(np.arange(2), np.arange(POINTS), np.arange(HALF), indexing="ij")
    row_column = (half * HALF + column).reshape(-1)
    row_point = point.reshape(-1)
    place = np.arange(POINTS * K)
    order = jnp.asarray(place[None, :] == (row_point * K + row_column)[:, None], jnp.bfloat16)
    by_column = jnp.asarray(np.arange(K)[None, :] == row_column[:, None], jnp.bfloat16)
    by_place = jnp.asarray(np.arange(K)[:, None] == place[None, :] % K, jnp.bfloat16)
    same_point = jnp.asarray(place[None, :] // K == row_point[:, None], jnp.float32)

    def in_one(count):
        return [[(0, 0, count)]]

    def in_two(count):
        cut = (count // 2 + 1) // 2 * 2
        return [[(0, 0, cut)], [(0, cut, count)]]

    def both_in_one(count):
        return [[(0, 0, count), (1, 0, count)]]

    def both_in_two(count):
        return [[(0, 0, count)], [(1, 0, count)]]

    smem = pl.BlockSpec(memory_space=pltpu.SMEM)
    vmem = pl.BlockSpec(memory_space=pltpu.VMEM)
    away = pl.BlockSpec(memory_space=pl.ANY)
    raw = sources[0]
    below = send(raw, (of_kind(1), -1, straight))
    incoming = None
    pair_source = wide_source = None
    candidates = []
    for g in reversed(of_kind(0)):
        pieces = [] if incoming is None else [(incoming, lambda side: (0, 0), ONE)]
        (share,) = march(
            turn, g, inverse_blocks, coupling, pieces, both_in_one, 2, POINTS, True, (raw, order)
        )
        crossed, edge_cross, edge_same, direct = pl.pallas_call(
            functools.partial(ship_kernel, g),
            out_shape=[jax.ShapeDtypeStruct((size, FN), jnp.bfloat16) for size in (2 * ONE, WIDE, WIDE, 2 * ONE)],
            in_specs=[smem, vmem, away, away, away],
            out_specs=[vmem] * 4,
            scratch_shapes=[
                pltpu.VMEM(raw.shape, jnp.bfloat16),
                pltpu.VMEM(order.shape, jnp.bfloat16),
                pltpu.VMEM((2, ONE, FN), jnp.float32),
                pltpu.VMEM(share.shape, jnp.bfloat16),
                pltpu.SemaphoreType.DMA((2,)),
            ],
            compiler_params=pltpu.CompilerParams(vmem_limit_bytes=SMALL),
        )(turn, share, below, raw, order)
        kept = direct
        first = incoming is None
        edge_cross = send(edge_cross, ([g], 1, outward_cross), (of_kind(3) if first else [], 0, neighbor(1)))
        edge_same = send(edge_same, ([g], 1, outward), (of_kind(3) if first else [], 0, neighbor(-1)))
        crossed = send(crossed, ([g], 1, partner), (of_kind(2) if first else [], 0, partner))
        direct = send(direct, ([g], 1, straight))
        if first:
            pair_source = [
                (kept, lambda side: (0, side * ONE), ONE),
                (crossed, lambda side: (0, (1 - side) * ONE), ONE),
            ]
            wide_source = [
                (edge_cross.reshape(2, EDGE, FN), lambda side: (0, 0), EDGE),
                (kept.reshape(2, ONE, FN), lambda side: (0, EDGE), ONE),
                (edge_same.reshape(2, EDGE, FN), lambda side: (0, EDGE + ONE), EDGE),
            ]

        (state,) = march(
            turn,
            g - 1,
            inverse_blocks,
            coupling,
            [
                (crossed, lambda side: (0, (1 - side) * ONE), 2 * ONE),
                (edge_cross, lambda side: (0, side * 2 * ONE), WIDE),
                (edge_same, lambda side: (0, (1 - side) * 2 * ONE), WIDE),
                (direct, lambda side: (0, side * ONE), 2 * ONE),
            ],
            in_one,
            1,
            3 * POINTS,
            False,
        )
        state = state[0]
        arrived = send(state, ([g - 1], 1, straight))

        crossed, edge_cross, edge_same, direct = march(
            turn,
            g - 2,
            inverse_blocks,
            coupling,
            [(arrived, lambda side: (0, 0), 2 * ONE)] + pair_source,
            in_two,
            1,
            2 * POINTS,
            True,
            (),
            (
                (share, state),
                (
                    (
                        g,
                        (
                            (0, 0, lambda side: EDGE + ONE, EDGE, 1, 0),
                            (0, 1, lambda side: EDGE + ONE, EDGE, 1, EDGE),
                            (0, 0, lambda side: 0, EDGE, 2, 0),
                            (0, 1, lambda side: 0, EDGE, 2, EDGE),
                        ),
                    ),
                    (g - 1, ((1, None, lambda side: (1 - side) * ONE, ONE, 0, 0),)),
                ),
                (
                    lambda side: (1 - side) * ONE,
                    lambda side: side * 2 * ONE,
                    lambda side: (1 - side) * 2 * ONE,
                    lambda side: side * ONE,
                ),
            ),
        )
        edge_cross = send(edge_cross, ([g - 2], 1, outward_cross), ([g], 0, neighbor(1)))
        edge_same = send(edge_same, ([g - 2], 1, inward), ([g], 0, neighbor(-1)))
        crossed = send(crossed, ([g - 2], 1, partner), ([g - 1], 0, partner))
        direct = send(direct, ([g - 2], 1, straight))

        middle = pl.pallas_call(
            functools.partial(center_kernel, g - 3),
            out_shape=jax.ShapeDtypeStruct((2, ONE, FN), jnp.bfloat16),
            in_specs=[smem] + [vmem] * 4,
            out_specs=vmem,
            compiler_params=pltpu.CompilerParams(vmem_limit_bytes=SMALL),
        )(turn, direct, crossed, edge_same, edge_cross)
        back = send(middle, ([g - 3], -1, straight))
        (last,) = march(
            turn,
            g - 3,
            inverse_blocks,
            coupling,
            [
                (crossed, lambda side: (1 - side, 0), 2 * ONE),
                (edge_cross, lambda side: (1 - side, side * ONE), WIDE),
                (edge_same, lambda side: (side, side * ONE), WIDE),
                (direct, lambda side: (side, 0), 2 * ONE),
            ]
            + wide_source,
            both_in_two,
            2,
            2 * POINTS,
            False,
        )
        candidates += [share, edge_cross, edge_same, state, crossed, back, last]
        if g > 3:
            incoming = send(last, ([g - 3], 1, straight))

    rows, gram = pl.pallas_call(
        functools.partial(gram_kernel, list(reversed(of_kind(0)))),
        out_shape=(
            jax.ShapeDtypeStruct((2, ONE, FN), jnp.bfloat16),
            jax.ShapeDtypeStruct((K, K), jnp.float32),
        ),
        in_specs=[smem] + [away] * len(candidates),
        out_specs=(vmem, vmem),
        scratch_shapes=[pltpu.VMEM((2, ONE, FN), jnp.bfloat16), pltpu.SemaphoreType.DMA((6,))],
        compiler_params=pltpu.CompilerParams(vmem_limit_bytes=SMALL),
    )(turn, *candidates)
    strides = [1 << at for at in range(spans.bit_length() - 1)]
    for stride in strides[:-1]:
        gram = gram + lax.ppermute(gram, "span", [(s, s ^ stride) for s in range(spans)])
    other = lax.ppermute(gram, "span", [(s, s ^ strides[-1]) for s in range(spans)])

    basis, upper = pl.pallas_call(
        functools.partial(factor_kernel, 1.0 / float(FN * POINTS * spans)),
        out_shape=(
            jax.ShapeDtypeStruct((FN, POINTS * K), jnp.bfloat16),
            jax.ShapeDtypeStruct((K, K), jnp.float32),
        ),
        in_specs=[vmem] * 6,
        out_specs=(vmem, vmem),
        compiler_params=pltpu.CompilerParams(vmem_limit_bytes=SMALL),
    )(gram, other, rows.reshape(POINTS * K, FN), by_column, by_place, same_point)
    return (basis[None], upper[None])


def solution(mesh):
    placed = (P("section", None, None), P("section", None), P("section", None, "span"))
    return jax.shard_map(
        local,
        mesh=mesh,
        in_specs=placed,
        out_specs=(P("section", None, "span"), P("section", None, None)),
        check_vma=False,
    )
```

```python
import functools

import jax
import jax.numpy as jnp
import numpy as np
from jax import lax
from jax.experimental import pallas as pl
from jax.experimental.pallas import tpu as pltpu
from jax.sharding import PartitionSpec as P

K = 48
STATIONS = 4
FN = 768
HALF = K // 2
POINTS = 8
ONE = POINTS * HALF
EDGE = STATIONS * HALF
WIDE = 2 * EDGE
STEP = 4
GRANT = 48 * 1024 * 1024
SMALL = 16 * 1024 * 1024
AXES = ("section", "span")


def one_hot_order():
    at = lax.broadcasted_iota(jnp.int32, (1, POINTS * K), 1)
    point = at * 1366 >> 16
    column = at - point * K
    half = (column >= HALF).astype(jnp.int32)
    target = half * (ONE - HALF) + point * HALF + column
    row = lax.broadcasted_iota(jnp.int32, (POINTS * K, POINTS * K), 0)
    return jnp.where(row == target, 1.0, 0.0).astype(jnp.bfloat16)


def ordered(raw):
    return lax.dot_general(one_hot_order(), raw, (((1,), (1,)), ((), ())), preferred_element_type=jnp.float32)


def march_kernel(number, places, others, plan, blocks, positions, grow, raw, turn, coupling, weights, *refs):
    refs = list(refs)
    pieces = [refs.pop(0) for _ in places]
    raws = [refs.pop(0) for _ in range(raw)]
    givers = [refs.pop(0) for _ in others[0]]
    outs, (first, second, held, sems) = refs[:-4], refs[-4:]
    result = outs[0]
    states = [first, second]
    order = list(reversed(range(STATIONS)))
    side = turn[1]

    @pl.when(turn[0] == number)
    def _():
        copies = [
            pltpu.make_async_copy(weights.at[station], held.at[step], sems.at[step])
            for step, station in enumerate(order)
        ]
        for copy in copies:
            copy.start()
        margin = 2 * HALF if grow else 0
        total = positions * HALF + 2 * margin
        first[:, :total, :] = jnp.zeros((blocks, total, FN), jnp.float32)
        if raw:
            rows = ordered(raws[0][...])
            for half in range(2):
                first[half, margin : margin + ONE, :] = rows[half * ONE : (half + 1) * ONE]
        for piece, (where, rows, pick) in zip(pieces, places):
            block, start = where(side)
            start = margin + start
            if not isinstance(start, int):
                start = pl.multiple_of(start, 8)
            if pick is not None:
                first[block, pl.ds(start, rows), :] += piece[pick(side), :rows, :].astype(jnp.float32)
            elif len(piece.shape) == 3:
                first[:, pl.ds(start, rows), :] += piece[:, :rows, :].astype(jnp.float32)
            else:
                first[block, pl.ds(start, rows), :] += piece[:rows, :].astype(jnp.float32)

        def stencil(step, chunk):
            block, begin, end = chunk
            at, rows = begin * HALF, (end - begin) * HALF
            source = states[step % 2]
            rates = coupling[order[step] : order[step] + 1, :]
            both = source[block, at : at + rows, :] + source[block, at + 2 * HALF : at + 2 * HALF + rows, :]
            update = (1.0 - 2.0 * rates) * source[block, at + HALF : at + HALF + rows, :] + rates * both
            return update.astype(jnp.bfloat16)

        jobs = [(step, chunk) for step in range(STATIONS) for chunk in plan[step]]
        update = stencil(*jobs[0])
        for at_job, (step, chunk) in enumerate(jobs):
            block, begin, end = chunk
            at, rows = begin * HALF, (end - begin) * HALF
            current = update
            if at_job + 1 < len(jobs):
                update = stencil(*jobs[at_job + 1])
            if chunk is plan[step][0]:
                copies[step].wait()
            moved = lax.dot_general(
                current, held[step], (((1,), (1,)), ((), ())), preferred_element_type=jnp.float32
            )
            if step == STATIONS - 1:
                result[block, at : at + rows, :] = moved.astype(jnp.bfloat16)
                continue
            target = states[1 - step % 2]
            target[block, margin + at : margin + at + rows, :] = moved
            if grow:
                empty = jnp.zeros((margin, FN), jnp.float32)
                count = max(last for place, _, last in plan[step] if place == block)
                if begin == 0:
                    target[block, :margin, :] = empty
                if end == count:
                    target[block, margin + count * HALF : 2 * margin + count * HALF, :] = empty
        for out, where in zip(outs[1:], others[2]):
            start = pl.multiple_of(where(side), EDGE)
            out[...] = result[0, pl.ds(start, out.shape[0]), :]

    relay(others[1], turn, givers, outs[1:], sems)


def relay(owners, turn, givers, outs, sems):
    side = turn[1]
    for slot, value, moves in owners:

        @pl.when(turn[slot] == value)
        def _():
            copies = []
            for at, (giver, block, start, rows, out, to) in enumerate(moves):
                start = start(side)
                if not isinstance(start, int):
                    start = pl.multiple_of(start, EDGE)
                source = givers[giver].at[block(side), pl.ds(start, rows)]
                copies.append(pltpu.make_async_copy(source, outs[out].at[pl.ds(to, rows)], sems.at[at]))
            for copy in copies:
                copy.start()
            for copy in copies:
                copy.wait()


def march(turn, number, inverse_blocks, coupling, pieces, cut, blocks, positions, grow, raw=(), others=((), (), ())):
    last = positions + (2 * STATIONS if grow else -2 * STATIONS)
    most = last + 2 if grow else positions
    counts = [positions + (2 if grow else -2) * (step + 1) for step in range(STATIONS)]
    if blocks == 2:
        plan = [[(0, 0, count), (1, 0, count)] for count in counts]
    else:
        cuts = [cut - (0 if grow else 2 * step) for step in range(STATIONS)]
        plan = [[(0, 0, at), (0, at, count)] for at, count in zip(cuts, counts)]
    vmem = pl.BlockSpec(memory_space=pltpu.VMEM)
    away = pl.BlockSpec(memory_space=pl.ANY)
    shapes = [jax.ShapeDtypeStruct((blocks, last * HALF, FN), jnp.bfloat16)]
    shapes += [jax.ShapeDtypeStruct((size, FN), jnp.bfloat16) for size in (2 * ONE, WIDE, WIDE, 2 * ONE)[: len(others[2])]]
    values = [piece[0] for piece in pieces]
    return pl.pallas_call(
        functools.partial(
            march_kernel,
            number,
            [piece[1:] for piece in pieces],
            others,
            plan,
            blocks,
            positions,
            grow,
            len(raw),
        ),
        out_shape=shapes,
        in_specs=[pl.BlockSpec(memory_space=pltpu.SMEM), vmem, away]
        + [vmem] * (len(values) + len(raw))
        + [away] * len(others[0]),
        out_specs=[vmem] * len(shapes),
        scratch_shapes=[pltpu.VMEM((blocks, most * HALF, FN), jnp.float32)] * 2
        + [pltpu.VMEM((STATIONS, FN, FN), jnp.bfloat16), pltpu.SemaphoreType.DMA((STATIONS,))],
        compiler_params=pltpu.CompilerParams(vmem_limit_bytes=GRANT),
        cost_estimate=pl.CostEstimate(
            flops=2 * blocks * HALF * sum(counts) * FN * FN,
            bytes_accessed=2 * STATIONS * FN * FN,
            transcendentals=0,
        ),
    )(turn, coupling, inverse_blocks, *values, *raw, *others[0])


def ship_kernel(
    number, turn, share, below, raw, crossed, edge_cross, edge_same, direct, whole, held, turned, sem
):
    side, kind = turn[1], turn[2]

    def turn_over(source):
        copy = pltpu.make_async_copy(source, held, sem)
        copy.start()
        copy.wait()
        rows = ordered(held[...])
        for half in range(2):
            turned[half, :, :] = rows[half * ONE : (half + 1) * ONE]

    @pl.when(turn[0] == number)
    def _():
        turn_over(below)
        whole[...] = share[...]
        middle = share[:, EDGE : EDGE + ONE, :].astype(jnp.float32) + turned[...]
        whole[:, EDGE : EDGE + ONE, :] = middle.astype(jnp.bfloat16)
        start = pl.multiple_of(side * ONE, ONE)
        edge_cross[...] = whole[1 - side, pl.ds(start, WIDE), :]
        edge_same[...] = whole[side, pl.ds(start, WIDE), :]
        crossed[...] = whole[1 - side]
        direct[...] = whole[side]

    @pl.when(kind >= 2)
    def _():
        turn_over(raw)
        whole[:, :ONE, :] = turned[...].astype(jnp.bfloat16)

    @pl.when(kind == 2)
    def _():
        crossed[:ONE, :] = whole[1 - side, :ONE, :]

    @pl.when(kind == 3)
    def _():
        for half in range(2):
            edge_cross[half * EDGE : (half + 1) * EDGE, :] = whole[half, ONE - EDGE : ONE, :]
            edge_same[half * EDGE : (half + 1) * EDGE, :] = whole[half, :EDGE, :]


def center_kernel(number, turn, direct, crossed, edge_same, edge_cross, out):
    @pl.when(turn[0] == number)
    def _():
        side = turn[1]
        start = pl.multiple_of(side * EDGE, EDGE)
        from_edge = pl.multiple_of((1 - side) * EDGE, EDGE)
        for block, share, edge in ((side, direct, edge_same), (1 - side, crossed, edge_cross)):
            out[block, :, :] = share[EDGE : EDGE + ONE, :]
            here = out[block, pl.ds(start, EDGE), :].astype(jnp.float32)
            more = edge[pl.ds(from_edge, EDGE), :].astype(jnp.float32)
            out[block, pl.ds(start, EDGE), :] = (here + more).astype(jnp.bfloat16)


def gram_kernel(numbers, turn, *refs):
    inputs, (rows, gram, edges, sems) = refs[: 7 * len(numbers)], refs[7 * len(numbers) :]
    side = turn[1]

    def fetch(*pairs):
        copies = [pltpu.make_async_copy(source, target, sems.at[at]) for at, (source, target) in enumerate(pairs)]
        for copy in copies:
            copy.start()
        for copy in copies:
            copy.wait()

    for at, number in enumerate(numbers):
        share, low, high, state, crossed, back, last = inputs[7 * at : 7 * at + 7]

        @pl.when(turn[0] == number)
        def _():
            halves = [slice(0, EDGE), slice(EDGE, 2 * EDGE)]
            fetch(
                *[(share.at[half, EDGE : EDGE + ONE], rows.at[half]) for half in range(2)],
                *[(low.at[halves[half]], edges.at[half, :EDGE]) for half in range(2)],
                *[(high.at[halves[half]], edges.at[half, EDGE:]) for half in range(2)],
            )
            rows[...] = (rows[...].astype(jnp.float32) + edges[...].astype(jnp.float32)).astype(jnp.bfloat16)

        @pl.when(turn[0] == number - 1)
        def _():
            start = pl.multiple_of(side * ONE, ONE)
            fetch((state.at[0, pl.ds(start, ONE)], rows.at[side]), (crossed.at[:ONE], rows.at[1 - side]))

        @pl.when(turn[0] == number - 2)
        def _():
            fetch((back, rows))

        @pl.when(turn[0] == number - 3)
        def _():
            fetch((last, rows))

    flat = rows[...].reshape(2 * ONE, FN)
    full = lax.dot_general(flat, flat, (((1,), (1,)), ((), ())), preferred_element_type=jnp.float32)
    lines = []
    for first in range(2):
        line = []
        for second in range(2):
            block = None
            for point in range(POINTS):
                down, along = first * ONE + point * HALF, second * ONE + point * HALF
                term = full[down : down + HALF, along : along + HALF]
                block = term if block is None else block + term
            line.append(block)
        lines.append(jnp.concatenate(line, 1))
    total = jnp.concatenate(lines, 0)
    for at in range(gram.shape[0]):
        gram[at, :, :] = total


def factor_kernel(scale, grams, rows, by_column, by_place, same_point, basis, upper):
    terms = [grams[at] for at in range(grams.shape[0])]
    while len(terms) > 1:
        terms = [one + other for one, other in zip(terms[::2], terms[1::2])]
    eye = (
        lax.broadcasted_iota(jnp.int32, (K, K), 0) == lax.broadcasted_iota(jnp.int32, (K, K), 1)
    ).astype(jnp.float32)
    table = jnp.concatenate([terms[0] * scale, eye], 1)
    row_index = lax.broadcasted_iota(jnp.int32, (K, 2 * K), 0)
    roots = jnp.zeros((K, 2 * K), jnp.float32)
    for j in range(0, K, STEP):
        lines = [table[j + m : j + m + 1, :] for m in range(STEP)]
        columns = [jnp.broadcast_to(table[:, j + m : j + m + 1], table.shape) for m in range(STEP)]
        entries = [
            [jnp.broadcast_to(lines[m][:, j + k : j + k + 1], lines[m].shape) for k in range(STEP)]
            for m in range(STEP)
        ]
        below = table
        for m in range(STEP):
            inverse = 1.0 / entries[m][m]
            for k in range(m + 1, STEP):
                ratio = entries[m][k] * inverse
                for n in range(k, STEP):
                    entries[k][n] = entries[k][n] - ratio * entries[m][n]
                lines[k] = lines[k] - ratio * lines[m]
                columns[k] = columns[k] - ratio * columns[m]
            below = below - columns[m] * (inverse * lines[m])
            roots = jnp.where(row_index == j + m, lax.rsqrt(entries[m][m]), roots)
        table = jnp.where(row_index >= j + STEP, below, table)
        for m in range(STEP):
            table = jnp.where(row_index == j + m, lines[m], table)
    table = table * roots
    column = lax.broadcasted_iota(jnp.int32, (K, K), 1)
    row = lax.broadcasted_iota(jnp.int32, (K, K), 0)
    upper[...] = jnp.where(column >= row, table[:, :K], 0.0)
    inverse = table[:, K:]
    total = None
    for _ in range(2):
        term = inverse.astype(jnp.bfloat16)
        inverse = inverse - term.astype(jnp.float32)
        tall = lax.dot_general(
            by_column[...], term, (((1,), (1,)), ((), ())), preferred_element_type=jnp.float32
        ).astype(jnp.bfloat16)
        spread = lax.dot_general(
            tall, by_place[...], (((1,), (0,)), ((), ())), preferred_element_type=jnp.float32
        )
        spread = (spread * same_point[...]).astype(jnp.bfloat16)
        part = lax.dot_general(
            rows[...], spread, (((0,), (0,)), ((), ())), preferred_element_type=jnp.float32
        )
        total = part if total is None else total + part
    basis[...] = total.astype(jnp.bfloat16)


def local(inverse_blocks, coupling, sources):
    sections = lax.axis_size("section")
    spans = lax.axis_size("span")
    pairs = spans // 2
    assert sections % 4 == 0 and spans % 2 == 0 and sources.shape[2] == POINTS * K
    group = lax.axis_index("section")
    side = (lax.axis_index("span") % 2).astype(jnp.int32)

    def send(value, *legs):
        routes = []
        for groups, down, route in legs:
            for g in groups:
                for s in range(spans):
                    routes.append((g * spans + s, (g - down) * spans + route(s)))
        return lax.ppermute(value, AXES, routes)

    def straight(s):
        return s

    def partner(s):
        return s ^ 1

    def neighbor(shift):
        return lambda s: (s + shift) % spans

    def pair_route(pair, side):
        return (pair % pairs) * 2 + side

    def outward(s):
        return pair_route(s // 2 + 2 * (s % 2) - 1, s % 2)

    def outward_cross(s):
        return pair_route(s // 2 + 2 * (s % 2) - 1, 1 - s % 2)

    def inward(s):
        return pair_route(s // 2 + 1 - 2 * (s % 2), s % 2)

    def of_kind(kind):
        return [g for g in range(sections) if (sections - 1 - g) % 4 == kind]

    turn = jnp.stack([group.astype(jnp.int32), side, ((sections - 1 - group) % 4).astype(jnp.int32)])

    half, point, column = np.meshgrid(np.arange(2), np.arange(POINTS), np.arange(HALF), indexing="ij")
    row_column = (half * HALF + column).reshape(-1)
    row_point = point.reshape(-1)
    place = np.arange(POINTS * K)
    by_column = jnp.asarray(np.arange(K)[None, :] == row_column[:, None], jnp.bfloat16)
    by_place = jnp.asarray(np.arange(K)[:, None] == place[None, :] % K, jnp.bfloat16)
    same_point = jnp.asarray(place[None, :] // K == row_point[:, None], jnp.float32)

    smem = pl.BlockSpec(memory_space=pltpu.SMEM)
    vmem = pl.BlockSpec(memory_space=pltpu.VMEM)
    away = pl.BlockSpec(memory_space=pl.ANY)
    raw = sources[0]
    below = send(raw, (of_kind(1), -1, straight))
    incoming = None
    pair_source = wide_source = None
    candidates = []
    for g in reversed(of_kind(0)):
        pieces = [] if incoming is None else [(incoming, lambda side: (0, 0), ONE, None)]
        (share,) = march(turn, g, inverse_blocks, coupling, pieces, 0, 2, POINTS, True, (raw,))
        crossed, edge_cross, edge_same, direct, whole = pl.pallas_call(
            functools.partial(ship_kernel, g),
            out_shape=[jax.ShapeDtypeStruct((size, FN), jnp.bfloat16) for size in (2 * ONE, WIDE, WIDE, 2 * ONE)]
            + [jax.ShapeDtypeStruct(share.shape, jnp.bfloat16)],
            in_specs=[smem, vmem, away, away],
            out_specs=[vmem] * 5,
            scratch_shapes=[
                pltpu.VMEM(raw.shape, jnp.bfloat16),
                pltpu.VMEM((2, ONE, FN), jnp.float32),
                pltpu.SemaphoreType.DMA,
            ],
            compiler_params=pltpu.CompilerParams(vmem_limit_bytes=SMALL),
        )(turn, share, below, raw)
        first = incoming is None
        edge_cross = send(edge_cross, ([g], 1, outward_cross), (of_kind(3) if first else [], 0, neighbor(1)))
        crossed = send(crossed, ([g], 1, partner), (of_kind(2) if first else [], 0, partner))
        edge_same = send(edge_same, ([g], 1, outward), (of_kind(3) if first else [], 0, neighbor(-1)))
        direct = send(direct, ([g], 1, straight))
        if first:
            pair_source = [
                (whole, lambda side: (0, side * ONE), ONE, lambda side: side),
                (crossed, lambda side: (0, (1 - side) * ONE), ONE, None),
            ]
            wide_source = [
                (edge_cross.reshape(2, EDGE, FN), lambda side: (0, 0), EDGE, None),
                (whole, lambda side: (0, EDGE), ONE, None),
                (edge_same.reshape(2, EDGE, FN), lambda side: (0, EDGE + ONE), EDGE, None),
            ]

        (state,) = march(
            turn,
            g - 1,
            inverse_blocks,
            coupling,
            [
                (crossed, lambda side: (0, (1 - side) * ONE), 2 * ONE, None),
                (edge_cross, lambda side: (0, side * 2 * ONE), WIDE, None),
                (edge_same, lambda side: (0, (1 - side) * 2 * ONE), WIDE, None),
                (direct, lambda side: (0, side * ONE), 2 * ONE, None),
            ],
            14,
            1,
            3 * POINTS,
            False,
        )
        arrived = send(state, ([g - 1], 1, straight))

        _, crossed, edge_cross, edge_same, direct = march(
            turn,
            g - 2,
            inverse_blocks,
            coupling,
            [(arrived, lambda side: (0, 0), 2 * ONE, None)] + pair_source,
            10,
            1,
            2 * POINTS,
            True,
            (),
            (
                (share, state),
                (
                    (
                        0,
                        g,
                        (
                            (0, lambda side: 0, lambda side: EDGE + ONE, EDGE, 1, 0),
                            (0, lambda side: 1, lambda side: EDGE + ONE, EDGE, 1, EDGE),
                            (0, lambda side: 0, lambda side: 0, EDGE, 2, 0),
                            (0, lambda side: 1, lambda side: 0, EDGE, 2, EDGE),
                        ),
                    ),
                    (0, g - 1, ((1, lambda side: 0, lambda side: (1 - side) * ONE, ONE, 0, 0),)),
                ),
                (
                    lambda side: (1 - side) * ONE,
                    lambda side: side * 2 * ONE,
                    lambda side: (1 - side) * 2 * ONE,
                    lambda side: side * ONE,
                ),
            ),
        )
        edge_cross = send(edge_cross, ([g - 2], 1, outward_cross), ([g], 0, neighbor(1)))
        crossed = send(crossed, ([g - 2], 1, partner), ([g - 1], 0, partner))
        edge_same = send(edge_same, ([g - 2], 1, inward), ([g], 0, neighbor(-1)))
        direct = send(direct, ([g - 2], 1, straight))

        middle = pl.pallas_call(
            functools.partial(center_kernel, g - 3),
            out_shape=jax.ShapeDtypeStruct((2, ONE, FN), jnp.bfloat16),
            in_specs=[smem] + [vmem] * 4,
            out_specs=vmem,
            compiler_params=pltpu.CompilerParams(vmem_limit_bytes=SMALL),
        )(turn, direct, crossed, edge_same, edge_cross)
        back = send(middle, ([g - 3], -1, straight))
        (last,) = march(
            turn,
            g - 3,
            inverse_blocks,
            coupling,
            [
                (crossed, lambda side: (1 - side, 0), 2 * ONE, None),
                (edge_cross, lambda side: (1 - side, side * ONE), WIDE, None),
                (edge_same, lambda side: (side, side * ONE), WIDE, None),
                (direct, lambda side: (side, 0), 2 * ONE, None),
            ]
            + wide_source,
            0,
            2,
            2 * POINTS,
            False,
        )
        candidates += [share, edge_cross, edge_same, state, crossed, back, last]
        if g > 3:
            incoming = send(last, ([g - 3], 1, straight))

    rows, grams = pl.pallas_call(
        functools.partial(gram_kernel, list(reversed(of_kind(0)))),
        out_shape=(
            jax.ShapeDtypeStruct((2, ONE, FN), jnp.bfloat16),
            jax.ShapeDtypeStruct((spans, K, K), jnp.float32),
        ),
        in_specs=[smem] + [away] * len(candidates),
        out_specs=(vmem, vmem),
        scratch_shapes=[pltpu.VMEM((2, ONE, FN), jnp.bfloat16), pltpu.SemaphoreType.DMA((6,))],
        compiler_params=pltpu.CompilerParams(vmem_limit_bytes=SMALL),
    )(turn, *candidates)
    grams = lax.all_to_all(grams, "span", 0, 0, tiled=True)

    basis, upper = pl.pallas_call(
        functools.partial(factor_kernel, 1.0 / float(FN * POINTS * spans)),
        out_shape=(
            jax.ShapeDtypeStruct((FN, POINTS * K), jnp.bfloat16),
            jax.ShapeDtypeStruct((K, K), jnp.float32),
        ),
        in_specs=[vmem] * 5,
        out_specs=(vmem, vmem),
        compiler_params=pltpu.CompilerParams(vmem_limit_bytes=SMALL),
    )(grams, rows.reshape(POINTS * K, FN), by_column, by_place, same_point)
    return (basis[None], upper[None])


def solution(mesh):
    placed = (P("section", None, None), P("section", None), P("section", None, "span"))
    return jax.shard_map(
        local,
        mesh=mesh,
        in_specs=placed,
        out_specs=(P("section", None, "span"), P("section", None, None)),
        check_vma=False,
    )
```

```python
import functools

import jax
import jax.numpy as jnp
import numpy as np
from jax import lax
from jax.experimental import pallas as pl
from jax.experimental.pallas import tpu as pltpu
from jax.sharding import PartitionSpec as P

K = 48
STATIONS = 4
FN = 768
HALF = K // 2
POINTS = 8
ONE = POINTS * HALF
EDGE = STATIONS * HALF
WIDE = 2 * EDGE
STEP = 4
GRANT = 48 * 1024 * 1024
SMALL = 16 * 1024 * 1024
AXES = ("section", "span")


def one_hot_order():
    at = lax.broadcasted_iota(jnp.int32, (1, POINTS * K), 1)
    point = at * 1366 >> 16
    column = at - point * K
    half = (column >= HALF).astype(jnp.int32)
    target = half * (ONE - HALF) + point * HALF + column
    row = lax.broadcasted_iota(jnp.int32, (POINTS * K, POINTS * K), 0)
    return jnp.where(row == target, 1.0, 0.0).astype(jnp.bfloat16)


def ordered(raw):
    return lax.dot_general(one_hot_order(), raw, (((1,), (1,)), ((), ())), preferred_element_type=jnp.float32)


def march_kernel(number, places, others, plan, blocks, positions, grow, raw, turn, coupling, weights, *refs):
    refs = list(refs)
    pieces = [refs.pop(0) for _ in places]
    raws = [refs.pop(0) for _ in range(raw)]
    givers = [refs.pop(0) for _ in others[0]]
    outs, (first, second, held, result, sems) = refs[:-5], refs[-5:]
    if not others[2]:
        result = outs[0]
    else:
        outs = [None] + outs
    states = [first, second]
    order = list(reversed(range(STATIONS)))
    side = turn[1]

    @pl.when(turn[0] == number)
    def _():
        copies = [
            pltpu.make_async_copy(weights.at[station], held.at[step], sems.at[step])
            for step, station in enumerate(order)
        ]
        copies[0].start()
        margin = 2 * HALF if grow else 0
        total = positions * HALF + 2 * margin
        first[:, :total, :] = jnp.zeros((blocks, total, FN), jnp.float32)
        if raw:
            rows = ordered(raws[0][...])
            for half in range(2):
                first[half, margin : margin + ONE, :] = rows[half * ONE : (half + 1) * ONE]
        for piece, (where, rows, pick) in zip(pieces, places):
            block, start = where(side)
            start = margin + start
            if not isinstance(start, int):
                start = pl.multiple_of(start, 8)
            if pick is not None:
                first[block, pl.ds(start, rows), :] += piece[pick(side), :rows, :].astype(jnp.float32)
            elif len(piece.shape) == 3:
                first[:, pl.ds(start, rows), :] += piece[:, :rows, :].astype(jnp.float32)
            else:
                first[block, pl.ds(start, rows), :] += piece[:rows, :].astype(jnp.float32)

        def stencil(step, chunk):
            block, begin, end = chunk
            at, rows = begin * HALF, (end - begin) * HALF
            source = states[step % 2]
            rates = coupling[order[step] : order[step] + 1, :]
            both = source[block, at : at + rows, :] + source[block, at + 2 * HALF : at + 2 * HALF + rows, :]
            update = (1.0 - 2.0 * rates) * source[block, at + HALF : at + HALF + rows, :] + rates * both
            return update.astype(jnp.bfloat16)

        copies[1].start()
        jobs = [(step, chunk) for step in range(STATIONS) for chunk in plan[step]]
        update = stencil(*jobs[0])
        for at_job, (step, chunk) in enumerate(jobs):
            block, begin, end = chunk
            at, rows = begin * HALF, (end - begin) * HALF
            current = update
            if at_job + 1 < len(jobs):
                update = stencil(*jobs[at_job + 1])
            if chunk is plan[step][0]:
                copies[step].wait()
                if step + 2 < STATIONS:
                    copies[step + 2].start()
            moved = lax.dot_general(
                current, held[step], (((1,), (1,)), ((), ())), preferred_element_type=jnp.float32
            )
            if step == STATIONS - 1:
                result[block, at : at + rows, :] = moved.astype(jnp.bfloat16)
                continue
            target = states[1 - step % 2]
            target[block, margin + at : margin + at + rows, :] = moved
            if grow:
                empty = jnp.zeros((margin, FN), jnp.float32)
                count = max(last for place, _, last in plan[step] if place == block)
                if begin == 0:
                    target[block, :margin, :] = empty
                if end == count:
                    target[block, margin + count * HALF : 2 * margin + count * HALF, :] = empty
        for out, where in zip(outs[1:], others[2]):
            start = pl.multiple_of(where(side), EDGE)
            out[...] = result[0, pl.ds(start, out.shape[0]), :]

    relay(others[1], turn, givers, outs[1:], sems)


def relay(owners, turn, givers, outs, sems):
    side = turn[1]
    for slot, value, moves in owners:

        @pl.when(turn[slot] == value)
        def _():
            copies = []
            for at, (giver, block, start, rows, out, to) in enumerate(moves):
                start = start(side)
                if not isinstance(start, int):
                    start = pl.multiple_of(start, EDGE)
                source = givers[giver].at[block(side), pl.ds(start, rows)]
                copies.append(pltpu.make_async_copy(source, outs[out].at[pl.ds(to, rows)], sems.at[at]))
            for copy in copies:
                copy.start()
            for copy in copies:
                copy.wait()


def march(turn, number, inverse_blocks, coupling, pieces, cut, blocks, positions, grow, raw=(), others=((), (), ())):
    last = positions + (2 * STATIONS if grow else -2 * STATIONS)
    most = last + 2 if grow else positions
    counts = [positions + (2 if grow else -2) * (step + 1) for step in range(STATIONS)]
    if blocks == 2:
        plan = [[(0, 0, count), (1, 0, count)] for count in counts]
    else:
        cuts = [cut - (0 if grow else 2 * step) for step in range(STATIONS)]
        plan = [[(0, 0, at), (0, at, count)] for at, count in zip(cuts, counts)]
    vmem = pl.BlockSpec(memory_space=pltpu.VMEM)
    away = pl.BlockSpec(memory_space=pl.ANY)
    whole = (blocks, last * HALF, FN)
    shapes = [jax.ShapeDtypeStruct(whole, jnp.bfloat16)]
    if others[2]:
        shapes = [jax.ShapeDtypeStruct((size, FN), jnp.bfloat16) for size in (2 * ONE, WIDE, WIDE, 2 * ONE)]
    values = [piece[0] for piece in pieces]
    return pl.pallas_call(
        functools.partial(
            march_kernel,
            number,
            [piece[1:] for piece in pieces],
            others,
            plan,
            blocks,
            positions,
            grow,
            len(raw),
        ),
        out_shape=shapes,
        in_specs=[pl.BlockSpec(memory_space=pltpu.SMEM), vmem, away]
        + [vmem] * (len(values) + len(raw))
        + [away] * len(others[0]),
        out_specs=[vmem] * len(shapes),
        scratch_shapes=[pltpu.VMEM((blocks, most * HALF, FN), jnp.float32)] * 2
        + [
            pltpu.VMEM((STATIONS, FN, FN), jnp.bfloat16),
            pltpu.VMEM(whole if others[2] else (1, 16, FN), jnp.bfloat16),
            pltpu.SemaphoreType.DMA((STATIONS,)),
        ],
        compiler_params=pltpu.CompilerParams(vmem_limit_bytes=GRANT),
        cost_estimate=pl.CostEstimate(
            flops=2 * blocks * HALF * sum(counts) * FN * FN,
            bytes_accessed=2 * STATIONS * FN * FN,
            transcendentals=0,
        ),
    )(turn, coupling, inverse_blocks, *values, *raw, *others[0])


def ship_kernel(
    number, turn, share, below, raw, crossed, edge_cross, edge_same, direct, whole, held, turned, sem
):
    side, kind = turn[1], turn[2]

    def turn_over(source):
        copy = pltpu.make_async_copy(source, held, sem)
        copy.start()
        copy.wait()
        rows = ordered(held[...])
        for half in range(2):
            turned[half, :, :] = rows[half * ONE : (half + 1) * ONE]

    @pl.when(turn[0] == number)
    def _():
        turn_over(below)
        whole[...] = share[...]
        middle = share[:, EDGE : EDGE + ONE, :].astype(jnp.float32) + turned[...]
        whole[:, EDGE : EDGE + ONE, :] = middle.astype(jnp.bfloat16)
        start = pl.multiple_of(side * ONE, ONE)
        edge_cross[...] = whole[1 - side, pl.ds(start, WIDE), :]
        edge_same[...] = whole[side, pl.ds(start, WIDE), :]
        crossed[...] = whole[1 - side]
        direct[...] = whole[side]

    @pl.when(kind >= 2)
    def _():
        turn_over(raw)
        whole[:, :ONE, :] = turned[...].astype(jnp.bfloat16)

    @pl.when(kind == 2)
    def _():
        crossed[:ONE, :] = whole[1 - side, :ONE, :]

    @pl.when(kind == 3)
    def _():
        for half in range(2):
            edge_cross[half * EDGE : (half + 1) * EDGE, :] = whole[half, ONE - EDGE : ONE, :]
            edge_same[half * EDGE : (half + 1) * EDGE, :] = whole[half, :EDGE, :]


def center_kernel(number, turn, direct, crossed, edge_same, edge_cross, out):
    @pl.when(turn[0] == number)
    def _():
        side = turn[1]
        start = pl.multiple_of(side * EDGE, EDGE)
        from_edge = pl.multiple_of((1 - side) * EDGE, EDGE)
        for block, share, edge in ((side, direct, edge_same), (1 - side, crossed, edge_cross)):
            out[block, :, :] = share[EDGE : EDGE + ONE, :]
            here = out[block, pl.ds(start, EDGE), :].astype(jnp.float32)
            more = edge[pl.ds(from_edge, EDGE), :].astype(jnp.float32)
            out[block, pl.ds(start, EDGE), :] = (here + more).astype(jnp.bfloat16)


def gram_kernel(numbers, turn, *refs):
    inputs, (rows, gram, edges, sems) = refs[: 7 * len(numbers)], refs[7 * len(numbers) :]
    side = turn[1]

    def fetch(*pairs):
        copies = [pltpu.make_async_copy(source, target, sems.at[at]) for at, (source, target) in enumerate(pairs)]
        for copy in copies:
            copy.start()
        for copy in copies:
            copy.wait()

    for at, number in enumerate(numbers):
        share, low, high, state, crossed, back, last = inputs[7 * at : 7 * at + 7]

        @pl.when(turn[0] == number)
        def _():
            halves = [slice(0, EDGE), slice(EDGE, 2 * EDGE)]
            fetch(
                *[(share.at[half, EDGE : EDGE + ONE], rows.at[half]) for half in range(2)],
                *[(low.at[halves[half]], edges.at[half, :EDGE]) for half in range(2)],
                *[(high.at[halves[half]], edges.at[half, EDGE:]) for half in range(2)],
            )
            rows[...] = (rows[...].astype(jnp.float32) + edges[...].astype(jnp.float32)).astype(jnp.bfloat16)

        @pl.when(turn[0] == number - 1)
        def _():
            start = pl.multiple_of(side * ONE, ONE)
            fetch((state.at[0, pl.ds(start, ONE)], rows.at[side]), (crossed.at[:ONE], rows.at[1 - side]))

        @pl.when(turn[0] == number - 2)
        def _():
            fetch((back, rows))

        @pl.when(turn[0] == number - 3)
        def _():
            fetch((last, rows))

    flat = rows[...].reshape(2 * ONE, FN)
    full = lax.dot_general(flat, flat, (((1,), (1,)), ((), ())), preferred_element_type=jnp.float32)
    lines = []
    for first in range(2):
        line = []
        for second in range(2):
            block = None
            for point in range(POINTS):
                down, along = first * ONE + point * HALF, second * ONE + point * HALF
                term = full[down : down + HALF, along : along + HALF]
                block = term if block is None else block + term
            line.append(block)
        lines.append(jnp.concatenate(line, 1))
    total = jnp.concatenate(lines, 0)
    total = jnp.concatenate([total, jnp.zeros((K, 128 - K), jnp.float32)], 1)
    for at in range(gram.shape[0]):
        gram[at, :, :] = total


def factor_kernel(scale, grams, rows, by_column, by_place, same_point, basis, upper):
    terms = [grams[at] for at in range(grams.shape[0])]
    while len(terms) > 1:
        terms = [one + other for one, other in zip(terms[::2], terms[1::2])]
    eye = (
        lax.broadcasted_iota(jnp.int32, (K, K), 0) == lax.broadcasted_iota(jnp.int32, (K, K), 1)
    ).astype(jnp.float32)
    table = jnp.concatenate([terms[0][:, :K] * scale, eye], 1)
    row_index = lax.broadcasted_iota(jnp.int32, (K, 2 * K), 0)
    roots = jnp.zeros((K, 2 * K), jnp.float32)
    for j in range(0, K, STEP):
        lines = [table[j + m : j + m + 1, :] for m in range(STEP)]
        columns = [jnp.broadcast_to(table[:, j + m : j + m + 1], table.shape) for m in range(STEP)]
        entries = [
            [jnp.broadcast_to(lines[m][:, j + k : j + k + 1], lines[m].shape) for k in range(STEP)]
            for m in range(STEP)
        ]
        below = table
        for m in range(STEP):
            inverse = 1.0 / entries[m][m]
            for k in range(m + 1, STEP):
                ratio = entries[m][k] * inverse
                for n in range(k, STEP):
                    entries[k][n] = entries[k][n] - ratio * entries[m][n]
                lines[k] = lines[k] - ratio * lines[m]
                columns[k] = columns[k] - ratio * columns[m]
            below = below - columns[m] * (inverse * lines[m])
            roots = jnp.where(row_index == j + m, lax.rsqrt(entries[m][m]), roots)
        table = jnp.where(row_index >= j + STEP, below, table)
        for m in range(STEP):
            table = jnp.where(row_index == j + m, lines[m], table)
    table = table * roots
    column = lax.broadcasted_iota(jnp.int32, (K, K), 1)
    row = lax.broadcasted_iota(jnp.int32, (K, K), 0)
    upper[...] = jnp.where(column >= row, table[:, :K], 0.0)
    inverse = table[:, K:]
    total = None
    for _ in range(2):
        term = inverse.astype(jnp.bfloat16)
        inverse = inverse - term.astype(jnp.float32)
        tall = lax.dot_general(
            by_column[...], term, (((1,), (1,)), ((), ())), preferred_element_type=jnp.float32
        ).astype(jnp.bfloat16)
        spread = lax.dot_general(
            tall, by_place[...], (((1,), (0,)), ((), ())), preferred_element_type=jnp.float32
        )
        spread = (spread * same_point[...]).astype(jnp.bfloat16)
        part = lax.dot_general(
            rows[...], spread, (((0,), (0,)), ((), ())), preferred_element_type=jnp.float32
        )
        total = part if total is None else total + part
    basis[...] = total.astype(jnp.bfloat16)


def local(inverse_blocks, coupling, sources):
    sections = lax.axis_size("section")
    spans = lax.axis_size("span")
    pairs = spans // 2
    assert sections % 4 == 0 and spans % 2 == 0 and sources.shape[2] == POINTS * K
    group = lax.axis_index("section")
    side = (lax.axis_index("span") % 2).astype(jnp.int32)

    def send(value, *legs):
        routes = []
        for groups, down, route in legs:
            for g in groups:
                for s in range(spans):
                    routes.append((g * spans + s, (g - down) * spans + route(s)))
        return lax.ppermute(value, AXES, routes)

    def straight(s):
        return s

    def partner(s):
        return s ^ 1

    def neighbor(shift):
        return lambda s: (s + shift) % spans

    def pair_route(pair, side):
        return (pair % pairs) * 2 + side

    def outward(s):
        return pair_route(s // 2 + 2 * (s % 2) - 1, s % 2)

    def outward_cross(s):
        return pair_route(s // 2 + 2 * (s % 2) - 1, 1 - s % 2)

    def inward(s):
        return pair_route(s // 2 + 1 - 2 * (s % 2), s % 2)

    def of_kind(kind):
        return [g for g in range(sections) if (sections - 1 - g) % 4 == kind]

    turn = jnp.stack([group.astype(jnp.int32), side, ((sections - 1 - group) % 4).astype(jnp.int32)])

    half, point, column = np.meshgrid(np.arange(2), np.arange(POINTS), np.arange(HALF), indexing="ij")
    row_column = (half * HALF + column).reshape(-1)
    row_point = point.reshape(-1)
    place = np.arange(POINTS * K)
    by_column = jnp.asarray(np.arange(K)[None, :] == row_column[:, None], jnp.bfloat16)
    by_place = jnp.asarray(np.arange(K)[:, None] == place[None, :] % K, jnp.bfloat16)
    same_point = jnp.asarray(place[None, :] // K == row_point[:, None], jnp.float32)

    smem = pl.BlockSpec(memory_space=pltpu.SMEM)
    vmem = pl.BlockSpec(memory_space=pltpu.VMEM)
    away = pl.BlockSpec(memory_space=pl.ANY)
    raw = sources[0]
    below = send(raw, (of_kind(1), -1, straight))
    incoming = None
    pair_source = wide_source = None
    candidates = []
    for g in reversed(of_kind(0)):
        pieces = [] if incoming is None else [(incoming, lambda side: (0, 0), ONE, None)]
        (share,) = march(turn, g, inverse_blocks, coupling, pieces, 0, 2, POINTS, True, (raw,))
        crossed, edge_cross, edge_same, direct, whole = pl.pallas_call(
            functools.partial(ship_kernel, g),
            out_shape=[jax.ShapeDtypeStruct((size, FN), jnp.bfloat16) for size in (2 * ONE, WIDE, WIDE, 2 * ONE)]
            + [jax.ShapeDtypeStruct(share.shape, jnp.bfloat16)],
            in_specs=[smem, vmem, away, away],
            out_specs=[vmem] * 5,
            scratch_shapes=[
                pltpu.VMEM(raw.shape, jnp.bfloat16),
                pltpu.VMEM((2, ONE, FN), jnp.float32),
                pltpu.SemaphoreType.DMA,
            ],
            compiler_params=pltpu.CompilerParams(vmem_limit_bytes=SMALL),
        )(turn, share, below, raw)
        first = incoming is None
        edge_cross = send(edge_cross, ([g], 1, outward_cross), (of_kind(3) if first else [], 0, neighbor(1)))
        crossed = send(crossed, ([g], 1, partner), (of_kind(2) if first else [], 0, partner))
        edge_same = send(edge_same, ([g], 1, outward), (of_kind(3) if first else [], 0, neighbor(-1)))
        direct = send(direct, ([g], 1, straight))
        if first:
            pair_source = [
                (whole, lambda side: (0, side * ONE), ONE, lambda side: side),
                (crossed, lambda side: (0, (1 - side) * ONE), ONE, None),
            ]
            wide_source = [
                (edge_cross.reshape(2, EDGE, FN), lambda side: (0, 0), EDGE, None),
                (whole, lambda side: (0, EDGE), ONE, None),
                (edge_same.reshape(2, EDGE, FN), lambda side: (0, EDGE + ONE), EDGE, None),
            ]

        (state,) = march(
            turn,
            g - 1,
            inverse_blocks,
            coupling,
            [
                (crossed, lambda side: (0, (1 - side) * ONE), 2 * ONE, None),
                (edge_cross, lambda side: (0, side * 2 * ONE), WIDE, None),
                (edge_same, lambda side: (0, (1 - side) * 2 * ONE), WIDE, None),
                (direct, lambda side: (0, side * ONE), 2 * ONE, None),
            ],
            14,
            1,
            3 * POINTS,
            False,
        )
        arrived = send(state, ([g - 1], 1, straight))

        crossed, edge_cross, edge_same, direct = march(
            turn,
            g - 2,
            inverse_blocks,
            coupling,
            [(arrived, lambda side: (0, 0), 2 * ONE, None)] + pair_source,
            10,
            1,
            2 * POINTS,
            True,
            (),
            (
                (share, state),
                (
                    (
                        0,
                        g,
                        (
                            (0, lambda side: 0, lambda side: EDGE + ONE, EDGE, 1, 0),
                            (0, lambda side: 1, lambda side: EDGE + ONE, EDGE, 1, EDGE),
                            (0, lambda side: 0, lambda side: 0, EDGE, 2, 0),
                            (0, lambda side: 1, lambda side: 0, EDGE, 2, EDGE),
                        ),
                    ),
                    (0, g - 1, ((1, lambda side: 0, lambda side: (1 - side) * ONE, ONE, 0, 0),)),
                ),
                (
                    lambda side: (1 - side) * ONE,
                    lambda side: side * 2 * ONE,
                    lambda side: (1 - side) * 2 * ONE,
                    lambda side: side * ONE,
                ),
            ),
        )
        edge_cross = send(edge_cross, ([g - 2], 1, outward_cross), ([g], 0, neighbor(1)))
        crossed = send(crossed, ([g - 2], 1, partner), ([g - 1], 0, partner))
        edge_same = send(edge_same, ([g - 2], 1, inward), ([g], 0, neighbor(-1)))
        direct = send(direct, ([g - 2], 1, straight))

        middle = pl.pallas_call(
            functools.partial(center_kernel, g - 3),
            out_shape=jax.ShapeDtypeStruct((2, ONE, FN), jnp.bfloat16),
            in_specs=[smem] + [vmem] * 4,
            out_specs=vmem,
            compiler_params=pltpu.CompilerParams(vmem_limit_bytes=SMALL),
        )(turn, direct, crossed, edge_same, edge_cross)
        back = send(middle, ([g - 3], -1, straight))
        (last,) = march(
            turn,
            g - 3,
            inverse_blocks,
            coupling,
            [
                (crossed, lambda side: (1 - side, 0), 2 * ONE, None),
                (edge_cross, lambda side: (1 - side, side * ONE), WIDE, None),
                (edge_same, lambda side: (side, side * ONE), WIDE, None),
                (direct, lambda side: (side, 0), 2 * ONE, None),
            ]
            + wide_source,
            0,
            2,
            2 * POINTS,
            False,
        )
        candidates += [share, edge_cross, edge_same, state, crossed, back, last]
        if g > 3:
            incoming = send(last, ([g - 3], 1, straight))

    rows, grams = pl.pallas_call(
        functools.partial(gram_kernel, list(reversed(of_kind(0)))),
        out_shape=(
            jax.ShapeDtypeStruct((2, ONE, FN), jnp.bfloat16),
            jax.ShapeDtypeStruct((spans, K, 128), jnp.float32),
        ),
        in_specs=[smem] + [away] * len(candidates),
        out_specs=(vmem, vmem),
        scratch_shapes=[pltpu.VMEM((2, ONE, FN), jnp.bfloat16), pltpu.SemaphoreType.DMA((6,))],
        compiler_params=pltpu.CompilerParams(vmem_limit_bytes=SMALL),
    )(turn, *candidates)
    grams = lax.all_to_all(grams, "span", 0, 0, tiled=True)

    basis, upper = pl.pallas_call(
        functools.partial(factor_kernel, 1.0 / float(FN * POINTS * spans)),
        out_shape=(
            jax.ShapeDtypeStruct((FN, POINTS * K), jnp.bfloat16),
            jax.ShapeDtypeStruct((K, K), jnp.float32),
        ),
        in_specs=[vmem] * 5,
        out_specs=(vmem, vmem),
        compiler_params=pltpu.CompilerParams(vmem_limit_bytes=SMALL),
    )(grams, rows.reshape(POINTS * K, FN), by_column, by_place, same_point)
    return (basis[None], upper[None])


def solution(mesh):
    placed = (P("section", None, None), P("section", None), P("section", None, "span"))
    return jax.shard_map(
        local,
        mesh=mesh,
        in_specs=placed,
        out_specs=(P("section", None, "span"), P("section", None, None)),
        check_vma=False,
    )
```

```python
import functools

import jax
import jax.numpy as jnp
import numpy as np
from jax import lax
from jax.experimental import pallas as pl
from jax.experimental.pallas import tpu as pltpu
from jax.sharding import PartitionSpec as P

K = 48
STATIONS = 4
FN = 768
HALF = K // 2
POINTS = 8
ONE = POINTS * HALF
EDGE = STATIONS * HALF
WIDE = 2 * EDGE
STEP = 4
GRANT = 48 * 1024 * 1024
SMALL = 16 * 1024 * 1024
AXES = ("section", "span")


def one_hot_order():
    at = lax.broadcasted_iota(jnp.int32, (1, POINTS * K), 1)
    point = at * 1366 >> 16
    column = at - point * K
    half = (column >= HALF).astype(jnp.int32)
    target = half * (ONE - HALF) + point * HALF + column
    row = lax.broadcasted_iota(jnp.int32, (POINTS * K, POINTS * K), 0)
    return jnp.where(row == target, 1.0, 0.0).astype(jnp.bfloat16)


def ordered(raw):
    return lax.dot_general(one_hot_order(), raw, (((1,), (1,)), ((), ())), preferred_element_type=jnp.float32)


def march_kernel(number, places, others, plan, blocks, positions, grow, raw, turn, coupling, weights, *refs):
    refs = list(refs)
    pieces = [refs.pop(0) for _ in places]
    raws = [refs.pop(0) for _ in range(raw)]
    givers = [refs.pop(0) for _ in others[0]]
    outs, (first, second, held, result, sems) = refs[:-5], refs[-5:]
    if not others[2]:
        result = outs[0]
    else:
        outs = [None] + outs
    states = [first, second]
    order = list(reversed(range(STATIONS)))
    side = turn[1]

    @pl.when(turn[0] == number)
    def _():
        copies = [
            pltpu.make_async_copy(weights.at[station], held.at[step], sems.at[step])
            for step, station in enumerate(order)
        ]
        copies[0].start()
        margin = 2 * HALF if grow else 0
        if margin:
            empty = jnp.zeros((blocks, margin, FN), jnp.float32)
            first[:, :margin, :] = empty
            first[:, margin + positions * HALF : 2 * margin + positions * HALF, :] = empty

        def total(on):
            covers = []
            if raw:
                turned = ordered(raws[0][...])
                for half in range(2):
                    covers.append((half, 0, ONE, lambda low, high, at=half * ONE: turned[at + low : at + high]))
            for piece, (where, rows, pick) in zip(pieces, places):
                block, start = where(on)
                if pick is not None:
                    covers.append((block, start, rows, lambda low, high, p=piece, k=pick(on): p[k, low:high, :]))
                elif len(piece.shape) == 3:
                    for k in range(blocks):
                        covers.append((k, start, rows, lambda low, high, p=piece, k=k: p[k, low:high, :]))
                else:
                    covers.append((block, start, rows, lambda low, high, p=piece: p[low:high, :]))
            for block in range(blocks):
                here = [cover for cover in covers if cover[0] == block]
                bounds = {0, positions * HALF}
                for _, start, rows, _ in here:
                    bounds |= {start, start + rows}
                bounds = sorted(bounds)
                for low, high in zip(bounds, bounds[1:]):
                    value = jnp.zeros((high - low, FN), jnp.float32)
                    for _, start, rows, read in here:
                        if start <= low and high <= start + rows:
                            value = value + read(low - start, high - start).astype(jnp.float32)
                    first[block, margin + low : margin + high, :] = value

        if pieces:
            for on in range(2):
                pl.when(side == on)(functools.partial(total, on))
        else:
            total(0)

        def stencil(step, chunk):
            block, begin, end = chunk
            at, rows = begin * HALF, (end - begin) * HALF
            source = states[step % 2]
            rates = coupling[order[step] : order[step] + 1, :]
            both = source[block, at : at + rows, :] + source[block, at + 2 * HALF : at + 2 * HALF + rows, :]
            update = (1.0 - 2.0 * rates) * source[block, at + HALF : at + HALF + rows, :] + rates * both
            return update.astype(jnp.bfloat16)

        copies[1].start()
        jobs = [(step, chunk) for step in range(STATIONS) for chunk in plan[step]]
        update = stencil(*jobs[0])
        for at_job, (step, chunk) in enumerate(jobs):
            block, begin, end = chunk
            at, rows = begin * HALF, (end - begin) * HALF
            current = update
            if at_job + 1 < len(jobs):
                update = stencil(*jobs[at_job + 1])
            if chunk is plan[step][0]:
                copies[step].wait()
                if step + 2 < STATIONS:
                    copies[step + 2].start()
            moved = lax.dot_general(
                current, held[step], (((1,), (1,)), ((), ())), preferred_element_type=jnp.float32
            )
            if step == STATIONS - 1:
                result[block, at : at + rows, :] = moved.astype(jnp.bfloat16)
                continue
            target = states[1 - step % 2]
            target[block, margin + at : margin + at + rows, :] = moved
            if grow:
                empty = jnp.zeros((margin, FN), jnp.float32)
                count = max(last for place, _, last in plan[step] if place == block)
                if begin == 0:
                    target[block, :margin, :] = empty
                if end == count:
                    target[block, margin + count * HALF : 2 * margin + count * HALF, :] = empty
        for out, where in zip(outs[1:], others[2]):
            start = pl.multiple_of(where(side), EDGE)
            out[...] = result[0, pl.ds(start, out.shape[0]), :]

    relay(others[1], turn, givers, outs[1:], sems)


def relay(owners, turn, givers, outs, sems):
    side = turn[1]
    for slot, value, moves in owners:

        @pl.when(turn[slot] == value)
        def _():
            copies = []
            for at, (giver, block, start, rows, out, to) in enumerate(moves):
                start = start(side)
                if not isinstance(start, int):
                    start = pl.multiple_of(start, EDGE)
                source = givers[giver].at[block(side), pl.ds(start, rows)]
                copies.append(pltpu.make_async_copy(source, outs[out].at[pl.ds(to, rows)], sems.at[at]))
            for copy in copies:
                copy.start()
            for copy in copies:
                copy.wait()


def march(turn, number, inverse_blocks, coupling, pieces, cut, blocks, positions, grow, raw=(), others=((), (), ())):
    last = positions + (2 * STATIONS if grow else -2 * STATIONS)
    most = last + 2 if grow else positions
    counts = [positions + (2 if grow else -2) * (step + 1) for step in range(STATIONS)]
    if blocks == 2:
        plan = [[(0, 0, count), (1, 0, count)] for count in counts]
    else:
        cuts = [cut - (0 if grow else 2 * step) for step in range(STATIONS)]
        plan = [[(0, 0, at), (0, at, count)] for at, count in zip(cuts, counts)]
    vmem = pl.BlockSpec(memory_space=pltpu.VMEM)
    away = pl.BlockSpec(memory_space=pl.ANY)
    whole = (blocks, last * HALF, FN)
    shapes = [jax.ShapeDtypeStruct(whole, jnp.bfloat16)]
    if others[2]:
        shapes = [jax.ShapeDtypeStruct((size, FN), jnp.bfloat16) for size in (2 * ONE, WIDE, WIDE, 2 * ONE)]
    values = [piece[0] for piece in pieces]
    return pl.pallas_call(
        functools.partial(
            march_kernel,
            number,
            [piece[1:] for piece in pieces],
            others,
            plan,
            blocks,
            positions,
            grow,
            len(raw),
        ),
        out_shape=shapes,
        in_specs=[pl.BlockSpec(memory_space=pltpu.SMEM), vmem, away]
        + [vmem] * (len(values) + len(raw))
        + [away] * len(others[0]),
        out_specs=[vmem] * len(shapes),
        scratch_shapes=[pltpu.VMEM((blocks, most * HALF, FN), jnp.float32)] * 2
        + [
            pltpu.VMEM((STATIONS, FN, FN), jnp.bfloat16),
            pltpu.VMEM(whole if others[2] else (1, 16, FN), jnp.bfloat16),
            pltpu.SemaphoreType.DMA((STATIONS,)),
        ],
        compiler_params=pltpu.CompilerParams(vmem_limit_bytes=GRANT),
        cost_estimate=pl.CostEstimate(
            flops=2 * blocks * HALF * sum(counts) * FN * FN,
            bytes_accessed=2 * STATIONS * FN * FN,
            transcendentals=0,
        ),
    )(turn, coupling, inverse_blocks, *values, *raw, *others[0])


def ship_kernel(
    number, turn, share, below, raw, crossed, edge_cross, edge_same, direct, whole, held, turned, sem
):
    side, kind = turn[1], turn[2]

    def turn_over(source):
        copy = pltpu.make_async_copy(source, held, sem)
        copy.start()
        copy.wait()
        rows = ordered(held[...])
        for half in range(2):
            turned[half, :, :] = rows[half * ONE : (half + 1) * ONE]

    @pl.when(turn[0] == number)
    def _():
        turn_over(below)
        whole[...] = share[...]
        middle = share[:, EDGE : EDGE + ONE, :].astype(jnp.float32) + turned[...]
        whole[:, EDGE : EDGE + ONE, :] = middle.astype(jnp.bfloat16)
        start = pl.multiple_of(side * ONE, ONE)
        edge_cross[...] = whole[1 - side, pl.ds(start, WIDE), :]
        edge_same[...] = whole[side, pl.ds(start, WIDE), :]
        crossed[...] = whole[1 - side]
        direct[...] = whole[side]

    @pl.when(kind >= 2)
    def _():
        turn_over(raw)
        whole[:, :ONE, :] = turned[...].astype(jnp.bfloat16)

    @pl.when(kind == 2)
    def _():
        crossed[:ONE, :] = whole[1 - side, :ONE, :]

    @pl.when(kind == 3)
    def _():
        for half in range(2):
            edge_cross[half * EDGE : (half + 1) * EDGE, :] = whole[half, ONE - EDGE : ONE, :]
            edge_same[half * EDGE : (half + 1) * EDGE, :] = whole[half, :EDGE, :]


def center_kernel(number, turn, direct, crossed, edge_same, edge_cross, out):
    @pl.when(turn[0] == number)
    def _():
        side = turn[1]
        start = pl.multiple_of(side * EDGE, EDGE)
        from_edge = pl.multiple_of((1 - side) * EDGE, EDGE)
        for block, share, edge in ((side, direct, edge_same), (1 - side, crossed, edge_cross)):
            out[block, :, :] = share[EDGE : EDGE + ONE, :]
            here = out[block, pl.ds(start, EDGE), :].astype(jnp.float32)
            more = edge[pl.ds(from_edge, EDGE), :].astype(jnp.float32)
            out[block, pl.ds(start, EDGE), :] = (here + more).astype(jnp.bfloat16)


def gram_kernel(numbers, turn, *refs):
    inputs, (rows, gram, edges, sems) = refs[: 7 * len(numbers)], refs[7 * len(numbers) :]
    side = turn[1]

    def fetch(*pairs):
        copies = [pltpu.make_async_copy(source, target, sems.at[at]) for at, (source, target) in enumerate(pairs)]
        for copy in copies:
            copy.start()
        for copy in copies:
            copy.wait()

    for at, number in enumerate(numbers):
        share, low, high, state, crossed, back, last = inputs[7 * at : 7 * at + 7]

        @pl.when(turn[0] == number)
        def _():
            halves = [slice(0, EDGE), slice(EDGE, 2 * EDGE)]
            fetch(
                *[(share.at[half, EDGE : EDGE + ONE], rows.at[half]) for half in range(2)],
                *[(low.at[halves[half]], edges.at[half, :EDGE]) for half in range(2)],
                *[(high.at[halves[half]], edges.at[half, EDGE:]) for half in range(2)],
            )
            rows[...] = (rows[...].astype(jnp.float32) + edges[...].astype(jnp.float32)).astype(jnp.bfloat16)

        @pl.when(turn[0] == number - 1)
        def _():
            start = pl.multiple_of(side * ONE, ONE)
            fetch((state.at[0, pl.ds(start, ONE)], rows.at[side]), (crossed.at[:ONE], rows.at[1 - side]))

        @pl.when(turn[0] == number - 2)
        def _():
            fetch((back, rows))

        @pl.when(turn[0] == number - 3)
        def _():
            fetch((last, rows))

    flat = rows[...].reshape(2 * ONE, FN)
    full = lax.dot_general(flat, flat, (((1,), (1,)), ((), ())), preferred_element_type=jnp.float32)
    lines = []
    for first in range(2):
        line = []
        for second in range(2):
            block = None
            for point in range(POINTS):
                down, along = first * ONE + point * HALF, second * ONE + point * HALF
                term = full[down : down + HALF, along : along + HALF]
                block = term if block is None else block + term
            line.append(block)
        lines.append(jnp.concatenate(line, 1))
    total = jnp.concatenate(lines, 0)
    total = jnp.concatenate([total, jnp.zeros((K, 128 - K), jnp.float32)], 1)
    for at in range(gram.shape[0]):
        gram[at, :, :] = total


def factor_kernel(scale, grams, rows, by_column, by_place, same_point, basis, upper):
    terms = [grams[at] for at in range(grams.shape[0])]
    while len(terms) > 1:
        terms = [one + other for one, other in zip(terms[::2], terms[1::2])]
    eye = (
        lax.broadcasted_iota(jnp.int32, (K, K), 0) == lax.broadcasted_iota(jnp.int32, (K, K), 1)
    ).astype(jnp.float32)
    table = jnp.concatenate([terms[0][:, :K] * scale, eye], 1)
    row_index = lax.broadcasted_iota(jnp.int32, (K, 2 * K), 0)
    roots = jnp.zeros((K, 2 * K), jnp.float32)
    for j in range(0, K, STEP):
        lines = [table[j + m : j + m + 1, :] for m in range(STEP)]
        columns = [jnp.broadcast_to(table[:, j + m : j + m + 1], table.shape) for m in range(STEP)]
        entries = [
            [jnp.broadcast_to(lines[m][:, j + k : j + k + 1], lines[m].shape) for k in range(STEP)]
            for m in range(STEP)
        ]
        below = table
        for m in range(STEP):
            inverse = 1.0 / entries[m][m]
            for k in range(m + 1, STEP):
                ratio = entries[m][k] * inverse
                for n in range(k, STEP):
                    entries[k][n] = entries[k][n] - ratio * entries[m][n]
                lines[k] = lines[k] - ratio * lines[m]
                columns[k] = columns[k] - ratio * columns[m]
            below = below - columns[m] * (inverse * lines[m])
            roots = jnp.where(row_index == j + m, lax.rsqrt(entries[m][m]), roots)
        table = jnp.where(row_index >= j + STEP, below, table)
        for m in range(STEP):
            table = jnp.where(row_index == j + m, lines[m], table)
    table = table * roots
    column = lax.broadcasted_iota(jnp.int32, (K, K), 1)
    row = lax.broadcasted_iota(jnp.int32, (K, K), 0)
    upper[...] = jnp.where(column >= row, table[:, :K], 0.0)
    inverse = table[:, K:]
    terms = []
    for _ in range(2):
        term = inverse.astype(jnp.bfloat16)
        inverse = inverse - term.astype(jnp.float32)
        tall = lax.dot_general(
            by_column[...], term, (((1,), (1,)), ((), ())), preferred_element_type=jnp.float32
        ).astype(jnp.bfloat16)
        spread = lax.dot_general(
            tall, by_place[...], (((1,), (0,)), ((), ())), preferred_element_type=jnp.float32
        )
        terms.append((spread * same_point[...]).astype(jnp.bfloat16))
    both = lax.dot_general(
        rows[...], jnp.concatenate(terms, 1), (((0,), (0,)), ((), ())), preferred_element_type=jnp.float32
    )
    total = both[:, : POINTS * K] + both[:, POINTS * K :]
    basis[...] = total.astype(jnp.bfloat16)


def local(inverse_blocks, coupling, sources):
    sections = lax.axis_size("section")
    spans = lax.axis_size("span")
    pairs = spans // 2
    assert sections % 4 == 0 and spans % 2 == 0 and sources.shape[2] == POINTS * K
    group = lax.axis_index("section")
    side = (lax.axis_index("span") % 2).astype(jnp.int32)

    def send(value, *legs):
        routes = []
        for groups, down, route in legs:
            for g in groups:
                for s in range(spans):
                    routes.append((g * spans + s, (g - down) * spans + route(s)))
        return lax.ppermute(value, AXES, routes)

    def straight(s):
        return s

    def partner(s):
        return s ^ 1

    def neighbor(shift):
        return lambda s: (s + shift) % spans

    def pair_route(pair, side):
        return (pair % pairs) * 2 + side

    def outward(s):
        return pair_route(s // 2 + 2 * (s % 2) - 1, s % 2)

    def outward_cross(s):
        return pair_route(s // 2 + 2 * (s % 2) - 1, 1 - s % 2)

    def inward(s):
        return pair_route(s // 2 + 1 - 2 * (s % 2), s % 2)

    def of_kind(kind):
        return [g for g in range(sections) if (sections - 1 - g) % 4 == kind]

    turn = jnp.stack([group.astype(jnp.int32), side, ((sections - 1 - group) % 4).astype(jnp.int32)])

    half, point, column = np.meshgrid(np.arange(2), np.arange(POINTS), np.arange(HALF), indexing="ij")
    row_column = (half * HALF + column).reshape(-1)
    row_point = point.reshape(-1)
    place = np.arange(POINTS * K)
    by_column = jnp.asarray(np.arange(K)[None, :] == row_column[:, None], jnp.bfloat16)
    by_place = jnp.asarray(np.arange(K)[:, None] == place[None, :] % K, jnp.bfloat16)
    same_point = jnp.asarray(place[None, :] // K == row_point[:, None], jnp.float32)

    smem = pl.BlockSpec(memory_space=pltpu.SMEM)
    vmem = pl.BlockSpec(memory_space=pltpu.VMEM)
    away = pl.BlockSpec(memory_space=pl.ANY)
    raw = sources[0]
    odds, evens = list(range(1, sections, 2)), list(range(0, sections, 2))
    below = send(raw, (evens, -1, straight), (odds, 1, straight))
    incoming = None
    pair_source = wide_source = None
    candidates = []
    for g in reversed(of_kind(0)):
        pieces = [] if incoming is None else [(incoming, lambda side: (0, 0), ONE, None)]
        (share,) = march(turn, g, inverse_blocks, coupling, pieces, 0, 2, POINTS, True, (raw,))
        crossed, edge_cross, edge_same, direct, whole = pl.pallas_call(
            functools.partial(ship_kernel, g),
            out_shape=[jax.ShapeDtypeStruct((size, FN), jnp.bfloat16) for size in (2 * ONE, WIDE, WIDE, 2 * ONE)]
            + [jax.ShapeDtypeStruct(share.shape, jnp.bfloat16)],
            in_specs=[smem, vmem, away, away],
            out_specs=[vmem] * 5,
            scratch_shapes=[
                pltpu.VMEM(raw.shape, jnp.bfloat16),
                pltpu.VMEM((2, ONE, FN), jnp.float32),
                pltpu.SemaphoreType.DMA,
            ],
            compiler_params=pltpu.CompilerParams(vmem_limit_bytes=SMALL),
        )(turn, share, below, raw)
        first = incoming is None
        edge_cross = send(edge_cross, ([g], 1, outward_cross), (of_kind(3) if first else [], 0, neighbor(1)))
        crossed = send(crossed, ([g], 1, partner), (of_kind(2) if first else [], 0, partner))
        edge_same = send(edge_same, ([g], 1, outward), (of_kind(3) if first else [], 0, neighbor(-1)))
        direct = send(direct, ([g], 1, straight))
        if first:
            pair_source = [
                (whole, lambda side: (0, side * ONE), ONE, lambda side: side),
                (crossed, lambda side: (0, (1 - side) * ONE), ONE, None),
            ]
            wide_source = [
                (edge_cross.reshape(2, EDGE, FN), lambda side: (0, 0), EDGE, None),
                (whole, lambda side: (0, EDGE), ONE, None),
                (edge_same.reshape(2, EDGE, FN), lambda side: (0, EDGE + ONE), EDGE, None),
            ]

        (state,) = march(
            turn,
            g - 1,
            inverse_blocks,
            coupling,
            [
                (crossed, lambda side: (0, (1 - side) * ONE), 2 * ONE, None),
                (edge_cross, lambda side: (0, side * 2 * ONE), WIDE, None),
                (edge_same, lambda side: (0, (1 - side) * 2 * ONE), WIDE, None),
                (direct, lambda side: (0, side * ONE), 2 * ONE, None),
            ],
            14,
            1,
            3 * POINTS,
            False,
        )
        arrived = send(state, ([g - 1], 1, straight))

        crossed, edge_cross, edge_same, direct = march(
            turn,
            g - 2,
            inverse_blocks,
            coupling,
            [(arrived, lambda side: (0, 0), 2 * ONE, None)] + pair_source,
            10,
            1,
            2 * POINTS,
            True,
            (),
            (
                (share, state),
                (
                    (
                        0,
                        g,
                        (
                            (0, lambda side: 0, lambda side: EDGE + ONE, EDGE, 1, 0),
                            (0, lambda side: 1, lambda side: EDGE + ONE, EDGE, 1, EDGE),
                            (0, lambda side: 0, lambda side: 0, EDGE, 2, 0),
                            (0, lambda side: 1, lambda side: 0, EDGE, 2, EDGE),
                        ),
                    ),
                    (0, g - 1, ((1, lambda side: 0, lambda side: (1 - side) * ONE, ONE, 0, 0),)),
                ),
                (
                    lambda side: (1 - side) * ONE,
                    lambda side: side * 2 * ONE,
                    lambda side: (1 - side) * 2 * ONE,
                    lambda side: side * ONE,
                ),
            ),
        )
        edge_cross = send(edge_cross, ([g - 2], 1, outward_cross), ([g], 0, neighbor(1)))
        crossed = send(crossed, ([g - 2], 1, partner), ([g - 1], 0, partner))
        edge_same = send(edge_same, ([g - 2], 1, inward), ([g], 0, neighbor(-1)))
        direct = send(direct, ([g - 2], 1, straight))

        middle = pl.pallas_call(
            functools.partial(center_kernel, g - 3),
            out_shape=jax.ShapeDtypeStruct((2, ONE, FN), jnp.bfloat16),
            in_specs=[smem] + [vmem] * 4,
            out_specs=vmem,
            compiler_params=pltpu.CompilerParams(vmem_limit_bytes=SMALL),
        )(turn, direct, crossed, edge_same, edge_cross)
        back = send(middle, (evens, -1, straight), (odds, 1, straight))
        (last,) = march(
            turn,
            g - 3,
            inverse_blocks,
            coupling,
            [
                (crossed, lambda side: (1 - side, 0), 2 * ONE, None),
                (edge_cross, lambda side: (1 - side, side * ONE), WIDE, None),
                (edge_same, lambda side: (side, side * ONE), WIDE, None),
                (direct, lambda side: (side, 0), 2 * ONE, None),
            ]
            + wide_source,
            0,
            2,
            2 * POINTS,
            False,
        )
        candidates += [share, edge_cross, edge_same, state, crossed, back, last]
        if g > 3:
            incoming = send(last, ([g - 3], 1, straight))

    rows, grams = pl.pallas_call(
        functools.partial(gram_kernel, list(reversed(of_kind(0)))),
        out_shape=(
            jax.ShapeDtypeStruct((2, ONE, FN), jnp.bfloat16),
            jax.ShapeDtypeStruct((spans, K, 128), jnp.float32),
        ),
        in_specs=[smem] + [away] * len(candidates),
        out_specs=(vmem, vmem),
        scratch_shapes=[pltpu.VMEM((2, ONE, FN), jnp.bfloat16), pltpu.SemaphoreType.DMA((6,))],
        compiler_params=pltpu.CompilerParams(vmem_limit_bytes=SMALL),
    )(turn, *candidates)
    grams = lax.all_to_all(grams, "span", 0, 0, tiled=True)

    basis, upper = pl.pallas_call(
        functools.partial(factor_kernel, 1.0 / float(FN * POINTS * spans)),
        out_shape=(
            jax.ShapeDtypeStruct((FN, POINTS * K), jnp.bfloat16),
            jax.ShapeDtypeStruct((K, K), jnp.float32),
        ),
        in_specs=[vmem] * 5,
        out_specs=(vmem, vmem),
        compiler_params=pltpu.CompilerParams(vmem_limit_bytes=SMALL),
    )(grams, rows.reshape(POINTS * K, FN), by_column, by_place, same_point)
    return (basis[None], upper[None])


def solution(mesh):
    placed = (P("section", None, None), P("section", None), P("section", None, "span"))
    return jax.shard_map(
        local,
        mesh=mesh,
        in_specs=placed,
        out_specs=(P("section", None, "span"), P("section", None, None)),
        check_vma=False,
    )
```

```python
import functools

import jax
import jax.numpy as jnp
import numpy as np
from jax import lax
from jax.experimental import pallas as pl
from jax.experimental.pallas import tpu as pltpu
from jax.sharding import PartitionSpec as P

K = 48
STATIONS = 4
FN = 768
HALF = K // 2
POINTS = 8
ONE = POINTS * HALF
EDGE = STATIONS * HALF
WIDE = 2 * EDGE
STEP = 4
GRANT = 48 * 1024 * 1024
SMALL = 16 * 1024 * 1024
AXES = ("section", "span")


def one_hot_order():
    at = lax.broadcasted_iota(jnp.int32, (1, POINTS * K), 1)
    point = at * 1366 >> 16
    column = at - point * K
    half = (column >= HALF).astype(jnp.int32)
    target = half * (ONE - HALF) + point * HALF + column
    row = lax.broadcasted_iota(jnp.int32, (POINTS * K, POINTS * K), 0)
    return jnp.where(row == target, 1.0, 0.0).astype(jnp.bfloat16)


def ordered(raw):
    return lax.dot_general(one_hot_order(), raw, (((1,), (1,)), ((), ())), preferred_element_type=jnp.float32)


def march_kernel(number, places, others, blocks, positions, grow, raw, turn, coupling, weights, *refs):
    refs = list(refs)
    pieces = [refs.pop(0) for _ in places]
    raws = [refs.pop(0) for _ in range(raw)]
    givers = [refs.pop(0) for _ in others[0]]
    outs, (states, held, sems) = refs[:-3], refs[-3:]
    side = turn[1]
    lead = (STATIONS + 1) * HALF if grow else 0
    count = positions + 2 * STATIONS if grow else positions - 2
    shift = HALF if grow else 0

    @pl.when(turn[0] == number)
    def _():
        def copy(step):
            return pltpu.make_async_copy(weights.at[STATIONS - 1 - step], held.at[step], sems.at[step])

        copy(0).start()
        if grow:
            empty = jnp.zeros((blocks, lead, FN), jnp.float32)
            states[0, :, :lead, :] = empty
            states[0, :, lead + positions * HALF :, :] = empty
            states[1, :, :HALF, :] = empty[:, :HALF]
            states[1, :, HALF + count * HALF :, :] = empty[:, :HALF]

        def total(on):
            covers = []
            if raw:
                turned = ordered(raws[0][...])
                for half in range(2):
                    covers.append((half, 0, ONE, lambda low, high, at=half * ONE: turned[at + low : at + high]))
            for piece, (where, rows, pick) in zip(pieces, places):
                block, start = where(on)
                if pick is not None:
                    covers.append((block, start, rows, lambda low, high, p=piece, k=pick(on): p[k, low:high, :]))
                elif len(piece.shape) == 3:
                    for k in range(blocks):
                        covers.append((k, start, rows, lambda low, high, p=piece, k=k: p[k, low:high, :]))
                else:
                    covers.append((block, start, rows, lambda low, high, p=piece: p[low:high, :]))
            for block in range(blocks):
                here = [cover for cover in covers if cover[0] == block]
                bounds = {0, positions * HALF}
                for _, start, rows, _ in here:
                    bounds |= {start, start + rows}
                bounds = sorted(bounds)
                for low, high in zip(bounds, bounds[1:]):
                    value = jnp.zeros((high - low, FN), jnp.float32)
                    for _, start, rows, read in here:
                        if start <= low and high <= start + rows:
                            value = value + read(low - start, high - start).astype(jnp.float32)
                    states[0, block, lead + low : lead + high, :] = value

        if pieces:
            for on in range(2):
                pl.when(side == on)(functools.partial(total, on))
        else:
            total(0)
        copy(1).start()

        def station(step, carry):
            now = lax.rem(step, 2)
            rates = coupling[pl.ds(STATIONS - 1 - step, 1), :]
            rest = 1.0 - 2.0 * rates
            copy(step).wait()

            @pl.when(step + 2 < STATIONS)
            def _():
                copy(step + 2).start()

            if blocks == 1:
                cut = (count // 2 + 1) // 2 * 2
                chunks = [(0, 0, cut), (0, cut, count)]
            else:
                chunks = [(block, 0, count) for block in range(blocks)]
            for block, begin, end in chunks:
                at, rows = begin * HALF, (end - begin) * HALF
                both = states[now, block, at : at + rows, :] + states[now, block, at + 2 * HALF : at + 2 * HALF + rows, :]
                update = rest * states[now, block, at + HALF : at + HALF + rows, :] + rates * both
                states[1 - now, block, shift + at : shift + at + rows, :] = lax.dot_general(
                    update.astype(jnp.bfloat16),
                    held[step],
                    (((1,), (1,)), ((), ())),
                    preferred_element_type=jnp.float32,
                )
            return carry

        lax.fori_loop(0, STATIONS, station, 0)
        if not others[2]:
            rows = outs[0].shape[1]
            outs[0][...] = states[0, :, shift : shift + rows, :].astype(jnp.bfloat16)
        else:
            for out, where in zip(outs, others[2]):
                start = pl.multiple_of(shift + where(side), HALF)
                out[...] = states[0, 0, pl.ds(start, out.shape[0]), :].astype(jnp.bfloat16)

    relay(others[1], turn, givers, outs, sems)


def relay(owners, turn, givers, outs, sems):
    side = turn[1]
    for slot, value, moves in owners:

        @pl.when(turn[slot] == value)
        def _():
            copies = []
            for at, (giver, block, start, rows, out, to) in enumerate(moves):
                start = start(side)
                if not isinstance(start, int):
                    start = pl.multiple_of(start, EDGE)
                source = givers[giver].at[block(side), pl.ds(start, rows)]
                copies.append(pltpu.make_async_copy(source, outs[out].at[pl.ds(to, rows)], sems.at[at]))
            for copy in copies:
                copy.start()
            for copy in copies:
                copy.wait()


def march(turn, number, inverse_blocks, coupling, pieces, blocks, positions, grow, raw=(), others=((), (), ())):
    last = positions + (2 * STATIONS if grow else -2 * STATIONS)
    frame = last + 2 if grow else positions
    count = frame - 2
    vmem = pl.BlockSpec(memory_space=pltpu.VMEM)
    away = pl.BlockSpec(memory_space=pl.ANY)
    shapes = [jax.ShapeDtypeStruct((blocks, last * HALF, FN), jnp.bfloat16)]
    if others[2]:
        shapes = [jax.ShapeDtypeStruct((size, FN), jnp.bfloat16) for size in (2 * ONE, WIDE, WIDE, 2 * ONE)]
    values = [piece[0] for piece in pieces]
    return pl.pallas_call(
        functools.partial(
            march_kernel, number, [piece[1:] for piece in pieces], others, blocks, positions, grow, len(raw)
        ),
        out_shape=shapes,
        in_specs=[pl.BlockSpec(memory_space=pltpu.SMEM), vmem, away]
        + [vmem] * (len(values) + len(raw))
        + [away] * len(others[0]),
        out_specs=[vmem] * len(shapes),
        scratch_shapes=[
            pltpu.VMEM((2, blocks, frame * HALF, FN), jnp.float32),
            pltpu.VMEM((STATIONS, FN, FN), jnp.bfloat16),
            pltpu.SemaphoreType.DMA((STATIONS,)),
        ],
        compiler_params=pltpu.CompilerParams(vmem_limit_bytes=GRANT),
        cost_estimate=pl.CostEstimate(
            flops=2 * blocks * HALF * STATIONS * count * FN * FN,
            bytes_accessed=2 * STATIONS * FN * FN,
            transcendentals=0,
        ),
    )(turn, coupling, inverse_blocks, *values, *raw, *others[0])


def ship_kernel(
    number, turn, share, below, raw, crossed, edge_cross, edge_same, direct, whole, held, turned, sem
):
    side, kind = turn[1], turn[2]

    def turn_over(source):
        copy = pltpu.make_async_copy(source, held, sem)
        copy.start()
        copy.wait()
        rows = ordered(held[...])
        for half in range(2):
            turned[half, :, :] = rows[half * ONE : (half + 1) * ONE]

    @pl.when(turn[0] == number)
    def _():
        turn_over(below)
        whole[...] = share[...]
        middle = share[:, EDGE : EDGE + ONE, :].astype(jnp.float32) + turned[...]
        whole[:, EDGE : EDGE + ONE, :] = middle.astype(jnp.bfloat16)
        start = pl.multiple_of(side * ONE, ONE)
        edge_cross[...] = whole[1 - side, pl.ds(start, WIDE), :]
        edge_same[...] = whole[side, pl.ds(start, WIDE), :]
        crossed[...] = whole[1 - side]
        direct[...] = whole[side]

    @pl.when(kind >= 2)
    def _():
        turn_over(raw)
        whole[:, :ONE, :] = turned[...].astype(jnp.bfloat16)

    @pl.when(kind == 2)
    def _():
        crossed[:ONE, :] = whole[1 - side, :ONE, :]

    @pl.when(kind == 3)
    def _():
        for half in range(2):
            edge_cross[half * EDGE : (half + 1) * EDGE, :] = whole[half, ONE - EDGE : ONE, :]
            edge_same[half * EDGE : (half + 1) * EDGE, :] = whole[half, :EDGE, :]


def center_kernel(number, turn, direct, crossed, edge_same, edge_cross, out):
    @pl.when(turn[0] == number)
    def _():
        side = turn[1]
        start = pl.multiple_of(side * EDGE, EDGE)
        from_edge = pl.multiple_of((1 - side) * EDGE, EDGE)
        for block, share, edge in ((side, direct, edge_same), (1 - side, crossed, edge_cross)):
            out[block, :, :] = share[EDGE : EDGE + ONE, :]
            here = out[block, pl.ds(start, EDGE), :].astype(jnp.float32)
            more = edge[pl.ds(from_edge, EDGE), :].astype(jnp.float32)
            out[block, pl.ds(start, EDGE), :] = (here + more).astype(jnp.bfloat16)


def gram_kernel(numbers, turn, *refs):
    inputs, (rows, gram, edges, sems) = refs[: 7 * len(numbers)], refs[7 * len(numbers) :]
    side = turn[1]

    def fetch(*pairs):
        copies = [pltpu.make_async_copy(source, target, sems.at[at]) for at, (source, target) in enumerate(pairs)]
        for copy in copies:
            copy.start()
        for copy in copies:
            copy.wait()

    for at, number in enumerate(numbers):
        share, low, high, state, crossed, back, last = inputs[7 * at : 7 * at + 7]

        @pl.when(turn[0] == number)
        def _():
            halves = [slice(0, EDGE), slice(EDGE, 2 * EDGE)]
            fetch(
                *[(share.at[half, EDGE : EDGE + ONE], rows.at[half]) for half in range(2)],
                *[(low.at[halves[half]], edges.at[half, :EDGE]) for half in range(2)],
                *[(high.at[halves[half]], edges.at[half, EDGE:]) for half in range(2)],
            )
            rows[...] = (rows[...].astype(jnp.float32) + edges[...].astype(jnp.float32)).astype(jnp.bfloat16)

        @pl.when(turn[0] == number - 1)
        def _():
            start = pl.multiple_of(side * ONE, ONE)
            fetch((state.at[0, pl.ds(start, ONE)], rows.at[side]), (crossed.at[:ONE], rows.at[1 - side]))

        @pl.when(turn[0] == number - 2)
        def _():
            fetch((back, rows))

        @pl.when(turn[0] == number - 3)
        def _():
            fetch((last, rows))

    flat = rows[...].reshape(2 * ONE, FN)
    full = lax.dot_general(flat, flat, (((1,), (1,)), ((), ())), preferred_element_type=jnp.float32)
    lines = []
    for first in range(2):
        line = []
        for second in range(2):
            block = None
            for point in range(POINTS):
                down, along = first * ONE + point * HALF, second * ONE + point * HALF
                term = full[down : down + HALF, along : along + HALF]
                block = term if block is None else block + term
            line.append(block)
        lines.append(jnp.concatenate(line, 1))
    total = jnp.concatenate(lines, 0)
    total = jnp.concatenate([total, jnp.zeros((K, 128 - K), jnp.float32)], 1)
    for at in range(gram.shape[0]):
        gram[at, :, :] = total


def factor_kernel(scale, grams, rows, by_column, by_place, same_point, basis, upper):
    terms = [grams[at] for at in range(grams.shape[0])]
    while len(terms) > 1:
        terms = [one + other for one, other in zip(terms[::2], terms[1::2])]
    eye = (
        lax.broadcasted_iota(jnp.int32, (K, K), 0) == lax.broadcasted_iota(jnp.int32, (K, K), 1)
    ).astype(jnp.float32)
    table = jnp.concatenate([terms[0][:, :K] * scale, eye], 1)
    row_index = lax.broadcasted_iota(jnp.int32, (K, 2 * K), 0)
    roots = jnp.zeros((K, 2 * K), jnp.float32)
    for j in range(0, K, STEP):
        lines = [table[j + m : j + m + 1, :] for m in range(STEP)]
        columns = [jnp.broadcast_to(table[:, j + m : j + m + 1], table.shape) for m in range(STEP)]
        entries = [
            [jnp.broadcast_to(lines[m][:, j + k : j + k + 1], lines[m].shape) for k in range(STEP)]
            for m in range(STEP)
        ]
        below = table
        for m in range(STEP):
            inverse = 1.0 / entries[m][m]
            for k in range(m + 1, STEP):
                ratio = entries[m][k] * inverse
                for n in range(k, STEP):
                    entries[k][n] = entries[k][n] - ratio * entries[m][n]
                lines[k] = lines[k] - ratio * lines[m]
                columns[k] = columns[k] - ratio * columns[m]
            below = below - columns[m] * (inverse * lines[m])
            roots = jnp.where(row_index == j + m, lax.rsqrt(entries[m][m]), roots)
        table = jnp.where(row_index >= j + STEP, below, table)
        for m in range(STEP):
            table = jnp.where(row_index == j + m, lines[m], table)
    table = table * roots
    column = lax.broadcasted_iota(jnp.int32, (K, K), 1)
    row = lax.broadcasted_iota(jnp.int32, (K, K), 0)
    upper[...] = jnp.where(column >= row, table[:, :K], 0.0)
    inverse = table[:, K:]
    terms = []
    for _ in range(2):
        term = inverse.astype(jnp.bfloat16)
        inverse = inverse - term.astype(jnp.float32)
        tall = lax.dot_general(
            by_column[...], term, (((1,), (1,)), ((), ())), preferred_element_type=jnp.float32
        ).astype(jnp.bfloat16)
        spread = lax.dot_general(
            tall, by_place[...], (((1,), (0,)), ((), ())), preferred_element_type=jnp.float32
        )
        terms.append((spread * same_point[...]).astype(jnp.bfloat16))
    both = lax.dot_general(
        rows[...], jnp.concatenate(terms, 1), (((0,), (0,)), ((), ())), preferred_element_type=jnp.float32
    )
    total = both[:, : POINTS * K] + both[:, POINTS * K :]
    basis[...] = total.astype(jnp.bfloat16)


def local(inverse_blocks, coupling, sources):
    sections = lax.axis_size("section")
    spans = lax.axis_size("span")
    pairs = spans // 2
    assert sections % 4 == 0 and spans % 2 == 0 and sources.shape[2] == POINTS * K
    group = lax.axis_index("section")
    side = (lax.axis_index("span") % 2).astype(jnp.int32)

    def send(value, *legs):
        routes = []
        for groups, down, route in legs:
            for g in groups:
                for s in range(spans):
                    routes.append((g * spans + s, (g - down) * spans + route(s)))
        return lax.ppermute(value, AXES, routes)

    def straight(s):
        return s

    def partner(s):
        return s ^ 1

    def neighbor(shift):
        return lambda s: (s + shift) % spans

    def pair_route(pair, side):
        return (pair % pairs) * 2 + side

    def outward(s):
        return pair_route(s // 2 + 2 * (s % 2) - 1, s % 2)

    def outward_cross(s):
        return pair_route(s // 2 + 2 * (s % 2) - 1, 1 - s % 2)

    def inward(s):
        return pair_route(s // 2 + 1 - 2 * (s % 2), s % 2)

    def of_kind(kind):
        return [g for g in range(sections) if (sections - 1 - g) % 4 == kind]

    turn = jnp.stack([group.astype(jnp.int32), side, ((sections - 1 - group) % 4).astype(jnp.int32)])

    half, point, column = np.meshgrid(np.arange(2), np.arange(POINTS), np.arange(HALF), indexing="ij")
    row_column = (half * HALF + column).reshape(-1)
    row_point = point.reshape(-1)
    place = np.arange(POINTS * K)
    by_column = jnp.asarray(np.arange(K)[None, :] == row_column[:, None], jnp.bfloat16)
    by_place = jnp.asarray(np.arange(K)[:, None] == place[None, :] % K, jnp.bfloat16)
    same_point = jnp.asarray(place[None, :] // K == row_point[:, None], jnp.float32)

    smem = pl.BlockSpec(memory_space=pltpu.SMEM)
    vmem = pl.BlockSpec(memory_space=pltpu.VMEM)
    away = pl.BlockSpec(memory_space=pl.ANY)
    raw = sources[0]
    odds, evens = list(range(1, sections, 2)), list(range(0, sections, 2))
    below = send(raw, (evens, -1, straight), (odds, 1, straight))
    incoming = None
    pair_source = wide_source = None
    candidates = []
    for g in reversed(of_kind(0)):
        pieces = [] if incoming is None else [(incoming, lambda side: (0, 0), ONE, None)]
        (share,) = march(turn, g, inverse_blocks, coupling, pieces, 2, POINTS, True, (raw,))
        crossed, edge_cross, edge_same, direct, whole = pl.pallas_call(
            functools.partial(ship_kernel, g),
            out_shape=[jax.ShapeDtypeStruct((size, FN), jnp.bfloat16) for size in (2 * ONE, WIDE, WIDE, 2 * ONE)]
            + [jax.ShapeDtypeStruct(share.shape, jnp.bfloat16)],
            in_specs=[smem, vmem, away, away],
            out_specs=[vmem] * 5,
            scratch_shapes=[
                pltpu.VMEM(raw.shape, jnp.bfloat16),
                pltpu.VMEM((2, ONE, FN), jnp.float32),
                pltpu.SemaphoreType.DMA,
            ],
            compiler_params=pltpu.CompilerParams(vmem_limit_bytes=SMALL),
        )(turn, share, below, raw)
        first = incoming is None
        edge_cross = send(edge_cross, ([g], 1, outward_cross), (of_kind(3) if first else [], 0, neighbor(1)))
        crossed = send(crossed, ([g], 1, partner), (of_kind(2) if first else [], 0, partner))
        edge_same = send(edge_same, ([g], 1, outward), (of_kind(3) if first else [], 0, neighbor(-1)))
        direct = send(direct, ([g], 1, straight))
        if first:
            pair_source = [
                (whole, lambda side: (0, side * ONE), ONE, lambda side: side),
                (crossed, lambda side: (0, (1 - side) * ONE), ONE, None),
            ]
            wide_source = [
                (edge_cross.reshape(2, EDGE, FN), lambda side: (0, 0), EDGE, None),
                (whole, lambda side: (0, EDGE), ONE, None),
                (edge_same.reshape(2, EDGE, FN), lambda side: (0, EDGE + ONE), EDGE, None),
            ]

        (state,) = march(
            turn,
            g - 1,
            inverse_blocks,
            coupling,
            [
                (crossed, lambda side: (0, (1 - side) * ONE), 2 * ONE, None),
                (edge_cross, lambda side: (0, side * 2 * ONE), WIDE, None),
                (edge_same, lambda side: (0, (1 - side) * 2 * ONE), WIDE, None),
                (direct, lambda side: (0, side * ONE), 2 * ONE, None),
            ],
            1,
            3 * POINTS,
            False,
        )
        arrived = send(state, ([g - 1], 1, straight))

        crossed, edge_cross, edge_same, direct = march(
            turn,
            g - 2,
            inverse_blocks,
            coupling,
            [(arrived, lambda side: (0, 0), 2 * ONE, None)] + pair_source,
            1,
            2 * POINTS,
            True,
            (),
            (
                (share, state),
                (
                    (
                        0,
                        g,
                        (
                            (0, lambda side: 0, lambda side: EDGE + ONE, EDGE, 1, 0),
                            (0, lambda side: 1, lambda side: EDGE + ONE, EDGE, 1, EDGE),
                            (0, lambda side: 0, lambda side: 0, EDGE, 2, 0),
                            (0, lambda side: 1, lambda side: 0, EDGE, 2, EDGE),
                        ),
                    ),
                    (0, g - 1, ((1, lambda side: 0, lambda side: (1 - side) * ONE, ONE, 0, 0),)),
                ),
                (
                    lambda side: (1 - side) * ONE,
                    lambda side: side * 2 * ONE,
                    lambda side: (1 - side) * 2 * ONE,
                    lambda side: side * ONE,
                ),
            ),
        )
        edge_cross = send(edge_cross, ([g - 2], 1, outward_cross), ([g], 0, neighbor(1)))
        crossed = send(crossed, ([g - 2], 1, partner), ([g - 1], 0, partner))
        edge_same = send(edge_same, ([g - 2], 1, inward), ([g], 0, neighbor(-1)))
        direct = send(direct, ([g - 2], 1, straight))

        middle = pl.pallas_call(
            functools.partial(center_kernel, g - 3),
            out_shape=jax.ShapeDtypeStruct((2, ONE, FN), jnp.bfloat16),
            in_specs=[smem] + [vmem] * 4,
            out_specs=vmem,
            compiler_params=pltpu.CompilerParams(vmem_limit_bytes=SMALL),
        )(turn, direct, crossed, edge_same, edge_cross)
        back = send(middle, (evens, -1, straight), (odds, 1, straight))
        (last,) = march(
            turn,
            g - 3,
            inverse_blocks,
            coupling,
            [
                (crossed, lambda side: (1 - side, 0), 2 * ONE, None),
                (edge_cross, lambda side: (1 - side, side * ONE), WIDE, None),
                (edge_same, lambda side: (side, side * ONE), WIDE, None),
                (direct, lambda side: (side, 0), 2 * ONE, None),
            ]
            + wide_source,
            2,
            2 * POINTS,
            False,
        )
        candidates += [share, edge_cross, edge_same, state, crossed, back, last]
        if g > 3:
            incoming = send(last, ([g - 3], 1, straight))

    rows, grams = pl.pallas_call(
        functools.partial(gram_kernel, list(reversed(of_kind(0)))),
        out_shape=(
            jax.ShapeDtypeStruct((2, ONE, FN), jnp.bfloat16),
            jax.ShapeDtypeStruct((spans, K, 128), jnp.float32),
        ),
        in_specs=[smem] + [away] * len(candidates),
        out_specs=(vmem, vmem),
        scratch_shapes=[pltpu.VMEM((2, ONE, FN), jnp.bfloat16), pltpu.SemaphoreType.DMA((6,))],
        compiler_params=pltpu.CompilerParams(vmem_limit_bytes=SMALL),
    )(turn, *candidates)
    grams = lax.all_to_all(grams, "span", 0, 0, tiled=True)

    basis, upper = pl.pallas_call(
        functools.partial(factor_kernel, 1.0 / float(FN * POINTS * spans)),
        out_shape=(
            jax.ShapeDtypeStruct((FN, POINTS * K), jnp.bfloat16),
            jax.ShapeDtypeStruct((K, K), jnp.float32),
        ),
        in_specs=[vmem] * 5,
        out_specs=(vmem, vmem),
        compiler_params=pltpu.CompilerParams(vmem_limit_bytes=SMALL),
    )(grams, rows.reshape(POINTS * K, FN), by_column, by_place, same_point)
    return (basis[None], upper[None])


def solution(mesh):
    placed = (P("section", None, None), P("section", None), P("section", None, "span"))
    return jax.shard_map(
        local,
        mesh=mesh,
        in_specs=placed,
        out_specs=(P("section", None, "span"), P("section", None, None)),
        check_vma=False,
    )
```

```python
import functools

import jax
import jax.numpy as jnp
import numpy as np
from jax import lax
from jax.experimental import pallas as pl
from jax.experimental.pallas import tpu as pltpu
from jax.sharding import PartitionSpec as P

K = 48
STATIONS = 4
FN = 768
HALF = K // 2
POINTS = 8
ONE = POINTS * HALF
EDGE = STATIONS * HALF
WIDE = 2 * EDGE
STEP = 4
TILE = 256
GRANT = 48 * 1024 * 1024
SMALL = 16 * 1024 * 1024
AXES = ("section", "span")


def one_hot_order():
    at = lax.broadcasted_iota(jnp.int32, (1, POINTS * K), 1)
    point = at * 1366 >> 16
    column = at - point * K
    half = (column >= HALF).astype(jnp.int32)
    target = half * (ONE - HALF) + point * HALF + column
    row = lax.broadcasted_iota(jnp.int32, (POINTS * K, POINTS * K), 0)
    return jnp.where(row == target, 1.0, 0.0).astype(jnp.bfloat16)


def ordered(raw):
    return lax.dot_general(one_hot_order(), raw, (((1,), (1,)), ((), ())), preferred_element_type=jnp.float32)


def march_kernel(number, places, others, plan, blocks, positions, grow, raw, turn, coupling, weights, *refs):
    refs = list(refs)
    pieces = [refs.pop(0) for _ in places]
    raws = [refs.pop(0) for _ in range(raw)]
    givers = [refs.pop(0) for _ in others[0]]
    outs, (first, second, held, result, turned, sems) = refs[:-6], refs[-6:]
    if not others[2] and not raw:
        result = outs[0]
    states = [first, second]
    order = list(reversed(range(STATIONS)))
    side = turn[1]

    @pl.when(turn[0] == number)
    def _():
        copies = [
            pltpu.make_async_copy(weights.at[station], held.at[step], sems.at[step])
            for step, station in enumerate(order)
        ]
        tiles = [slice(at, at + TILE) for at in range(0, FN, TILE)]
        opening = [
            pltpu.make_async_copy(weights.at[order[0], tile], held.at[0, tile], sems.at[STATIONS + at])
            for at, tile in enumerate(tiles)
        ]
        for copy in opening:
            copy.start()
        margin = 2 * HALF if grow else 0
        if margin:
            empty = jnp.zeros((blocks, margin, FN), jnp.float32)
            first[:, :margin, :] = empty
            first[:, margin + positions * HALF : 2 * margin + positions * HALF, :] = empty

        def total(on):
            covers = []
            if raw:
                own = ordered(raws[0][...])
                for half in range(2):
                    covers.append((half, 0, ONE, lambda low, high, at=half * ONE: own[at + low : at + high]))
            for piece, (where, rows, pick) in zip(pieces, places):
                block, start = where(on)
                if pick is not None:
                    covers.append((block, start, rows, lambda low, high, p=piece, k=pick(on): p[k, low:high, :]))
                elif len(piece.shape) == 3:
                    for k in range(blocks):
                        covers.append((k, start, rows, lambda low, high, p=piece, k=k: p[k, low:high, :]))
                else:
                    covers.append((block, start, rows, lambda low, high, p=piece: p[low:high, :]))
            for block in range(blocks):
                here = [cover for cover in covers if cover[0] == block]
                bounds = {0, positions * HALF}
                for _, start, rows, _ in here:
                    bounds |= {start, start + rows}
                bounds = sorted(bounds)
                for low, high in zip(bounds, bounds[1:]):
                    value = jnp.zeros((high - low, FN), jnp.float32)
                    for _, start, rows, read in here:
                        if start <= low and high <= start + rows:
                            value = value + read(low - start, high - start).astype(jnp.float32)
                    first[block, margin + low : margin + high, :] = value

        if pieces:
            for on in range(2):
                pl.when(side == on)(functools.partial(total, on))
        else:
            total(0)
        if raw:
            rows = ordered(raws[1][...])
            for half in range(2):
                turned[half, :, :] = rows[half * ONE : (half + 1) * ONE]

        def stencil(step, chunk):
            block, begin, end = chunk
            at, rows = begin * HALF, (end - begin) * HALF
            source = states[step % 2]
            rates = coupling[order[step] : order[step] + 1, :]
            both = source[block, at : at + rows, :] + source[block, at + 2 * HALF : at + 2 * HALF + rows, :]
            update = (1.0 - 2.0 * rates) * source[block, at + HALF : at + HALF + rows, :] + rates * both
            return update.astype(jnp.bfloat16)

        copies[1].start()
        jobs = [(step, chunk) for step in range(STATIONS) for chunk in plan[step]]
        update = stencil(*jobs[0])
        for at_job, (step, chunk) in enumerate(jobs):
            block, begin, end = chunk
            at, rows = begin * HALF, (end - begin) * HALF
            current = update
            if at_job + 1 < len(jobs):
                update = stencil(*jobs[at_job + 1])
            target = states[1 - step % 2]
            if at_job == 0:
                for tile, copy in zip(tiles, opening):
                    copy.wait()
                    target[block, margin + at : margin + at + rows, tile] = lax.dot_general(
                        current, held[0, tile], (((1,), (1,)), ((), ())), preferred_element_type=jnp.float32
                    )
                copies[2].start()
            else:
                if step and chunk is plan[step][0]:
                    copies[step].wait()
                    if step + 2 < STATIONS:
                        copies[step + 2].start()
                moved = lax.dot_general(
                    current, held[step], (((1,), (1,)), ((), ())), preferred_element_type=jnp.float32
                )
            if step == STATIONS - 1:
                result[block, at : at + rows, :] = moved.astype(jnp.bfloat16)
                continue
            if at_job:
                target[block, margin + at : margin + at + rows, :] = moved
            if grow:
                empty = jnp.zeros((margin, FN), jnp.float32)
                count = max(last for place, _, last in plan[step] if place == block)
                if begin == 0:
                    target[block, :margin, :] = empty
                if end == count:
                    target[block, margin + count * HALF : 2 * margin + count * HALF, :] = empty
        if raw:
            outs[4][...] = result[...]
            middle = result[:, EDGE : EDGE + ONE, :].astype(jnp.float32) + turned[...]
            result[:, EDGE : EDGE + ONE, :] = middle.astype(jnp.bfloat16)
            start = pl.multiple_of(side * ONE, ONE)
            outs[0][...] = result[1 - side]
            outs[1][...] = result[1 - side, pl.ds(start, WIDE), :]
            outs[2][...] = result[side, pl.ds(start, WIDE), :]
            outs[3][...] = result[side]
        for out, where in zip(outs, others[2]):
            start = pl.multiple_of(where(side), EDGE)
            out[...] = result[0, pl.ds(start, out.shape[0]), :]

    relay(others[1], turn, givers, outs, sems)
    if raw:
        kind = turn[2]
        crossed, edge_cross, edge_same, _, kept = outs

        @pl.when(kind >= 2)
        def _():
            rows = ordered(raws[0][...]).astype(jnp.bfloat16)
            for half in range(2):
                kept[half, :ONE, :] = rows[half * ONE : (half + 1) * ONE]

        @pl.when(kind == 2)
        def _():
            crossed[:ONE, :] = kept[1 - side, :ONE, :]

        @pl.when(kind == 3)
        def _():
            for half in range(2):
                edge_cross[half * EDGE : (half + 1) * EDGE, :] = kept[half, ONE - EDGE : ONE, :]
                edge_same[half * EDGE : (half + 1) * EDGE, :] = kept[half, :EDGE, :]


def relay(owners, turn, givers, outs, sems):
    side = turn[1]
    for slot, value, moves in owners:

        @pl.when(turn[slot] == value)
        def _():
            copies = []
            for at, (giver, block, start, rows, out, to) in enumerate(moves):
                start = start(side)
                if not isinstance(start, int):
                    start = pl.multiple_of(start, EDGE)
                source = givers[giver].at[block(side), pl.ds(start, rows)]
                copies.append(pltpu.make_async_copy(source, outs[out].at[pl.ds(to, rows)], sems.at[at]))
            for copy in copies:
                copy.start()
            for copy in copies:
                copy.wait()


def march(turn, number, inverse_blocks, coupling, pieces, cut, blocks, positions, grow, raw=(), others=((), (), ())):
    last = positions + (2 * STATIONS if grow else -2 * STATIONS)
    most = last + 2 if grow else positions
    counts = [positions + (2 if grow else -2) * (step + 1) for step in range(STATIONS)]
    if blocks == 2:
        plan = [[(0, 0, count), (1, 0, count)] for count in counts]
    else:
        cuts = [cut - (0 if grow else 2 * step) for step in range(STATIONS)]
        plan = [[(0, 0, at), (0, at, count)] for at, count in zip(cuts, counts)]
    vmem = pl.BlockSpec(memory_space=pltpu.VMEM)
    away = pl.BlockSpec(memory_space=pl.ANY)
    whole = (blocks, last * HALF, FN)
    shapes = [jax.ShapeDtypeStruct(whole, jnp.bfloat16)]
    if others[2] or raw:
        shapes = [jax.ShapeDtypeStruct((size, FN), jnp.bfloat16) for size in (2 * ONE, WIDE, WIDE, 2 * ONE)]
    if raw:
        shapes.append(jax.ShapeDtypeStruct(whole, jnp.bfloat16))
    values = [piece[0] for piece in pieces]
    return pl.pallas_call(
        functools.partial(
            march_kernel,
            number,
            [piece[1:] for piece in pieces],
            others,
            plan,
            blocks,
            positions,
            grow,
            len(raw),
        ),
        out_shape=shapes,
        in_specs=[pl.BlockSpec(memory_space=pltpu.SMEM), vmem, away]
        + [vmem] * (len(values) + len(raw))
        + [away] * len(others[0]),
        out_specs=[vmem] * len(shapes),
        scratch_shapes=[pltpu.VMEM((blocks, most * HALF, FN), jnp.float32)] * 2
        + [
            pltpu.VMEM((STATIONS, FN, FN), jnp.bfloat16),
            pltpu.VMEM(whole if others[2] or raw else (1, 16, FN), jnp.bfloat16),
            pltpu.VMEM((2, ONE, FN) if raw else (1, 8, FN), jnp.float32),
            pltpu.SemaphoreType.DMA((STATIONS + FN // TILE,)),
        ],
        compiler_params=pltpu.CompilerParams(vmem_limit_bytes=GRANT),
        cost_estimate=pl.CostEstimate(
            flops=2 * blocks * HALF * sum(counts) * FN * FN,
            bytes_accessed=2 * STATIONS * FN * FN,
            transcendentals=0,
        ),
    )(turn, coupling, inverse_blocks, *values, *raw, *others[0])


def center_kernel(number, turn, direct, crossed, edge_same, edge_cross, out):
    @pl.when(turn[0] == number)
    def _():
        side = turn[1]
        start = pl.multiple_of(side * EDGE, EDGE)
        from_edge = pl.multiple_of((1 - side) * EDGE, EDGE)
        for block, share, edge in ((side, direct, edge_same), (1 - side, crossed, edge_cross)):
            out[block, :, :] = share[EDGE : EDGE + ONE, :]
            here = out[block, pl.ds(start, EDGE), :].astype(jnp.float32)
            more = edge[pl.ds(from_edge, EDGE), :].astype(jnp.float32)
            out[block, pl.ds(start, EDGE), :] = (here + more).astype(jnp.bfloat16)


def gram_kernel(numbers, turn, *refs):
    inputs, (rows, gram, edges, sems) = refs[: 7 * len(numbers)], refs[7 * len(numbers) :]
    side = turn[1]

    def fetch(*pairs):
        copies = [pltpu.make_async_copy(source, target, sems.at[at]) for at, (source, target) in enumerate(pairs)]
        for copy in copies:
            copy.start()
        for copy in copies:
            copy.wait()

    for at, number in enumerate(numbers):
        share, low, high, state, crossed, back, last = inputs[7 * at : 7 * at + 7]

        @pl.when(turn[0] == number)
        def _():
            halves = [slice(0, EDGE), slice(EDGE, 2 * EDGE)]
            fetch(
                *[(share.at[half, EDGE : EDGE + ONE], rows.at[half]) for half in range(2)],
                *[(low.at[halves[half]], edges.at[half, :EDGE]) for half in range(2)],
                *[(high.at[halves[half]], edges.at[half, EDGE:]) for half in range(2)],
            )
            rows[...] = (rows[...].astype(jnp.float32) + edges[...].astype(jnp.float32)).astype(jnp.bfloat16)

        @pl.when(turn[0] == number - 1)
        def _():
            start = pl.multiple_of(side * ONE, ONE)
            fetch((state.at[0, pl.ds(start, ONE)], rows.at[side]), (crossed.at[:ONE], rows.at[1 - side]))

        @pl.when(turn[0] == number - 2)
        def _():
            fetch((back, rows))

        @pl.when(turn[0] == number - 3)
        def _():
            fetch((last, rows))

    flat = rows[...].reshape(2 * ONE, FN)
    full = lax.dot_general(flat, flat, (((1,), (1,)), ((), ())), preferred_element_type=jnp.float32)
    lines = []
    for first in range(2):
        line = []
        for second in range(2):
            block = None
            for point in range(POINTS):
                down, along = first * ONE + point * HALF, second * ONE + point * HALF
                term = full[down : down + HALF, along : along + HALF]
                block = term if block is None else block + term
            line.append(block)
        lines.append(jnp.concatenate(line, 1))
    total = jnp.concatenate(lines, 0)
    total = jnp.concatenate([total, jnp.zeros((K, 128 - K), jnp.float32)], 1)
    for at in range(gram.shape[0]):
        gram[at, :, :] = total


def factor_kernel(scale, grams, rows, by_column, by_place, same_point, basis, upper):
    terms = [grams[at] for at in range(grams.shape[0])]
    while len(terms) > 1:
        terms = [one + other for one, other in zip(terms[::2], terms[1::2])]
    eye = (
        lax.broadcasted_iota(jnp.int32, (K, K), 0) == lax.broadcasted_iota(jnp.int32, (K, K), 1)
    ).astype(jnp.float32)
    table = jnp.concatenate([terms[0][:, :K] * scale, eye], 1)
    row_index = lax.broadcasted_iota(jnp.int32, (K, 2 * K), 0)
    roots = jnp.zeros((K, 2 * K), jnp.float32)
    for j in range(0, K, STEP):
        lines = [table[j + m : j + m + 1, :] for m in range(STEP)]
        columns = [jnp.broadcast_to(table[:, j + m : j + m + 1], table.shape) for m in range(STEP)]
        entries = [
            [jnp.broadcast_to(lines[m][:, j + k : j + k + 1], lines[m].shape) for k in range(STEP)]
            for m in range(STEP)
        ]
        below = table
        for m in range(STEP):
            inverse = 1.0 / entries[m][m]
            for k in range(m + 1, STEP):
                ratio = entries[m][k] * inverse
                for n in range(k, STEP):
                    entries[k][n] = entries[k][n] - ratio * entries[m][n]
                lines[k] = lines[k] - ratio * lines[m]
                columns[k] = columns[k] - ratio * columns[m]
            below = below - columns[m] * (inverse * lines[m])
            roots = jnp.where(row_index == j + m, lax.rsqrt(entries[m][m]), roots)
        table = jnp.where(row_index >= j + STEP, below, table)
        for m in range(STEP):
            table = jnp.where(row_index == j + m, lines[m], table)
    table = table * roots
    column = lax.broadcasted_iota(jnp.int32, (K, K), 1)
    row = lax.broadcasted_iota(jnp.int32, (K, K), 0)
    upper[...] = jnp.where(column >= row, table[:, :K], 0.0)
    inverse = table[:, K:]
    terms = []
    for _ in range(2):
        term = inverse.astype(jnp.bfloat16)
        inverse = inverse - term.astype(jnp.float32)
        tall = lax.dot_general(
            by_column[...], term, (((1,), (1,)), ((), ())), preferred_element_type=jnp.float32
        ).astype(jnp.bfloat16)
        spread = lax.dot_general(
            tall, by_place[...], (((1,), (0,)), ((), ())), preferred_element_type=jnp.float32
        )
        terms.append((spread * same_point[...]).astype(jnp.bfloat16))
    both = lax.dot_general(
        rows[...], jnp.concatenate(terms, 1), (((0,), (0,)), ((), ())), preferred_element_type=jnp.float32
    )
    total = both[:, : POINTS * K] + both[:, POINTS * K :]
    basis[...] = total.astype(jnp.bfloat16)


def local(inverse_blocks, coupling, sources):
    sections = lax.axis_size("section")
    spans = lax.axis_size("span")
    pairs = spans // 2
    assert sections % 4 == 0 and spans % 2 == 0 and sources.shape[2] == POINTS * K
    group = lax.axis_index("section")
    side = (lax.axis_index("span") % 2).astype(jnp.int32)

    def send(value, *legs):
        routes = []
        for groups, down, route in legs:
            for g in groups:
                for s in range(spans):
                    routes.append((g * spans + s, (g - down) % sections * spans + route(s)))
        return lax.ppermute(value, AXES, routes)

    def straight(s):
        return s

    def partner(s):
        return s ^ 1

    def neighbor(shift):
        return lambda s: (s + shift) % spans

    def pair_route(pair, side):
        return (pair % pairs) * 2 + side

    def outward(s):
        return pair_route(s // 2 + 2 * (s % 2) - 1, s % 2)

    def outward_cross(s):
        return pair_route(s // 2 + 2 * (s % 2) - 1, 1 - s % 2)

    def inward(s):
        return pair_route(s // 2 + 1 - 2 * (s % 2), s % 2)

    def of_kind(kind):
        return [g for g in range(sections) if (sections - 1 - g) % 4 == kind]

    turn = jnp.stack([group.astype(jnp.int32), side, ((sections - 1 - group) % 4).astype(jnp.int32)])

    half, point, column = np.meshgrid(np.arange(2), np.arange(POINTS), np.arange(HALF), indexing="ij")
    row_column = (half * HALF + column).reshape(-1)
    row_point = point.reshape(-1)
    place = np.arange(POINTS * K)
    by_column = jnp.asarray(np.arange(K)[None, :] == row_column[:, None], jnp.bfloat16)
    by_place = jnp.asarray(np.arange(K)[:, None] == place[None, :] % K, jnp.bfloat16)
    same_point = jnp.asarray(place[None, :] // K == row_point[:, None], jnp.float32)

    smem = pl.BlockSpec(memory_space=pltpu.SMEM)
    vmem = pl.BlockSpec(memory_space=pltpu.VMEM)
    away = pl.BlockSpec(memory_space=pl.ANY)
    raw = sources[0]
    odds, evens = list(range(1, sections, 2)), list(range(0, sections, 2))
    below = send(raw, (evens, -1, straight), (odds, 1, straight))
    incoming = None
    pair_source = wide_source = None
    candidates = []
    for g in reversed(of_kind(0)):
        pieces = [] if incoming is None else [(incoming, lambda side: (0, 0), ONE, None)]
        crossed, edge_cross, edge_same, direct, share = march(
            turn, g, inverse_blocks, coupling, pieces, 0, 2, POINTS, True, (raw, below)
        )
        first = incoming is None
        edge_cross = send(edge_cross, ([g], 1, outward_cross), (of_kind(3) if first else [], 0, neighbor(1)))
        crossed = send(crossed, ([g], 1, partner), (of_kind(2) if first else [], 0, partner))
        edge_same = send(edge_same, ([g], 1, outward), (of_kind(3) if first else [], 0, neighbor(-1)))
        direct = send(direct, ([g], 1, straight))
        if first:
            pair_source = [
                (share, lambda side: (0, side * ONE), ONE, lambda side: side),
                (crossed, lambda side: (0, (1 - side) * ONE), ONE, None),
            ]
            wide_source = [
                (edge_cross.reshape(2, EDGE, FN), lambda side: (0, 0), EDGE, None),
                (share, lambda side: (0, EDGE), ONE, None),
                (edge_same.reshape(2, EDGE, FN), lambda side: (0, EDGE + ONE), EDGE, None),
            ]

        (state,) = march(
            turn,
            g - 1,
            inverse_blocks,
            coupling,
            [
                (crossed, lambda side: (0, (1 - side) * ONE), 2 * ONE, None),
                (edge_cross, lambda side: (0, side * 2 * ONE), WIDE, None),
                (edge_same, lambda side: (0, (1 - side) * 2 * ONE), WIDE, None),
                (direct, lambda side: (0, side * ONE), 2 * ONE, None),
            ],
            14,
            1,
            3 * POINTS,
            False,
        )
        arrived = send(state, (list(range(sections)), 1, straight))

        crossed, edge_cross, edge_same, direct = march(
            turn,
            g - 2,
            inverse_blocks,
            coupling,
            [(arrived, lambda side: (0, 0), 2 * ONE, None)] + pair_source,
            10,
            1,
            2 * POINTS,
            True,
            (),
            (
                (share, state),
                (
                    (
                        0,
                        g,
                        (
                            (0, lambda side: 0, lambda side: EDGE + ONE, EDGE, 1, 0),
                            (0, lambda side: 1, lambda side: EDGE + ONE, EDGE, 1, EDGE),
                            (0, lambda side: 0, lambda side: 0, EDGE, 2, 0),
                            (0, lambda side: 1, lambda side: 0, EDGE, 2, EDGE),
                        ),
                    ),
                    (0, g - 1, ((1, lambda side: 0, lambda side: (1 - side) * ONE, ONE, 0, 0),)),
                ),
                (
                    lambda side: (1 - side) * ONE,
                    lambda side: side * 2 * ONE,
                    lambda side: (1 - side) * 2 * ONE,
                    lambda side: side * ONE,
                ),
            ),
        )
        edge_cross = send(edge_cross, ([g - 2], 1, outward_cross), ([g], 0, neighbor(1)))
        crossed = send(crossed, ([g - 2], 1, partner), ([g - 1], 0, partner))
        edge_same = send(edge_same, ([g - 2], 1, inward), ([g], 0, neighbor(-1)))
        direct = send(direct, ([g - 2], 1, straight))

        middle = pl.pallas_call(
            functools.partial(center_kernel, g - 3),
            out_shape=jax.ShapeDtypeStruct((2, ONE, FN), jnp.bfloat16),
            in_specs=[smem] + [vmem] * 4,
            out_specs=vmem,
            compiler_params=pltpu.CompilerParams(vmem_limit_bytes=SMALL),
        )(turn, direct, crossed, edge_same, edge_cross)
        back = send(middle, (evens, -1, straight), (odds, 1, straight))
        (last,) = march(
            turn,
            g - 3,
            inverse_blocks,
            coupling,
            [
                (crossed, lambda side: (1 - side, 0), 2 * ONE, None),
                (edge_cross, lambda side: (1 - side, side * ONE), WIDE, None),
                (edge_same, lambda side: (side, side * ONE), WIDE, None),
                (direct, lambda side: (side, 0), 2 * ONE, None),
            ]
            + wide_source,
            0,
            2,
            2 * POINTS,
            False,
        )
        candidates += [share, edge_cross, edge_same, state, crossed, back, last]
        if g > 3:
            incoming = send(last, ([g - 3], 1, straight))

    rows, grams = pl.pallas_call(
        functools.partial(gram_kernel, list(reversed(of_kind(0)))),
        out_shape=(
            jax.ShapeDtypeStruct((2, ONE, FN), jnp.bfloat16),
            jax.ShapeDtypeStruct((spans, K, 128), jnp.float32),
        ),
        in_specs=[smem] + [away] * len(candidates),
        out_specs=(vmem, vmem),
        scratch_shapes=[pltpu.VMEM((2, ONE, FN), jnp.bfloat16), pltpu.SemaphoreType.DMA((6,))],
        compiler_params=pltpu.CompilerParams(vmem_limit_bytes=SMALL),
    )(turn, *candidates)
    grams = lax.all_to_all(grams, "span", 0, 0, tiled=True)

    basis, upper = pl.pallas_call(
        functools.partial(factor_kernel, 1.0 / float(FN * POINTS * spans)),
        out_shape=(
            jax.ShapeDtypeStruct((FN, POINTS * K), jnp.bfloat16),
            jax.ShapeDtypeStruct((K, K), jnp.float32),
        ),
        in_specs=[vmem] * 5,
        out_specs=(vmem, vmem),
        compiler_params=pltpu.CompilerParams(vmem_limit_bytes=SMALL),
    )(grams, rows.reshape(POINTS * K, FN), by_column, by_place, same_point)
    return (basis[None], upper[None])


def solution(mesh):
    placed = (P("section", None, None), P("section", None), P("section", None, "span"))
    return jax.shard_map(
        local,
        mesh=mesh,
        in_specs=placed,
        out_specs=(P("section", None, "span"), P("section", None, None)),
        check_vma=False,
    )
```

```python
import functools

import jax
import jax.numpy as jnp
import numpy as np
from jax import lax
from jax.experimental import pallas as pl
from jax.experimental.pallas import tpu as pltpu
from jax.sharding import PartitionSpec as P

K = 48
STATIONS = 4
FN = 768
HALF = K // 2
POINTS = 8
ONE = POINTS * HALF
EDGE = STATIONS * HALF
WIDE = 2 * EDGE
STEP = 6
GRANT = 48 * 1024 * 1024
SMALL = 16 * 1024 * 1024
AXES = ("section", "span")


def one_hot_order():
    at = lax.broadcasted_iota(jnp.int32, (1, POINTS * K), 1)
    point = at * 1366 >> 16
    column = at - point * K
    half = (column >= HALF).astype(jnp.int32)
    target = half * (ONE - HALF) + point * HALF + column
    row = lax.broadcasted_iota(jnp.int32, (POINTS * K, POINTS * K), 0)
    return jnp.where(row == target, 1.0, 0.0).astype(jnp.bfloat16)


def ordered(raw):
    return lax.dot_general(one_hot_order(), raw, (((1,), (1,)), ((), ())), preferred_element_type=jnp.float32)


def march_kernel(number, places, others, plan, blocks, positions, grow, raw, turn, coupling, weights, *refs):
    refs = list(refs)
    pieces = [refs.pop(0) for _ in places]
    raws = [refs.pop(0) for _ in range(raw)]
    givers = [refs.pop(0) for _ in others[0]]
    outs, (first, second, held, result, sems) = refs[:-5], refs[-5:]
    if not others[2]:
        result = outs[0]
    else:
        outs = [None] + outs
    states = [first, second]
    order = list(reversed(range(STATIONS)))
    side = turn[1]

    @pl.when(turn[0] == number)
    def _():
        copies = [
            pltpu.make_async_copy(weights.at[station], held.at[step], sems.at[step])
            for step, station in enumerate(order)
        ]
        copies[0].start()
        margin = 2 * HALF if grow else 0
        if margin:
            empty = jnp.zeros((blocks, margin, FN), jnp.float32)
            first[:, :margin, :] = empty
            first[:, margin + positions * HALF : 2 * margin + positions * HALF, :] = empty

        def total(on):
            covers = []
            if raw:
                turned = ordered(raws[0][...])
                for half in range(2):
                    covers.append((half, 0, ONE, lambda low, high, at=half * ONE: turned[at + low : at + high]))
            for piece, (where, rows, pick) in zip(pieces, places):
                block, start = where(on)
                if pick is not None:
                    covers.append((block, start, rows, lambda low, high, p=piece, k=pick(on): p[k, low:high, :]))
                elif len(piece.shape) == 3:
                    for k in range(blocks):
                        covers.append((k, start, rows, lambda low, high, p=piece, k=k: p[k, low:high, :]))
                else:
                    covers.append((block, start, rows, lambda low, high, p=piece: p[low:high, :]))
            for block in range(blocks):
                here = [cover for cover in covers if cover[0] == block]
                bounds = {0, positions * HALF}
                for _, start, rows, _ in here:
                    bounds |= {start, start + rows}
                bounds = sorted(bounds)
                for low, high in zip(bounds, bounds[1:]):
                    value = jnp.zeros((high - low, FN), jnp.float32)
                    for _, start, rows, read in here:
                        if start <= low and high <= start + rows:
                            value = value + read(low - start, high - start).astype(jnp.float32)
                    first[block, margin + low : margin + high, :] = value

        if pieces:
            for on in range(2):
                pl.when(side == on)(functools.partial(total, on))
        else:
            total(0)

        def stencil(step, chunk):
            block, begin, end = chunk
            at, rows = begin * HALF, (end - begin) * HALF
            source = states[step % 2]
            rates = coupling[order[step] : order[step] + 1, :]
            both = source[block, at : at + rows, :] + source[block, at + 2 * HALF : at + 2 * HALF + rows, :]
            update = (1.0 - 2.0 * rates) * source[block, at + HALF : at + HALF + rows, :] + rates * both
            return update.astype(jnp.bfloat16)

        copies[1].start()
        jobs = [(step, chunk) for step in range(STATIONS) for chunk in plan[step]]
        update = stencil(*jobs[0])
        for at_job, (step, chunk) in enumerate(jobs):
            block, begin, end = chunk
            at, rows = begin * HALF, (end - begin) * HALF
            current = update
            if at_job + 1 < len(jobs):
                update = stencil(*jobs[at_job + 1])
            if chunk is plan[step][0]:
                copies[step].wait()
                if step + 2 < STATIONS:
                    copies[step + 2].start()
            moved = lax.dot_general(
                current, held[step], (((1,), (1,)), ((), ())), preferred_element_type=jnp.float32
            )
            if step == STATIONS - 1:
                result[block, at : at + rows, :] = moved.astype(jnp.bfloat16)
                continue
            target = states[1 - step % 2]
            target[block, margin + at : margin + at + rows, :] = moved
            if grow:
                empty = jnp.zeros((margin, FN), jnp.float32)
                count = max(last for place, _, last in plan[step] if place == block)
                if begin == 0:
                    target[block, :margin, :] = empty
                if end == count:
                    target[block, margin + count * HALF : 2 * margin + count * HALF, :] = empty
        for out, where in zip(outs[1:], others[2]):
            start = pl.multiple_of(where(side), EDGE)
            out[...] = result[0, pl.ds(start, out.shape[0]), :]

    relay(others[1], turn, givers, outs[1:], sems)


def relay(owners, turn, givers, outs, sems):
    side = turn[1]
    for slot, value, moves in owners:

        @pl.when(turn[slot] == value)
        def _():
            copies = []
            for at, (giver, block, start, rows, out, to) in enumerate(moves):
                start = start(side)
                if not isinstance(start, int):
                    start = pl.multiple_of(start, EDGE)
                source = givers[giver].at[block(side), pl.ds(start, rows)]
                copies.append(pltpu.make_async_copy(source, outs[out].at[pl.ds(to, rows)], sems.at[at]))
            for copy in copies:
                copy.start()
            for copy in copies:
                copy.wait()


def march(turn, number, inverse_blocks, coupling, pieces, cut, blocks, positions, grow, raw=(), others=((), (), ())):
    last = positions + (2 * STATIONS if grow else -2 * STATIONS)
    most = last + 2 if grow else positions
    counts = [positions + (2 if grow else -2) * (step + 1) for step in range(STATIONS)]
    if blocks == 2:
        plan = [[(0, 0, count), (1, 0, count)] for count in counts]
    else:
        cuts = [cut - (0 if grow else 2 * step) for step in range(STATIONS)]
        plan = [[(0, 0, at), (0, at, count)] for at, count in zip(cuts, counts)]
    vmem = pl.BlockSpec(memory_space=pltpu.VMEM)
    away = pl.BlockSpec(memory_space=pl.ANY)
    whole = (blocks, last * HALF, FN)
    shapes = [jax.ShapeDtypeStruct(whole, jnp.bfloat16)]
    if others[2]:
        shapes = [jax.ShapeDtypeStruct((size, FN), jnp.bfloat16) for size in (2 * ONE, WIDE, WIDE, 2 * ONE)]
    values = [piece[0] for piece in pieces]
    return pl.pallas_call(
        functools.partial(
            march_kernel,
            number,
            [piece[1:] for piece in pieces],
            others,
            plan,
            blocks,
            positions,
            grow,
            len(raw),
        ),
        out_shape=shapes,
        in_specs=[pl.BlockSpec(memory_space=pltpu.SMEM), vmem, away]
        + [vmem] * (len(values) + len(raw))
        + [away] * len(others[0]),
        out_specs=[vmem] * len(shapes),
        scratch_shapes=[pltpu.VMEM((blocks, most * HALF, FN), jnp.float32)] * 2
        + [
            pltpu.VMEM((STATIONS, FN, FN), jnp.bfloat16),
            pltpu.VMEM(whole if others[2] else (1, 16, FN), jnp.bfloat16),
            pltpu.SemaphoreType.DMA((STATIONS,)),
        ],
        compiler_params=pltpu.CompilerParams(vmem_limit_bytes=GRANT),
        cost_estimate=pl.CostEstimate(
            flops=2 * blocks * HALF * sum(counts) * FN * FN,
            bytes_accessed=2 * STATIONS * FN * FN,
            transcendentals=0,
        ),
    )(turn, coupling, inverse_blocks, *values, *raw, *others[0])


def ship_kernel(
    number, turn, share, below, raw, crossed, edge_cross, edge_same, direct, whole, held, turned, sem
):
    side, kind = turn[1], turn[2]

    def turn_over(source):
        copy = pltpu.make_async_copy(source, held, sem)
        copy.start()
        copy.wait()
        rows = ordered(held[...])
        for half in range(2):
            turned[half, :, :] = rows[half * ONE : (half + 1) * ONE]

    @pl.when(turn[0] == number)
    def _():
        turn_over(below)
        whole[...] = share[...]
        middle = share[:, EDGE : EDGE + ONE, :].astype(jnp.float32) + turned[...]
        whole[:, EDGE : EDGE + ONE, :] = middle.astype(jnp.bfloat16)
        start = pl.multiple_of(side * ONE, ONE)
        edge_cross[...] = whole[1 - side, pl.ds(start, WIDE), :]
        edge_same[...] = whole[side, pl.ds(start, WIDE), :]
        crossed[...] = whole[1 - side]
        direct[...] = whole[side]

    @pl.when(kind >= 2)
    def _():
        turn_over(raw)
        whole[:, :ONE, :] = turned[...].astype(jnp.bfloat16)

    @pl.when(kind == 2)
    def _():
        crossed[:ONE, :] = whole[1 - side, :ONE, :]

    @pl.when(kind == 3)
    def _():
        for half in range(2):
            edge_cross[half * EDGE : (half + 1) * EDGE, :] = whole[half, ONE - EDGE : ONE, :]
            edge_same[half * EDGE : (half + 1) * EDGE, :] = whole[half, :EDGE, :]


def center_kernel(number, turn, direct, crossed, edge_same, edge_cross, out):
    @pl.when(turn[0] == number)
    def _():
        side = turn[1]
        start = pl.multiple_of(side * EDGE, EDGE)
        from_edge = pl.multiple_of((1 - side) * EDGE, EDGE)
        for block, share, edge in ((side, direct, edge_same), (1 - side, crossed, edge_cross)):
            out[block, :, :] = share[EDGE : EDGE + ONE, :]
            here = out[block, pl.ds(start, EDGE), :].astype(jnp.float32)
            more = edge[pl.ds(from_edge, EDGE), :].astype(jnp.float32)
            out[block, pl.ds(start, EDGE), :] = (here + more).astype(jnp.bfloat16)


def gram_kernel(numbers, turn, *refs):
    inputs, (rows, gram, edges, sems) = refs[: 7 * len(numbers)], refs[7 * len(numbers) :]
    side = turn[1]

    def fetch(*pairs):
        copies = [pltpu.make_async_copy(source, target, sems.at[at]) for at, (source, target) in enumerate(pairs)]
        for copy in copies:
            copy.start()
        for copy in copies:
            copy.wait()

    for at, number in enumerate(numbers):
        share, low, high, state, crossed, back, last = inputs[7 * at : 7 * at + 7]

        @pl.when(turn[0] == number)
        def _():
            halves = [slice(0, EDGE), slice(EDGE, 2 * EDGE)]
            fetch(
                *[(share.at[half, EDGE : EDGE + ONE], rows.at[half]) for half in range(2)],
                *[(low.at[halves[half]], edges.at[half, :EDGE]) for half in range(2)],
                *[(high.at[halves[half]], edges.at[half, EDGE:]) for half in range(2)],
            )
            rows[...] = (rows[...].astype(jnp.float32) + edges[...].astype(jnp.float32)).astype(jnp.bfloat16)

        @pl.when(turn[0] == number - 1)
        def _():
            start = pl.multiple_of(side * ONE, ONE)
            fetch((state.at[0, pl.ds(start, ONE)], rows.at[side]), (crossed.at[:ONE], rows.at[1 - side]))

        @pl.when(turn[0] == number - 2)
        def _():
            fetch((back, rows))

        @pl.when(turn[0] == number - 3)
        def _():
            fetch((last, rows))

    flat = rows[...].reshape(2 * ONE, FN)
    full = lax.dot_general(flat, flat, (((1,), (1,)), ((), ())), preferred_element_type=jnp.float32)
    lines = []
    for first in range(2):
        line = []
        for second in range(2):
            block = None
            for point in range(POINTS):
                down, along = first * ONE + point * HALF, second * ONE + point * HALF
                term = full[down : down + HALF, along : along + HALF]
                block = term if block is None else block + term
            line.append(block)
        lines.append(jnp.concatenate(line, 1))
    total = jnp.concatenate(lines, 0)
    total = jnp.concatenate([total, jnp.zeros((K, 128 - K), jnp.float32)], 1)
    for at in range(gram.shape[0]):
        gram[at, :, :] = total


def factor_kernel(scale, grams, rows, by_column, by_place, same_point, basis, upper):
    terms = [grams[at] for at in range(grams.shape[0])]
    while len(terms) > 1:
        terms = [one + other for one, other in zip(terms[::2], terms[1::2])]
    eye = (
        lax.broadcasted_iota(jnp.int32, (K, K), 0) == lax.broadcasted_iota(jnp.int32, (K, K), 1)
    ).astype(jnp.float32)
    table = jnp.concatenate([terms[0][:, :K] * scale, eye], 1)
    row_index = lax.broadcasted_iota(jnp.int32, (K, 2 * K), 0)
    roots = jnp.zeros((K, 2 * K), jnp.float32)
    for j in range(0, K, STEP):
        lines = [table[j + m : j + m + 1, :] for m in range(STEP)]
        columns = [jnp.broadcast_to(table[:, j + m : j + m + 1], table.shape) for m in range(STEP)]
        entries = [
            [jnp.broadcast_to(lines[m][:, j + k : j + k + 1], lines[m].shape) for k in range(STEP)]
            for m in range(STEP)
        ]
        below = table
        for m in range(STEP):
            inverse = 1.0 / entries[m][m]
            for k in range(m + 1, STEP):
                ratio = entries[m][k] * inverse
                for n in range(k, STEP):
                    entries[k][n] = entries[k][n] - ratio * entries[m][n]
                lines[k] = lines[k] - ratio * lines[m]
                columns[k] = columns[k] - ratio * columns[m]
            below = below - columns[m] * (inverse * lines[m])
            roots = jnp.where(row_index == j + m, lax.rsqrt(entries[m][m]), roots)
        table = jnp.where(row_index >= j + STEP, below, table)
        for m in range(STEP):
            table = jnp.where(row_index == j + m, lines[m], table)
    table = table * roots
    column = lax.broadcasted_iota(jnp.int32, (K, K), 1)
    row = lax.broadcasted_iota(jnp.int32, (K, K), 0)
    upper[...] = jnp.where(column >= row, table[:, :K], 0.0)
    inverse = table[:, K:]
    terms = []
    for _ in range(2):
        term = inverse.astype(jnp.bfloat16)
        inverse = inverse - term.astype(jnp.float32)
        tall = lax.dot_general(
            by_column[...], term, (((1,), (1,)), ((), ())), preferred_element_type=jnp.float32
        ).astype(jnp.bfloat16)
        spread = lax.dot_general(
            tall, by_place[...], (((1,), (0,)), ((), ())), preferred_element_type=jnp.float32
        )
        terms.append((spread * same_point[...]).astype(jnp.bfloat16))
    both = lax.dot_general(
        rows[...], jnp.concatenate(terms, 1), (((0,), (0,)), ((), ())), preferred_element_type=jnp.float32
    )
    total = both[:, : POINTS * K] + both[:, POINTS * K :]
    basis[...] = total.astype(jnp.bfloat16)


def local(inverse_blocks, coupling, sources):
    sections = lax.axis_size("section")
    spans = lax.axis_size("span")
    pairs = spans // 2
    assert sections % 4 == 0 and spans % 2 == 0 and sources.shape[2] == POINTS * K
    group = lax.axis_index("section")
    side = (lax.axis_index("span") % 2).astype(jnp.int32)

    def send(value, *legs):
        routes = []
        for groups, down, route in legs:
            for g in groups:
                for s in range(spans):
                    routes.append((g * spans + s, (g - down) % sections * spans + route(s)))
        return lax.ppermute(value, AXES, routes)

    def straight(s):
        return s

    def partner(s):
        return s ^ 1

    def neighbor(shift):
        return lambda s: (s + shift) % spans

    def pair_route(pair, side):
        return (pair % pairs) * 2 + side

    def outward(s):
        return pair_route(s // 2 + 2 * (s % 2) - 1, s % 2)

    def outward_cross(s):
        return pair_route(s // 2 + 2 * (s % 2) - 1, 1 - s % 2)

    def inward(s):
        return pair_route(s // 2 + 1 - 2 * (s % 2), s % 2)

    def of_kind(kind):
        return [g for g in range(sections) if (sections - 1 - g) % 4 == kind]

    turn = jnp.stack([group.astype(jnp.int32), side, ((sections - 1 - group) % 4).astype(jnp.int32)])

    half, point, column = np.meshgrid(np.arange(2), np.arange(POINTS), np.arange(HALF), indexing="ij")
    row_column = (half * HALF + column).reshape(-1)
    row_point = point.reshape(-1)
    place = np.arange(POINTS * K)
    by_column = jnp.asarray(np.arange(K)[None, :] == row_column[:, None], jnp.bfloat16)
    by_place = jnp.asarray(np.arange(K)[:, None] == place[None, :] % K, jnp.bfloat16)
    same_point = jnp.asarray(place[None, :] // K == row_point[:, None], jnp.float32)

    smem = pl.BlockSpec(memory_space=pltpu.SMEM)
    vmem = pl.BlockSpec(memory_space=pltpu.VMEM)
    away = pl.BlockSpec(memory_space=pl.ANY)
    raw = sources[0]
    odds, evens = list(range(1, sections, 2)), list(range(0, sections, 2))
    below = send(raw, (evens, -1, straight), (odds, 1, straight))
    incoming = None
    pair_source = wide_source = None
    candidates = []
    for g in reversed(of_kind(0)):
        pieces = [] if incoming is None else [(incoming, lambda side: (0, 0), ONE, None)]
        (share,) = march(turn, g, inverse_blocks, coupling, pieces, 0, 2, POINTS, True, (raw,))
        crossed, edge_cross, edge_same, direct, whole = pl.pallas_call(
            functools.partial(ship_kernel, g),
            out_shape=[jax.ShapeDtypeStruct((size, FN), jnp.bfloat16) for size in (2 * ONE, WIDE, WIDE, 2 * ONE)]
            + [jax.ShapeDtypeStruct(share.shape, jnp.bfloat16)],
            in_specs=[smem, vmem, away, away],
            out_specs=[vmem] * 5,
            scratch_shapes=[
                pltpu.VMEM(raw.shape, jnp.bfloat16),
                pltpu.VMEM((2, ONE, FN), jnp.float32),
                pltpu.SemaphoreType.DMA,
            ],
            compiler_params=pltpu.CompilerParams(vmem_limit_bytes=SMALL),
        )(turn, share, below, raw)
        first = incoming is None
        edge_cross = send(edge_cross, ([g], 1, outward_cross), (of_kind(3) if first else [], 0, neighbor(1)))
        crossed = send(crossed, ([g], 1, partner), (of_kind(2) if first else [], 0, partner))
        edge_same = send(edge_same, ([g], 1, outward), (of_kind(3) if first else [], 0, neighbor(-1)))
        direct = send(direct, ([g], 1, straight))
        if first:
            pair_source = [
                (whole, lambda side: (0, side * ONE), ONE, lambda side: side),
                (crossed, lambda side: (0, (1 - side) * ONE), ONE, None),
            ]
            wide_source = [
                (edge_cross.reshape(2, EDGE, FN), lambda side: (0, 0), EDGE, None),
                (whole, lambda side: (0, EDGE), ONE, None),
                (edge_same.reshape(2, EDGE, FN), lambda side: (0, EDGE + ONE), EDGE, None),
            ]

        (state,) = march(
            turn,
            g - 1,
            inverse_blocks,
            coupling,
            [
                (crossed, lambda side: (0, (1 - side) * ONE), 2 * ONE, None),
                (edge_cross, lambda side: (0, side * 2 * ONE), WIDE, None),
                (edge_same, lambda side: (0, (1 - side) * 2 * ONE), WIDE, None),
                (direct, lambda side: (0, side * ONE), 2 * ONE, None),
            ],
            14,
            1,
            3 * POINTS,
            False,
        )
        arrived = send(state, (list(range(sections)), 1, straight))

        crossed, edge_cross, edge_same, direct = march(
            turn,
            g - 2,
            inverse_blocks,
            coupling,
            [(arrived, lambda side: (0, 0), 2 * ONE, None)] + pair_source,
            10,
            1,
            2 * POINTS,
            True,
            (),
            (
                (share, state),
                (
                    (
                        0,
                        g,
                        (
                            (0, lambda side: 0, lambda side: EDGE + ONE, EDGE, 1, 0),
                            (0, lambda side: 1, lambda side: EDGE + ONE, EDGE, 1, EDGE),
                            (0, lambda side: 0, lambda side: 0, EDGE, 2, 0),
                            (0, lambda side: 1, lambda side: 0, EDGE, 2, EDGE),
                        ),
                    ),
                    (0, g - 1, ((1, lambda side: 0, lambda side: (1 - side) * ONE, ONE, 0, 0),)),
                ),
                (
                    lambda side: (1 - side) * ONE,
                    lambda side: side * 2 * ONE,
                    lambda side: (1 - side) * 2 * ONE,
                    lambda side: side * ONE,
                ),
            ),
        )
        edge_cross = send(edge_cross, ([g - 2], 1, outward_cross), ([g], 0, neighbor(1)))
        crossed = send(crossed, ([g - 2], 1, partner), ([g - 1], 0, partner))
        edge_same = send(edge_same, ([g - 2], 1, inward), ([g], 0, neighbor(-1)))
        direct = send(direct, ([g - 2], 1, straight))

        middle = pl.pallas_call(
            functools.partial(center_kernel, g - 3),
            out_shape=jax.ShapeDtypeStruct((2, ONE, FN), jnp.bfloat16),
            in_specs=[smem] + [vmem] * 4,
            out_specs=vmem,
            compiler_params=pltpu.CompilerParams(vmem_limit_bytes=SMALL),
        )(turn, direct, crossed, edge_same, edge_cross)
        back = send(middle, (evens, -1, straight), (odds, 1, straight))
        (last,) = march(
            turn,
            g - 3,
            inverse_blocks,
            coupling,
            [
                (crossed, lambda side: (1 - side, 0), 2 * ONE, None),
                (edge_cross, lambda side: (1 - side, side * ONE), WIDE, None),
                (edge_same, lambda side: (side, side * ONE), WIDE, None),
                (direct, lambda side: (side, 0), 2 * ONE, None),
            ]
            + wide_source,
            0,
            2,
            2 * POINTS,
            False,
        )
        candidates += [share, edge_cross, edge_same, state, crossed, back, last]
        if g > 3:
            incoming = send(last, ([g - 3], 1, straight))

    rows, grams = pl.pallas_call(
        functools.partial(gram_kernel, list(reversed(of_kind(0)))),
        out_shape=(
            jax.ShapeDtypeStruct((2, ONE, FN), jnp.bfloat16),
            jax.ShapeDtypeStruct((spans, K, 128), jnp.float32),
        ),
        in_specs=[smem] + [away] * len(candidates),
        out_specs=(vmem, vmem),
        scratch_shapes=[pltpu.VMEM((2, ONE, FN), jnp.bfloat16), pltpu.SemaphoreType.DMA((6,))],
        compiler_params=pltpu.CompilerParams(vmem_limit_bytes=SMALL),
    )(turn, *candidates)
    grams = lax.all_to_all(grams, "span", 0, 0, tiled=True)

    basis, upper = pl.pallas_call(
        functools.partial(factor_kernel, 1.0 / float(FN * POINTS * spans)),
        out_shape=(
            jax.ShapeDtypeStruct((FN, POINTS * K), jnp.bfloat16),
            jax.ShapeDtypeStruct((K, K), jnp.float32),
        ),
        in_specs=[vmem] * 5,
        out_specs=(vmem, vmem),
        compiler_params=pltpu.CompilerParams(vmem_limit_bytes=SMALL),
    )(grams, rows.reshape(POINTS * K, FN), by_column, by_place, same_point)
    return (basis[None], upper[None])


def solution(mesh):
    placed = (P("section", None, None), P("section", None), P("section", None, "span"))
    return jax.shard_map(
        local,
        mesh=mesh,
        in_specs=placed,
        out_specs=(P("section", None, "span"), P("section", None, None)),
        check_vma=False,
    )
```

```python
import functools

import jax
import jax.numpy as jnp
import numpy as np
from jax import lax
from jax.experimental import pallas as pl
from jax.experimental.pallas import tpu as pltpu
from jax.sharding import PartitionSpec as P

K = 48
STATIONS = 4
FN = 768
HALF = K // 2
POINTS = 8
ONE = POINTS * HALF
EDGE = STATIONS * HALF
WIDE = 2 * EDGE
STEP = 6
GRANT = 48 * 1024 * 1024
SMALL = 16 * 1024 * 1024
AXES = ("section", "span")


def one_hot_order():
    at = lax.broadcasted_iota(jnp.int32, (1, POINTS * K), 1)
    point = at * 1366 >> 16
    column = at - point * K
    half = (column >= HALF).astype(jnp.int32)
    target = half * (ONE - HALF) + point * HALF + column
    row = lax.broadcasted_iota(jnp.int32, (POINTS * K, POINTS * K), 0)
    return jnp.where(row == target, 1.0, 0.0).astype(jnp.bfloat16)


def ordered(raw):
    return lax.dot_general(one_hot_order(), raw, (((1,), (1,)), ((), ())), preferred_element_type=jnp.float32)


def march_kernel(number, places, others, plan, blocks, positions, grow, raw, turn, coupling, weights, *refs):
    refs = list(refs)
    pieces = [refs.pop(0) for _ in places]
    raws = [refs.pop(0) for _ in range(raw)]
    givers = [refs.pop(0) for _ in others[0]]
    outs, (first, second, held, result, sems) = refs[:-5], refs[-5:]
    if not others[2]:
        result = outs[0]
    else:
        outs = [None] + outs
    states = [first, second]
    order = list(reversed(range(STATIONS)))
    side = turn[1]

    @pl.when(turn[0] == number)
    def _():
        copies = [
            pltpu.make_async_copy(weights.at[station], held.at[step], sems.at[step])
            for step, station in enumerate(order)
        ]
        copies[0].start()
        margin = 2 * HALF if grow else 0
        if margin:
            empty = jnp.zeros((blocks, margin, FN), jnp.float32)
            first[:, :margin, :] = empty
            first[:, margin + positions * HALF : 2 * margin + positions * HALF, :] = empty

        def total(on):
            covers = []
            if raw:
                turned = ordered(raws[0][...])
                for half in range(2):
                    covers.append((half, 0, ONE, lambda low, high, at=half * ONE: turned[at + low : at + high]))
            for piece, (where, rows, pick) in zip(pieces, places):
                block, start = where(on)
                if pick is not None:
                    covers.append((block, start, rows, lambda low, high, p=piece, k=pick(on): p[k, low:high, :]))
                elif len(piece.shape) == 3:
                    for k in range(blocks):
                        covers.append((k, start, rows, lambda low, high, p=piece, k=k: p[k, low:high, :]))
                else:
                    covers.append((block, start, rows, lambda low, high, p=piece: p[low:high, :]))
            for block in range(blocks):
                here = [cover for cover in covers if cover[0] == block]
                bounds = {0, positions * HALF}
                for _, start, rows, _ in here:
                    bounds |= {start, start + rows}
                bounds = sorted(bounds)
                for low, high in zip(bounds, bounds[1:]):
                    value = jnp.zeros((high - low, FN), jnp.float32)
                    for _, start, rows, read in here:
                        if start <= low and high <= start + rows:
                            value = value + read(low - start, high - start).astype(jnp.float32)
                    first[block, margin + low : margin + high, :] = value

        if pieces:
            for on in range(2):
                pl.when(side == on)(functools.partial(total, on))
        else:
            total(0)

        def stencil(step, chunk):
            block, begin, end = chunk
            at, rows = begin * HALF, (end - begin) * HALF
            source = states[step % 2]
            rates = coupling[order[step] : order[step] + 1, :]
            both = source[block, at : at + rows, :] + source[block, at + 2 * HALF : at + 2 * HALF + rows, :]
            update = (1.0 - 2.0 * rates) * source[block, at + HALF : at + HALF + rows, :] + rates * both
            return update.astype(jnp.bfloat16)

        copies[1].start()
        jobs = [(step, chunk) for step in range(STATIONS) for chunk in plan[step]]
        update = stencil(*jobs[0])
        for at_job, (step, chunk) in enumerate(jobs):
            block, begin, end = chunk
            at, rows = begin * HALF, (end - begin) * HALF
            current = update
            if at_job + 1 < len(jobs):
                update = stencil(*jobs[at_job + 1])
            if chunk is plan[step][0]:
                copies[step].wait()
                if step + 2 < STATIONS:
                    copies[step + 2].start()
            moved = lax.dot_general(
                current, held[step], (((1,), (1,)), ((), ())), preferred_element_type=jnp.float32
            )
            if step == STATIONS - 1:
                result[block, at : at + rows, :] = moved.astype(jnp.bfloat16)
                continue
            target = states[1 - step % 2]
            target[block, margin + at : margin + at + rows, :] = moved
            if grow:
                empty = jnp.zeros((margin, FN), jnp.float32)
                count = max(last for place, _, last in plan[step] if place == block)
                if begin == 0:
                    target[block, :margin, :] = empty
                if end == count:
                    target[block, margin + count * HALF : 2 * margin + count * HALF, :] = empty
        for out, where in zip(outs[1:], others[2]):
            start = pl.multiple_of(where(side), EDGE)
            out[...] = result[0, pl.ds(start, out.shape[0]), :]

    relay(others[1], turn, givers, outs[1:], sems)


def relay(owners, turn, givers, outs, sems):
    side = turn[1]
    for slot, value, moves in owners:

        @pl.when(turn[slot] == value)
        def _():
            copies = []
            for at, (giver, block, start, rows, out, to) in enumerate(moves):
                start = start(side)
                if not isinstance(start, int):
                    start = pl.multiple_of(start, EDGE)
                source = givers[giver].at[block(side), pl.ds(start, rows)]
                copies.append(pltpu.make_async_copy(source, outs[out].at[pl.ds(to, rows)], sems.at[at]))
            for copy in copies:
                copy.start()
            for copy in copies:
                copy.wait()


def march(turn, number, inverse_blocks, coupling, pieces, cut, blocks, positions, grow, raw=(), others=((), (), ())):
    last = positions + (2 * STATIONS if grow else -2 * STATIONS)
    most = last + 2 if grow else positions
    counts = [positions + (2 if grow else -2) * (step + 1) for step in range(STATIONS)]
    if blocks == 2:
        plan = [[(0, 0, count), (1, 0, count)] for count in counts]
    else:
        cuts = [cut - (0 if grow else 2 * step) for step in range(STATIONS)]
        plan = [[(0, 0, at), (0, at, count)] for at, count in zip(cuts, counts)]
    vmem = pl.BlockSpec(memory_space=pltpu.VMEM)
    away = pl.BlockSpec(memory_space=pl.ANY)
    whole = (blocks, last * HALF, FN)
    shapes = [jax.ShapeDtypeStruct(whole, jnp.bfloat16)]
    if others[2]:
        shapes = [jax.ShapeDtypeStruct((size, FN), jnp.bfloat16) for size in (2 * ONE, WIDE, WIDE, 2 * ONE)]
    values = [piece[0] for piece in pieces]
    return pl.pallas_call(
        functools.partial(
            march_kernel,
            number,
            [piece[1:] for piece in pieces],
            others,
            plan,
            blocks,
            positions,
            grow,
            len(raw),
        ),
        out_shape=shapes,
        in_specs=[pl.BlockSpec(memory_space=pltpu.SMEM), vmem, away]
        + [vmem] * (len(values) + len(raw))
        + [away] * len(others[0]),
        out_specs=[vmem] * len(shapes),
        scratch_shapes=[pltpu.VMEM((blocks, most * HALF, FN), jnp.float32)] * 2
        + [
            pltpu.VMEM((STATIONS, FN, FN), jnp.bfloat16),
            pltpu.VMEM(whole if others[2] else (1, 16, FN), jnp.bfloat16),
            pltpu.SemaphoreType.DMA((STATIONS,)),
        ],
        compiler_params=pltpu.CompilerParams(vmem_limit_bytes=GRANT),
        cost_estimate=pl.CostEstimate(
            flops=2 * blocks * HALF * sum(counts) * FN * FN,
            bytes_accessed=2 * STATIONS * FN * FN,
            transcendentals=0,
        ),
    )(turn, coupling, inverse_blocks, *values, *raw, *others[0])


def ship_kernel(
    number, turn, share, below, raw, crossed, edge_cross, edge_same, direct, whole, turned
):
    side, kind = turn[1], turn[2]

    def turn_over(source):
        rows = ordered(source[...])
        for half in range(2):
            turned[half, :, :] = rows[half * ONE : (half + 1) * ONE]

    @pl.when(turn[0] == number)
    def _():
        turn_over(below)
        whole[...] = share[...]
        middle = share[:, EDGE : EDGE + ONE, :].astype(jnp.float32) + turned[...]
        whole[:, EDGE : EDGE + ONE, :] = middle.astype(jnp.bfloat16)
        start = pl.multiple_of(side * ONE, ONE)
        edge_cross[...] = whole[1 - side, pl.ds(start, WIDE), :]
        edge_same[...] = whole[side, pl.ds(start, WIDE), :]
        crossed[...] = whole[1 - side]
        direct[...] = whole[side]

    @pl.when(kind >= 2)
    def _():
        turn_over(raw)
        whole[:, :ONE, :] = turned[...].astype(jnp.bfloat16)

    @pl.when(kind == 2)
    def _():
        crossed[:ONE, :] = whole[1 - side, :ONE, :]

    @pl.when(kind == 3)
    def _():
        for half in range(2):
            edge_cross[half * EDGE : (half + 1) * EDGE, :] = whole[half, ONE - EDGE : ONE, :]
            edge_same[half * EDGE : (half + 1) * EDGE, :] = whole[half, :EDGE, :]


def center_kernel(number, turn, direct, crossed, edge_same, edge_cross, out):
    @pl.when(turn[0] == number)
    def _():
        side = turn[1]
        start = pl.multiple_of(side * EDGE, EDGE)
        from_edge = pl.multiple_of((1 - side) * EDGE, EDGE)
        for block, share, edge in ((side, direct, edge_same), (1 - side, crossed, edge_cross)):
            out[block, :, :] = share[EDGE : EDGE + ONE, :]
            here = out[block, pl.ds(start, EDGE), :].astype(jnp.float32)
            more = edge[pl.ds(from_edge, EDGE), :].astype(jnp.float32)
            out[block, pl.ds(start, EDGE), :] = (here + more).astype(jnp.bfloat16)


def gram_kernel(numbers, turn, *refs):
    inputs, (rows, gram, edges, sems) = refs[: 7 * len(numbers)], refs[7 * len(numbers) :]
    side = turn[1]

    def fetch(*pairs):
        copies = [pltpu.make_async_copy(source, target, sems.at[at]) for at, (source, target) in enumerate(pairs)]
        for copy in copies:
            copy.start()
        for copy in copies:
            copy.wait()

    for at, number in enumerate(numbers):
        share, low, high, state, crossed, back, last = inputs[7 * at : 7 * at + 7]

        @pl.when(turn[0] == number)
        def _():
            halves = [slice(0, EDGE), slice(EDGE, 2 * EDGE)]
            fetch(
                *[(share.at[half, EDGE : EDGE + ONE], rows.at[half]) for half in range(2)],
                *[(low.at[halves[half]], edges.at[half, :EDGE]) for half in range(2)],
                *[(high.at[halves[half]], edges.at[half, EDGE:]) for half in range(2)],
            )
            rows[...] = (rows[...].astype(jnp.float32) + edges[...].astype(jnp.float32)).astype(jnp.bfloat16)

        @pl.when(turn[0] == number - 1)
        def _():
            start = pl.multiple_of(side * ONE, ONE)
            fetch((state.at[0, pl.ds(start, ONE)], rows.at[side]), (crossed.at[:ONE], rows.at[1 - side]))

        @pl.when(turn[0] == number - 2)
        def _():
            fetch((back, rows))

        @pl.when(turn[0] == number - 3)
        def _():
            fetch((last, rows))

    flat = rows[...].reshape(2 * ONE, FN)
    full = lax.dot_general(flat, flat, (((1,), (1,)), ((), ())), preferred_element_type=jnp.float32)
    lines = []
    for first in range(2):
        line = []
        for second in range(2):
            block = None
            for point in range(POINTS):
                down, along = first * ONE + point * HALF, second * ONE + point * HALF
                term = full[down : down + HALF, along : along + HALF]
                block = term if block is None else block + term
            line.append(block)
        lines.append(jnp.concatenate(line, 1))
    total = jnp.concatenate(lines, 0)
    gram[...] = total


def factor_kernel(scale, first, second, rows, by_column, by_place, same_point, basis, upper):
    eye = (
        lax.broadcasted_iota(jnp.int32, (K, K), 0) == lax.broadcasted_iota(jnp.int32, (K, K), 1)
    ).astype(jnp.float32)
    table = jnp.concatenate([(first[...] + second[...]) * scale, eye], 1)
    row_index = lax.broadcasted_iota(jnp.int32, (K, 2 * K), 0)
    roots = jnp.zeros((K, 2 * K), jnp.float32)
    for j in range(0, K, STEP):
        lines = [table[j + m : j + m + 1, :] for m in range(STEP)]
        columns = [jnp.broadcast_to(table[:, j + m : j + m + 1], table.shape) for m in range(STEP)]
        entries = [
            [jnp.broadcast_to(lines[m][:, j + k : j + k + 1], lines[m].shape) for k in range(STEP)]
            for m in range(STEP)
        ]
        below = table
        for m in range(STEP):
            inverse = 1.0 / entries[m][m]
            for k in range(m + 1, STEP):
                ratio = entries[m][k] * inverse
                for n in range(k, STEP):
                    entries[k][n] = entries[k][n] - ratio * entries[m][n]
                lines[k] = lines[k] - ratio * lines[m]
                columns[k] = columns[k] - ratio * columns[m]
            below = below - columns[m] * (inverse * lines[m])
            roots = jnp.where(row_index == j + m, lax.rsqrt(entries[m][m]), roots)
        table = jnp.where(row_index >= j + STEP, below, table)
        for m in range(STEP):
            table = jnp.where(row_index == j + m, lines[m], table)
    table = table * roots
    column = lax.broadcasted_iota(jnp.int32, (K, K), 1)
    row = lax.broadcasted_iota(jnp.int32, (K, K), 0)
    upper[...] = jnp.where(column >= row, table[:, :K], 0.0)
    inverse = table[:, K:]
    terms = []
    for _ in range(2):
        term = inverse.astype(jnp.bfloat16)
        inverse = inverse - term.astype(jnp.float32)
        tall = lax.dot_general(
            by_column[...], term, (((1,), (1,)), ((), ())), preferred_element_type=jnp.float32
        ).astype(jnp.bfloat16)
        spread = lax.dot_general(
            tall, by_place[...], (((1,), (0,)), ((), ())), preferred_element_type=jnp.float32
        )
        terms.append((spread * same_point[...]).astype(jnp.bfloat16))
    both = lax.dot_general(
        rows[...], jnp.concatenate(terms, 1), (((0,), (0,)), ((), ())), preferred_element_type=jnp.float32
    )
    total = both[:, : POINTS * K] + both[:, POINTS * K :]
    basis[...] = total.astype(jnp.bfloat16)


def local(inverse_blocks, coupling, sources):
    sections = lax.axis_size("section")
    spans = lax.axis_size("span")
    pairs = spans // 2
    assert sections % 4 == 0 and spans % 2 == 0 and sources.shape[2] == POINTS * K
    group = lax.axis_index("section")
    side = (lax.axis_index("span") % 2).astype(jnp.int32)

    def send(value, *legs):
        routes = []
        for groups, down, route in legs:
            for g in groups:
                for s in range(spans):
                    routes.append((g * spans + s, (g - down) % sections * spans + route(s)))
        return lax.ppermute(value, AXES, routes)

    def straight(s):
        return s

    def partner(s):
        return s ^ 1

    def neighbor(shift):
        return lambda s: (s + shift) % spans

    def pair_route(pair, side):
        return (pair % pairs) * 2 + side

    def outward(s):
        return pair_route(s // 2 + 2 * (s % 2) - 1, s % 2)

    def outward_cross(s):
        return pair_route(s // 2 + 2 * (s % 2) - 1, 1 - s % 2)

    def inward(s):
        return pair_route(s // 2 + 1 - 2 * (s % 2), s % 2)

    def of_kind(kind):
        return [g for g in range(sections) if (sections - 1 - g) % 4 == kind]

    turn = jnp.stack([group.astype(jnp.int32), side, ((sections - 1 - group) % 4).astype(jnp.int32)])

    half, point, column = np.meshgrid(np.arange(2), np.arange(POINTS), np.arange(HALF), indexing="ij")
    row_column = (half * HALF + column).reshape(-1)
    row_point = point.reshape(-1)
    place = np.arange(POINTS * K)
    by_column = jnp.asarray(np.arange(K)[None, :] == row_column[:, None], jnp.bfloat16)
    by_place = jnp.asarray(np.arange(K)[:, None] == place[None, :] % K, jnp.bfloat16)
    same_point = jnp.asarray(place[None, :] // K == row_point[:, None], jnp.float32)

    smem = pl.BlockSpec(memory_space=pltpu.SMEM)
    vmem = pl.BlockSpec(memory_space=pltpu.VMEM)
    away = pl.BlockSpec(memory_space=pl.ANY)
    raw = sources[0]
    odds, evens = list(range(1, sections, 2)), list(range(0, sections, 2))
    below = send(raw, (evens, -1, straight), (odds, 1, straight))
    incoming = None
    pair_source = wide_source = None
    candidates = []
    for g in reversed(of_kind(0)):
        pieces = [] if incoming is None else [(incoming, lambda side: (0, 0), ONE, None)]
        (share,) = march(turn, g, inverse_blocks, coupling, pieces, 0, 2, POINTS, True, (raw,))
        crossed, edge_cross, edge_same, direct, whole = pl.pallas_call(
            functools.partial(ship_kernel, g),
            out_shape=[jax.ShapeDtypeStruct((size, FN), jnp.bfloat16) for size in (2 * ONE, WIDE, WIDE, 2 * ONE)]
            + [jax.ShapeDtypeStruct(share.shape, jnp.bfloat16)],
            in_specs=[smem, vmem, vmem, vmem],
            out_specs=[vmem] * 5,
            scratch_shapes=[pltpu.VMEM((2, ONE, FN), jnp.float32)],
            compiler_params=pltpu.CompilerParams(vmem_limit_bytes=SMALL),
        )(turn, share, below, raw)
        first = incoming is None
        edge_cross = send(edge_cross, ([g], 1, outward_cross), (of_kind(3) if first else [], 0, neighbor(1)))
        crossed = send(crossed, ([g], 1, partner), (of_kind(2) if first else [], 0, partner))
        edge_same = send(edge_same, ([g], 1, outward), (of_kind(3) if first else [], 0, neighbor(-1)))
        direct = send(direct, ([g], 1, straight))
        if first:
            pair_source = [
                (whole, lambda side: (0, side * ONE), ONE, lambda side: side),
                (crossed, lambda side: (0, (1 - side) * ONE), ONE, None),
            ]
            wide_source = [
                (edge_cross.reshape(2, EDGE, FN), lambda side: (0, 0), EDGE, None),
                (whole, lambda side: (0, EDGE), ONE, None),
                (edge_same.reshape(2, EDGE, FN), lambda side: (0, EDGE + ONE), EDGE, None),
            ]

        (state,) = march(
            turn,
            g - 1,
            inverse_blocks,
            coupling,
            [
                (crossed, lambda side: (0, (1 - side) * ONE), 2 * ONE, None),
                (edge_cross, lambda side: (0, side * 2 * ONE), WIDE, None),
                (edge_same, lambda side: (0, (1 - side) * 2 * ONE), WIDE, None),
                (direct, lambda side: (0, side * ONE), 2 * ONE, None),
            ],
            14,
            1,
            3 * POINTS,
            False,
        )
        arrived = send(state, (list(range(sections)), 1, straight))

        crossed, edge_cross, edge_same, direct = march(
            turn,
            g - 2,
            inverse_blocks,
            coupling,
            [(arrived, lambda side: (0, 0), 2 * ONE, None)] + pair_source,
            10,
            1,
            2 * POINTS,
            True,
            (),
            (
                (share, state),
                (
                    (
                        0,
                        g,
                        (
                            (0, lambda side: 0, lambda side: EDGE + ONE, EDGE, 1, 0),
                            (0, lambda side: 1, lambda side: EDGE + ONE, EDGE, 1, EDGE),
                            (0, lambda side: 0, lambda side: 0, EDGE, 2, 0),
                            (0, lambda side: 1, lambda side: 0, EDGE, 2, EDGE),
                        ),
                    ),
                    (0, g - 1, ((1, lambda side: 0, lambda side: (1 - side) * ONE, ONE, 0, 0),)),
                ),
                (
                    lambda side: (1 - side) * ONE,
                    lambda side: side * 2 * ONE,
                    lambda side: (1 - side) * 2 * ONE,
                    lambda side: side * ONE,
                ),
            ),
        )
        edge_cross = send(edge_cross, ([g - 2], 1, outward_cross), ([g], 0, neighbor(1)))
        crossed = send(crossed, ([g - 2], 1, partner), ([g - 1], 0, partner))
        edge_same = send(edge_same, ([g - 2], 1, inward), ([g], 0, neighbor(-1)))
        direct = send(direct, ([g - 2], 1, straight))

        middle = pl.pallas_call(
            functools.partial(center_kernel, g - 3),
            out_shape=jax.ShapeDtypeStruct((2, ONE, FN), jnp.bfloat16),
            in_specs=[smem] + [vmem] * 4,
            out_specs=vmem,
            compiler_params=pltpu.CompilerParams(vmem_limit_bytes=SMALL),
        )(turn, direct, crossed, edge_same, edge_cross)
        back = send(middle, (evens, -1, straight), (odds, 1, straight))
        (last,) = march(
            turn,
            g - 3,
            inverse_blocks,
            coupling,
            [
                (crossed, lambda side: (1 - side, 0), 2 * ONE, None),
                (edge_cross, lambda side: (1 - side, side * ONE), WIDE, None),
                (edge_same, lambda side: (side, side * ONE), WIDE, None),
                (direct, lambda side: (side, 0), 2 * ONE, None),
            ]
            + wide_source,
            0,
            2,
            2 * POINTS,
            False,
        )
        candidates += [share, edge_cross, edge_same, state, crossed, back, last]
        if g > 3:
            incoming = send(last, ([g - 3], 1, straight))

    rows, gram = pl.pallas_call(
        functools.partial(gram_kernel, list(reversed(of_kind(0)))),
        out_shape=(
            jax.ShapeDtypeStruct((2, ONE, FN), jnp.bfloat16),
            jax.ShapeDtypeStruct((K, K), jnp.float32),
        ),
        in_specs=[smem] + [away] * len(candidates),
        out_specs=(vmem, vmem),
        scratch_shapes=[pltpu.VMEM((2, ONE, FN), jnp.bfloat16), pltpu.SemaphoreType.DMA((6,))],
        compiler_params=pltpu.CompilerParams(vmem_limit_bytes=SMALL),
    )(turn, *candidates)
    stride = 1
    terms = [gram]
    while stride < spans:
        radix = 2 if stride == 1 else min(4, spans // stride)
        total = terms[0]
        for term in terms[1:]:
            total = total + term
        terms = [total] + [
            lax.ppermute(total, "span", [(s, s ^ (digit * stride)) for s in range(spans)])
            for digit in range(1, radix)
        ]
        if radix == 4:
            terms = [terms[0] + terms[1], terms[2] + terms[3]]
        stride *= radix

    basis, upper = pl.pallas_call(
        functools.partial(factor_kernel, 1.0 / float(FN * POINTS * spans)),
        out_shape=(
            jax.ShapeDtypeStruct((FN, POINTS * K), jnp.bfloat16),
            jax.ShapeDtypeStruct((K, K), jnp.float32),
        ),
        in_specs=[vmem] * 6,
        out_specs=(vmem, vmem),
        compiler_params=pltpu.CompilerParams(vmem_limit_bytes=SMALL),
    )(*terms, rows.reshape(POINTS * K, FN), by_column, by_place, same_point)
    return (basis[None], upper[None])


def solution(mesh):
    placed = (P("section", None, None), P("section", None), P("section", None, "span"))
    return jax.shard_map(
        local,
        mesh=mesh,
        in_specs=placed,
        out_specs=(P("section", None, "span"), P("section", None, None)),
        check_vma=False,
    )
```

```python
import functools

import jax
import jax.numpy as jnp
import numpy as np
from jax import lax
from jax.experimental import pallas as pl
from jax.experimental.pallas import tpu as pltpu
from jax.sharding import PartitionSpec as P

K = 48
STATIONS = 4
FN = 768
HALF = K // 2
POINTS = 8
ONE = POINTS * HALF
EDGE = STATIONS * HALF
WIDE = 2 * EDGE
STEP = 6
GRANT = 48 * 1024 * 1024
SMALL = 16 * 1024 * 1024
AXES = ("section", "span")


def one_hot_order():
    at = lax.broadcasted_iota(jnp.int32, (1, POINTS * K), 1)
    point = at * 1366 >> 16
    column = at - point * K
    half = (column >= HALF).astype(jnp.int32)
    target = half * (ONE - HALF) + point * HALF + column
    row = lax.broadcasted_iota(jnp.int32, (POINTS * K, POINTS * K), 0)
    return jnp.where(row == target, 1.0, 0.0).astype(jnp.bfloat16)


def ordered(raw):
    return lax.dot_general(one_hot_order(), raw, (((1,), (1,)), ((), ())), preferred_element_type=jnp.float32)


def march_kernel(number, places, others, plan, blocks, positions, grow, raw, turn, coupling, weights, *refs):
    refs = list(refs)
    pieces = [refs.pop(0) for _ in places]
    raws = [refs.pop(0) for _ in range(raw)]
    givers = [refs.pop(0) for _ in others[0]]
    outs, (first, second, held, result, sems) = refs[:-5], refs[-5:]
    if not others[2]:
        result = outs[0]
    else:
        outs = [None] + outs
    states = [first, second]
    order = list(reversed(range(STATIONS)))
    side = turn[1]

    @pl.when(turn[0] == number)
    def _():
        copies = [
            pltpu.make_async_copy(weights.at[station], held.at[step], sems.at[step])
            for step, station in enumerate(order)
        ]
        copies[0].start()
        margin = 2 * HALF if grow else 0
        if margin:
            empty = jnp.zeros((blocks, margin, FN), jnp.float32)
            first[:, :margin, :] = empty
            first[:, margin + positions * HALF : 2 * margin + positions * HALF, :] = empty

        def total(on):
            covers = []
            if raw:
                turned = ordered(raws[0][...])
                for half in range(2):
                    covers.append((half, 0, ONE, lambda low, high, at=half * ONE: turned[at + low : at + high]))
            for piece, (where, rows, pick) in zip(pieces, places):
                block, start = where(on)
                if pick is not None:
                    covers.append((block, start, rows, lambda low, high, p=piece, k=pick(on): p[k, low:high, :]))
                elif len(piece.shape) == 3:
                    for k in range(blocks):
                        covers.append((k, start, rows, lambda low, high, p=piece, k=k: p[k, low:high, :]))
                else:
                    covers.append((block, start, rows, lambda low, high, p=piece: p[low:high, :]))
            for block in range(blocks):
                here = [cover for cover in covers if cover[0] == block]
                bounds = {0, positions * HALF}
                for _, start, rows, _ in here:
                    bounds |= {start, start + rows}
                bounds = sorted(bounds)
                for low, high in zip(bounds, bounds[1:]):
                    value = jnp.zeros((high - low, FN), jnp.float32)
                    for _, start, rows, read in here:
                        if start <= low and high <= start + rows:
                            value = value + read(low - start, high - start).astype(jnp.float32)
                    first[block, margin + low : margin + high, :] = value

        if pieces:
            for on in range(2):
                pl.when(side == on)(functools.partial(total, on))
        else:
            total(0)

        def stencil(step, chunk):
            block, begin, end = chunk
            at, rows = begin * HALF, (end - begin) * HALF
            source = states[step % 2]
            rates = coupling[order[step] : order[step] + 1, :]
            both = source[block, at : at + rows, :] + source[block, at + 2 * HALF : at + 2 * HALF + rows, :]
            update = (1.0 - 2.0 * rates) * source[block, at + HALF : at + HALF + rows, :] + rates * both
            return update.astype(jnp.bfloat16)

        copies[1].start()
        jobs = [(step, chunk) for step in range(STATIONS) for chunk in plan[step]]
        update = stencil(*jobs[0])
        for at_job, (step, chunk) in enumerate(jobs):
            block, begin, end = chunk
            at, rows = begin * HALF, (end - begin) * HALF
            current = update
            if at_job + 1 < len(jobs):
                update = stencil(*jobs[at_job + 1])
            if chunk is plan[step][0]:
                copies[step].wait()
                if step + 2 < STATIONS:
                    copies[step + 2].start()
            moved = lax.dot_general(
                current,
                held[step],
                (((1,), (1 if raw else 0,)), ((), ())),
                preferred_element_type=jnp.float32,
            )
            if step == STATIONS - 1:
                result[block, at : at + rows, :] = moved.astype(jnp.bfloat16)
                continue
            target = states[1 - step % 2]
            target[block, margin + at : margin + at + rows, :] = moved
            if grow:
                empty = jnp.zeros((margin, FN), jnp.float32)
                count = max(last for place, _, last in plan[step] if place == block)
                if begin == 0:
                    target[block, :margin, :] = empty
                if end == count:
                    target[block, margin + count * HALF : 2 * margin + count * HALF, :] = empty
        for out, where in zip(outs[1:], others[2]):
            start = pl.multiple_of(where(side), EDGE)
            out[...] = result[0, pl.ds(start, out.shape[0]), :]

    relay(others[1], turn, givers, outs[1:], sems)


def relay(owners, turn, givers, outs, sems):
    side = turn[1]
    for slot, value, moves in owners:

        @pl.when(turn[slot] == value)
        def _():
            copies = []
            for at, (giver, block, start, rows, out, to) in enumerate(moves):
                start = start(side)
                if not isinstance(start, int):
                    start = pl.multiple_of(start, EDGE)
                source = givers[giver].at[block(side), pl.ds(start, rows)]
                copies.append(pltpu.make_async_copy(source, outs[out].at[pl.ds(to, rows)], sems.at[at]))
            for copy in copies:
                copy.start()
            for copy in copies:
                copy.wait()


def march(turn, number, inverse_blocks, coupling, pieces, cut, blocks, positions, grow, raw=(), others=((), (), ())):
    last = positions + (2 * STATIONS if grow else -2 * STATIONS)
    most = last + 2 if grow else positions
    counts = [positions + (2 if grow else -2) * (step + 1) for step in range(STATIONS)]
    if blocks == 2:
        plan = [[(0, 0, count), (1, 0, count)] for count in counts]
    else:
        cuts = [cut - (0 if grow else 2 * step) for step in range(STATIONS)]
        plan = [[(0, 0, at), (0, at, count)] for at, count in zip(cuts, counts)]
    vmem = pl.BlockSpec(memory_space=pltpu.VMEM)
    away = pl.BlockSpec(memory_space=pl.ANY)
    whole = (blocks, last * HALF, FN)
    shapes = [jax.ShapeDtypeStruct(whole, jnp.bfloat16)]
    if others[2]:
        shapes = [jax.ShapeDtypeStruct((size, FN), jnp.bfloat16) for size in (2 * ONE, WIDE, WIDE, 2 * ONE)]
    values = [piece[0] for piece in pieces]
    return pl.pallas_call(
        functools.partial(
            march_kernel,
            number,
            [piece[1:] for piece in pieces],
            others,
            plan,
            blocks,
            positions,
            grow,
            len(raw),
        ),
        out_shape=shapes,
        in_specs=[pl.BlockSpec(memory_space=pltpu.SMEM), vmem, away]
        + [vmem] * (len(values) + len(raw))
        + [away] * len(others[0]),
        out_specs=[vmem] * len(shapes),
        scratch_shapes=[pltpu.VMEM((blocks, most * HALF, FN), jnp.float32)] * 2
        + [
            pltpu.VMEM((STATIONS, FN, FN), jnp.bfloat16),
            pltpu.VMEM(whole if others[2] else (1, 16, FN), jnp.bfloat16),
            pltpu.SemaphoreType.DMA((STATIONS,)),
        ],
        compiler_params=pltpu.CompilerParams(vmem_limit_bytes=GRANT),
        cost_estimate=pl.CostEstimate(
            flops=2 * blocks * HALF * sum(counts) * FN * FN,
            bytes_accessed=2 * STATIONS * FN * FN,
            transcendentals=0,
        ),
    )(turn, coupling, inverse_blocks, *values, *raw, *others[0])


def ship_kernel(
    number, turn, share, below, raw, crossed, edge_cross, edge_same, direct, whole, turned
):
    side, kind = turn[1], turn[2]

    def turn_over(source):
        rows = ordered(source[...])
        for half in range(2):
            turned[half, :, :] = rows[half * ONE : (half + 1) * ONE]

    @pl.when(turn[0] == number)
    def _():
        turn_over(below)
        whole[...] = share[...]
        middle = share[:, EDGE : EDGE + ONE, :].astype(jnp.float32) + turned[...]
        whole[:, EDGE : EDGE + ONE, :] = middle.astype(jnp.bfloat16)
        start = pl.multiple_of(side * ONE, ONE)
        edge_cross[...] = whole[1 - side, pl.ds(start, WIDE), :]
        edge_same[...] = whole[side, pl.ds(start, WIDE), :]
        crossed[...] = whole[1 - side]
        direct[...] = whole[side]

    @pl.when(kind >= 2)
    def _():
        turn_over(raw)
        whole[:, :ONE, :] = turned[...].astype(jnp.bfloat16)

    @pl.when(kind == 2)
    def _():
        crossed[:ONE, :] = whole[1 - side, :ONE, :]

    @pl.when(kind == 3)
    def _():
        for half in range(2):
            edge_cross[half * EDGE : (half + 1) * EDGE, :] = whole[half, ONE - EDGE : ONE, :]
            edge_same[half * EDGE : (half + 1) * EDGE, :] = whole[half, :EDGE, :]


def center_kernel(number, turn, direct, crossed, edge_same, edge_cross, out):
    @pl.when(turn[0] == number)
    def _():
        side = turn[1]
        start = pl.multiple_of(side * EDGE, EDGE)
        from_edge = pl.multiple_of((1 - side) * EDGE, EDGE)
        for block, share, edge in ((side, direct, edge_same), (1 - side, crossed, edge_cross)):
            out[block, :, :] = share[EDGE : EDGE + ONE, :]
            here = out[block, pl.ds(start, EDGE), :].astype(jnp.float32)
            more = edge[pl.ds(from_edge, EDGE), :].astype(jnp.float32)
            out[block, pl.ds(start, EDGE), :] = (here + more).astype(jnp.bfloat16)


def gram_kernel(numbers, turn, *refs):
    inputs, (rows, gram, edges, sems) = refs[: 7 * len(numbers)], refs[7 * len(numbers) :]
    side = turn[1]

    def fetch(*pairs):
        copies = [pltpu.make_async_copy(source, target, sems.at[at]) for at, (source, target) in enumerate(pairs)]
        for copy in copies:
            copy.start()
        for copy in copies:
            copy.wait()

    for at, number in enumerate(numbers):
        share, low, high, state, crossed, back, last = inputs[7 * at : 7 * at + 7]

        @pl.when(turn[0] == number)
        def _():
            halves = [slice(0, EDGE), slice(EDGE, 2 * EDGE)]
            fetch(
                *[(share.at[half, EDGE : EDGE + ONE], rows.at[half]) for half in range(2)],
                *[(low.at[halves[half]], edges.at[half, :EDGE]) for half in range(2)],
                *[(high.at[halves[half]], edges.at[half, EDGE:]) for half in range(2)],
            )
            rows[...] = (rows[...].astype(jnp.float32) + edges[...].astype(jnp.float32)).astype(jnp.bfloat16)

        @pl.when(turn[0] == number - 1)
        def _():
            start = pl.multiple_of(side * ONE, ONE)
            fetch((state.at[0, pl.ds(start, ONE)], rows.at[side]), (crossed.at[:ONE], rows.at[1 - side]))

        @pl.when(turn[0] == number - 2)
        def _():
            fetch((back, rows))

        @pl.when(turn[0] == number - 3)
        def _():
            fetch((last, rows))

    flat = rows[...].reshape(2 * ONE, FN)
    full = lax.dot_general(flat, flat, (((1,), (1,)), ((), ())), preferred_element_type=jnp.float32)
    lines = []
    for first in range(2):
        line = []
        for second in range(2):
            block = None
            for point in range(POINTS):
                down, along = first * ONE + point * HALF, second * ONE + point * HALF
                term = full[down : down + HALF, along : along + HALF]
                block = term if block is None else block + term
            line.append(block)
        lines.append(jnp.concatenate(line, 1))
    total = jnp.concatenate(lines, 0)
    gram[...] = total


def factor_kernel(scale, first, second, rows, by_column, by_place, same_point, basis, upper):
    eye = (
        lax.broadcasted_iota(jnp.int32, (K, K), 0) == lax.broadcasted_iota(jnp.int32, (K, K), 1)
    ).astype(jnp.float32)
    table = jnp.concatenate([(first[...] + second[...]) * scale, eye], 1)
    row_index = lax.broadcasted_iota(jnp.int32, (K, 2 * K), 0)
    roots = jnp.zeros((K, 2 * K), jnp.float32)
    for j in range(0, K, STEP):
        lines = [table[j + m : j + m + 1, :] for m in range(STEP)]
        columns = [jnp.broadcast_to(table[:, j + m : j + m + 1], table.shape) for m in range(STEP)]
        entries = [
            [jnp.broadcast_to(lines[m][:, j + k : j + k + 1], lines[m].shape) for k in range(STEP)]
            for m in range(STEP)
        ]
        below = table
        for m in range(STEP):
            inverse = 1.0 / entries[m][m]
            for k in range(m + 1, STEP):
                ratio = entries[m][k] * inverse
                for n in range(k, STEP):
                    entries[k][n] = entries[k][n] - ratio * entries[m][n]
                lines[k] = lines[k] - ratio * lines[m]
                columns[k] = columns[k] - ratio * columns[m]
            below = below - columns[m] * (inverse * lines[m])
            roots = jnp.where(row_index == j + m, lax.rsqrt(entries[m][m]), roots)
        table = jnp.where(row_index >= j + STEP, below, table)
        for m in range(STEP):
            table = jnp.where(row_index == j + m, lines[m], table)
    table = table * roots
    column = lax.broadcasted_iota(jnp.int32, (K, K), 1)
    row = lax.broadcasted_iota(jnp.int32, (K, K), 0)
    upper[...] = jnp.where(column >= row, table[:, :K], 0.0)
    inverse = table[:, K:]
    terms = []
    for _ in range(2):
        term = inverse.astype(jnp.bfloat16)
        inverse = inverse - term.astype(jnp.float32)
        tall = lax.dot_general(
            by_column[...], term, (((1,), (1,)), ((), ())), preferred_element_type=jnp.float32
        ).astype(jnp.bfloat16)
        spread = lax.dot_general(
            tall, by_place[...], (((1,), (0,)), ((), ())), preferred_element_type=jnp.float32
        )
        terms.append((spread * same_point[...]).astype(jnp.bfloat16))
    both = lax.dot_general(
        rows[...], jnp.concatenate(terms, 1), (((0,), (0,)), ((), ())), preferred_element_type=jnp.float32
    )
    total = both[:, : POINTS * K] + both[:, POINTS * K :]
    basis[...] = total.astype(jnp.bfloat16)


def local(inverse_blocks, coupling, sources):
    sections = lax.axis_size("section")
    spans = lax.axis_size("span")
    pairs = spans // 2
    assert sections % 4 == 0 and spans % 2 == 0 and sources.shape[2] == POINTS * K
    group = lax.axis_index("section")
    side = (lax.axis_index("span") % 2).astype(jnp.int32)

    def send(value, *legs):
        routes = []
        for groups, down, route in legs:
            for g in groups:
                for s in range(spans):
                    routes.append((g * spans + s, (g - down) % sections * spans + route(s)))
        return lax.ppermute(value, AXES, routes)

    def straight(s):
        return s

    def partner(s):
        return s ^ 1

    def neighbor(shift):
        return lambda s: (s + shift) % spans

    def pair_route(pair, side):
        return (pair % pairs) * 2 + side

    def outward(s):
        return pair_route(s // 2 + 2 * (s % 2) - 1, s % 2)

    def outward_cross(s):
        return pair_route(s // 2 + 2 * (s % 2) - 1, 1 - s % 2)

    def inward(s):
        return pair_route(s // 2 + 1 - 2 * (s % 2), s % 2)

    def of_kind(kind):
        return [g for g in range(sections) if (sections - 1 - g) % 4 == kind]

    turn = jnp.stack([group.astype(jnp.int32), side, ((sections - 1 - group) % 4).astype(jnp.int32)])

    half, point, column = np.meshgrid(np.arange(2), np.arange(POINTS), np.arange(HALF), indexing="ij")
    row_column = (half * HALF + column).reshape(-1)
    row_point = point.reshape(-1)
    place = np.arange(POINTS * K)
    by_column = jnp.asarray(np.arange(K)[None, :] == row_column[:, None], jnp.bfloat16)
    by_place = jnp.asarray(np.arange(K)[:, None] == place[None, :] % K, jnp.bfloat16)
    same_point = jnp.asarray(place[None, :] // K == row_point[:, None], jnp.float32)

    smem = pl.BlockSpec(memory_space=pltpu.SMEM)
    vmem = pl.BlockSpec(memory_space=pltpu.VMEM)
    away = pl.BlockSpec(memory_space=pl.ANY)
    raw = sources[0]
    odds, evens = list(range(1, sections, 2)), list(range(0, sections, 2))
    below = send(raw, (evens, -1, straight), (odds, 1, straight))
    incoming = None
    pair_source = wide_source = turned_blocks = None
    candidates = []
    for g in reversed(of_kind(0)):
        pieces = [] if incoming is None else [(incoming, lambda side: (0, 0), ONE, None)]
        (share,) = march(turn, g, inverse_blocks, coupling, pieces, 0, 2, POINTS, True, (raw,))
        crossed, edge_cross, edge_same, direct, whole = pl.pallas_call(
            functools.partial(ship_kernel, g),
            out_shape=[jax.ShapeDtypeStruct((size, FN), jnp.bfloat16) for size in (2 * ONE, WIDE, WIDE, 2 * ONE)]
            + [jax.ShapeDtypeStruct(share.shape, jnp.bfloat16)],
            in_specs=[smem, vmem, vmem, vmem],
            out_specs=[vmem] * 5,
            scratch_shapes=[pltpu.VMEM((2, ONE, FN), jnp.float32)],
            compiler_params=pltpu.CompilerParams(vmem_limit_bytes=SMALL),
        )(turn, share, below, raw)
        first = incoming is None
        edge_cross = send(edge_cross, ([g], 1, outward_cross), (of_kind(3) if first else [], 0, neighbor(1)))
        crossed = send(crossed, ([g], 1, partner), (of_kind(2) if first else [], 0, partner))
        edge_same = send(edge_same, ([g], 1, outward), (of_kind(3) if first else [], 0, neighbor(-1)))
        direct = send(direct, ([g], 1, straight))
        if first:
            later, _ = lax.optimization_barrier((inverse_blocks, whole))
            turned_blocks = jnp.swapaxes(later, 1, 2)
            pair_source = [
                (whole, lambda side: (0, side * ONE), ONE, lambda side: side),
                (crossed, lambda side: (0, (1 - side) * ONE), ONE, None),
            ]
            wide_source = [
                (edge_cross.reshape(2, EDGE, FN), lambda side: (0, 0), EDGE, None),
                (whole, lambda side: (0, EDGE), ONE, None),
                (edge_same.reshape(2, EDGE, FN), lambda side: (0, EDGE + ONE), EDGE, None),
            ]

        (state,) = march(
            turn,
            g - 1,
            turned_blocks,
            coupling,
            [
                (crossed, lambda side: (0, (1 - side) * ONE), 2 * ONE, None),
                (edge_cross, lambda side: (0, side * 2 * ONE), WIDE, None),
                (edge_same, lambda side: (0, (1 - side) * 2 * ONE), WIDE, None),
                (direct, lambda side: (0, side * ONE), 2 * ONE, None),
            ],
            14,
            1,
            3 * POINTS,
            False,
        )
        arrived = send(state, (list(range(sections)), 1, straight))

        crossed, edge_cross, edge_same, direct = march(
            turn,
            g - 2,
            turned_blocks,
            coupling,
            [(arrived, lambda side: (0, 0), 2 * ONE, None)] + pair_source,
            10,
            1,
            2 * POINTS,
            True,
            (),
            (
                (share, state),
                (
                    (
                        0,
                        g,
                        (
                            (0, lambda side: 0, lambda side: EDGE + ONE, EDGE, 1, 0),
                            (0, lambda side: 1, lambda side: EDGE + ONE, EDGE, 1, EDGE),
                            (0, lambda side: 0, lambda side: 0, EDGE, 2, 0),
                            (0, lambda side: 1, lambda side: 0, EDGE, 2, EDGE),
                        ),
                    ),
                    (0, g - 1, ((1, lambda side: 0, lambda side: (1 - side) * ONE, ONE, 0, 0),)),
                ),
                (
                    lambda side: (1 - side) * ONE,
                    lambda side: side * 2 * ONE,
                    lambda side: (1 - side) * 2 * ONE,
                    lambda side: side * ONE,
                ),
            ),
        )
        edge_cross = send(edge_cross, ([g - 2], 1, outward_cross), ([g], 0, neighbor(1)))
        crossed = send(crossed, ([g - 2], 1, partner), ([g - 1], 0, partner))
        edge_same = send(edge_same, ([g - 2], 1, inward), ([g], 0, neighbor(-1)))
        direct = send(direct, ([g - 2], 1, straight))

        middle = pl.pallas_call(
            functools.partial(center_kernel, g - 3),
            out_shape=jax.ShapeDtypeStruct((2, ONE, FN), jnp.bfloat16),
            in_specs=[smem] + [vmem] * 4,
            out_specs=vmem,
            compiler_params=pltpu.CompilerParams(vmem_limit_bytes=SMALL),
        )(turn, direct, crossed, edge_same, edge_cross)
        back = send(middle, (evens, -1, straight), (odds, 1, straight))
        (last,) = march(
            turn,
            g - 3,
            turned_blocks,
            coupling,
            [
                (crossed, lambda side: (1 - side, 0), 2 * ONE, None),
                (edge_cross, lambda side: (1 - side, side * ONE), WIDE, None),
                (edge_same, lambda side: (side, side * ONE), WIDE, None),
                (direct, lambda side: (side, 0), 2 * ONE, None),
            ]
            + wide_source,
            0,
            2,
            2 * POINTS,
            False,
        )
        candidates += [share, edge_cross, edge_same, state, crossed, back, last]
        if g > 3:
            incoming = send(last, ([g - 3], 1, straight))

    rows, gram = pl.pallas_call(
        functools.partial(gram_kernel, list(reversed(of_kind(0)))),
        out_shape=(
            jax.ShapeDtypeStruct((2, ONE, FN), jnp.bfloat16),
            jax.ShapeDtypeStruct((K, K), jnp.float32),
        ),
        in_specs=[smem] + [away] * len(candidates),
        out_specs=(vmem, vmem),
        scratch_shapes=[pltpu.VMEM((2, ONE, FN), jnp.bfloat16), pltpu.SemaphoreType.DMA((6,))],
        compiler_params=pltpu.CompilerParams(vmem_limit_bytes=SMALL),
    )(turn, *candidates)
    stride = 1
    terms = [gram]
    while stride < spans:
        radix = 2 if stride == 1 else min(4, spans // stride)
        total = terms[0]
        for term in terms[1:]:
            total = total + term
        terms = [total] + [
            lax.ppermute(total, "span", [(s, s ^ (digit * stride)) for s in range(spans)])
            for digit in range(1, radix)
        ]
        if radix == 4:
            terms = [terms[0] + terms[1], terms[2] + terms[3]]
        stride *= radix

    basis, upper = pl.pallas_call(
        functools.partial(factor_kernel, 1.0 / float(FN * POINTS * spans)),
        out_shape=(
            jax.ShapeDtypeStruct((FN, POINTS * K), jnp.bfloat16),
            jax.ShapeDtypeStruct((K, K), jnp.float32),
        ),
        in_specs=[vmem] * 6,
        out_specs=(vmem, vmem),
        compiler_params=pltpu.CompilerParams(vmem_limit_bytes=SMALL),
    )(*terms, rows.reshape(POINTS * K, FN), by_column, by_place, same_point)
    return (basis[None], upper[None])


def solution(mesh):
    placed = (P("section", None, None), P("section", None), P("section", None, "span"))
    return jax.shard_map(
        local,
        mesh=mesh,
        in_specs=placed,
        out_specs=(P("section", None, "span"), P("section", None, None)),
        check_vma=False,
    )
```

```python
import functools

import jax
import jax.numpy as jnp
import numpy as np
from jax import lax
from jax.experimental import pallas as pl
from jax.experimental.pallas import tpu as pltpu
from jax.sharding import PartitionSpec as P

K = 48
STATIONS = 4
FN = 768
HALF = K // 2
POINTS = 8
ONE = POINTS * HALF
EDGE = STATIONS * HALF
WIDE = 2 * EDGE
STEP = 6
GRANT = 48 * 1024 * 1024
SMALL = 16 * 1024 * 1024
AXES = ("section", "span")


def one_hot_order():
    at = lax.broadcasted_iota(jnp.int32, (1, POINTS * K), 1)
    point = at * 1366 >> 16
    column = at - point * K
    half = (column >= HALF).astype(jnp.int32)
    target = half * (ONE - HALF) + point * HALF + column
    row = lax.broadcasted_iota(jnp.int32, (POINTS * K, POINTS * K), 0)
    return jnp.where(row == target, 1.0, 0.0).astype(jnp.bfloat16)


def ordered(raw):
    return lax.dot_general(one_hot_order(), raw, (((1,), (1,)), ((), ())), preferred_element_type=jnp.float32)


def march_kernel(number, places, others, plan, blocks, positions, grow, raw, turn, coupling, weights, *refs):
    refs = list(refs)
    pieces = [refs.pop(0) for _ in places]
    raws = [refs.pop(0) for _ in range(raw)]
    givers = [refs.pop(0) for _ in others[0]]
    outs, (first, second, held, result, sems) = refs[:-5], refs[-5:]
    if not others[2]:
        result = outs[0]
    else:
        outs = [None] + outs
    states = [first, second]
    order = list(reversed(range(STATIONS)))
    side = turn[1]

    @pl.when(turn[0] == number)
    def _():
        copies = [
            pltpu.make_async_copy(weights.at[station], held.at[step], sems.at[step])
            for step, station in enumerate(order)
        ]
        copies[0].start()
        margin = 2 * HALF if grow else 0
        if margin:
            empty = jnp.zeros((blocks, margin, FN), jnp.float32)
            first[:, :margin, :] = empty
            first[:, margin + positions * HALF : 2 * margin + positions * HALF, :] = empty

        def total(on):
            covers = []
            if raw:
                turned = ordered(raws[0][...])
                for half in range(2):
                    covers.append((half, 0, ONE, lambda low, high, at=half * ONE: turned[at + low : at + high]))
            for piece, (where, rows, pick) in zip(pieces, places):
                block, start = where(on)
                if pick is not None:
                    covers.append((block, start, rows, lambda low, high, p=piece, k=pick(on): p[k, low:high, :]))
                elif len(piece.shape) == 3:
                    for k in range(blocks):
                        covers.append((k, start, rows, lambda low, high, p=piece, k=k: p[k, low:high, :]))
                else:
                    covers.append((block, start, rows, lambda low, high, p=piece: p[low:high, :]))
            for block in range(blocks):
                here = [cover for cover in covers if cover[0] == block]
                bounds = {0, positions * HALF}
                for _, start, rows, _ in here:
                    bounds |= {start, start + rows}
                bounds = sorted(bounds)
                for low, high in zip(bounds, bounds[1:]):
                    value = jnp.zeros((high - low, FN), jnp.float32)
                    for _, start, rows, read in here:
                        if start <= low and high <= start + rows:
                            value = value + read(low - start, high - start).astype(jnp.float32)
                    first[block, margin + low : margin + high, :] = value

        if pieces:
            for on in range(2):
                pl.when(side == on)(functools.partial(total, on))
        else:
            total(0)

        def stencil(step, chunk):
            block, begin, end = chunk
            at, rows = begin * HALF, (end - begin) * HALF
            source = states[step % 2]
            rates = coupling[order[step] : order[step] + 1, :]
            both = source[block, at : at + rows, :] + source[block, at + 2 * HALF : at + 2 * HALF + rows, :]
            update = (1.0 - 2.0 * rates) * source[block, at + HALF : at + HALF + rows, :] + rates * both
            return update.astype(jnp.bfloat16)

        copies[1].start()
        jobs = [(step, chunk) for step in range(STATIONS) for chunk in plan[step]]
        update = stencil(*jobs[0])
        for at_job, (step, chunk) in enumerate(jobs):
            block, begin, end = chunk
            at, rows = begin * HALF, (end - begin) * HALF
            current = update
            if at_job + 1 < len(jobs):
                update = stencil(*jobs[at_job + 1])
            if chunk is plan[step][0]:
                copies[step].wait()
                if step + 2 < STATIONS:
                    copies[step + 2].start()
            moved = lax.dot_general(
                current, held[step], (((1,), (1,)), ((), ())), preferred_element_type=jnp.float32
            )
            if step == STATIONS - 1:
                result[block, at : at + rows, :] = moved.astype(jnp.bfloat16)
                continue
            target = states[1 - step % 2]
            target[block, margin + at : margin + at + rows, :] = moved
            if grow:
                empty = jnp.zeros((margin, FN), jnp.float32)
                count = max(last for place, _, last in plan[step] if place == block)
                if begin == 0:
                    target[block, :margin, :] = empty
                if end == count:
                    target[block, margin + count * HALF : 2 * margin + count * HALF, :] = empty
        for out, where in zip(outs[1:], others[2]):
            start = pl.multiple_of(where(side), EDGE)
            out[...] = result[0, pl.ds(start, out.shape[0]), :]

    relay(others[1], turn, givers, outs[1:], sems)


def relay(owners, turn, givers, outs, sems):
    side = turn[1]
    for slot, value, moves in owners:

        @pl.when(turn[slot] == value)
        def _():
            copies = []
            for at, (giver, block, start, rows, out, to) in enumerate(moves):
                start = start(side)
                if not isinstance(start, int):
                    start = pl.multiple_of(start, EDGE)
                source = givers[giver].at[block(side), pl.ds(start, rows)]
                copies.append(pltpu.make_async_copy(source, outs[out].at[pl.ds(to, rows)], sems.at[at]))
            for copy in copies:
                copy.start()
            for copy in copies:
                copy.wait()


def march(turn, number, inverse_blocks, coupling, pieces, cut, blocks, positions, grow, raw=(), others=((), (), ())):
    last = positions + (2 * STATIONS if grow else -2 * STATIONS)
    most = last + 2 if grow else positions
    counts = [positions + (2 if grow else -2) * (step + 1) for step in range(STATIONS)]
    if blocks == 2:
        plan = [[(0, 0, count), (1, 0, count)] for count in counts]
    else:
        cuts = [cut - (0 if grow else 2 * step) for step in range(STATIONS)]
        plan = [[(0, 0, at), (0, at, count)] for at, count in zip(cuts, counts)]
    vmem = pl.BlockSpec(memory_space=pltpu.VMEM)
    away = pl.BlockSpec(memory_space=pl.ANY)
    whole = (blocks, last * HALF, FN)
    shapes = [jax.ShapeDtypeStruct(whole, jnp.bfloat16)]
    if others[2]:
        shapes = [jax.ShapeDtypeStruct((size, FN), jnp.bfloat16) for size in (2 * ONE, WIDE, WIDE, 2 * ONE)]
    values = [piece[0] for piece in pieces]
    return pl.pallas_call(
        functools.partial(
            march_kernel,
            number,
            [piece[1:] for piece in pieces],
            others,
            plan,
            blocks,
            positions,
            grow,
            len(raw),
        ),
        out_shape=shapes,
        in_specs=[pl.BlockSpec(memory_space=pltpu.SMEM), vmem, away]
        + [vmem] * (len(values) + len(raw))
        + [away] * len(others[0]),
        out_specs=[vmem] * len(shapes),
        scratch_shapes=[pltpu.VMEM((blocks, most * HALF, FN), jnp.float32)] * 2
        + [
            pltpu.VMEM((STATIONS, FN, FN), jnp.bfloat16),
            pltpu.VMEM(whole if others[2] else (1, 16, FN), jnp.bfloat16),
            pltpu.SemaphoreType.DMA((STATIONS,)),
        ],
        compiler_params=pltpu.CompilerParams(vmem_limit_bytes=GRANT),
        cost_estimate=pl.CostEstimate(
            flops=2 * blocks * HALF * sum(counts) * FN * FN,
            bytes_accessed=2 * STATIONS * FN * FN,
            transcendentals=0,
        ),
    )(turn, coupling, inverse_blocks, *values, *raw, *others[0])


def ship_kernel(
    number, turn, share, below, raw, crossed, edge_cross, edge_same, direct, whole, turned
):
    side, kind = turn[1], turn[2]

    def turn_over(source):
        rows = ordered(source[...])
        for half in range(2):
            turned[half, :, :] = rows[half * ONE : (half + 1) * ONE]

    @pl.when(turn[0] == number)
    def _():
        turn_over(below)
        whole[...] = share[...]
        middle = share[:, EDGE : EDGE + ONE, :].astype(jnp.float32) + turned[...]
        whole[:, EDGE : EDGE + ONE, :] = middle.astype(jnp.bfloat16)
        start = pl.multiple_of(side * ONE, ONE)
        edge_cross[...] = whole[1 - side, pl.ds(start, WIDE), :]
        edge_same[...] = whole[side, pl.ds(start, WIDE), :]
        crossed[...] = whole[1 - side]
        direct[...] = whole[side]

    @pl.when(kind >= 2)
    def _():
        turn_over(raw)
        whole[:, :ONE, :] = turned[...].astype(jnp.bfloat16)

    @pl.when(kind == 2)
    def _():
        crossed[:ONE, :] = whole[1 - side, :ONE, :]

    @pl.when(kind == 3)
    def _():
        for half in range(2):
            edge_cross[half * EDGE : (half + 1) * EDGE, :] = whole[half, ONE - EDGE : ONE, :]
            edge_same[half * EDGE : (half + 1) * EDGE, :] = whole[half, :EDGE, :]


def center_kernel(number, turn, direct, crossed, edge_same, edge_cross, out):
    @pl.when(turn[0] == number)
    def _():
        side = turn[1]
        start = pl.multiple_of(side * EDGE, EDGE)
        from_edge = pl.multiple_of((1 - side) * EDGE, EDGE)
        for block, share, edge in ((side, direct, edge_same), (1 - side, crossed, edge_cross)):
            out[block, :, :] = share[EDGE : EDGE + ONE, :]
            here = out[block, pl.ds(start, EDGE), :].astype(jnp.float32)
            more = edge[pl.ds(from_edge, EDGE), :].astype(jnp.float32)
            out[block, pl.ds(start, EDGE), :] = (here + more).astype(jnp.bfloat16)


def gram_kernel(numbers, turn, *refs):
    inputs, (rows, gram, edges, sems) = refs[: 7 * len(numbers)], refs[7 * len(numbers) :]
    side = turn[1]

    def fetch(*pairs):
        copies = [pltpu.make_async_copy(source, target, sems.at[at]) for at, (source, target) in enumerate(pairs)]
        for copy in copies:
            copy.start()
        for copy in copies:
            copy.wait()

    for at, number in enumerate(numbers):
        share, low, high, state, crossed, back, last = inputs[7 * at : 7 * at + 7]

        @pl.when(turn[0] == number)
        def _():
            halves = [slice(0, EDGE), slice(EDGE, 2 * EDGE)]
            fetch(
                *[(share.at[half, EDGE : EDGE + ONE], rows.at[half]) for half in range(2)],
                *[(low.at[halves[half]], edges.at[half, :EDGE]) for half in range(2)],
                *[(high.at[halves[half]], edges.at[half, EDGE:]) for half in range(2)],
            )
            rows[...] = (rows[...].astype(jnp.float32) + edges[...].astype(jnp.float32)).astype(jnp.bfloat16)

        @pl.when(turn[0] == number - 1)
        def _():
            start = pl.multiple_of(side * ONE, ONE)
            fetch((state.at[0, pl.ds(start, ONE)], rows.at[side]), (crossed.at[:ONE], rows.at[1 - side]))

        @pl.when(turn[0] == number - 2)
        def _():
            fetch((back, rows))

    def inner(state):
        flat = state[...].reshape(2 * ONE, FN)
        full = lax.dot_general(flat, flat, (((1,), (1,)), ((), ())), preferred_element_type=jnp.float32)
        lines = []
        for first in range(2):
            line = []
            for second in range(2):
                block = None
                for point in range(POINTS):
                    down, along = first * ONE + point * HALF, second * ONE + point * HALF
                    term = full[down : down + HALF, along : along + HALF]
                    block = term if block is None else block + term
                line.append(block)
            lines.append(jnp.concatenate(line, 1))
        gram[...] = jnp.concatenate(lines, 0)

    @pl.when(turn[2] < 3)
    def _():
        inner(rows)

    for at, number in enumerate(numbers):
        last = inputs[7 * at + 6]

        @pl.when(turn[0] == number - 3)
        def _():
            copy = pltpu.make_async_copy(last, rows, sems.at[0])
            copy.start()
            inner(last)
            copy.wait()


def turn_kernel(rows, turned):
    turned[...] = rows[...].reshape(2 * ONE, FN).T


def factor_kernel(scale, first, second, rows, by_column, by_place, same_point, basis, upper):
    eye = (
        lax.broadcasted_iota(jnp.int32, (K, K), 0) == lax.broadcasted_iota(jnp.int32, (K, K), 1)
    ).astype(jnp.float32)
    table = jnp.concatenate([(first[...] + second[...]) * scale, eye], 1)
    row_index = lax.broadcasted_iota(jnp.int32, (K, 2 * K), 0)
    roots = jnp.zeros((K, 2 * K), jnp.float32)
    for j in range(0, K, STEP):
        lines = [table[j + m : j + m + 1, :] for m in range(STEP)]
        columns = [jnp.broadcast_to(table[:, j + m : j + m + 1], table.shape) for m in range(STEP)]
        entries = [
            [jnp.broadcast_to(lines[m][:, j + k : j + k + 1], lines[m].shape) for k in range(STEP)]
            for m in range(STEP)
        ]
        below = table
        for m in range(STEP):
            inverse = 1.0 / entries[m][m]
            for k in range(m + 1, STEP):
                ratio = entries[m][k] * inverse
                for n in range(k, STEP):
                    entries[k][n] = entries[k][n] - ratio * entries[m][n]
                lines[k] = lines[k] - ratio * lines[m]
                columns[k] = columns[k] - ratio * columns[m]
            below = below - columns[m] * (inverse * lines[m])
            roots = jnp.where(row_index == j + m, lax.rsqrt(entries[m][m]), roots)
        table = jnp.where(row_index >= j + STEP, below, table)
        for m in range(STEP):
            table = jnp.where(row_index == j + m, lines[m], table)
    table = table * roots
    column = lax.broadcasted_iota(jnp.int32, (K, K), 1)
    row = lax.broadcasted_iota(jnp.int32, (K, K), 0)
    upper[...] = jnp.where(column >= row, table[:, :K], 0.0)
    inverse = table[:, K:]
    terms = []
    for _ in range(2):
        term = inverse.astype(jnp.bfloat16)
        inverse = inverse - term.astype(jnp.float32)
        tall = lax.dot_general(
            by_column[...], term, (((1,), (1,)), ((), ())), preferred_element_type=jnp.float32
        ).astype(jnp.bfloat16)
        spread = lax.dot_general(
            tall, by_place[...], (((1,), (0,)), ((), ())), preferred_element_type=jnp.float32
        )
        terms.append((spread * same_point[...]).astype(jnp.bfloat16))
    both = lax.dot_general(
        rows[...], jnp.concatenate(terms, 1), (((1,), (0,)), ((), ())), preferred_element_type=jnp.float32
    )
    total = both[:, : POINTS * K] + both[:, POINTS * K :]
    basis[...] = total.astype(jnp.bfloat16)


def local(inverse_blocks, coupling, sources):
    sections = lax.axis_size("section")
    spans = lax.axis_size("span")
    pairs = spans // 2
    assert sections % 4 == 0 and spans % 2 == 0 and sources.shape[2] == POINTS * K
    group = lax.axis_index("section")
    side = (lax.axis_index("span") % 2).astype(jnp.int32)

    def send(value, *legs):
        routes = []
        for groups, down, route in legs:
            for g in groups:
                for s in range(spans):
                    routes.append((g * spans + s, (g - down) % sections * spans + route(s)))
        return lax.ppermute(value, AXES, routes)

    def straight(s):
        return s

    def partner(s):
        return s ^ 1

    def neighbor(shift):
        return lambda s: (s + shift) % spans

    def pair_route(pair, side):
        return (pair % pairs) * 2 + side

    def outward(s):
        return pair_route(s // 2 + 2 * (s % 2) - 1, s % 2)

    def outward_cross(s):
        return pair_route(s // 2 + 2 * (s % 2) - 1, 1 - s % 2)

    def inward(s):
        return pair_route(s // 2 + 1 - 2 * (s % 2), s % 2)

    def of_kind(kind):
        return [g for g in range(sections) if (sections - 1 - g) % 4 == kind]

    turn = jnp.stack([group.astype(jnp.int32), side, ((sections - 1 - group) % 4).astype(jnp.int32)])

    half, point, column = np.meshgrid(np.arange(2), np.arange(POINTS), np.arange(HALF), indexing="ij")
    row_column = (half * HALF + column).reshape(-1)
    row_point = point.reshape(-1)
    place = np.arange(POINTS * K)
    by_column = jnp.asarray(np.arange(K)[None, :] == row_column[:, None], jnp.bfloat16)
    by_place = jnp.asarray(np.arange(K)[:, None] == place[None, :] % K, jnp.bfloat16)
    same_point = jnp.asarray(place[None, :] // K == row_point[:, None], jnp.float32)

    smem = pl.BlockSpec(memory_space=pltpu.SMEM)
    vmem = pl.BlockSpec(memory_space=pltpu.VMEM)
    away = pl.BlockSpec(memory_space=pl.ANY)
    raw = sources[0]
    odds, evens = list(range(1, sections, 2)), list(range(0, sections, 2))
    below = send(raw, (evens, -1, straight), (odds, 1, straight))
    incoming = None
    pair_source = wide_source = None
    candidates = []
    for g in reversed(of_kind(0)):
        pieces = [] if incoming is None else [(incoming, lambda side: (0, 0), ONE, None)]
        (share,) = march(turn, g, inverse_blocks, coupling, pieces, 0, 2, POINTS, True, (raw,))
        crossed, edge_cross, edge_same, direct, whole = pl.pallas_call(
            functools.partial(ship_kernel, g),
            out_shape=[jax.ShapeDtypeStruct((size, FN), jnp.bfloat16) for size in (2 * ONE, WIDE, WIDE, 2 * ONE)]
            + [jax.ShapeDtypeStruct(share.shape, jnp.bfloat16)],
            in_specs=[smem, vmem, vmem, vmem],
            out_specs=[vmem] * 5,
            scratch_shapes=[pltpu.VMEM((2, ONE, FN), jnp.float32)],
            compiler_params=pltpu.CompilerParams(vmem_limit_bytes=SMALL),
        )(turn, share, below, raw)
        first = incoming is None
        edge_cross = send(edge_cross, ([g], 1, outward_cross), (of_kind(3) if first else [], 0, neighbor(1)))
        crossed = send(crossed, ([g], 1, partner), (of_kind(2) if first else [], 0, partner))
        edge_same = send(edge_same, ([g], 1, outward), (of_kind(3) if first else [], 0, neighbor(-1)))
        direct = send(direct, ([g], 1, straight))
        if first:
            pair_source = [
                (whole, lambda side: (0, side * ONE), ONE, lambda side: side),
                (crossed, lambda side: (0, (1 - side) * ONE), ONE, None),
            ]
            wide_source = [
                (edge_cross.reshape(2, EDGE, FN), lambda side: (0, 0), EDGE, None),
                (whole, lambda side: (0, EDGE), ONE, None),
                (edge_same.reshape(2, EDGE, FN), lambda side: (0, EDGE + ONE), EDGE, None),
            ]

        (state,) = march(
            turn,
            g - 1,
            inverse_blocks,
            coupling,
            [
                (crossed, lambda side: (0, (1 - side) * ONE), 2 * ONE, None),
                (edge_cross, lambda side: (0, side * 2 * ONE), WIDE, None),
                (edge_same, lambda side: (0, (1 - side) * 2 * ONE), WIDE, None),
                (direct, lambda side: (0, side * ONE), 2 * ONE, None),
            ],
            14,
            1,
            3 * POINTS,
            False,
        )
        arrived = send(state, (list(range(sections)), 1, straight))

        crossed, edge_cross, edge_same, direct = march(
            turn,
            g - 2,
            inverse_blocks,
            coupling,
            [(arrived, lambda side: (0, 0), 2 * ONE, None)] + pair_source,
            10,
            1,
            2 * POINTS,
            True,
            (),
            (
                (share, state),
                (
                    (
                        0,
                        g,
                        (
                            (0, lambda side: 0, lambda side: EDGE + ONE, EDGE, 1, 0),
                            (0, lambda side: 1, lambda side: EDGE + ONE, EDGE, 1, EDGE),
                            (0, lambda side: 0, lambda side: 0, EDGE, 2, 0),
                            (0, lambda side: 1, lambda side: 0, EDGE, 2, EDGE),
                        ),
                    ),
                    (0, g - 1, ((1, lambda side: 0, lambda side: (1 - side) * ONE, ONE, 0, 0),)),
                ),
                (
                    lambda side: (1 - side) * ONE,
                    lambda side: side * 2 * ONE,
                    lambda side: (1 - side) * 2 * ONE,
                    lambda side: side * ONE,
                ),
            ),
        )
        edge_cross = send(edge_cross, ([g - 2], 1, outward_cross), ([g], 0, neighbor(1)))
        crossed = send(crossed, ([g - 2], 1, partner), ([g - 1], 0, partner))
        edge_same = send(edge_same, ([g - 2], 1, inward), ([g], 0, neighbor(-1)))
        direct = send(direct, ([g - 2], 1, straight))

        middle = pl.pallas_call(
            functools.partial(center_kernel, g - 3),
            out_shape=jax.ShapeDtypeStruct((2, ONE, FN), jnp.bfloat16),
            in_specs=[smem] + [vmem] * 4,
            out_specs=vmem,
            compiler_params=pltpu.CompilerParams(vmem_limit_bytes=SMALL),
        )(turn, direct, crossed, edge_same, edge_cross)
        back = send(middle, (evens, -1, straight), (odds, 1, straight))
        (last,) = march(
            turn,
            g - 3,
            inverse_blocks,
            coupling,
            [
                (crossed, lambda side: (1 - side, 0), 2 * ONE, None),
                (edge_cross, lambda side: (1 - side, side * ONE), WIDE, None),
                (edge_same, lambda side: (side, side * ONE), WIDE, None),
                (direct, lambda side: (side, 0), 2 * ONE, None),
            ]
            + wide_source,
            0,
            2,
            2 * POINTS,
            False,
        )
        candidates += [share, edge_cross, edge_same, state, crossed, back, last]
        if g > 3:
            incoming = send(last, ([g - 3], 1, straight))

    rows, gram = pl.pallas_call(
        functools.partial(gram_kernel, list(reversed(of_kind(0)))),
        out_shape=(
            jax.ShapeDtypeStruct((2, ONE, FN), jnp.bfloat16),
            jax.ShapeDtypeStruct((K, K), jnp.float32),
        ),
        in_specs=[smem] + ([away] * 6 + [vmem]) * (len(candidates) // 7),
        out_specs=(vmem, vmem),
        scratch_shapes=[pltpu.VMEM((2, ONE, FN), jnp.bfloat16), pltpu.SemaphoreType.DMA((6,))],
        compiler_params=pltpu.CompilerParams(vmem_limit_bytes=SMALL),
    )(turn, *candidates)
    turned_rows = pl.pallas_call(
        turn_kernel,
        out_shape=jax.ShapeDtypeStruct((FN, POINTS * K), jnp.bfloat16),
        in_specs=[vmem],
        out_specs=vmem,
        compiler_params=pltpu.CompilerParams(vmem_limit_bytes=SMALL),
    )(rows)
    stride = 1
    terms = [gram]
    while stride < spans:
        radix = 2 if stride == 1 else min(4, spans // stride)
        total = terms[0]
        for term in terms[1:]:
            total = total + term
        terms = [total] + [
            lax.ppermute(total, "span", [(s, s ^ (digit * stride)) for s in range(spans)])
            for digit in range(1, radix)
        ]
        if radix == 4:
            terms = [terms[0] + terms[1], terms[2] + terms[3]]
        stride *= radix

    basis, upper = pl.pallas_call(
        functools.partial(factor_kernel, 1.0 / float(FN * POINTS * spans)),
        out_shape=(
            jax.ShapeDtypeStruct((FN, POINTS * K), jnp.bfloat16),
            jax.ShapeDtypeStruct((K, K), jnp.float32),
        ),
        in_specs=[vmem] * 6,
        out_specs=(vmem, vmem),
        compiler_params=pltpu.CompilerParams(vmem_limit_bytes=SMALL),
    )(*terms, turned_rows, by_column, by_place, same_point)
    return (basis[None], upper[None])


def solution(mesh):
    placed = (P("section", None, None), P("section", None), P("section", None, "span"))
    return jax.shard_map(
        local,
        mesh=mesh,
        in_specs=placed,
        out_specs=(P("section", None, "span"), P("section", None, None)),
        check_vma=False,
    )
```

```python
import functools

import jax
import jax.numpy as jnp
import numpy as np
from jax import lax
from jax.experimental import pallas as pl
from jax.experimental.pallas import tpu as pltpu
from jax.sharding import PartitionSpec as P

K = 48
STATIONS = 4
FN = 768
HALF = K // 2
POINTS = 8
ONE = POINTS * HALF
EDGE = STATIONS * HALF
WIDE = 2 * EDGE
STEP = 6
GRANT = 48 * 1024 * 1024
SMALL = 16 * 1024 * 1024
AXES = ("section", "span")


def one_hot_order():
    at = lax.broadcasted_iota(jnp.int32, (1, POINTS * K), 1)
    point = at * 1366 >> 16
    column = at - point * K
    half = (column >= HALF).astype(jnp.int32)
    target = half * (ONE - HALF) + point * HALF + column
    row = lax.broadcasted_iota(jnp.int32, (POINTS * K, POINTS * K), 0)
    return jnp.where(row == target, 1.0, 0.0).astype(jnp.bfloat16)


def ordered(raw):
    return lax.dot_general(one_hot_order(), raw, (((1,), (1,)), ((), ())), preferred_element_type=jnp.float32)


def march_kernel(number, places, others, plan, blocks, positions, grow, raw, turn, coupling, weights, *refs):
    refs = list(refs)
    pieces = [refs.pop(0) for _ in places]
    raws = [refs.pop(0) for _ in range(raw)]
    ahead = [] if raw else [refs.pop(0)]
    givers = [refs.pop(0) for _ in others[0]]
    outs, (first, second, held, result, sems) = refs[:-5], refs[-5:]
    if not others[2]:
        result = outs[0]
    else:
        outs = [None] + outs
    states = [first, second]
    order = list(reversed(range(STATIONS)))
    side = turn[1]

    @pl.when(turn[0] == number)
    def _():
        copies = [
            pltpu.make_async_copy(weights.at[station], held.at[step], sems.at[step])
            for step, station in enumerate(order)
        ]
        copies[1 if ahead else 0].start()
        margin = 2 * HALF if grow else 0
        if margin:
            empty = jnp.zeros((blocks, margin, FN), jnp.float32)
            first[:, :margin, :] = empty
            first[:, margin + positions * HALF : 2 * margin + positions * HALF, :] = empty

        def total(on):
            covers = []
            if raw:
                turned = ordered(raws[0][...])
                for half in range(2):
                    covers.append((half, 0, ONE, lambda low, high, at=half * ONE: turned[at + low : at + high]))
            for piece, (where, rows, pick) in zip(pieces, places):
                block, start = where(on)
                if pick is not None:
                    covers.append((block, start, rows, lambda low, high, p=piece, k=pick(on): p[k, low:high, :]))
                elif len(piece.shape) == 3:
                    for k in range(blocks):
                        covers.append((k, start, rows, lambda low, high, p=piece, k=k: p[k, low:high, :]))
                else:
                    covers.append((block, start, rows, lambda low, high, p=piece: p[low:high, :]))
            for block in range(blocks):
                here = [cover for cover in covers if cover[0] == block]
                bounds = {0, positions * HALF}
                for _, start, rows, _ in here:
                    bounds |= {start, start + rows}
                bounds = sorted(bounds)
                for low, high in zip(bounds, bounds[1:]):
                    value = jnp.zeros((high - low, FN), jnp.float32)
                    for _, start, rows, read in here:
                        if start <= low and high <= start + rows:
                            value = value + read(low - start, high - start).astype(jnp.float32)
                    first[block, margin + low : margin + high, :] = value

        if pieces:
            for on in range(2):
                pl.when(side == on)(functools.partial(total, on))
        else:
            total(0)

        def stencil(step, chunk):
            block, begin, end = chunk
            at, rows = begin * HALF, (end - begin) * HALF
            source = states[step % 2]
            rates = coupling[order[step] : order[step] + 1, :]
            both = source[block, at : at + rows, :] + source[block, at + 2 * HALF : at + 2 * HALF + rows, :]
            update = (1.0 - 2.0 * rates) * source[block, at + HALF : at + HALF + rows, :] + rates * both
            return update.astype(jnp.bfloat16)

        copies[2 if ahead else 1].start()
        jobs = [(step, chunk) for step in range(STATIONS) for chunk in plan[step]]
        update = stencil(*jobs[0])
        for at_job, (step, chunk) in enumerate(jobs):
            block, begin, end = chunk
            at, rows = begin * HALF, (end - begin) * HALF
            current = update
            if at_job + 1 < len(jobs):
                update = stencil(*jobs[at_job + 1])
            if chunk is plan[step][0]:
                if step or not ahead:
                    copies[step].wait()
                later = step + (3 if ahead else 2)
                if later < STATIONS:
                    copies[later].start()
            moved = lax.dot_general(
                current,
                ahead[0][...] if ahead and not step else held[step],
                (((1,), (1,)), ((), ())),
                preferred_element_type=jnp.float32,
            )
            if step == STATIONS - 1:
                result[block, at : at + rows, :] = moved.astype(jnp.bfloat16)
                continue
            target = states[1 - step % 2]
            target[block, margin + at : margin + at + rows, :] = moved
            if grow:
                empty = jnp.zeros((margin, FN), jnp.float32)
                count = max(last for place, _, last in plan[step] if place == block)
                if begin == 0:
                    target[block, :margin, :] = empty
                if end == count:
                    target[block, margin + count * HALF : 2 * margin + count * HALF, :] = empty
        for out, where in zip(outs[1:], others[2]):
            start = pl.multiple_of(where(side), EDGE)
            out[...] = result[0, pl.ds(start, out.shape[0]), :]

    relay(others[1], turn, givers, outs[1:], sems)


def relay(owners, turn, givers, outs, sems):
    side = turn[1]
    for slot, value, moves in owners:

        @pl.when(turn[slot] == value)
        def _():
            copies = []
            for at, (giver, block, start, rows, out, to) in enumerate(moves):
                start = start(side)
                if not isinstance(start, int):
                    start = pl.multiple_of(start, EDGE)
                source = givers[giver].at[block(side), pl.ds(start, rows)]
                copies.append(pltpu.make_async_copy(source, outs[out].at[pl.ds(to, rows)], sems.at[at]))
            for copy in copies:
                copy.start()
            for copy in copies:
                copy.wait()


def march(turn, number, inverse_blocks, coupling, pieces, cut, blocks, positions, grow, raw=(), ahead=(), others=((), (), ())):
    last = positions + (2 * STATIONS if grow else -2 * STATIONS)
    most = last + 2 if grow else positions
    counts = [positions + (2 if grow else -2) * (step + 1) for step in range(STATIONS)]
    if blocks == 2:
        plan = [[(0, 0, count), (1, 0, count)] for count in counts]
    else:
        cuts = [cut - (0 if grow else 2 * step) for step in range(STATIONS)]
        plan = [[(0, 0, at), (0, at, count)] for at, count in zip(cuts, counts)]
    vmem = pl.BlockSpec(memory_space=pltpu.VMEM)
    away = pl.BlockSpec(memory_space=pl.ANY)
    whole = (blocks, last * HALF, FN)
    shapes = [jax.ShapeDtypeStruct(whole, jnp.bfloat16)]
    if others[2]:
        shapes = [jax.ShapeDtypeStruct((size, FN), jnp.bfloat16) for size in (2 * ONE, WIDE, WIDE, 2 * ONE)]
    values = [piece[0] for piece in pieces]
    return pl.pallas_call(
        functools.partial(
            march_kernel,
            number,
            [piece[1:] for piece in pieces],
            others,
            plan,
            blocks,
            positions,
            grow,
            len(raw),
        ),
        out_shape=shapes,
        in_specs=[pl.BlockSpec(memory_space=pltpu.SMEM), vmem, away]
        + [vmem] * (len(values) + len(raw) + len(ahead))
        + [away] * len(others[0]),
        out_specs=[vmem] * len(shapes),
        scratch_shapes=[pltpu.VMEM((blocks, most * HALF, FN), jnp.float32)] * 2
        + [
            pltpu.VMEM((STATIONS, FN, FN), jnp.bfloat16),
            pltpu.VMEM(whole if others[2] else (1, 16, FN), jnp.bfloat16),
            pltpu.SemaphoreType.DMA((STATIONS,)),
        ],
        compiler_params=pltpu.CompilerParams(vmem_limit_bytes=GRANT),
        cost_estimate=pl.CostEstimate(
            flops=2 * blocks * HALF * sum(counts) * FN * FN,
            bytes_accessed=2 * STATIONS * FN * FN,
            transcendentals=0,
        ),
    )(turn, coupling, inverse_blocks, *values, *raw, *ahead, *others[0])


def ship_kernel(
    number, turn, share, below, raw, crossed, edge_cross, edge_same, direct, kept, turned, whole
):
    side, kind = turn[1], turn[2]

    def turn_over(source):
        rows = ordered(source[...])
        for half in range(2):
            turned[half, :, :] = rows[half * ONE : (half + 1) * ONE]

    @pl.when(turn[0] == number)
    def _():
        turn_over(below)
        whole[...] = share[...]
        kept[...] = share[...]
        middle = share[:, EDGE : EDGE + ONE, :].astype(jnp.float32) + turned[...]
        whole[:, EDGE : EDGE + ONE, :] = middle.astype(jnp.bfloat16)
        start = pl.multiple_of(side * ONE, ONE)
        edge_cross[...] = whole[1 - side, pl.ds(start, WIDE), :]
        edge_same[...] = whole[side, pl.ds(start, WIDE), :]
        crossed[...] = whole[1 - side]
        direct[...] = whole[side]

    @pl.when(kind >= 2)
    def _():
        turn_over(raw)
        kept[:, :ONE, :] = turned[...].astype(jnp.bfloat16)

    @pl.when(kind == 2)
    def _():
        crossed[:ONE, :] = kept[1 - side, :ONE, :]

    @pl.when(kind == 3)
    def _():
        for half in range(2):
            edge_cross[half * EDGE : (half + 1) * EDGE, :] = kept[half, ONE - EDGE : ONE, :]
            edge_same[half * EDGE : (half + 1) * EDGE, :] = kept[half, :EDGE, :]


def hold_kernel(turn, weights, ahead, sem):
    @pl.when(turn[2] >= 1)
    def _():
        copy = pltpu.make_async_copy(weights.at[STATIONS - 1], ahead, sem)
        copy.start()
        copy.wait()


def center_kernel(number, turn, direct, crossed, edge_same, edge_cross, out):
    @pl.when(turn[0] == number)
    def _():
        side = turn[1]
        start = pl.multiple_of(side * EDGE, EDGE)
        from_edge = pl.multiple_of((1 - side) * EDGE, EDGE)
        for block, share, edge in ((side, direct, edge_same), (1 - side, crossed, edge_cross)):
            out[block, :, :] = share[EDGE : EDGE + ONE, :]
            here = out[block, pl.ds(start, EDGE), :].astype(jnp.float32)
            more = edge[pl.ds(from_edge, EDGE), :].astype(jnp.float32)
            out[block, pl.ds(start, EDGE), :] = (here + more).astype(jnp.bfloat16)


def gram_kernel(numbers, turn, *refs):
    inputs, (rows, gram, edges, sems) = refs[: 7 * len(numbers)], refs[7 * len(numbers) :]
    side = turn[1]

    def fetch(*pairs):
        copies = [pltpu.make_async_copy(source, target, sems.at[at]) for at, (source, target) in enumerate(pairs)]
        for copy in copies:
            copy.start()
        for copy in copies:
            copy.wait()

    for at, number in enumerate(numbers):
        share, low, high, state, crossed, back, last = inputs[7 * at : 7 * at + 7]

        @pl.when(turn[0] == number)
        def _():
            halves = [slice(0, EDGE), slice(EDGE, 2 * EDGE)]
            fetch(
                *[(share.at[half, EDGE : EDGE + ONE], rows.at[half]) for half in range(2)],
                *[(low.at[halves[half]], edges.at[half, :EDGE]) for half in range(2)],
                *[(high.at[halves[half]], edges.at[half, EDGE:]) for half in range(2)],
            )
            rows[...] = (rows[...].astype(jnp.float32) + edges[...].astype(jnp.float32)).astype(jnp.bfloat16)

        @pl.when(turn[0] == number - 1)
        def _():
            start = pl.multiple_of(side * ONE, ONE)
            fetch((state.at[0, pl.ds(start, ONE)], rows.at[side]), (crossed.at[:ONE], rows.at[1 - side]))

        @pl.when(turn[0] == number - 2)
        def _():
            fetch((back, rows))

        @pl.when(turn[0] == number - 3)
        def _():
            fetch((last, rows))

    flat = rows[...].reshape(2 * ONE, FN)
    full = lax.dot_general(flat, flat, (((1,), (1,)), ((), ())), preferred_element_type=jnp.float32)
    lines = []
    for first in range(2):
        line = []
        for second in range(2):
            block = None
            for point in range(POINTS):
                down, along = first * ONE + point * HALF, second * ONE + point * HALF
                term = full[down : down + HALF, along : along + HALF]
                block = term if block is None else block + term
            line.append(block)
        lines.append(jnp.concatenate(line, 1))
    total = jnp.concatenate(lines, 0)
    gram[...] = total


def factor_kernel(scale, first, second, rows, by_column, by_place, same_point, basis, upper):
    eye = (
        lax.broadcasted_iota(jnp.int32, (K, K), 0) == lax.broadcasted_iota(jnp.int32, (K, K), 1)
    ).astype(jnp.float32)
    table = jnp.concatenate([(first[...] + second[...]) * scale, eye], 1)
    row_index = lax.broadcasted_iota(jnp.int32, (K, 2 * K), 0)
    roots = jnp.zeros((K, 2 * K), jnp.float32)
    for j in range(0, K, STEP):
        lines = [table[j + m : j + m + 1, :] for m in range(STEP)]
        columns = [jnp.broadcast_to(table[:, j + m : j + m + 1], table.shape) for m in range(STEP)]
        entries = [
            [jnp.broadcast_to(lines[m][:, j + k : j + k + 1], lines[m].shape) for k in range(STEP)]
            for m in range(STEP)
        ]
        below = table
        for m in range(STEP):
            inverse = 1.0 / entries[m][m]
            for k in range(m + 1, STEP):
                ratio = entries[m][k] * inverse
                for n in range(k, STEP):
                    entries[k][n] = entries[k][n] - ratio * entries[m][n]
                lines[k] = lines[k] - ratio * lines[m]
                columns[k] = columns[k] - ratio * columns[m]
            below = below - columns[m] * (inverse * lines[m])
            roots = jnp.where(row_index == j + m, lax.rsqrt(entries[m][m]), roots)
        table = jnp.where(row_index >= j + STEP, below, table)
        for m in range(STEP):
            table = jnp.where(row_index == j + m, lines[m], table)
    table = table * roots
    column = lax.broadcasted_iota(jnp.int32, (K, K), 1)
    row = lax.broadcasted_iota(jnp.int32, (K, K), 0)
    upper[...] = jnp.where(column >= row, table[:, :K], 0.0)
    inverse = table[:, K:]
    terms = []
    for _ in range(2):
        term = inverse.astype(jnp.bfloat16)
        inverse = inverse - term.astype(jnp.float32)
        tall = lax.dot_general(
            by_column[...], term, (((1,), (1,)), ((), ())), preferred_element_type=jnp.float32
        ).astype(jnp.bfloat16)
        spread = lax.dot_general(
            tall, by_place[...], (((1,), (0,)), ((), ())), preferred_element_type=jnp.float32
        )
        terms.append((spread * same_point[...]).astype(jnp.bfloat16))
    both = lax.dot_general(
        rows[...], jnp.concatenate(terms, 1), (((0,), (0,)), ((), ())), preferred_element_type=jnp.float32
    )
    total = both[:, : POINTS * K] + both[:, POINTS * K :]
    basis[...] = total.astype(jnp.bfloat16)


def local(inverse_blocks, coupling, sources):
    sections = lax.axis_size("section")
    spans = lax.axis_size("span")
    pairs = spans // 2
    assert sections % 4 == 0 and spans % 2 == 0 and sources.shape[2] == POINTS * K
    group = lax.axis_index("section")
    side = (lax.axis_index("span") % 2).astype(jnp.int32)

    def send(value, *legs):
        routes = []
        for groups, down, route in legs:
            for g in groups:
                for s in range(spans):
                    routes.append((g * spans + s, (g - down) % sections * spans + route(s)))
        return lax.ppermute(value, AXES, routes)

    def straight(s):
        return s

    def partner(s):
        return s ^ 1

    def neighbor(shift):
        return lambda s: (s + shift) % spans

    def pair_route(pair, side):
        return (pair % pairs) * 2 + side

    def outward(s):
        return pair_route(s // 2 + 2 * (s % 2) - 1, s % 2)

    def outward_cross(s):
        return pair_route(s // 2 + 2 * (s % 2) - 1, 1 - s % 2)

    def inward(s):
        return pair_route(s // 2 + 1 - 2 * (s % 2), s % 2)

    def of_kind(kind):
        return [g for g in range(sections) if (sections - 1 - g) % 4 == kind]

    turn = jnp.stack([group.astype(jnp.int32), side, ((sections - 1 - group) % 4).astype(jnp.int32)])

    half, point, column = np.meshgrid(np.arange(2), np.arange(POINTS), np.arange(HALF), indexing="ij")
    row_column = (half * HALF + column).reshape(-1)
    row_point = point.reshape(-1)
    place = np.arange(POINTS * K)
    by_column = jnp.asarray(np.arange(K)[None, :] == row_column[:, None], jnp.bfloat16)
    by_place = jnp.asarray(np.arange(K)[:, None] == place[None, :] % K, jnp.bfloat16)
    same_point = jnp.asarray(place[None, :] // K == row_point[:, None], jnp.float32)

    smem = pl.BlockSpec(memory_space=pltpu.SMEM)
    vmem = pl.BlockSpec(memory_space=pltpu.VMEM)
    away = pl.BlockSpec(memory_space=pl.ANY)
    raw = sources[0]
    odds, evens = list(range(1, sections, 2)), list(range(0, sections, 2))
    below = send(raw, (evens, -1, straight), (odds, 1, straight))
    incoming = None
    pair_source = wide_source = ahead = None
    candidates = []
    for g in reversed(of_kind(0)):
        pieces = [] if incoming is None else [(incoming, lambda side: (0, 0), ONE, None)]
        (share,) = march(turn, g, inverse_blocks, coupling, pieces, 0, 2, POINTS, True, (raw,))
        crossed, edge_cross, edge_same, direct, kept = pl.pallas_call(
            functools.partial(ship_kernel, g),
            out_shape=[jax.ShapeDtypeStruct((size, FN), jnp.bfloat16) for size in (2 * ONE, WIDE, WIDE, 2 * ONE)]
            + [jax.ShapeDtypeStruct(share.shape, jnp.bfloat16)],
            in_specs=[smem, vmem, vmem, vmem],
            out_specs=[vmem] * 5,
            scratch_shapes=[pltpu.VMEM((2, ONE, FN), jnp.float32), pltpu.VMEM(share.shape, jnp.bfloat16)],
            compiler_params=pltpu.CompilerParams(vmem_limit_bytes=SMALL),
        )(turn, share, below, raw)
        first = incoming is None
        edge_cross = send(edge_cross, ([g], 1, outward_cross), (of_kind(3) if first else [], 0, neighbor(1)))
        crossed = send(crossed, ([g], 1, partner), (of_kind(2) if first else [], 0, partner))
        edge_same = send(edge_same, ([g], 1, outward), (of_kind(3) if first else [], 0, neighbor(-1)))
        direct = send(direct, ([g], 1, straight))
        if first:
            later, _ = lax.optimization_barrier((turn, kept))
            ahead = pl.pallas_call(
                hold_kernel,
                out_shape=jax.ShapeDtypeStruct((FN, FN), jnp.bfloat16),
                in_specs=[smem, away],
                out_specs=vmem,
                scratch_shapes=[pltpu.SemaphoreType.DMA],
                compiler_params=pltpu.CompilerParams(vmem_limit_bytes=GRANT),
            )(later, inverse_blocks)
            pair_source = [
                (kept, lambda side: (0, side * ONE), ONE, lambda side: side),
                (crossed, lambda side: (0, (1 - side) * ONE), ONE, None),
            ]
            wide_source = [
                (edge_cross.reshape(2, EDGE, FN), lambda side: (0, 0), EDGE, None),
                (kept, lambda side: (0, EDGE), ONE, None),
                (edge_same.reshape(2, EDGE, FN), lambda side: (0, EDGE + ONE), EDGE, None),
            ]

        (state,) = march(
            turn,
            g - 1,
            inverse_blocks,
            coupling,
            [
                (crossed, lambda side: (0, (1 - side) * ONE), 2 * ONE, None),
                (edge_cross, lambda side: (0, side * 2 * ONE), WIDE, None),
                (edge_same, lambda side: (0, (1 - side) * 2 * ONE), WIDE, None),
                (direct, lambda side: (0, side * ONE), 2 * ONE, None),
            ],
            14,
            1,
            3 * POINTS,
            False,
            (),
            (ahead,),
        )
        arrived = send(state, (list(range(sections)), 1, straight))

        crossed, edge_cross, edge_same, direct = march(
            turn,
            g - 2,
            inverse_blocks,
            coupling,
            [(arrived, lambda side: (0, 0), 2 * ONE, None)] + pair_source,
            10,
            1,
            2 * POINTS,
            True,
            (),
            (ahead,),
            (
                (kept, state),
                (
                    (
                        0,
                        g,
                        (
                            (0, lambda side: 0, lambda side: EDGE + ONE, EDGE, 1, 0),
                            (0, lambda side: 1, lambda side: EDGE + ONE, EDGE, 1, EDGE),
                            (0, lambda side: 0, lambda side: 0, EDGE, 2, 0),
                            (0, lambda side: 1, lambda side: 0, EDGE, 2, EDGE),
                        ),
                    ),
                    (0, g - 1, ((1, lambda side: 0, lambda side: (1 - side) * ONE, ONE, 0, 0),)),
                ),
                (
                    lambda side: (1 - side) * ONE,
                    lambda side: side * 2 * ONE,
                    lambda side: (1 - side) * 2 * ONE,
                    lambda side: side * ONE,
                ),
            ),
        )
        edge_cross = send(edge_cross, ([g - 2], 1, outward_cross), ([g], 0, neighbor(1)))
        crossed = send(crossed, ([g - 2], 1, partner), ([g - 1], 0, partner))
        edge_same = send(edge_same, ([g - 2], 1, inward), ([g], 0, neighbor(-1)))
        direct = send(direct, ([g - 2], 1, straight))

        middle = pl.pallas_call(
            functools.partial(center_kernel, g - 3),
            out_shape=jax.ShapeDtypeStruct((2, ONE, FN), jnp.bfloat16),
            in_specs=[smem] + [vmem] * 4,
            out_specs=vmem,
            compiler_params=pltpu.CompilerParams(vmem_limit_bytes=SMALL),
        )(turn, direct, crossed, edge_same, edge_cross)
        back = send(middle, (evens, -1, straight), (odds, 1, straight))
        (last,) = march(
            turn,
            g - 3,
            inverse_blocks,
            coupling,
            [
                (crossed, lambda side: (1 - side, 0), 2 * ONE, None),
                (edge_cross, lambda side: (1 - side, side * ONE), WIDE, None),
                (edge_same, lambda side: (side, side * ONE), WIDE, None),
                (direct, lambda side: (side, 0), 2 * ONE, None),
            ]
            + wide_source,
            0,
            2,
            2 * POINTS,
            False,
            (),
            (ahead,),
        )
        candidates += [kept, edge_cross, edge_same, state, crossed, back, last]
        if g > 3:
            incoming = send(last, ([g - 3], 1, straight))

    rows, gram = pl.pallas_call(
        functools.partial(gram_kernel, list(reversed(of_kind(0)))),
        out_shape=(
            jax.ShapeDtypeStruct((2, ONE, FN), jnp.bfloat16),
            jax.ShapeDtypeStruct((K, K), jnp.float32),
        ),
        in_specs=[smem] + [away] * len(candidates),
        out_specs=(vmem, vmem),
        scratch_shapes=[pltpu.VMEM((2, ONE, FN), jnp.bfloat16), pltpu.SemaphoreType.DMA((6,))],
        compiler_params=pltpu.CompilerParams(vmem_limit_bytes=SMALL),
    )(turn, *candidates)
    stride = 1
    terms = [gram]
    while stride < spans:
        radix = 2 if stride == 1 else min(4, spans // stride)
        total = terms[0]
        for term in terms[1:]:
            total = total + term
        terms = [total] + [
            lax.ppermute(total, "span", [(s, s ^ (digit * stride)) for s in range(spans)])
            for digit in range(1, radix)
        ]
        if radix == 4:
            terms = [terms[0] + terms[1], terms[2] + terms[3]]
        stride *= radix

    basis, upper = pl.pallas_call(
        functools.partial(factor_kernel, 1.0 / float(FN * POINTS * spans)),
        out_shape=(
            jax.ShapeDtypeStruct((FN, POINTS * K), jnp.bfloat16),
            jax.ShapeDtypeStruct((K, K), jnp.float32),
        ),
        in_specs=[vmem] * 6,
        out_specs=(vmem, vmem),
        compiler_params=pltpu.CompilerParams(vmem_limit_bytes=SMALL),
    )(*terms, rows.reshape(POINTS * K, FN), by_column, by_place, same_point)
    return (basis[None], upper[None])


def solution(mesh):
    placed = (P("section", None, None), P("section", None), P("section", None, "span"))
    return jax.shard_map(
        local,
        mesh=mesh,
        in_specs=placed,
        out_specs=(P("section", None, "span"), P("section", None, None)),
        check_vma=False,
    )
```

```python
import functools

import jax
import jax.numpy as jnp
import numpy as np
from jax import lax
from jax.experimental import pallas as pl
from jax.experimental.pallas import tpu as pltpu
from jax.sharding import PartitionSpec as P

K = 48
STATIONS = 4
FN = 768
HALF = K // 2
POINTS = 8
ONE = POINTS * HALF
EDGE = STATIONS * HALF
WIDE = 2 * EDGE
STEP = 8
GRANT = 48 * 1024 * 1024
SMALL = 16 * 1024 * 1024
AXES = ("section", "span")


def one_hot_order():
    at = lax.broadcasted_iota(jnp.int32, (1, POINTS * K), 1)
    point = at * 1366 >> 16
    column = at - point * K
    half = (column >= HALF).astype(jnp.int32)
    target = half * (ONE - HALF) + point * HALF + column
    row = lax.broadcasted_iota(jnp.int32, (POINTS * K, POINTS * K), 0)
    return jnp.where(row == target, 1.0, 0.0).astype(jnp.bfloat16)


def ordered(raw):
    return lax.dot_general(one_hot_order(), raw, (((1,), (1,)), ((), ())), preferred_element_type=jnp.float32)


def march_kernel(number, places, others, plan, blocks, positions, grow, raw, turn, coupling, weights, *refs):
    refs = list(refs)
    pieces = [refs.pop(0) for _ in places]
    raws = [refs.pop(0) for _ in range(raw)]
    ahead = [] if raw else [refs.pop(0)]
    givers = [refs.pop(0) for _ in others[0]]
    outs, (first, second, held, result, sems) = refs[:-5], refs[-5:]
    if not others[2]:
        result = outs[0]
    else:
        outs = [None] + outs
    states = [first, second]
    order = list(reversed(range(STATIONS)))
    side = turn[1]

    @pl.when(turn[0] == number)
    def _():
        copies = [
            pltpu.make_async_copy(weights.at[station], held.at[step], sems.at[step])
            for step, station in enumerate(order)
        ]
        copies[1 if ahead else 0].start()
        margin = 2 * HALF if grow else 0
        if margin:
            empty = jnp.zeros((blocks, margin, FN), jnp.float32)
            first[:, :margin, :] = empty
            first[:, margin + positions * HALF : 2 * margin + positions * HALF, :] = empty

        def total(on):
            covers = []
            if raw:
                turned = ordered(raws[0][...])
                for half in range(2):
                    covers.append((half, 0, ONE, lambda low, high, at=half * ONE: turned[at + low : at + high]))
            for piece, (where, rows, pick) in zip(pieces, places):
                block, start = where(on)
                if pick is not None:
                    covers.append((block, start, rows, lambda low, high, p=piece, k=pick(on): p[k, low:high, :]))
                elif len(piece.shape) == 3:
                    for k in range(blocks):
                        covers.append((k, start, rows, lambda low, high, p=piece, k=k: p[k, low:high, :]))
                else:
                    covers.append((block, start, rows, lambda low, high, p=piece: p[low:high, :]))
            for block in range(blocks):
                here = [cover for cover in covers if cover[0] == block]
                bounds = {0, positions * HALF}
                for _, start, rows, _ in here:
                    bounds |= {start, start + rows}
                bounds = sorted(bounds)
                for low, high in zip(bounds, bounds[1:]):
                    value = jnp.zeros((high - low, FN), jnp.float32)
                    for _, start, rows, read in here:
                        if start <= low and high <= start + rows:
                            value = value + read(low - start, high - start).astype(jnp.float32)
                    first[block, margin + low : margin + high, :] = value

        if pieces:
            for on in range(2):
                pl.when(side == on)(functools.partial(total, on))
        else:
            total(0)

        def stencil(step, chunk):
            block, begin, end = chunk
            at, rows = begin * HALF, (end - begin) * HALF
            source = states[step % 2]
            rates = coupling[order[step] : order[step] + 1, :]
            both = source[block, at : at + rows, :] + source[block, at + 2 * HALF : at + 2 * HALF + rows, :]
            update = (1.0 - 2.0 * rates) * source[block, at + HALF : at + HALF + rows, :] + rates * both
            return update.astype(jnp.bfloat16)

        copies[2 if ahead else 1].start()
        jobs = [(step, chunk) for step in range(STATIONS) for chunk in plan[step]]
        update = stencil(*jobs[0])
        for at_job, (step, chunk) in enumerate(jobs):
            block, begin, end = chunk
            at, rows = begin * HALF, (end - begin) * HALF
            current = update
            if at_job + 1 < len(jobs):
                update = stencil(*jobs[at_job + 1])
            if chunk is plan[step][0]:
                if step or not ahead:
                    copies[step].wait()
                later = step + (3 if ahead else 2)
                if later < STATIONS:
                    copies[later].start()
            moved = lax.dot_general(
                current,
                ahead[0][...] if ahead and not step else held[step],
                (((1,), (1,)), ((), ())),
                preferred_element_type=jnp.float32,
            )
            if step == STATIONS - 1:
                result[block, at : at + rows, :] = moved.astype(jnp.bfloat16)
                continue
            target = states[1 - step % 2]
            target[block, margin + at : margin + at + rows, :] = moved
            if grow:
                empty = jnp.zeros((margin, FN), jnp.float32)
                count = max(last for place, _, last in plan[step] if place == block)
                if begin == 0:
                    target[block, :margin, :] = empty
                if end == count:
                    target[block, margin + count * HALF : 2 * margin + count * HALF, :] = empty
        for out, where in zip(outs[1:], others[2]):
            start = pl.multiple_of(where(side), EDGE)
            out[...] = result[0, pl.ds(start, out.shape[0]), :]

    relay(others[1], turn, givers, outs[1:], sems)


def relay(owners, turn, givers, outs, sems):
    side = turn[1]
    for slot, value, moves in owners:

        @pl.when(turn[slot] == value)
        def _():
            copies = []
            for at, (giver, block, start, rows, out, to) in enumerate(moves):
                start = start(side)
                if not isinstance(start, int):
                    start = pl.multiple_of(start, EDGE)
                source = givers[giver].at[block(side), pl.ds(start, rows)]
                copies.append(pltpu.make_async_copy(source, outs[out].at[pl.ds(to, rows)], sems.at[at]))
            for copy in copies:
                copy.start()
            for copy in copies:
                copy.wait()


def march(turn, number, inverse_blocks, coupling, pieces, cut, blocks, positions, grow, raw=(), ahead=(), others=((), (), ())):
    last = positions + (2 * STATIONS if grow else -2 * STATIONS)
    most = last + 2 if grow else positions
    counts = [positions + (2 if grow else -2) * (step + 1) for step in range(STATIONS)]
    if blocks == 2:
        plan = [[(0, 0, count), (1, 0, count)] for count in counts]
    else:
        cuts = [cut - (0 if grow else 2 * step) for step in range(STATIONS)]
        plan = [[(0, 0, at), (0, at, count)] for at, count in zip(cuts, counts)]
    vmem = pl.BlockSpec(memory_space=pltpu.VMEM)
    away = pl.BlockSpec(memory_space=pl.ANY)
    whole = (blocks, last * HALF, FN)
    shapes = [jax.ShapeDtypeStruct(whole, jnp.bfloat16)]
    if others[2]:
        shapes = [jax.ShapeDtypeStruct((size, FN), jnp.bfloat16) for size in (2 * ONE, WIDE, WIDE, 2 * ONE)]
    values = [piece[0] for piece in pieces]
    return pl.pallas_call(
        functools.partial(
            march_kernel,
            number,
            [piece[1:] for piece in pieces],
            others,
            plan,
            blocks,
            positions,
            grow,
            len(raw),
        ),
        out_shape=shapes,
        in_specs=[pl.BlockSpec(memory_space=pltpu.SMEM), vmem, away]
        + [vmem] * (len(values) + len(raw) + len(ahead))
        + [away] * len(others[0]),
        out_specs=[vmem] * len(shapes),
        scratch_shapes=[pltpu.VMEM((blocks, most * HALF, FN), jnp.float32)] * 2
        + [
            pltpu.VMEM((STATIONS, FN, FN), jnp.bfloat16),
            pltpu.VMEM(whole if others[2] else (1, 16, FN), jnp.bfloat16),
            pltpu.SemaphoreType.DMA((STATIONS,)),
        ],
        compiler_params=pltpu.CompilerParams(vmem_limit_bytes=GRANT),
        cost_estimate=pl.CostEstimate(
            flops=2 * blocks * HALF * sum(counts) * FN * FN,
            bytes_accessed=2 * STATIONS * FN * FN,
            transcendentals=0,
        ),
    )(turn, coupling, inverse_blocks, *values, *raw, *ahead, *others[0])


def ship_kernel(
    number, turn, share, below, raw, crossed, edge_cross, edge_same, direct, kept, turned, whole
):
    side, kind = turn[1], turn[2]

    def turn_over(source):
        rows = ordered(source[...])
        for half in range(2):
            turned[half, :, :] = rows[half * ONE : (half + 1) * ONE]

    @pl.when(turn[0] == number)
    def _():
        turn_over(below)
        whole[...] = share[...]
        kept[...] = share[...]
        middle = share[:, EDGE : EDGE + ONE, :].astype(jnp.float32) + turned[...]
        whole[:, EDGE : EDGE + ONE, :] = middle.astype(jnp.bfloat16)
        start = pl.multiple_of(side * ONE, ONE)
        edge_cross[...] = whole[1 - side, pl.ds(start, WIDE), :]
        edge_same[...] = whole[side, pl.ds(start, WIDE), :]
        crossed[...] = whole[1 - side]
        direct[...] = whole[side]

    @pl.when(kind >= 2)
    def _():
        turn_over(raw)
        kept[:, :ONE, :] = turned[...].astype(jnp.bfloat16)

    @pl.when(kind == 2)
    def _():
        crossed[:ONE, :] = kept[1 - side, :ONE, :]

    @pl.when(kind == 3)
    def _():
        for half in range(2):
            edge_cross[half * EDGE : (half + 1) * EDGE, :] = kept[half, ONE - EDGE : ONE, :]
            edge_same[half * EDGE : (half + 1) * EDGE, :] = kept[half, :EDGE, :]


def hold_kernel(turn, weights, ahead, sem):
    @pl.when(turn[2] >= 1)
    def _():
        copy = pltpu.make_async_copy(weights.at[STATIONS - 1], ahead, sem)
        copy.start()
        copy.wait()


def center_kernel(number, turn, direct, crossed, edge_same, edge_cross, out):
    @pl.when(turn[0] == number)
    def _():
        side = turn[1]
        start = pl.multiple_of(side * EDGE, EDGE)
        from_edge = pl.multiple_of((1 - side) * EDGE, EDGE)
        for block, share, edge in ((side, direct, edge_same), (1 - side, crossed, edge_cross)):
            out[block, :, :] = share[EDGE : EDGE + ONE, :]
            here = out[block, pl.ds(start, EDGE), :].astype(jnp.float32)
            more = edge[pl.ds(from_edge, EDGE), :].astype(jnp.float32)
            out[block, pl.ds(start, EDGE), :] = (here + more).astype(jnp.bfloat16)


def gram_kernel(numbers, turn, *refs):
    inputs, (rows, gram, edges, sems) = refs[: 7 * len(numbers)], refs[7 * len(numbers) :]
    side = turn[1]

    def fetch(*pairs):
        copies = [pltpu.make_async_copy(source, target, sems.at[at]) for at, (source, target) in enumerate(pairs)]
        for copy in copies:
            copy.start()
        for copy in copies:
            copy.wait()

    for at, number in enumerate(numbers):
        share, low, high, state, crossed, back, last = inputs[7 * at : 7 * at + 7]

        @pl.when(turn[0] == number)
        def _():
            halves = [slice(0, EDGE), slice(EDGE, 2 * EDGE)]
            fetch(
                *[(share.at[half, EDGE : EDGE + ONE], rows.at[half]) for half in range(2)],
                *[(low.at[halves[half]], edges.at[half, :EDGE]) for half in range(2)],
                *[(high.at[halves[half]], edges.at[half, EDGE:]) for half in range(2)],
            )
            rows[...] = (rows[...].astype(jnp.float32) + edges[...].astype(jnp.float32)).astype(jnp.bfloat16)

        @pl.when(turn[0] == number - 1)
        def _():
            start = pl.multiple_of(side * ONE, ONE)
            fetch((state.at[0, pl.ds(start, ONE)], rows.at[side]), (crossed.at[:ONE], rows.at[1 - side]))

        @pl.when(turn[0] == number - 2)
        def _():
            fetch((back, rows))

        @pl.when(turn[0] == number - 3)
        def _():
            fetch((last, rows))

    flat = rows[...].reshape(2 * ONE, FN)
    full = lax.dot_general(flat, flat, (((1,), (1,)), ((), ())), preferred_element_type=jnp.float32)
    lines = []
    for first in range(2):
        line = []
        for second in range(2):
            block = None
            for point in range(POINTS):
                down, along = first * ONE + point * HALF, second * ONE + point * HALF
                term = full[down : down + HALF, along : along + HALF]
                block = term if block is None else block + term
            line.append(block)
        lines.append(jnp.concatenate(line, 1))
    total = jnp.concatenate(lines, 0)
    gram[...] = total


def factor_kernel(scale, first, second, rows, by_column, by_place, same_point, basis, upper):
    eye = (
        lax.broadcasted_iota(jnp.int32, (K, K), 0) == lax.broadcasted_iota(jnp.int32, (K, K), 1)
    ).astype(jnp.float32)
    table = jnp.concatenate([(first[...] + second[...]) * scale, eye], 1)
    row_index = lax.broadcasted_iota(jnp.int32, (K, 2 * K), 0)
    roots = jnp.zeros((K, 2 * K), jnp.float32)
    for j in range(0, K, STEP):
        lines = [table[j + m : j + m + 1, :] for m in range(STEP)]
        columns = [jnp.broadcast_to(table[:, j + m : j + m + 1], table.shape) for m in range(STEP)]
        entries = [
            [jnp.broadcast_to(lines[m][:, j + k : j + k + 1], lines[m].shape) for k in range(STEP)]
            for m in range(STEP)
        ]
        below = table
        for m in range(STEP):
            inverse = 1.0 / entries[m][m]
            for k in range(m + 1, STEP):
                ratio = entries[m][k] * inverse
                for n in range(k, STEP):
                    entries[k][n] = entries[k][n] - ratio * entries[m][n]
                lines[k] = lines[k] - ratio * lines[m]
                columns[k] = columns[k] - ratio * columns[m]
            below = below - columns[m] * (inverse * lines[m])
            roots = jnp.where(row_index == j + m, lax.rsqrt(entries[m][m]), roots)
        table = jnp.where(row_index >= j + STEP, below, table)
        for m in range(STEP):
            table = jnp.where(row_index == j + m, lines[m], table)
    table = table * roots
    column = lax.broadcasted_iota(jnp.int32, (K, K), 1)
    row = lax.broadcasted_iota(jnp.int32, (K, K), 0)
    upper[...] = jnp.where(column >= row, table[:, :K], 0.0)
    inverse = table[:, K:]
    terms = []
    for _ in range(2):
        term = inverse.astype(jnp.bfloat16)
        inverse = inverse - term.astype(jnp.float32)
        tall = lax.dot_general(
            by_column[...], term, (((1,), (1,)), ((), ())), preferred_element_type=jnp.float32
        ).astype(jnp.bfloat16)
        spread = lax.dot_general(
            tall, by_place[...], (((1,), (0,)), ((), ())), preferred_element_type=jnp.float32
        )
        terms.append((spread * same_point[...]).astype(jnp.bfloat16))
    both = lax.dot_general(
        rows[...], jnp.concatenate(terms, 1), (((0,), (0,)), ((), ())), preferred_element_type=jnp.float32
    )
    total = both[:, : POINTS * K] + both[:, POINTS * K :]
    basis[...] = total.astype(jnp.bfloat16)


def local(inverse_blocks, coupling, sources):
    sections = lax.axis_size("section")
    spans = lax.axis_size("span")
    pairs = spans // 2
    assert sections % 4 == 0 and spans % 2 == 0 and sources.shape[2] == POINTS * K
    group = lax.axis_index("section")
    side = (lax.axis_index("span") % 2).astype(jnp.int32)

    def send(value, *legs):
        routes = []
        for groups, down, route in legs:
            for g in groups:
                for s in range(spans):
                    routes.append((g * spans + s, (g - down) % sections * spans + route(s)))
        return lax.ppermute(value, AXES, routes)

    def straight(s):
        return s

    def partner(s):
        return s ^ 1

    def neighbor(shift):
        return lambda s: (s + shift) % spans

    def pair_route(pair, side):
        return (pair % pairs) * 2 + side

    def outward(s):
        return pair_route(s // 2 + 2 * (s % 2) - 1, s % 2)

    def outward_cross(s):
        return pair_route(s // 2 + 2 * (s % 2) - 1, 1 - s % 2)

    def inward(s):
        return pair_route(s // 2 + 1 - 2 * (s % 2), s % 2)

    def of_kind(kind):
        return [g for g in range(sections) if (sections - 1 - g) % 4 == kind]

    turn = jnp.stack([group.astype(jnp.int32), side, ((sections - 1 - group) % 4).astype(jnp.int32)])

    half, point, column = np.meshgrid(np.arange(2), np.arange(POINTS), np.arange(HALF), indexing="ij")
    row_column = (half * HALF + column).reshape(-1)
    row_point = point.reshape(-1)
    place = np.arange(POINTS * K)
    by_column = jnp.asarray(np.arange(K)[None, :] == row_column[:, None], jnp.bfloat16)
    by_place = jnp.asarray(np.arange(K)[:, None] == place[None, :] % K, jnp.bfloat16)
    same_point = jnp.asarray(place[None, :] // K == row_point[:, None], jnp.float32)

    smem = pl.BlockSpec(memory_space=pltpu.SMEM)
    vmem = pl.BlockSpec(memory_space=pltpu.VMEM)
    away = pl.BlockSpec(memory_space=pl.ANY)
    raw = sources[0]
    odds, evens = list(range(1, sections, 2)), list(range(0, sections, 2))
    below = send(raw, (evens, -1, straight), (odds, 1, straight))
    incoming = None
    pair_source = wide_source = ahead = None
    candidates = []
    for g in reversed(of_kind(0)):
        pieces = [] if incoming is None else [(incoming, lambda side: (0, 0), ONE, None)]
        (share,) = march(turn, g, inverse_blocks, coupling, pieces, 0, 2, POINTS, True, (raw,))
        crossed, edge_cross, edge_same, direct, kept = pl.pallas_call(
            functools.partial(ship_kernel, g),
            out_shape=[jax.ShapeDtypeStruct((size, FN), jnp.bfloat16) for size in (2 * ONE, WIDE, WIDE, 2 * ONE)]
            + [jax.ShapeDtypeStruct(share.shape, jnp.bfloat16)],
            in_specs=[smem, vmem, vmem, vmem],
            out_specs=[vmem] * 5,
            scratch_shapes=[pltpu.VMEM((2, ONE, FN), jnp.float32), pltpu.VMEM(share.shape, jnp.bfloat16)],
            compiler_params=pltpu.CompilerParams(vmem_limit_bytes=SMALL),
        )(turn, share, below, raw)
        first = incoming is None
        edge_cross = send(edge_cross, ([g], 1, outward_cross), (of_kind(3) if first else [], 0, neighbor(1)))
        crossed = send(crossed, ([g], 1, partner), (of_kind(2) if first else [], 0, partner))
        edge_same = send(edge_same, ([g], 1, outward), (of_kind(3) if first else [], 0, neighbor(-1)))
        direct = send(direct, ([g], 1, straight))
        if first:
            later, _ = lax.optimization_barrier((turn, kept))
            ahead = pl.pallas_call(
                hold_kernel,
                out_shape=jax.ShapeDtypeStruct((FN, FN), jnp.bfloat16),
                in_specs=[smem, away],
                out_specs=vmem,
                scratch_shapes=[pltpu.SemaphoreType.DMA],
                compiler_params=pltpu.CompilerParams(vmem_limit_bytes=GRANT),
            )(later, inverse_blocks)
            pair_source = [
                (kept, lambda side: (0, side * ONE), ONE, lambda side: side),
                (crossed, lambda side: (0, (1 - side) * ONE), ONE, None),
            ]
            wide_source = [
                (edge_cross.reshape(2, EDGE, FN), lambda side: (0, 0), EDGE, None),
                (kept, lambda side: (0, EDGE), ONE, None),
                (edge_same.reshape(2, EDGE, FN), lambda side: (0, EDGE + ONE), EDGE, None),
            ]

        (state,) = march(
            turn,
            g - 1,
            inverse_blocks,
            coupling,
            [
                (crossed, lambda side: (0, (1 - side) * ONE), 2 * ONE, None),
                (edge_cross, lambda side: (0, side * 2 * ONE), WIDE, None),
                (edge_same, lambda side: (0, (1 - side) * 2 * ONE), WIDE, None),
                (direct, lambda side: (0, side * ONE), 2 * ONE, None),
            ],
            14,
            1,
            3 * POINTS,
            False,
            (),
            (ahead,),
        )
        arrived = send(state, (list(range(sections)), 1, straight))

        crossed, edge_cross, edge_same, direct = march(
            turn,
            g - 2,
            inverse_blocks,
            coupling,
            [(arrived, lambda side: (0, 0), 2 * ONE, None)] + pair_source,
            10,
            1,
            2 * POINTS,
            True,
            (),
            (ahead,),
            (
                (kept, state),
                (
                    (
                        0,
                        g,
                        (
                            (0, lambda side: 0, lambda side: EDGE + ONE, EDGE, 1, 0),
                            (0, lambda side: 1, lambda side: EDGE + ONE, EDGE, 1, EDGE),
                            (0, lambda side: 0, lambda side: 0, EDGE, 2, 0),
                            (0, lambda side: 1, lambda side: 0, EDGE, 2, EDGE),
                        ),
                    ),
                    (0, g - 1, ((1, lambda side: 0, lambda side: (1 - side) * ONE, ONE, 0, 0),)),
                ),
                (
                    lambda side: (1 - side) * ONE,
                    lambda side: side * 2 * ONE,
                    lambda side: (1 - side) * 2 * ONE,
                    lambda side: side * ONE,
                ),
            ),
        )
        edge_cross = send(edge_cross, ([g - 2], 1, outward_cross), ([g], 0, neighbor(1)))
        crossed = send(crossed, ([g - 2], 1, partner), ([g - 1], 0, partner))
        edge_same = send(edge_same, ([g - 2], 1, inward), ([g], 0, neighbor(-1)))
        direct = send(direct, ([g - 2], 1, straight))

        middle = pl.pallas_call(
            functools.partial(center_kernel, g - 3),
            out_shape=jax.ShapeDtypeStruct((2, ONE, FN), jnp.bfloat16),
            in_specs=[smem] + [vmem] * 4,
            out_specs=vmem,
            compiler_params=pltpu.CompilerParams(vmem_limit_bytes=SMALL),
        )(turn, direct, crossed, edge_same, edge_cross)
        back = send(middle, (evens, -1, straight), (odds, 1, straight))
        (last,) = march(
            turn,
            g - 3,
            inverse_blocks,
            coupling,
            [
                (crossed, lambda side: (1 - side, 0), 2 * ONE, None),
                (edge_cross, lambda side: (1 - side, side * ONE), WIDE, None),
                (edge_same, lambda side: (side, side * ONE), WIDE, None),
                (direct, lambda side: (side, 0), 2 * ONE, None),
            ]
            + wide_source,
            0,
            2,
            2 * POINTS,
            False,
            (),
            (ahead,),
        )
        candidates += [kept, edge_cross, edge_same, state, crossed, back, last]
        if g > 3:
            incoming = send(last, ([g - 3], 1, straight))

    rows, gram = pl.pallas_call(
        functools.partial(gram_kernel, list(reversed(of_kind(0)))),
        out_shape=(
            jax.ShapeDtypeStruct((2, ONE, FN), jnp.bfloat16),
            jax.ShapeDtypeStruct((K, K), jnp.float32),
        ),
        in_specs=[smem] + [away] * len(candidates),
        out_specs=(vmem, vmem),
        scratch_shapes=[pltpu.VMEM((2, ONE, FN), jnp.bfloat16), pltpu.SemaphoreType.DMA((6,))],
        compiler_params=pltpu.CompilerParams(vmem_limit_bytes=SMALL),
    )(turn, *candidates)
    stride = 1
    terms = [gram]
    while stride < spans:
        radix = 2 if stride == 1 else min(4, spans // stride)
        total = terms[0]
        for term in terms[1:]:
            total = total + term
        terms = [total] + [
            lax.ppermute(total, "span", [(s, s ^ (digit * stride)) for s in range(spans)])
            for digit in range(1, radix)
        ]
        if radix == 4:
            terms = [terms[0] + terms[1], terms[2] + terms[3]]
        stride *= radix

    basis, upper = pl.pallas_call(
        functools.partial(factor_kernel, 1.0 / float(FN * POINTS * spans)),
        out_shape=(
            jax.ShapeDtypeStruct((FN, POINTS * K), jnp.bfloat16),
            jax.ShapeDtypeStruct((K, K), jnp.float32),
        ),
        in_specs=[vmem] * 6,
        out_specs=(vmem, vmem),
        compiler_params=pltpu.CompilerParams(vmem_limit_bytes=SMALL),
    )(*terms, rows.reshape(POINTS * K, FN), by_column, by_place, same_point)
    return (basis[None], upper[None])


def solution(mesh):
    placed = (P("section", None, None), P("section", None), P("section", None, "span"))
    return jax.shard_map(
        local,
        mesh=mesh,
        in_specs=placed,
        out_specs=(P("section", None, "span"), P("section", None, None)),
        check_vma=False,
    )
```

```python
import functools

import jax
import jax.numpy as jnp
import numpy as np
from jax import lax
from jax.experimental import pallas as pl
from jax.experimental.pallas import tpu as pltpu
from jax.sharding import PartitionSpec as P

K = 48
STATIONS = 4
FN = 768
HALF = K // 2
POINTS = 8
ONE = POINTS * HALF
EDGE = STATIONS * HALF
WIDE = 2 * EDGE
STEP = 12
GRANT = 48 * 1024 * 1024
SMALL = 16 * 1024 * 1024
AXES = ("section", "span")


def one_hot_order():
    at = lax.broadcasted_iota(jnp.int32, (1, POINTS * K), 1)
    point = at * 1366 >> 16
    column = at - point * K
    half = (column >= HALF).astype(jnp.int32)
    target = half * (ONE - HALF) + point * HALF + column
    row = lax.broadcasted_iota(jnp.int32, (POINTS * K, POINTS * K), 0)
    return jnp.where(row == target, 1.0, 0.0).astype(jnp.bfloat16)


def ordered(raw):
    return lax.dot_general(one_hot_order(), raw, (((1,), (1,)), ((), ())), preferred_element_type=jnp.float32)


def march_kernel(number, places, others, plan, blocks, positions, grow, raw, turn, coupling, weights, *refs):
    refs = list(refs)
    pieces = [refs.pop(0) for _ in places]
    raws = [refs.pop(0) for _ in range(raw)]
    ahead = [] if raw else [refs.pop(0)]
    givers = [refs.pop(0) for _ in others[0]]
    outs, (first, second, held, result, sems) = refs[:-5], refs[-5:]
    if not others[2]:
        result = outs[0]
    else:
        outs = [None] + outs
    states = [first, second]
    order = list(reversed(range(STATIONS)))
    side = turn[1]

    @pl.when(turn[0] == number)
    def _():
        copies = [
            pltpu.make_async_copy(weights.at[station], held.at[step], sems.at[step])
            for step, station in enumerate(order)
        ]
        copies[1 if ahead else 0].start()
        margin = 2 * HALF if grow else 0
        if margin:
            empty = jnp.zeros((blocks, margin, FN), jnp.float32)
            first[:, :margin, :] = empty
            first[:, margin + positions * HALF : 2 * margin + positions * HALF, :] = empty

        def total(on):
            covers = []
            if raw:
                turned = ordered(raws[0][...])
                for half in range(2):
                    covers.append((half, 0, ONE, lambda low, high, at=half * ONE: turned[at + low : at + high]))
            for piece, (where, rows, pick) in zip(pieces, places):
                block, start = where(on)
                if pick is not None:
                    covers.append((block, start, rows, lambda low, high, p=piece, k=pick(on): p[k, low:high, :]))
                elif len(piece.shape) == 3:
                    for k in range(blocks):
                        covers.append((k, start, rows, lambda low, high, p=piece, k=k: p[k, low:high, :]))
                else:
                    covers.append((block, start, rows, lambda low, high, p=piece: p[low:high, :]))
            for block in range(blocks):
                here = [cover for cover in covers if cover[0] == block]
                bounds = {0, positions * HALF}
                for _, start, rows, _ in here:
                    bounds |= {start, start + rows}
                bounds = sorted(bounds)
                for low, high in zip(bounds, bounds[1:]):
                    value = jnp.zeros((high - low, FN), jnp.float32)
                    for _, start, rows, read in here:
                        if start <= low and high <= start + rows:
                            value = value + read(low - start, high - start).astype(jnp.float32)
                    first[block, margin + low : margin + high, :] = value

        if pieces:
            for on in range(2):
                pl.when(side == on)(functools.partial(total, on))
        else:
            total(0)

        def stencil(step, chunk):
            block, begin, end = chunk
            at, rows = begin * HALF, (end - begin) * HALF
            source = states[step % 2]
            rates = coupling[order[step] : order[step] + 1, :]
            both = source[block, at : at + rows, :] + source[block, at + 2 * HALF : at + 2 * HALF + rows, :]
            update = (1.0 - 2.0 * rates) * source[block, at + HALF : at + HALF + rows, :] + rates * both
            return update.astype(jnp.bfloat16)

        copies[2 if ahead else 1].start()
        jobs = [(step, chunk) for step in range(STATIONS) for chunk in plan[step]]
        update = stencil(*jobs[0])
        for at_job, (step, chunk) in enumerate(jobs):
            block, begin, end = chunk
            at, rows = begin * HALF, (end - begin) * HALF
            current = update
            if at_job + 1 < len(jobs):
                update = stencil(*jobs[at_job + 1])
            if chunk is plan[step][0]:
                if step or not ahead:
                    copies[step].wait()
                later = step + (3 if ahead else 2)
                if later < STATIONS:
                    copies[later].start()
            moved = lax.dot_general(
                current,
                ahead[0][...] if ahead and not step else held[step],
                (((1,), (1,)), ((), ())),
                preferred_element_type=jnp.float32,
            )
            if step == STATIONS - 1:
                result[block, at : at + rows, :] = moved.astype(jnp.bfloat16)
                continue
            target = states[1 - step % 2]
            target[block, margin + at : margin + at + rows, :] = moved
            if grow:
                empty = jnp.zeros((margin, FN), jnp.float32)
                count = max(last for place, _, last in plan[step] if place == block)
                if begin == 0:
                    target[block, :margin, :] = empty
                if end == count:
                    target[block, margin + count * HALF : 2 * margin + count * HALF, :] = empty
        for out, where in zip(outs[1:], others[2]):
            start = pl.multiple_of(where(side), EDGE)
            out[...] = result[0, pl.ds(start, out.shape[0]), :]

    relay(others[1], turn, givers, outs[1:], sems)


def relay(owners, turn, givers, outs, sems):
    side = turn[1]
    for slot, value, moves in owners:

        @pl.when(turn[slot] == value)
        def _():
            copies = []
            for at, (giver, block, start, rows, out, to) in enumerate(moves):
                start = start(side)
                if not isinstance(start, int):
                    start = pl.multiple_of(start, EDGE)
                source = givers[giver].at[block(side), pl.ds(start, rows)]
                copies.append(pltpu.make_async_copy(source, outs[out].at[pl.ds(to, rows)], sems.at[at]))
            for copy in copies:
                copy.start()
            for copy in copies:
                copy.wait()


def march(turn, number, inverse_blocks, coupling, pieces, cut, blocks, positions, grow, raw=(), ahead=(), others=((), (), ())):
    last = positions + (2 * STATIONS if grow else -2 * STATIONS)
    most = last + 2 if grow else positions
    counts = [positions + (2 if grow else -2) * (step + 1) for step in range(STATIONS)]
    if blocks == 2:
        plan = [[(0, 0, count), (1, 0, count)] for count in counts]
    else:
        cuts = [cut - (0 if grow else 2 * step) for step in range(STATIONS)]
        plan = [[(0, 0, at), (0, at, count)] for at, count in zip(cuts, counts)]
    vmem = pl.BlockSpec(memory_space=pltpu.VMEM)
    away = pl.BlockSpec(memory_space=pl.ANY)
    whole = (blocks, last * HALF, FN)
    shapes = [jax.ShapeDtypeStruct(whole, jnp.bfloat16)]
    if others[2]:
        shapes = [jax.ShapeDtypeStruct((size, FN), jnp.bfloat16) for size in (2 * ONE, WIDE, WIDE, 2 * ONE)]
    values = [piece[0] for piece in pieces]
    return pl.pallas_call(
        functools.partial(
            march_kernel,
            number,
            [piece[1:] for piece in pieces],
            others,
            plan,
            blocks,
            positions,
            grow,
            len(raw),
        ),
        out_shape=shapes,
        in_specs=[pl.BlockSpec(memory_space=pltpu.SMEM), vmem, away]
        + [vmem] * (len(values) + len(raw) + len(ahead))
        + [away] * len(others[0]),
        out_specs=[vmem] * len(shapes),
        scratch_shapes=[pltpu.VMEM((blocks, most * HALF, FN), jnp.float32)] * 2
        + [
            pltpu.VMEM((STATIONS, FN, FN), jnp.bfloat16),
            pltpu.VMEM(whole if others[2] else (1, 16, FN), jnp.bfloat16),
            pltpu.SemaphoreType.DMA((STATIONS,)),
        ],
        compiler_params=pltpu.CompilerParams(vmem_limit_bytes=GRANT),
        cost_estimate=pl.CostEstimate(
            flops=2 * blocks * HALF * sum(counts) * FN * FN,
            bytes_accessed=2 * STATIONS * FN * FN,
            transcendentals=0,
        ),
    )(turn, coupling, inverse_blocks, *values, *raw, *ahead, *others[0])


def ship_kernel(
    number, turn, share, below, raw, crossed, edge_cross, edge_same, direct, kept, turned, whole
):
    side, kind = turn[1], turn[2]

    def turn_over(source):
        rows = ordered(source[...])
        for half in range(2):
            turned[half, :, :] = rows[half * ONE : (half + 1) * ONE]

    @pl.when(turn[0] == number)
    def _():
        turn_over(below)
        whole[...] = share[...]
        kept[...] = share[...]
        middle = share[:, EDGE : EDGE + ONE, :].astype(jnp.float32) + turned[...]
        whole[:, EDGE : EDGE + ONE, :] = middle.astype(jnp.bfloat16)
        start = pl.multiple_of(side * ONE, ONE)
        edge_cross[...] = whole[1 - side, pl.ds(start, WIDE), :]
        edge_same[...] = whole[side, pl.ds(start, WIDE), :]
        crossed[...] = whole[1 - side]
        direct[...] = whole[side]

    @pl.when(kind >= 2)
    def _():
        turn_over(raw)
        kept[:, :ONE, :] = turned[...].astype(jnp.bfloat16)

    @pl.when(kind == 2)
    def _():
        crossed[:ONE, :] = kept[1 - side, :ONE, :]

    @pl.when(kind == 3)
    def _():
        for half in range(2):
            edge_cross[half * EDGE : (half + 1) * EDGE, :] = kept[half, ONE - EDGE : ONE, :]
            edge_same[half * EDGE : (half + 1) * EDGE, :] = kept[half, :EDGE, :]


def hold_kernel(turn, weights, ahead, sem):
    @pl.when(turn[2] >= 1)
    def _():
        copy = pltpu.make_async_copy(weights.at[STATIONS - 1], ahead, sem)
        copy.start()
        copy.wait()


def center_kernel(number, turn, direct, crossed, edge_same, edge_cross, out):
    @pl.when(turn[0] == number)
    def _():
        side = turn[1]
        start = pl.multiple_of(side * EDGE, EDGE)
        from_edge = pl.multiple_of((1 - side) * EDGE, EDGE)
        for block, share, edge in ((side, direct, edge_same), (1 - side, crossed, edge_cross)):
            out[block, :, :] = share[EDGE : EDGE + ONE, :]
            here = out[block, pl.ds(start, EDGE), :].astype(jnp.float32)
            more = edge[pl.ds(from_edge, EDGE), :].astype(jnp.float32)
            out[block, pl.ds(start, EDGE), :] = (here + more).astype(jnp.bfloat16)


def gram_kernel(numbers, turn, *refs):
    inputs, (rows, gram, edges, sems) = refs[: 7 * len(numbers)], refs[7 * len(numbers) :]
    side = turn[1]

    def fetch(*pairs):
        copies = [pltpu.make_async_copy(source, target, sems.at[at]) for at, (source, target) in enumerate(pairs)]
        for copy in copies:
            copy.start()
        for copy in copies:
            copy.wait()

    for at, number in enumerate(numbers):
        share, low, high, state, crossed, back, last = inputs[7 * at : 7 * at + 7]

        @pl.when(turn[0] == number)
        def _():
            halves = [slice(0, EDGE), slice(EDGE, 2 * EDGE)]
            fetch(
                *[(share.at[half, EDGE : EDGE + ONE], rows.at[half]) for half in range(2)],
                *[(low.at[halves[half]], edges.at[half, :EDGE]) for half in range(2)],
                *[(high.at[halves[half]], edges.at[half, EDGE:]) for half in range(2)],
            )
            rows[...] = (rows[...].astype(jnp.float32) + edges[...].astype(jnp.float32)).astype(jnp.bfloat16)

        @pl.when(turn[0] == number - 1)
        def _():
            start = pl.multiple_of(side * ONE, ONE)
            fetch((state.at[0, pl.ds(start, ONE)], rows.at[side]), (crossed.at[:ONE], rows.at[1 - side]))

        @pl.when(turn[0] == number - 2)
        def _():
            fetch((back, rows))

        @pl.when(turn[0] == number - 3)
        def _():
            fetch((last, rows))

    flat = rows[...].reshape(2 * ONE, FN)
    full = lax.dot_general(flat, flat, (((1,), (1,)), ((), ())), preferred_element_type=jnp.float32)
    lines = []
    for first in range(2):
        line = []
        for second in range(2):
            block = None
            for point in range(POINTS):
                down, along = first * ONE + point * HALF, second * ONE + point * HALF
                term = full[down : down + HALF, along : along + HALF]
                block = term if block is None else block + term
            line.append(block)
        lines.append(jnp.concatenate(line, 1))
    total = jnp.concatenate(lines, 0)
    gram[...] = total


def factor_kernel(scale, first, second, rows, by_column, by_place, same_point, basis, upper):
    eye = (
        lax.broadcasted_iota(jnp.int32, (K, K), 0) == lax.broadcasted_iota(jnp.int32, (K, K), 1)
    ).astype(jnp.float32)
    table = jnp.concatenate([(first[...] + second[...]) * scale, eye], 1)
    row_index = lax.broadcasted_iota(jnp.int32, (K, 2 * K), 0)
    roots = jnp.zeros((K, 2 * K), jnp.float32)
    for j in range(0, K, STEP):
        lines = [table[j + m : j + m + 1, :] for m in range(STEP)]
        columns = [jnp.broadcast_to(table[:, j + m : j + m + 1], table.shape) for m in range(STEP)]
        entries = [
            [jnp.broadcast_to(lines[m][:, j + k : j + k + 1], lines[m].shape) for k in range(STEP)]
            for m in range(STEP)
        ]
        below = table
        for m in range(STEP):
            inverse = 1.0 / entries[m][m]
            for k in range(m + 1, STEP):
                ratio = entries[m][k] * inverse
                for n in range(k, STEP):
                    entries[k][n] = entries[k][n] - ratio * entries[m][n]
                lines[k] = lines[k] - ratio * lines[m]
                columns[k] = columns[k] - ratio * columns[m]
            below = below - columns[m] * (inverse * lines[m])
            roots = jnp.where(row_index == j + m, lax.rsqrt(entries[m][m]), roots)
        table = jnp.where(row_index >= j + STEP, below, table)
        for m in range(STEP):
            table = jnp.where(row_index == j + m, lines[m], table)
    table = table * roots
    column = lax.broadcasted_iota(jnp.int32, (K, K), 1)
    row = lax.broadcasted_iota(jnp.int32, (K, K), 0)
    upper[...] = jnp.where(column >= row, table[:, :K], 0.0)
    inverse = table[:, K:]
    terms = []
    for _ in range(2):
        term = inverse.astype(jnp.bfloat16)
        inverse = inverse - term.astype(jnp.float32)
        tall = lax.dot_general(
            by_column[...], term, (((1,), (1,)), ((), ())), preferred_element_type=jnp.float32
        ).astype(jnp.bfloat16)
        spread = lax.dot_general(
            tall, by_place[...], (((1,), (0,)), ((), ())), preferred_element_type=jnp.float32
        )
        terms.append((spread * same_point[...]).astype(jnp.bfloat16))
    both = lax.dot_general(
        rows[...], jnp.concatenate(terms, 1), (((0,), (0,)), ((), ())), preferred_element_type=jnp.float32
    )
    total = both[:, : POINTS * K] + both[:, POINTS * K :]
    basis[...] = total.astype(jnp.bfloat16)


def local(inverse_blocks, coupling, sources):
    sections = lax.axis_size("section")
    spans = lax.axis_size("span")
    pairs = spans // 2
    assert sections % 4 == 0 and spans % 2 == 0 and sources.shape[2] == POINTS * K
    group = lax.axis_index("section")
    side = (lax.axis_index("span") % 2).astype(jnp.int32)

    def send(value, *legs):
        routes = []
        for groups, down, route in legs:
            for g in groups:
                for s in range(spans):
                    routes.append((g * spans + s, (g - down) % sections * spans + route(s)))
        return lax.ppermute(value, AXES, routes)

    def straight(s):
        return s

    def partner(s):
        return s ^ 1

    def neighbor(shift):
        return lambda s: (s + shift) % spans

    def pair_route(pair, side):
        return (pair % pairs) * 2 + side

    def outward(s):
        return pair_route(s // 2 + 2 * (s % 2) - 1, s % 2)

    def outward_cross(s):
        return pair_route(s // 2 + 2 * (s % 2) - 1, 1 - s % 2)

    def inward(s):
        return pair_route(s // 2 + 1 - 2 * (s % 2), s % 2)

    def of_kind(kind):
        return [g for g in range(sections) if (sections - 1 - g) % 4 == kind]

    turn = jnp.stack([group.astype(jnp.int32), side, ((sections - 1 - group) % 4).astype(jnp.int32)])

    half, point, column = np.meshgrid(np.arange(2), np.arange(POINTS), np.arange(HALF), indexing="ij")
    row_column = (half * HALF + column).reshape(-1)
    row_point = point.reshape(-1)
    place = np.arange(POINTS * K)
    by_column = jnp.asarray(np.arange(K)[None, :] == row_column[:, None], jnp.bfloat16)
    by_place = jnp.asarray(np.arange(K)[:, None] == place[None, :] % K, jnp.bfloat16)
    same_point = jnp.asarray(place[None, :] // K == row_point[:, None], jnp.float32)

    smem = pl.BlockSpec(memory_space=pltpu.SMEM)
    vmem = pl.BlockSpec(memory_space=pltpu.VMEM)
    away = pl.BlockSpec(memory_space=pl.ANY)
    raw = sources[0]
    odds, evens = list(range(1, sections, 2)), list(range(0, sections, 2))
    below = send(raw, (evens, -1, straight), (odds, 1, straight))
    incoming = None
    pair_source = wide_source = ahead = None
    candidates = []
    for g in reversed(of_kind(0)):
        pieces = [] if incoming is None else [(incoming, lambda side: (0, 0), ONE, None)]
        (share,) = march(turn, g, inverse_blocks, coupling, pieces, 0, 2, POINTS, True, (raw,))
        crossed, edge_cross, edge_same, direct, kept = pl.pallas_call(
            functools.partial(ship_kernel, g),
            out_shape=[jax.ShapeDtypeStruct((size, FN), jnp.bfloat16) for size in (2 * ONE, WIDE, WIDE, 2 * ONE)]
            + [jax.ShapeDtypeStruct(share.shape, jnp.bfloat16)],
            in_specs=[smem, vmem, vmem, vmem],
            out_specs=[vmem] * 5,
            scratch_shapes=[pltpu.VMEM((2, ONE, FN), jnp.float32), pltpu.VMEM(share.shape, jnp.bfloat16)],
            compiler_params=pltpu.CompilerParams(vmem_limit_bytes=SMALL),
        )(turn, share, below, raw)
        first = incoming is None
        edge_cross = send(edge_cross, ([g], 1, outward_cross), (of_kind(3) if first else [], 0, neighbor(1)))
        crossed = send(crossed, ([g], 1, partner), (of_kind(2) if first else [], 0, partner))
        edge_same = send(edge_same, ([g], 1, outward), (of_kind(3) if first else [], 0, neighbor(-1)))
        direct = send(direct, ([g], 1, straight))
        if first:
            later, _ = lax.optimization_barrier((turn, kept))
            ahead = pl.pallas_call(
                hold_kernel,
                out_shape=jax.ShapeDtypeStruct((FN, FN), jnp.bfloat16),
                in_specs=[smem, away],
                out_specs=vmem,
                scratch_shapes=[pltpu.SemaphoreType.DMA],
                compiler_params=pltpu.CompilerParams(vmem_limit_bytes=GRANT),
            )(later, inverse_blocks)
            pair_source = [
                (kept, lambda side: (0, side * ONE), ONE, lambda side: side),
                (crossed, lambda side: (0, (1 - side) * ONE), ONE, None),
            ]
            wide_source = [
                (edge_cross.reshape(2, EDGE, FN), lambda side: (0, 0), EDGE, None),
                (kept, lambda side: (0, EDGE), ONE, None),
                (edge_same.reshape(2, EDGE, FN), lambda side: (0, EDGE + ONE), EDGE, None),
            ]

        (state,) = march(
            turn,
            g - 1,
            inverse_blocks,
            coupling,
            [
                (crossed, lambda side: (0, (1 - side) * ONE), 2 * ONE, None),
                (edge_cross, lambda side: (0, side * 2 * ONE), WIDE, None),
                (edge_same, lambda side: (0, (1 - side) * 2 * ONE), WIDE, None),
                (direct, lambda side: (0, side * ONE), 2 * ONE, None),
            ],
            14,
            1,
            3 * POINTS,
            False,
            (),
            (ahead,),
        )
        arrived = send(state, (list(range(sections)), 1, straight))

        crossed, edge_cross, edge_same, direct = march(
            turn,
            g - 2,
            inverse_blocks,
            coupling,
            [(arrived, lambda side: (0, 0), 2 * ONE, None)] + pair_source,
            10,
            1,
            2 * POINTS,
            True,
            (),
            (ahead,),
            (
                (kept, state),
                (
                    (
                        0,
                        g,
                        (
                            (0, lambda side: 0, lambda side: EDGE + ONE, EDGE, 1, 0),
                            (0, lambda side: 1, lambda side: EDGE + ONE, EDGE, 1, EDGE),
                            (0, lambda side: 0, lambda side: 0, EDGE, 2, 0),
                            (0, lambda side: 1, lambda side: 0, EDGE, 2, EDGE),
                        ),
                    ),
                    (0, g - 1, ((1, lambda side: 0, lambda side: (1 - side) * ONE, ONE, 0, 0),)),
                ),
                (
                    lambda side: (1 - side) * ONE,
                    lambda side: side * 2 * ONE,
                    lambda side: (1 - side) * 2 * ONE,
                    lambda side: side * ONE,
                ),
            ),
        )
        edge_cross = send(edge_cross, ([g - 2], 1, outward_cross), ([g], 0, neighbor(1)))
        crossed = send(crossed, ([g - 2], 1, partner), ([g - 1], 0, partner))
        edge_same = send(edge_same, ([g - 2], 1, inward), ([g], 0, neighbor(-1)))
        direct = send(direct, ([g - 2], 1, straight))

        middle = pl.pallas_call(
            functools.partial(center_kernel, g - 3),
            out_shape=jax.ShapeDtypeStruct((2, ONE, FN), jnp.bfloat16),
            in_specs=[smem] + [vmem] * 4,
            out_specs=vmem,
            compiler_params=pltpu.CompilerParams(vmem_limit_bytes=SMALL),
        )(turn, direct, crossed, edge_same, edge_cross)
        back = send(middle, (evens, -1, straight), (odds, 1, straight))
        (last,) = march(
            turn,
            g - 3,
            inverse_blocks,
            coupling,
            [
                (crossed, lambda side: (1 - side, 0), 2 * ONE, None),
                (edge_cross, lambda side: (1 - side, side * ONE), WIDE, None),
                (edge_same, lambda side: (side, side * ONE), WIDE, None),
                (direct, lambda side: (side, 0), 2 * ONE, None),
            ]
            + wide_source,
            0,
            2,
            2 * POINTS,
            False,
            (),
            (ahead,),
        )
        candidates += [kept, edge_cross, edge_same, state, crossed, back, last]
        if g > 3:
            incoming = send(last, ([g - 3], 1, straight))

    rows, gram = pl.pallas_call(
        functools.partial(gram_kernel, list(reversed(of_kind(0)))),
        out_shape=(
            jax.ShapeDtypeStruct((2, ONE, FN), jnp.bfloat16),
            jax.ShapeDtypeStruct((K, K), jnp.float32),
        ),
        in_specs=[smem] + [away] * len(candidates),
        out_specs=(vmem, vmem),
        scratch_shapes=[pltpu.VMEM((2, ONE, FN), jnp.bfloat16), pltpu.SemaphoreType.DMA((6,))],
        compiler_params=pltpu.CompilerParams(vmem_limit_bytes=SMALL),
    )(turn, *candidates)
    stride = 1
    terms = [gram]
    while stride < spans:
        radix = 2 if stride == 1 else min(4, spans // stride)
        total = terms[0]
        for term in terms[1:]:
            total = total + term
        terms = [total] + [
            lax.ppermute(total, "span", [(s, s ^ (digit * stride)) for s in range(spans)])
            for digit in range(1, radix)
        ]
        if radix == 4:
            terms = [terms[0] + terms[1], terms[2] + terms[3]]
        stride *= radix

    basis, upper = pl.pallas_call(
        functools.partial(factor_kernel, 1.0 / float(FN * POINTS * spans)),
        out_shape=(
            jax.ShapeDtypeStruct((FN, POINTS * K), jnp.bfloat16),
            jax.ShapeDtypeStruct((K, K), jnp.float32),
        ),
        in_specs=[vmem] * 6,
        out_specs=(vmem, vmem),
        compiler_params=pltpu.CompilerParams(vmem_limit_bytes=SMALL),
    )(*terms, rows.reshape(POINTS * K, FN), by_column, by_place, same_point)
    return (basis[None], upper[None])


def solution(mesh):
    placed = (P("section", None, None), P("section", None), P("section", None, "span"))
    return jax.shard_map(
        local,
        mesh=mesh,
        in_specs=placed,
        out_specs=(P("section", None, "span"), P("section", None, None)),
        check_vma=False,
    )
```

```python
import functools

import jax
import jax.numpy as jnp
import numpy as np
from jax import lax
from jax.experimental import pallas as pl
from jax.experimental.pallas import tpu as pltpu
from jax.sharding import PartitionSpec as P

K = 48
STATIONS = 4
FN = 768
HALF = K // 2
POINTS = 8
ONE = POINTS * HALF
EDGE = STATIONS * HALF
WIDE = 2 * EDGE
STEP = 8
GRANT = 48 * 1024 * 1024
SMALL = 16 * 1024 * 1024
AXES = ("section", "span")


def one_hot_order():
    at = lax.broadcasted_iota(jnp.int32, (1, POINTS * K), 1)
    point = at * 1366 >> 16
    column = at - point * K
    half = (column >= HALF).astype(jnp.int32)
    target = half * (ONE - HALF) + point * HALF + column
    row = lax.broadcasted_iota(jnp.int32, (POINTS * K, POINTS * K), 0)
    return jnp.where(row == target, 1.0, 0.0).astype(jnp.bfloat16)


def ordered(raw):
    return lax.dot_general(one_hot_order(), raw, (((1,), (1,)), ((), ())), preferred_element_type=jnp.float32)


def march_kernel(number, places, others, plan, blocks, positions, grow, raw, turn, coupling, weights, *refs):
    refs = list(refs)
    pieces = [refs.pop(0) for _ in places]
    raws = [refs.pop(0) for _ in range(raw)]
    ahead = [] if raw else [refs.pop(0)]
    givers = [refs.pop(0) for _ in others[0]]
    outs, (first, second, held, result, sems) = refs[:-5], refs[-5:]
    if not others[2]:
        result = outs[0]
    else:
        outs = [None] + outs
    states = [first, second]
    order = list(reversed(range(STATIONS)))
    side = turn[1]

    @pl.when(turn[0] == number)
    def _():
        copies = [
            pltpu.make_async_copy(weights.at[station], held.at[step], sems.at[step])
            for step, station in enumerate(order)
        ]
        copies[1 if ahead else 0].start()
        margin = 2 * HALF if grow else 0
        if margin:
            empty = jnp.zeros((blocks, margin, FN), jnp.float32)
            first[:, :margin, :] = empty
            first[:, margin + positions * HALF : 2 * margin + positions * HALF, :] = empty

        def total(on):
            covers = []
            if raw:
                turned = ordered(raws[0][...])
                for half in range(2):
                    covers.append((half, 0, ONE, lambda low, high, at=half * ONE: turned[at + low : at + high]))
            for piece, (where, rows, pick) in zip(pieces, places):
                block, start = where(on)
                if pick is not None:
                    covers.append((block, start, rows, lambda low, high, p=piece, k=pick(on): p[k, low:high, :]))
                elif len(piece.shape) == 3:
                    for k in range(blocks):
                        covers.append((k, start, rows, lambda low, high, p=piece, k=k: p[k, low:high, :]))
                else:
                    covers.append((block, start, rows, lambda low, high, p=piece: p[low:high, :]))
            for block in range(blocks):
                here = [cover for cover in covers if cover[0] == block]
                bounds = {0, positions * HALF}
                for _, start, rows, _ in here:
                    bounds |= {start, start + rows}
                bounds = sorted(bounds)
                for low, high in zip(bounds, bounds[1:]):
                    value = jnp.zeros((high - low, FN), jnp.float32)
                    for _, start, rows, read in here:
                        if start <= low and high <= start + rows:
                            value = value + read(low - start, high - start).astype(jnp.float32)
                    first[block, margin + low : margin + high, :] = value

        if pieces:
            for on in range(2):
                pl.when(side == on)(functools.partial(total, on))
        else:
            total(0)

        def stencil(step, chunk):
            block, begin, end = chunk
            at, rows = begin * HALF, (end - begin) * HALF
            source = states[step % 2]
            rates = coupling[order[step] : order[step] + 1, :]
            both = source[block, at : at + rows, :] + source[block, at + 2 * HALF : at + 2 * HALF + rows, :]
            update = (1.0 - 2.0 * rates) * source[block, at + HALF : at + HALF + rows, :] + rates * both
            return update.astype(jnp.bfloat16)

        copies[2 if ahead else 1].start()
        jobs = [(step, chunk) for step in range(STATIONS) for chunk in plan[step]]
        update = stencil(*jobs[0])
        for at_job, (step, chunk) in enumerate(jobs):
            block, begin, end = chunk
            at, rows = begin * HALF, (end - begin) * HALF
            current = update
            if at_job + 1 < len(jobs):
                update = stencil(*jobs[at_job + 1])
            if chunk is plan[step][0]:
                if step or not ahead:
                    copies[step].wait()
                later = step + (3 if ahead else 2)
                if later < STATIONS:
                    copies[later].start()
            moved = lax.dot_general(
                current,
                ahead[0][...] if ahead and not step else held[step],
                (((1,), (1,)), ((), ())),
                preferred_element_type=jnp.float32,
            )
            if step == STATIONS - 1:
                result[block, at : at + rows, :] = moved.astype(jnp.bfloat16)
                continue
            target = states[1 - step % 2]
            target[block, margin + at : margin + at + rows, :] = moved
            if grow:
                empty = jnp.zeros((margin, FN), jnp.float32)
                count = max(last for place, _, last in plan[step] if place == block)
                if begin == 0:
                    target[block, :margin, :] = empty
                if end == count:
                    target[block, margin + count * HALF : 2 * margin + count * HALF, :] = empty
        for out, where in zip(outs[1:], others[2]):
            start = pl.multiple_of(where(side), EDGE)
            out[...] = result[0, pl.ds(start, out.shape[0]), :]

    relay(others[1], turn, givers, outs[1:], sems)


def relay(owners, turn, givers, outs, sems):
    side = turn[1]
    for slot, value, moves in owners:

        @pl.when(turn[slot] == value)
        def _():
            copies = []
            for at, (giver, block, start, rows, out, to) in enumerate(moves):
                start = start(side)
                if not isinstance(start, int):
                    start = pl.multiple_of(start, EDGE)
                source = givers[giver].at[block(side), pl.ds(start, rows)]
                copies.append(pltpu.make_async_copy(source, outs[out].at[pl.ds(to, rows)], sems.at[at]))
            for copy in copies:
                copy.start()
            for copy in copies:
                copy.wait()


def march(turn, number, inverse_blocks, coupling, pieces, cut, blocks, positions, grow, raw=(), ahead=(), others=((), (), ())):
    last = positions + (2 * STATIONS if grow else -2 * STATIONS)
    most = last + 2 if grow else positions
    counts = [positions + (2 if grow else -2) * (step + 1) for step in range(STATIONS)]
    if blocks == 2:
        plan = [[(0, 0, count), (1, 0, count)] for count in counts]
    else:
        cuts = [cut - (0 if grow else 2 * step) for step in range(STATIONS)]
        plan = [[(0, 0, at), (0, at, count)] for at, count in zip(cuts, counts)]
    vmem = pl.BlockSpec(memory_space=pltpu.VMEM)
    away = pl.BlockSpec(memory_space=pl.ANY)
    whole = (blocks, last * HALF, FN)
    shapes = [jax.ShapeDtypeStruct(whole, jnp.bfloat16)]
    if others[2]:
        shapes = [jax.ShapeDtypeStruct((size, FN), jnp.bfloat16) for size in (2 * ONE, WIDE, WIDE, 2 * ONE)]
    values = [piece[0] for piece in pieces]
    return pl.pallas_call(
        functools.partial(
            march_kernel,
            number,
            [piece[1:] for piece in pieces],
            others,
            plan,
            blocks,
            positions,
            grow,
            len(raw),
        ),
        out_shape=shapes,
        in_specs=[pl.BlockSpec(memory_space=pltpu.SMEM), vmem, away]
        + [vmem] * (len(values) + len(raw) + len(ahead))
        + [away] * len(others[0]),
        out_specs=[vmem] * len(shapes),
        scratch_shapes=[pltpu.VMEM((blocks, most * HALF, FN), jnp.float32)] * 2
        + [
            pltpu.VMEM((STATIONS, FN, FN), jnp.bfloat16),
            pltpu.VMEM(whole if others[2] else (1, 16, FN), jnp.bfloat16),
            pltpu.SemaphoreType.DMA((STATIONS,)),
        ],
        compiler_params=pltpu.CompilerParams(vmem_limit_bytes=GRANT),
        cost_estimate=pl.CostEstimate(
            flops=2 * blocks * HALF * sum(counts) * FN * FN,
            bytes_accessed=2 * STATIONS * FN * FN,
            transcendentals=0,
        ),
    )(turn, coupling, inverse_blocks, *values, *raw, *ahead, *others[0])


def ship_kernel(
    number, turn, share, below, raw, crossed, edge_cross, edge_same, direct, kept, turned, whole
):
    side, kind = turn[1], turn[2]

    def turn_over(source):
        rows = ordered(source[...])
        for half in range(2):
            turned[half, :, :] = rows[half * ONE : (half + 1) * ONE]

    @pl.when(turn[0] == number)
    def _():
        turn_over(below)
        whole[...] = share[...]
        kept[...] = share[...]
        middle = share[:, EDGE : EDGE + ONE, :].astype(jnp.float32) + turned[...]
        whole[:, EDGE : EDGE + ONE, :] = middle.astype(jnp.bfloat16)
        start = pl.multiple_of(side * ONE, ONE)
        edge_cross[...] = whole[1 - side, pl.ds(start, WIDE), :]
        edge_same[...] = whole[side, pl.ds(start, WIDE), :]
        crossed[...] = whole[1 - side]
        direct[...] = whole[side]

    @pl.when(kind >= 2)
    def _():
        turn_over(raw)
        kept[:, :ONE, :] = turned[...].astype(jnp.bfloat16)

    @pl.when(kind == 2)
    def _():
        crossed[:ONE, :] = kept[1 - side, :ONE, :]

    @pl.when(kind == 3)
    def _():
        for half in range(2):
            edge_cross[half * EDGE : (half + 1) * EDGE, :] = kept[half, ONE - EDGE : ONE, :]
            edge_same[half * EDGE : (half + 1) * EDGE, :] = kept[half, :EDGE, :]


def hold_kernel(turn, weights, ahead, sem):
    @pl.when(turn[2] >= 1)
    def _():
        copy = pltpu.make_async_copy(weights.at[STATIONS - 1], ahead, sem)
        copy.start()
        copy.wait()


def center_kernel(number, turn, direct, crossed, edge_same, edge_cross, out):
    @pl.when(turn[0] == number)
    def _():
        side = turn[1]
        start = pl.multiple_of(side * EDGE, EDGE)
        from_edge = pl.multiple_of((1 - side) * EDGE, EDGE)
        for block, share, edge in ((side, direct, edge_same), (1 - side, crossed, edge_cross)):
            out[block, :, :] = share[EDGE : EDGE + ONE, :]
            here = out[block, pl.ds(start, EDGE), :].astype(jnp.float32)
            more = edge[pl.ds(from_edge, EDGE), :].astype(jnp.float32)
            out[block, pl.ds(start, EDGE), :] = (here + more).astype(jnp.bfloat16)


def gram_kernel(numbers, turn, *refs):
    inputs, (rows, gram, edges, sems) = refs[: 7 * len(numbers)], refs[7 * len(numbers) :]
    side = turn[1]

    def fetch(*pairs):
        copies = [pltpu.make_async_copy(source, target, sems.at[at]) for at, (source, target) in enumerate(pairs)]
        for copy in copies:
            copy.start()
        for copy in copies:
            copy.wait()

    for at, number in enumerate(numbers):
        share, low, high, state, crossed, back, last = inputs[7 * at : 7 * at + 7]

        @pl.when(turn[0] == number)
        def _():
            halves = [slice(0, EDGE), slice(EDGE, 2 * EDGE)]
            fetch(
                *[(share.at[half, EDGE : EDGE + ONE], rows.at[half]) for half in range(2)],
                *[(low.at[halves[half]], edges.at[half, :EDGE]) for half in range(2)],
                *[(high.at[halves[half]], edges.at[half, EDGE:]) for half in range(2)],
            )
            rows[...] = (rows[...].astype(jnp.float32) + edges[...].astype(jnp.float32)).astype(jnp.bfloat16)

        @pl.when(turn[0] == number - 1)
        def _():
            start = pl.multiple_of(side * ONE, ONE)
            fetch((state.at[0, pl.ds(start, ONE)], rows.at[side]), (crossed.at[:ONE], rows.at[1 - side]))

        @pl.when(turn[0] == number - 2)
        def _():
            fetch((back, rows))

        @pl.when(turn[0] == number - 3)
        def _():
            fetch((last, rows))

    flat = rows[...].reshape(2 * ONE, FN)
    full = lax.dot_general(flat, flat, (((1,), (1,)), ((), ())), preferred_element_type=jnp.float32)
    lines = []
    for first in range(2):
        line = []
        for second in range(2):
            block = None
            for point in range(POINTS):
                down, along = first * ONE + point * HALF, second * ONE + point * HALF
                term = full[down : down + HALF, along : along + HALF]
                block = term if block is None else block + term
            line.append(block)
        lines.append(jnp.concatenate(line, 1))
    total = jnp.concatenate(lines, 0)
    gram[...] = total


def factor_kernel(scale, first, second, rows, by_column, by_place, same_point, basis, upper):
    eye = (
        lax.broadcasted_iota(jnp.int32, (K, K), 0) == lax.broadcasted_iota(jnp.int32, (K, K), 1)
    ).astype(jnp.float32)
    table = jnp.concatenate([(first[...] + second[...]) * scale, eye], 1)
    row_index = lax.broadcasted_iota(jnp.int32, (K, 2 * K), 0)
    roots = jnp.zeros((K, 2 * K), jnp.float32)
    for j in range(0, K, STEP):
        lines = [table[j + m : j + m + 1, :] for m in range(STEP)]
        columns = [jnp.broadcast_to(table[:, j + m : j + m + 1], table.shape) for m in range(STEP)]
        entries = [
            [jnp.broadcast_to(lines[m][:, j + k : j + k + 1], lines[m].shape) for k in range(STEP)]
            for m in range(STEP)
        ]
        below = table
        for m in range(STEP):
            inverse = 1.0 / entries[m][m]
            for k in range(m + 1, STEP):
                ratio = entries[m][k] * inverse
                for n in range(k, STEP):
                    entries[k][n] = entries[k][n] - ratio * entries[m][n]
                lines[k] = lines[k] - ratio * lines[m]
                columns[k] = columns[k] - ratio * columns[m]
            below = below - columns[m] * (inverse * lines[m])
            roots = jnp.where(row_index == j + m, lax.rsqrt(entries[m][m]), roots)
        table = jnp.where(row_index >= j + STEP, below, table)
        for m in range(STEP):
            table = jnp.where(row_index == j + m, lines[m], table)
    table = table * roots
    column = lax.broadcasted_iota(jnp.int32, (K, K), 1)
    row = lax.broadcasted_iota(jnp.int32, (K, K), 0)
    upper[...] = jnp.where(column >= row, table[:, :K], 0.0)
    inverse = table[:, K:]
    terms = []
    for _ in range(2):
        term = inverse.astype(jnp.bfloat16)
        inverse = inverse - term.astype(jnp.float32)
        tall = lax.dot_general(
            by_column[...], term, (((1,), (1,)), ((), ())), preferred_element_type=jnp.float32
        ).astype(jnp.bfloat16)
        spread = lax.dot_general(
            tall, by_place[...], (((1,), (0,)), ((), ())), preferred_element_type=jnp.float32
        )
        terms.append((spread * same_point[...]).astype(jnp.bfloat16))
    both = lax.dot_general(
        rows[...], jnp.concatenate(terms, 1), (((0,), (0,)), ((), ())), preferred_element_type=jnp.float32
    )
    total = both[:, : POINTS * K] + both[:, POINTS * K :]
    basis[...] = total.astype(jnp.bfloat16)


def local(inverse_blocks, coupling, sources):
    sections = lax.axis_size("section")
    spans = lax.axis_size("span")
    pairs = spans // 2
    assert sections % 4 == 0 and spans % 2 == 0 and sources.shape[2] == POINTS * K
    group = lax.axis_index("section")
    side = (lax.axis_index("span") % 2).astype(jnp.int32)

    def send(value, *legs):
        routes = []
        for groups, down, route in legs:
            for g in groups:
                for s in range(spans):
                    routes.append((g * spans + s, (g - down) % sections * spans + route(s)))
        return lax.ppermute(value, AXES, routes)

    def straight(s):
        return s

    def partner(s):
        return s ^ 1

    def neighbor(shift):
        return lambda s: (s + shift) % spans

    def pair_route(pair, side):
        return (pair % pairs) * 2 + side

    def outward(s):
        return pair_route(s // 2 + 2 * (s % 2) - 1, s % 2)

    def outward_cross(s):
        return pair_route(s // 2 + 2 * (s % 2) - 1, 1 - s % 2)

    def inward(s):
        return pair_route(s // 2 + 1 - 2 * (s % 2), s % 2)

    def of_kind(kind):
        return [g for g in range(sections) if (sections - 1 - g) % 4 == kind]

    turn = jnp.stack([group.astype(jnp.int32), side, ((sections - 1 - group) % 4).astype(jnp.int32)])

    half, point, column = np.meshgrid(np.arange(2), np.arange(POINTS), np.arange(HALF), indexing="ij")
    row_column = (half * HALF + column).reshape(-1)
    row_point = point.reshape(-1)
    place = np.arange(POINTS * K)
    by_column = jnp.asarray(np.arange(K)[None, :] == row_column[:, None], jnp.bfloat16)
    by_place = jnp.asarray(np.arange(K)[:, None] == place[None, :] % K, jnp.bfloat16)
    same_point = jnp.asarray(place[None, :] // K == row_point[:, None], jnp.float32)

    smem = pl.BlockSpec(memory_space=pltpu.SMEM)
    vmem = pl.BlockSpec(memory_space=pltpu.VMEM)
    away = pl.BlockSpec(memory_space=pl.ANY)
    raw = sources[0]
    odds, evens = list(range(1, sections, 2)), list(range(0, sections, 2))
    below = send(raw, (evens, -1, straight), (odds, 1, straight))
    incoming = None
    pair_source = wide_source = ahead = None
    candidates = []
    for g in reversed(of_kind(0)):
        pieces = [] if incoming is None else [(incoming, lambda side: (0, 0), ONE, None)]
        (share,) = march(turn, g, inverse_blocks, coupling, pieces, 0, 2, POINTS, True, (raw,))
        crossed, edge_cross, edge_same, direct, kept = pl.pallas_call(
            functools.partial(ship_kernel, g),
            out_shape=[jax.ShapeDtypeStruct((size, FN), jnp.bfloat16) for size in (2 * ONE, WIDE, WIDE, 2 * ONE)]
            + [jax.ShapeDtypeStruct(share.shape, jnp.bfloat16)],
            in_specs=[smem, vmem, vmem, vmem],
            out_specs=[vmem] * 5,
            scratch_shapes=[pltpu.VMEM((2, ONE, FN), jnp.float32), pltpu.VMEM(share.shape, jnp.bfloat16)],
            compiler_params=pltpu.CompilerParams(vmem_limit_bytes=SMALL),
        )(turn, share, below, raw)
        first = incoming is None
        edge_cross = send(edge_cross, ([g], 1, outward_cross), (of_kind(3) if first else [], 0, neighbor(1)))
        crossed = send(crossed, ([g], 1, partner), (of_kind(2) if first else [], 0, partner))
        edge_same = send(edge_same, ([g], 1, outward), (of_kind(3) if first else [], 0, neighbor(-1)))
        direct = send(direct, ([g], 1, straight))
        if first:
            later, _ = lax.optimization_barrier((turn, kept))
            ahead = pl.pallas_call(
                hold_kernel,
                out_shape=jax.ShapeDtypeStruct((FN, FN), jnp.bfloat16),
                in_specs=[smem, away],
                out_specs=vmem,
                scratch_shapes=[pltpu.SemaphoreType.DMA],
                compiler_params=pltpu.CompilerParams(vmem_limit_bytes=GRANT),
            )(later, inverse_blocks)
            pair_source = [
                (kept, lambda side: (0, side * ONE), ONE, lambda side: side),
                (crossed, lambda side: (0, (1 - side) * ONE), ONE, None),
            ]
            wide_source = [
                (edge_cross.reshape(2, EDGE, FN), lambda side: (0, 0), EDGE, None),
                (kept, lambda side: (0, EDGE), ONE, None),
                (edge_same.reshape(2, EDGE, FN), lambda side: (0, EDGE + ONE), EDGE, None),
            ]

        (state,) = march(
            turn,
            g - 1,
            inverse_blocks,
            coupling,
            [
                (crossed, lambda side: (0, (1 - side) * ONE), 2 * ONE, None),
                (edge_cross, lambda side: (0, side * 2 * ONE), WIDE, None),
                (edge_same, lambda side: (0, (1 - side) * 2 * ONE), WIDE, None),
                (direct, lambda side: (0, side * ONE), 2 * ONE, None),
            ],
            12,
            1,
            3 * POINTS,
            False,
            (),
            (ahead,),
        )
        arrived = send(state, (list(range(sections)), 1, straight))

        crossed, edge_cross, edge_same, direct = march(
            turn,
            g - 2,
            inverse_blocks,
            coupling,
            [(arrived, lambda side: (0, 0), 2 * ONE, None)] + pair_source,
            10,
            1,
            2 * POINTS,
            True,
            (),
            (ahead,),
            (
                (kept, state),
                (
                    (
                        0,
                        g,
                        (
                            (0, lambda side: 0, lambda side: EDGE + ONE, EDGE, 1, 0),
                            (0, lambda side: 1, lambda side: EDGE + ONE, EDGE, 1, EDGE),
                            (0, lambda side: 0, lambda side: 0, EDGE, 2, 0),
                            (0, lambda side: 1, lambda side: 0, EDGE, 2, EDGE),
                        ),
                    ),
                    (0, g - 1, ((1, lambda side: 0, lambda side: (1 - side) * ONE, ONE, 0, 0),)),
                ),
                (
                    lambda side: (1 - side) * ONE,
                    lambda side: side * 2 * ONE,
                    lambda side: (1 - side) * 2 * ONE,
                    lambda side: side * ONE,
                ),
            ),
        )
        edge_cross = send(edge_cross, ([g - 2], 1, outward_cross), ([g], 0, neighbor(1)))
        crossed = send(crossed, ([g - 2], 1, partner), ([g - 1], 0, partner))
        edge_same = send(edge_same, ([g - 2], 1, inward), ([g], 0, neighbor(-1)))
        direct = send(direct, ([g - 2], 1, straight))

        middle = pl.pallas_call(
            functools.partial(center_kernel, g - 3),
            out_shape=jax.ShapeDtypeStruct((2, ONE, FN), jnp.bfloat16),
            in_specs=[smem] + [vmem] * 4,
            out_specs=vmem,
            compiler_params=pltpu.CompilerParams(vmem_limit_bytes=SMALL),
        )(turn, direct, crossed, edge_same, edge_cross)
        back = send(middle, (evens, -1, straight), (odds, 1, straight))
        (last,) = march(
            turn,
            g - 3,
            inverse_blocks,
            coupling,
            [
                (crossed, lambda side: (1 - side, 0), 2 * ONE, None),
                (edge_cross, lambda side: (1 - side, side * ONE), WIDE, None),
                (edge_same, lambda side: (side, side * ONE), WIDE, None),
                (direct, lambda side: (side, 0), 2 * ONE, None),
            ]
            + wide_source,
            0,
            2,
            2 * POINTS,
            False,
            (),
            (ahead,),
        )
        candidates += [kept, edge_cross, edge_same, state, crossed, back, last]
        if g > 3:
            incoming = send(last, ([g - 3], 1, straight))

    rows, gram = pl.pallas_call(
        functools.partial(gram_kernel, list(reversed(of_kind(0)))),
        out_shape=(
            jax.ShapeDtypeStruct((2, ONE, FN), jnp.bfloat16),
            jax.ShapeDtypeStruct((K, K), jnp.float32),
        ),
        in_specs=[smem] + [away] * len(candidates),
        out_specs=(vmem, vmem),
        scratch_shapes=[pltpu.VMEM((2, ONE, FN), jnp.bfloat16), pltpu.SemaphoreType.DMA((6,))],
        compiler_params=pltpu.CompilerParams(vmem_limit_bytes=SMALL),
    )(turn, *candidates)
    stride = 1
    terms = [gram]
    while stride < spans:
        radix = 2 if stride == 1 else min(4, spans // stride)
        total = terms[0]
        for term in terms[1:]:
            total = total + term
        terms = [total] + [
            lax.ppermute(total, "span", [(s, s ^ (digit * stride)) for s in range(spans)])
            for digit in range(1, radix)
        ]
        if radix == 4:
            terms = [terms[0] + terms[1], terms[2] + terms[3]]
        stride *= radix

    basis, upper = pl.pallas_call(
        functools.partial(factor_kernel, 1.0 / float(FN * POINTS * spans)),
        out_shape=(
            jax.ShapeDtypeStruct((FN, POINTS * K), jnp.bfloat16),
            jax.ShapeDtypeStruct((K, K), jnp.float32),
        ),
        in_specs=[vmem] * 6,
        out_specs=(vmem, vmem),
        compiler_params=pltpu.CompilerParams(vmem_limit_bytes=SMALL),
    )(*terms, rows.reshape(POINTS * K, FN), by_column, by_place, same_point)
    return (basis[None], upper[None])


def solution(mesh):
    placed = (P("section", None, None), P("section", None), P("section", None, "span"))
    return jax.shard_map(
        local,
        mesh=mesh,
        in_specs=placed,
        out_specs=(P("section", None, "span"), P("section", None, None)),
        check_vma=False,
    )
```
